32 devices in a mesh: seq: 8 (over z, x), doc: 4 (over y, core).
Axes of the slice: x: 2, y: 2, z: 4, core: 2. Of those that a mesh axis runs over, the one named last changes fastest.
Arguments:
- arriving_features: bfloat16 [8, 1024, 1024], P('doc', 'seq'), may hold values from -6 to 6
- valid_extents: int32 [8], P('doc'), may hold values from 256 to 1024, as said below
- sampled_target_tiles: int32 [8, 16, 16, 3], P('doc'), may hold values from 0 to 15
- query_context_mapping: bfloat16 [1024, 3072], P(('seq', 'doc')), may hold values from -0.1875 to 0.1875
- attention_outflow_weights: bfloat16 [1024, 1024], P(('seq', 'doc')), may hold values from -1.5 to 1.5
- expansion_weights: bfloat16 [1024, 4096], P(('seq', 'doc')), may hold values from -0.1875 to 0.1875
- contraction_weights: bfloat16 [4096, 1024], P(('seq', 'doc')), may hold values from -0.09375 to 0.09375
- opening_scale_vector: bfloat16 [1024], P(('seq', 'doc')), may hold values from 0.5 to 1.5
- opening_shift_vector: bfloat16 [1024], P(('seq', 'doc')), may hold values from -1 to 1
- closing_scale_vector: bfloat16 [1024], P(('seq', 'doc')), may hold values from 0.5 to 1.5
- closing_shift_vector: bfloat16 [1024], P(('seq', 'doc')), may hold values from -1 to 1
- expansion_shift: bfloat16 [4096], P(('seq', 'doc')), may hold values from -1 to 1
- contraction_shift: bfloat16 [1024], P(('seq', 'doc')), may hold values from -1.5 to 1.5
- output_sensitivity: bfloat16 [8, 1024, 1024], P('doc', 'seq'), may hold values from -6 to 6
Outputs:
- output: bfloat16 [8, 1024, 1024], P('doc', 'seq')
- grad_inputs: float32 [8, 1024, 1024], P('doc', 'seq')
- inward_grad: float32 [1024, 3072], P(('seq', 'doc'))
- outward_grad: float32 [1024, 1024], P(('seq', 'doc'))
- expand_grad: float32 [1024, 4096], P(('seq', 'doc'))
- contract_grad: float32 [4096, 1024], P(('seq', 'doc'))
- leading_gain_sensitivity: float32 [1024], P(('seq', 'doc'))
- leading_offset_sensitivity: float32 [1024], P(('seq', 'doc'))
- midscale_grad: float32 [1024], P(('seq', 'doc'))
- midshift_grad: float32 [1024], P(('seq', 'doc'))
- upshift_grad: float32 [4096], P(('seq', 'doc'))
- downshift_grad: float32 [1024], P(('seq', 'doc'))
The draws below stay inside these ranges and needn't reach their ends.
Inputs may be any that keep to these rules, and one draw needn't show every extreme that they name: `valid_extents`: of the 2 documents on each index of doc (that many in a row), one has length 1024.
All inputs are finite; a program needn't handle non-finite values.
Results may differ from the reference program's by a relative error of at most 0.014.
Values may be sent and summed in bfloat16 or wider, within the bound.
A program may use at most 512 MiB of HBM per device.

```python
import jax
import jax.numpy as jnp
from jax import lax

HIDDEN_SIZE = 1024
HEADS = 16
HEAD = 64
FF = 4096
BLOCK = 64
RANDOM = 3
SEQ_GRP = 2
SLOT = 1024
NB = 16
DOCS = 8


def draw_valid_extents(key, part):
    key = jax.random.fold_in(key, 7)
    base_key, pick_key = jax.random.split(key)
    drawn = jax.random.randint(base_key, (DOCS,), SLOT // 4, SLOT + 1, dtype=jnp.int32)
    picked = jax.random.randint(pick_key, (DOCS // SEQ_GRP,), 0, SEQ_GRP, dtype=jnp.int32)
    members = jnp.arange(DOCS, dtype=jnp.int32)
    longest = members % SEQ_GRP == jnp.repeat(picked, SEQ_GRP)
    return jnp.where(longest, SLOT, drawn).astype(jnp.int32)


def place_ends(values, own_key, low, largest):
    spot = [jax.random.randint(jax.random.fold_in(own_key, axis), (), 0, length) for axis, length in enumerate(values.shape)]
    widest = values.shape.index(max(values.shape))
    next_to = spot[:widest] + [(spot[widest] + 1) % values.shape[widest]] + spot[widest + 1:]
    return values.at[tuple(spot)].set(low).at[tuple(next_to)].set(largest)


def levels(stream_key, shape, shards, least, top_value):
    def one(position, parts):
        draws = jax.random.uniform(jax.random.fold_in(jax.random.fold_in(stream_key, 6), position), (parts,), jnp.float32, least / len(shards), top_value / len(shards))
        return jnp.repeat(jnp.exp(draws), shape[position] // parts).reshape((-1,) + (1,) * (len(shape) - position - 1))

    gain = one(*shards[0])
    for cut in shards[1:]:
        gain = gain * one(*cut)
    return gain


def gaussian(stream_key, extent, width, most, shards=(), kind=jnp.bfloat16):
    entries = width * jax.random.normal(stream_key, extent, jnp.float32)
    if shards:
        entries = entries * levels(stream_key, extent, shards, -0.22, 0.18)
    return jnp.clip(entries, -most, most).astype(kind)


def setup_inputs(seed: int = 0) -> dict:
    arg_keys = jax.random.split(jax.random.key(seed), 15)
    return {
        "arriving_features": gaussian(arg_keys[0], (DOCS, SLOT, HIDDEN_SIZE), 1.0, 6.0, ((0, 4), (1, 8))),
        "valid_extents": draw_valid_extents(jax.random.fold_in(arg_keys[14], 71), 0),
        "sampled_target_tiles": place_ends(jax.random.randint(arg_keys[2], (DOCS, HEADS, NB, RANDOM), 0, NB), jax.random.fold_in(arg_keys[2], 1), 0, NB - 1).astype(jnp.int32),
        "query_context_mapping": gaussian(arg_keys[3], (HIDDEN_SIZE, 3 * HIDDEN_SIZE), HIDDEN_SIZE ** -0.5, 0.1875, ((0, 32),)),
        "attention_outflow_weights": gaussian(arg_keys[4], (HIDDEN_SIZE, HIDDEN_SIZE), (HIDDEN_SIZE // 64) ** -0.5, 1.5, ((0, 32),)),
        "expansion_weights": gaussian(arg_keys[5], (HIDDEN_SIZE, FF), HIDDEN_SIZE ** -0.5, 0.1875, ((0, 32),)),
        "contraction_weights": gaussian(arg_keys[6], (FF, HIDDEN_SIZE), FF ** -0.5, 0.09375, ((0, 32),)),
        "opening_scale_vector": jnp.clip(1.0 + 0.1 * jax.random.normal(arg_keys[7], (HIDDEN_SIZE,), jnp.float32), 0.5, 1.5).astype(jnp.bfloat16),
        "opening_shift_vector": gaussian(arg_keys[8], (HIDDEN_SIZE,), 0.2, 1.0, ((0, 32),)),
        "closing_scale_vector": jnp.clip(1.0 + 0.1 * jax.random.normal(arg_keys[9], (HIDDEN_SIZE,), jnp.float32), 0.5, 1.5).astype(jnp.bfloat16),
        "closing_shift_vector": gaussian(arg_keys[10], (HIDDEN_SIZE,), 0.2, 1.0, ((0, 32),)),
        "expansion_shift": gaussian(arg_keys[11], (FF,), 0.2, 1.0, ((0, 32),)),
        "contraction_shift": gaussian(arg_keys[12], (HIDDEN_SIZE,), 0.3, 1.5, ((0, 32),)),
        "output_sensitivity": gaussian(arg_keys[13], (DOCS, SLOT, HIDDEN_SIZE), 1.0, 6.0, ((0, 4), (1, 8))),
    }


epsilon = 1e-05
negative = -1e+30
highest = lax.Precision.HIGHEST

@jax.custom_vjp
def variance_epsilon_guard(v):
    return lax.optimization_barrier(v.astype(jnp.bfloat16)).astype(jnp.float32)

@jax.custom_vjp
def reduced_reverse(v):
    return v

def low_keep(v):
    return (variance_epsilon_guard(v), None)

def low_pass(kept, grad):
    return (grad,)

def back_keep(v):
    return (v, None)

def back_low(kept, grad):
    return (variance_epsilon_guard(grad),)
variance_epsilon_guard.defvjp(low_keep, low_pass)
reduced_reverse.defvjp(back_keep, back_low)

def multiplied_result(left, right):
    return jnp.dot(left, right, precision=highest, preferred_element_type=jnp.float32)

def normalise_each_line(values, scaling, shifting):
    centered = values - lax.optimization_barrier(jnp.mean(values, axis=-1, keepdims=True))
    inverse = lax.rsqrt(lax.optimization_barrier(jnp.mean(centered * centered, axis=-1, keepdims=True)) + epsilon)
    return centered * inverse * scaling + shifting

def head_attention(query_head, key_head, value_head, random_head, span_number):
    block_count = SLOT // BLOCK
    scale = HEAD ** (-0.5)
    blocks = jnp.arange(block_count, dtype=jnp.int32)
    last_block = (span_number - 1) // BLOCK
    near_cols = jnp.stack([blocks - 1, blocks, blocks + 1], axis=1)
    global_cols = jnp.stack([jnp.zeros_like(blocks), jnp.zeros_like(blocks) + last_block], axis=1)
    candidates = jnp.concatenate([near_cols, random_head.astype(jnp.int32), global_cols], axis=1)
    cand_count = candidates.shape[1]
    inside = (candidates >= 0) & (candidates < block_count)
    earlier = jnp.arange(cand_count)[:, None] > jnp.arange(cand_count)[None, :]
    repeated = jnp.any((candidates[:, :, None] == candidates[:, None, :]) & earlier[None], axis=2)
    usable = inside & jnp.logical_not(repeated)
    clipped = jnp.clip(candidates, 0, block_count - 1)
    key_blocks = key_head.reshape(block_count, BLOCK, HEAD)[clipped]
    value_blocks = value_head.reshape(block_count, BLOCK, HEAD)[clipped]
    places = clipped[:, :, None] * BLOCK + jnp.arange(BLOCK, dtype=jnp.int32)[None, None, :]
    keep_mask = usable[:, :, None] & (places < span_number)
    query_blocks = query_head.reshape(block_count, BLOCK, HEAD)
    scores = reduced_reverse(jnp.einsum('ntd,nckd->ntck', query_blocks, key_blocks, precision=highest) * scale)
    scores = jnp.where(keep_mask[:, None, :, :], scores, negative).reshape(block_count, BLOCK, cand_count * BLOCK)
    chances = variance_epsilon_guard(jax.nn.softmax(scores, axis=-1))
    mixed = jnp.einsum('ntm,nmd->ntd', chances, value_blocks.reshape(block_count, cand_count * BLOCK, HEAD), precision=highest)
    edge_rows = jnp.stack([query_blocks[0], query_blocks[last_block]])
    wide_scores = reduced_reverse(jnp.einsum('etd,kd->etk', edge_rows, key_head, precision=highest) * scale)
    valid_keys = jnp.arange(SLOT, dtype=jnp.int32) < span_number
    wide_scores = jnp.where(valid_keys[None, None, :], wide_scores, negative)
    wide_chances = variance_epsilon_guard(jax.nn.softmax(wide_scores, axis=-1))
    wide_mixed = jnp.einsum('etk,kd->etd', wide_chances, value_head, precision=highest)
    mixed = mixed.at[0].set(wide_mixed[0]).at[last_block].set(wide_mixed[1])
    return mixed.reshape(SLOT, HEAD)

def thinned_attention_unit(shortcut_holder, query_context_mapping, attention_outflow_weights, expansion_weights, contraction_weights, opening_scale_vector, opening_shift_vector, closing_scale_vector, closing_shift_vector, expansion_shift, contraction_shift, span_number, drawn_ordering):
    opening_normalised = variance_epsilon_guard(normalise_each_line(shortcut_holder, opening_scale_vector, opening_shift_vector))
    projected = reduced_reverse(variance_epsilon_guard(multiplied_result(opening_normalised, query_context_mapping)))
    query_all = projected[:, :HIDDEN_SIZE].reshape(SLOT, HEADS, HEAD).transpose(1, 0, 2)
    key_all = projected[:, HIDDEN_SIZE:2 * HIDDEN_SIZE].reshape(SLOT, HEADS, HEAD).transpose(1, 0, 2)
    value_all = projected[:, 2 * HIDDEN_SIZE:].reshape(SLOT, HEADS, HEAD).transpose(1, 0, 2)

    def per_head(items):
        return head_attention(items[0], items[1], items[2], items[3], span_number)
    mixed = lax.map(jax.checkpoint(per_head), (query_all, key_all, value_all, drawn_ordering))
    context_mixture = reduced_reverse(variance_epsilon_guard(mixed.transpose(1, 0, 2).reshape(SLOT, HIDDEN_SIZE)))
    intermediate_state = shortcut_holder + reduced_reverse(multiplied_result(context_mixture, attention_outflow_weights))
    normed_two = variance_epsilon_guard(normalise_each_line(intermediate_state, closing_scale_vector, closing_shift_vector))
    pre_act = reduced_reverse(multiplied_result(normed_two, expansion_weights) + expansion_shift)
    activated = variance_epsilon_guard(jax.nn.gelu(pre_act, approximate=False))
    return intermediate_state + multiplied_result(activated, contraction_weights) + contraction_shift

def reference(arriving_features, valid_extents, sampled_target_tiles, query_context_mapping, attention_outflow_weights, expansion_weights, contraction_weights, opening_scale_vector, opening_shift_vector, closing_scale_vector, closing_shift_vector, expansion_shift, contraction_shift, output_sensitivity):
    parameter_nest = tuple((tensor_item.astype(jnp.float32) for tensor_item in (query_context_mapping, attention_outflow_weights, expansion_weights, contraction_weights, opening_scale_vector, opening_shift_vector, closing_scale_vector, closing_shift_vector, expansion_shift, contraction_shift)))

    def advance(totals, pieces):
        member_input, member_cotangent, span_number, drawn_ordering = pieces

        def evaluate_onward(shortcut_holder, *learned_quantities):
            return thinned_attention_unit(shortcut_holder, *learned_quantities, span_number, drawn_ordering)
        result, pullback = jax.vjp(evaluate_onward, member_input.astype(jnp.float32), *parameter_nest)
        grads = pullback(member_cotangent.astype(jnp.float32))
        new_totals = tuple((partial_sum + new_grad for partial_sum, new_grad in zip(totals, grads[1:])))
        return (new_totals, (result.astype(jnp.bfloat16), grads[0]))
    start_totals = tuple((jnp.zeros_like(weight_item) for weight_item in parameter_nest))
    totals, (outputs, grad_inputs) = lax.scan(advance, start_totals, (arriving_features, output_sensitivity, valid_extents, sampled_target_tiles))
    return (outputs, grad_inputs, totals[0], totals[1], totals[2], totals[3], totals[4], totals[5], totals[6], totals[7], totals[8], totals[9])
```

```python
import types

import jax
import jax.numpy as jnp
from jax import lax
from jax.experimental import pallas as pl
from jax.experimental.pallas import tpu as pltpu
from jax.sharding import PartitionSpec as P

group_heads = 4
epsilon = 1e-05
negative = -1e30


def normalise_each_line(values, scaling, shifting):
    centered = values - jnp.mean(values, axis=-1, keepdims=True)
    inverse = lax.rsqrt(jnp.mean(centered * centered, axis=-1, keepdims=True) + epsilon)
    scaled = centered * inverse
    return (scaled * scaling + shifting, scaled, inverse)


def standardize_rows_pullback(grad_norm, scaled, inverse, scaling):
    grad_scaled = grad_norm * scaling
    centred_grad = grad_scaled - jnp.mean(grad_scaled, axis=-1, keepdims=True)
    centred_grad = centred_grad - scaled * jnp.mean(grad_scaled * scaled, axis=-1, keepdims=True)
    return (centred_grad * inverse, jnp.sum(grad_norm * scaled, axis=0), jnp.sum(grad_norm, axis=0))


def exact_gelu(values):
    return jax.nn.gelu(values, approximate=False)


def dense_width():
    return 8


def split_heads(array):
    return array.reshape((array.shape[0] // group_heads, group_heads) + array.shape[1:])


def join_heads(array):
    return array.reshape((array.shape[0] * array.shape[1],) + array.shape[2:])


def candidate_table(span_number, drawn_ordering, first_block, local_blocks, block_size):
    head_count, slot_blocks, random_count = drawn_ordering.shape
    query_blocks = first_block + jnp.arange(local_blocks, dtype=jnp.int32)
    last_block = (span_number - 1) // block_size
    picked = lax.dynamic_slice_in_dim(drawn_ordering, first_block, local_blocks, 1)
    window = jnp.stack([query_blocks - 1, query_blocks, query_blocks + 1], axis=1)
    edges = jnp.stack(
        [jnp.zeros_like(query_blocks), jnp.zeros_like(query_blocks) + last_block], axis=1
    )
    window = jnp.broadcast_to(window[None], (head_count, local_blocks, 3))
    edges = jnp.broadcast_to(edges[None], (head_count, local_blocks, 2))
    candidates = jnp.concatenate([window, picked, edges], axis=2)
    candidate_count = candidates.shape[2]
    inside = (candidates >= 0) & (candidates < slot_blocks)
    earlier = jnp.arange(candidate_count)[:, None] > jnp.arange(candidate_count)[None, :]
    repeated = jnp.any((candidates[:, :, :, None] == candidates[:, :, None, :]) & earlier, axis=3)
    usable = inside & jnp.logical_not(repeated)
    clipped = jnp.clip(candidates, 0, slot_blocks - 1)
    places = clipped[:, :, :, None] * block_size + jnp.arange(block_size, dtype=jnp.int32)
    keep = usable[:, :, :, None] & (places < span_number)
    flags = (query_blocks == 0) | (query_blocks == last_block)
    return (clipped, keep, flags)


def select_blocks(rows, clipped, block_size):
    slot_size, head_count, head_dim = rows.shape
    shaped = rows.reshape(slot_size // block_size, block_size, head_count, head_dim)
    head_index = jnp.arange(head_count, dtype=jnp.int32)[:, None, None]
    return shaped[clipped, :, head_index, :]


def sparse_forward(parts):
    query_group, key_group, value_group, keep_group = parts
    scale = query_group.shape[-1] ** (-0.5)
    scores = (
        jnp.einsum("hitd,hickd->hitck", query_group, key_group, preferred_element_type=jnp.float32)
        * scale
    )
    scores = jnp.where(keep_group[:, :, None], scores, negative)
    shape = scores.shape
    flat = scores.reshape(shape[0], shape[1], shape[2], shape[3] * shape[4])
    highest = jnp.max(flat, axis=-1, keepdims=True)
    weights_exp = jnp.exp(flat - highest)
    totals = jnp.sum(weights_exp, axis=-1, keepdims=True)
    chances_low = (weights_exp / totals).astype(jnp.bfloat16).reshape(shape)
    mixed = jnp.einsum(
        "hitck,hickd->hitd", chances_low, value_group, preferred_element_type=jnp.float32
    )
    return (mixed, (highest + jnp.log(totals))[..., 0])


def sparse_backward(parts):
    query_group, key_group, value_group, keep_group, log_group, grad_group = parts
    scale = query_group.shape[-1] ** (-0.5)
    scores = (
        jnp.einsum("hitd,hickd->hitck", query_group, key_group, preferred_element_type=jnp.float32)
        * scale
    )
    scores = jnp.where(keep_group[:, :, None], scores, negative)
    chances = jnp.exp(scores - log_group[..., None, None])
    grad_chances = jnp.einsum(
        "hitd,hickd->hitck", grad_group, value_group, preferred_element_type=jnp.float32
    )
    central = jnp.sum(chances * grad_chances, axis=(3, 4), keepdims=True)
    grad_scores = (chances * (grad_chances - central)).astype(jnp.bfloat16)
    query_term = (
        jnp.einsum("hitck,hickd->hitd", grad_scores, key_group, preferred_element_type=jnp.float32)
        * scale
    )
    key_term = (
        jnp.einsum(
            "hitck,hitd->hickd", grad_scores, query_group, preferred_element_type=jnp.float32
        )
        * scale
    )
    value_term = jnp.einsum(
        "hitck,hitd->hickd",
        chances.astype(jnp.bfloat16),
        grad_group,
        preferred_element_type=jnp.float32,
    )
    return (query_term, key_term, value_term)


def dense_forward(query_block, key_rows, value_rows, span_number):
    block_size, head_count, head_dim = query_block.shape
    width_group = dense_width()
    scale = head_dim ** (-0.5)
    valid = jnp.arange(key_rows.shape[0], dtype=jnp.int32) < span_number

    def one_group(number):
        offset = number * width_group
        query_part = lax.dynamic_slice_in_dim(query_block, offset, width_group, 1)
        key_part = lax.dynamic_slice_in_dim(key_rows, offset, width_group, 1)
        value_part = lax.dynamic_slice_in_dim(value_rows, offset, width_group, 1)
        scores = (
            jnp.einsum("tgd,kgd->gtk", query_part, key_part, preferred_element_type=jnp.float32)
            * scale
        )
        scores = jnp.where(valid[None, None, :], scores, negative)
        highest = jnp.max(scores, axis=-1, keepdims=True)
        weights_exp = jnp.exp(scores - highest)
        totals = jnp.sum(weights_exp, axis=-1, keepdims=True)
        chances_low = (weights_exp / totals).astype(jnp.bfloat16)
        mixed = jnp.einsum(
            "gtk,kgd->gtd", chances_low, value_part, preferred_element_type=jnp.float32
        )
        return (mixed, (highest + jnp.log(totals))[:, :, 0])

    mixed_all, logs_all = lax.map(one_group, jnp.arange(head_count // width_group, dtype=jnp.int32))
    mixed_all = mixed_all.reshape(head_count, block_size, head_dim).transpose(1, 0, 2)
    return (mixed_all, logs_all.reshape(head_count, block_size))


def dense_skip(query_block, key_rows, value_rows, span_number):
    block_size, head_count, head_dim = query_block.shape
    return (
        jnp.zeros((block_size, head_count, head_dim), jnp.float32),
        jnp.zeros((head_count, block_size), jnp.float32),
    )


def dense_back(query_block, grad_block, key_rows, value_rows, log_block, span_number):
    block_size, head_count, head_dim = query_block.shape
    slot_size = key_rows.shape[0]
    width_group = dense_width()
    scale = head_dim ** (-0.5)
    valid = jnp.arange(slot_size, dtype=jnp.int32) < span_number

    def one_group(number):
        offset = number * width_group
        query_part = lax.dynamic_slice_in_dim(query_block, offset, width_group, 1)
        grad_part = lax.dynamic_slice_in_dim(grad_block, offset, width_group, 1)
        key_part = lax.dynamic_slice_in_dim(key_rows, offset, width_group, 1)
        value_part = lax.dynamic_slice_in_dim(value_rows, offset, width_group, 1)
        scores = (
            jnp.einsum("tgd,kgd->gtk", query_part, key_part, preferred_element_type=jnp.float32)
            * scale
        )
        scores = jnp.where(valid[None, None, :], scores, negative)
        chances = jnp.exp(
            scores - lax.dynamic_slice_in_dim(log_block, offset, width_group, 0)[:, :, None]
        )
        grad_chances = jnp.einsum(
            "tgd,kgd->gtk", grad_part, value_part, preferred_element_type=jnp.float32
        )
        central = jnp.sum(chances * grad_chances, axis=-1, keepdims=True)
        grad_scores = (chances * (grad_chances - central)).astype(jnp.bfloat16)
        query_new = (
            jnp.einsum("gtk,kgd->gtd", grad_scores, key_part, preferred_element_type=jnp.float32)
            * scale
        )
        key_new = (
            jnp.einsum("gtk,tgd->gkd", grad_scores, query_part, preferred_element_type=jnp.float32)
            * scale
        )
        value_new = jnp.einsum(
            "gtk,tgd->gkd",
            chances.astype(jnp.bfloat16),
            grad_part,
            preferred_element_type=jnp.float32,
        )
        return (key_new, value_new, query_new)

    key_all, value_all, query_all = lax.map(
        one_group, jnp.arange(head_count // width_group, dtype=jnp.int32)
    )
    slot_terms = jnp.stack(
        [
            key_all.reshape(head_count, slot_size, head_dim),
            value_all.reshape(head_count, slot_size, head_dim),
        ]
    )
    return (slot_terms, query_all.reshape(head_count, block_size, head_dim).transpose(1, 0, 2))


def dense_pass(query_block, grad_block, key_rows, value_rows, log_block, span_number):
    block_size, head_count, head_dim = query_block.shape
    return (
        jnp.zeros((2, head_count, key_rows.shape[0], head_dim), jnp.float32),
        jnp.zeros(query_block.shape, jnp.float32),
    )


def return_grads(slot_grads):
    owned = lax.psum_scatter(
        slot_grads.astype(jnp.bfloat16), "seq", scatter_dimension=2, tiled=True
    ).astype(jnp.float32)
    pair_count, head_count, tok_count, head_dim = owned.shape
    return owned.transpose(2, 0, 1, 3).reshape(tok_count, pair_count * head_count * head_dim)


def flagged_place(flags):
    return jnp.sum(jnp.where(flags, jnp.arange(flags.shape[0], dtype=jnp.int32), 0))


def local(
    arriving_features,
    valid_extents,
    sampled_target_tiles,
    query_context_mapping,
    attention_outflow_weights,
    expansion_weights,
    contraction_weights,
    opening_scale_vector,
    opening_shift_vector,
    closing_scale_vector,
    closing_shift_vector,
    expansion_shift,
    contraction_shift,
    output_sensitivity,
):
    doc_count, tok_count, feature_breadth = arriving_features.shape
    head_count = sampled_target_tiles.shape[1]
    slot_blocks = sampled_target_tiles.shape[2]
    head_dim = feature_breadth // head_count
    slot_size = tok_count * lax.axis_size("seq")
    block_size = slot_size // slot_blocks
    local_blocks = tok_count // block_size
    first_block = lax.axis_index("seq") * local_blocks
    per_line_summation = doc_count * tok_count
    (
        full_inward,
        entire_outflow,
        full_expand,
        full_contract,
        overall_premultiplier,
        overall_shift_term,
        full_midscale,
        full_midshift,
        full_upshift,
        full_downshift,
    ) = (
        lax.all_gather(query_context_mapping, ("seq", "doc"), axis=0, tiled=True),
        lax.all_gather(attention_outflow_weights, ("seq", "doc"), axis=0, tiled=True),
        lax.all_gather(expansion_weights, ("seq", "doc"), axis=0, tiled=True),
        lax.all_gather(contraction_weights, ("seq", "doc"), axis=0, tiled=True),
        lax.all_gather(opening_scale_vector, ("seq", "doc"), axis=0, tiled=True),
        lax.all_gather(opening_shift_vector, ("seq", "doc"), axis=0, tiled=True),
        lax.all_gather(closing_scale_vector, ("seq", "doc"), axis=0, tiled=True),
        lax.all_gather(closing_shift_vector, ("seq", "doc"), axis=0, tiled=True),
        lax.all_gather(expansion_shift, ("seq", "doc"), axis=0, tiled=True),
        lax.all_gather(contraction_shift, ("seq", "doc"), axis=0, tiled=True),
    )
    shortcut_holder = arriving_features.reshape(per_line_summation, feature_breadth).astype(
        jnp.float32
    )
    opening_normalised, scaled_one, inverse_one = normalise_each_line(
        shortcut_holder,
        overall_premultiplier.astype(jnp.float32),
        overall_shift_term.astype(jnp.float32),
    )
    opening_normalised = opening_normalised.astype(jnp.bfloat16)
    projected = jnp.dot(opening_normalised, full_inward, preferred_element_type=jnp.float32).astype(
        jnp.bfloat16
    )
    query_local = projected[:, :feature_breadth].reshape(doc_count, tok_count, head_count, head_dim)
    pair_local = projected[:, feature_breadth:].reshape(doc_count, tok_count, 2 * feature_breadth)
    pair_full = lax.all_gather(pair_local, "seq", axis=1, tiled=True)

    def table_one(span_number, drawn_ordering):
        return candidate_table(span_number, drawn_ordering, first_block, local_blocks, block_size)

    clipped_all, keep_all, flags_all = jax.vmap(table_one)(valid_extents, sampled_target_tiles)
    query_heads = query_local.reshape(
        doc_count, local_blocks, block_size, head_count, head_dim
    ).transpose(0, 3, 1, 2, 4)
    block_flags = flags_all[:, :, None, None, None]

    def doc_forward(items):
        queries, pair_rows, clipped, keep = items
        key_sel = select_blocks(
            pair_rows[:, :feature_breadth].reshape(slot_size, head_count, head_dim),
            clipped,
            block_size,
        )
        value_sel = select_blocks(
            pair_rows[:, feature_breadth:].reshape(slot_size, head_count, head_dim),
            clipped,
            block_size,
        )
        mixed, log_sums = lax.map(
            sparse_forward,
            (split_heads(queries), split_heads(key_sel), split_heads(value_sel), split_heads(keep)),
        )
        return (join_heads(mixed), join_heads(log_sums))

    sparse_mixed, sparse_logs = lax.map(
        doc_forward, (query_heads, pair_full, clipped_all, keep_all)
    )
    mixed_rows = sparse_mixed.transpose(0, 2, 3, 1, 4)

    def doc_dense(items):
        queries, pair_rows, span_number, flags = items
        key_rows = pair_rows[:, :feature_breadth].reshape(slot_size, head_count, head_dim)
        value_rows = pair_rows[:, feature_breadth:].reshape(slot_size, head_count, head_dim)
        query_block = lax.dynamic_slice_in_dim(
            queries, flagged_place(flags) * block_size, block_size, 0
        )
        return lax.cond(
            jnp.any(flags),
            dense_forward,
            dense_skip,
            query_block,
            key_rows,
            value_rows,
            span_number,
        )

    dense_mixed, dense_logs = lax.map(doc_dense, (query_local, pair_full, valid_extents, flags_all))
    mixed_rows = jnp.where(block_flags, dense_mixed[:, None], mixed_rows)
    context_mixture = mixed_rows.reshape(per_line_summation, feature_breadth).astype(jnp.bfloat16)
    intermediate_state = shortcut_holder + jnp.dot(
        context_mixture, entire_outflow, preferred_element_type=jnp.float32
    )
    normed_two, scaled_two, inverse_two = normalise_each_line(
        intermediate_state, full_midscale.astype(jnp.float32), full_midshift.astype(jnp.float32)
    )
    normed_two = normed_two.astype(jnp.bfloat16)
    pre_act = jnp.dot(
        normed_two, full_expand, preferred_element_type=jnp.float32
    ) + full_upshift.astype(jnp.float32)
    activated = exact_gelu(pre_act).astype(jnp.bfloat16)
    final_rows = (
        intermediate_state
        + jnp.dot(activated, full_contract, preferred_element_type=jnp.float32)
        + full_downshift.astype(jnp.float32)
    )
    output = final_rows.astype(jnp.bfloat16).reshape(doc_count, tok_count, feature_breadth)
    back_inward, back_outward, back_expand, back_contract, back_prescale, back_midscale = (
        full_inward,
        entire_outflow,
        full_expand,
        full_contract,
        overall_premultiplier,
        full_midscale,
    )
    grad_out_rows = output_sensitivity.reshape(per_line_summation, feature_breadth)
    grad_out_wide = grad_out_rows.astype(jnp.float32)
    contract_grad = jnp.einsum(
        "rf,rd->fd", activated, grad_out_rows, preferred_element_type=jnp.float32
    )
    downshift_grad = jnp.sum(grad_out_wide, axis=0)
    grad_act = jnp.einsum(
        "rd,fd->rf", grad_out_rows, back_contract, preferred_element_type=jnp.float32
    )
    unused_value, gelu_back = jax.vjp(exact_gelu, pre_act)
    grad_pre = gelu_back(grad_act)[0].astype(jnp.bfloat16)
    expand_grad = jnp.einsum("rd,rf->df", normed_two, grad_pre, preferred_element_type=jnp.float32)
    upshift_grad = jnp.sum(grad_pre.astype(jnp.float32), axis=0)
    grad_norm_two = jnp.einsum(
        "rf,df->rd", grad_pre, back_expand, preferred_element_type=jnp.float32
    )
    middle_part, midscale_grad, midshift_grad = standardize_rows_pullback(
        grad_norm_two, scaled_two, inverse_two, back_midscale.astype(jnp.float32)
    )
    grad_middle = grad_out_wide + middle_part
    grad_branch = grad_middle.astype(jnp.bfloat16)
    outward_grad = jnp.einsum(
        "rd,re->de", context_mixture, grad_branch, preferred_element_type=jnp.float32
    )
    grad_attended = jnp.einsum(
        "re,de->rd", grad_branch, back_outward, preferred_element_type=jnp.float32
    ).astype(jnp.bfloat16)
    grad_attended = grad_attended.reshape(doc_count, tok_count, head_count, head_dim)
    grad_blocks = grad_attended.reshape(doc_count, local_blocks, block_size, head_count, head_dim)
    sparse_grads = jnp.where(block_flags, jnp.zeros_like(grad_blocks), grad_blocks).transpose(
        0, 3, 1, 2, 4
    )
    block_ids = jnp.arange(slot_blocks, dtype=jnp.int32)

    def sparse_back(queries, pair_rows, clipped, keep, log_sums, grad_part):
        key_rows = pair_rows[:, :feature_breadth].reshape(slot_size, head_count, head_dim)
        value_rows = pair_rows[:, feature_breadth:].reshape(slot_size, head_count, head_dim)
        key_sel = select_blocks(key_rows, clipped, block_size)
        value_sel = select_blocks(value_rows, clipped, block_size)
        grouped = (
            split_heads(queries),
            split_heads(key_sel),
            split_heads(value_sel),
            split_heads(keep),
            split_heads(log_sums),
            split_heads(grad_part),
        )
        query_term, key_term, value_term = lax.map(sparse_backward, grouped)
        query_term = join_heads(query_term)
        key_term = join_heads(key_term)
        value_term = join_heads(value_term)
        placing = (clipped[..., None] == block_ids).astype(jnp.float32)
        key_slot = jnp.einsum(
            "hlcn,hlcbd->hnbd",
            placing,
            key_term,
            precision=lax.Precision.HIGHEST,
            preferred_element_type=jnp.float32,
        )
        value_slot = jnp.einsum(
            "hlcn,hlcbd->hnbd",
            placing,
            value_term,
            precision=lax.Precision.HIGHEST,
            preferred_element_type=jnp.float32,
        )
        slot_grads = jnp.stack(
            [
                key_slot.reshape(head_count, slot_size, head_dim),
                value_slot.reshape(head_count, slot_size, head_dim),
            ]
        )
        return (query_term, slot_grads, key_rows, value_rows)

    def doc_backward(carry, items):
        (
            queries,
            pair_rows,
            clipped,
            keep,
            log_sums,
            grad_part,
            grad_rows,
            query_rows,
            dense_log,
            span_number,
            flags,
        ) = items
        query_term, slot_grads, key_rows, value_rows = sparse_back(
            queries, pair_rows, clipped, keep, log_sums, grad_part
        )
        start = flagged_place(flags) * block_size
        query_block = lax.dynamic_slice_in_dim(query_rows, start, block_size, 0)
        grad_block = lax.dynamic_slice_in_dim(grad_rows, start, block_size, 0)
        dense_slot, dense_term = lax.cond(
            jnp.any(flags),
            dense_back,
            dense_pass,
            query_block,
            grad_block,
            key_rows,
            value_rows,
            dense_log,
            span_number,
        )
        owned = return_grads(slot_grads + dense_slot)
        return (carry, (query_term, dense_term, owned))

    unused_carry, (sparse_query, dense_query, pair_grads) = lax.scan(
        doc_backward,
        jnp.zeros((), jnp.int32),
        (
            query_heads,
            pair_full,
            clipped_all,
            keep_all,
            sparse_logs,
            sparse_grads,
            grad_attended,
            query_local,
            dense_logs,
            valid_extents,
            flags_all,
        ),
    )
    query_grad = sparse_query.transpose(0, 2, 3, 1, 4) + jnp.where(
        block_flags, dense_query[:, None], 0.0
    )
    grad_projected = jnp.concatenate(
        [
            query_grad.reshape(per_line_summation, feature_breadth),
            pair_grads.reshape(per_line_summation, 2 * feature_breadth),
        ],
        axis=1,
    ).astype(jnp.bfloat16)
    inward_grad = jnp.einsum(
        "rd,re->de", opening_normalised, grad_projected, preferred_element_type=jnp.float32
    )
    grad_norm_one = jnp.einsum(
        "re,de->rd", grad_projected, back_inward, preferred_element_type=jnp.float32
    )
    incoming_slice, leading_gain_sensitivity, leading_offset_sensitivity = (
        standardize_rows_pullback(
            grad_norm_one, scaled_one, inverse_one, back_prescale.astype(jnp.float32)
        )
    )
    grad_inputs = (grad_middle + incoming_slice).reshape(doc_count, tok_count, feature_breadth)
    summed = (
        lax.psum_scatter(inward_grad, ("seq", "doc"), scatter_dimension=0, tiled=True),
        lax.psum_scatter(outward_grad, ("seq", "doc"), scatter_dimension=0, tiled=True),
        lax.psum_scatter(expand_grad, ("seq", "doc"), scatter_dimension=0, tiled=True),
        lax.psum_scatter(contract_grad, ("seq", "doc"), scatter_dimension=0, tiled=True),
        lax.psum_scatter(leading_gain_sensitivity, ("seq", "doc"), scatter_dimension=0, tiled=True),
        lax.psum_scatter(
            leading_offset_sensitivity, ("seq", "doc"), scatter_dimension=0, tiled=True
        ),
        lax.psum_scatter(midscale_grad, ("seq", "doc"), scatter_dimension=0, tiled=True),
        lax.psum_scatter(midshift_grad, ("seq", "doc"), scatter_dimension=0, tiled=True),
        lax.psum_scatter(upshift_grad, ("seq", "doc"), scatter_dimension=0, tiled=True),
        lax.psum_scatter(downshift_grad, ("seq", "doc"), scatter_dimension=0, tiled=True),
    )
    return (output, grad_inputs) + tuple(summed)


ROUTE = pl.DeviceIdType.MESH
NZ, NX, NY, NC = 4, 2, 2, 2
bf16, f32 = jnp.bfloat16, jnp.float32


def nn(left, right):
    return lax.dot_general(left, right, (((1,), (0,)), ((), ())), preferred_element_type=f32)


def nt(left, right):
    return lax.dot_general(left, right, (((1,), (1,)), ((), ())), preferred_element_type=f32)


def tn(left, right):
    return lax.dot_general(left, right, (((0,), (0,)), ((), ())), preferred_element_type=f32)


class Net:
    def __init__(self, send_sems, recv_sems, here):
        self.send_sems, self.recv_sems, self.here = send_sems, recv_sems, here
        self.sent, self.taken = 0, 0
        self.open = []

    def slots(self, count):
        first = self.taken
        self.taken += count
        assert self.taken <= RECVS
        return first

    def send(self, src, dst, device, slot, group=None):
        index = self.sent
        self.sent += 1
        assert self.sent <= SENDS

        def make():
            return pltpu.make_async_remote_copy(
                src_ref=src,
                dst_ref=dst,
                send_sem=self.send_sems.at[index],
                recv_sem=self.recv_sems.at[slot],
                device_id=device,
                device_id_type=ROUTE,
            )

        make().start()
        self.open.append((group, None, make))

    def send_or_keep(self, src, dst, device, slot, is_self, group=None):
        index = self.sent
        self.sent += 1
        assert self.sent <= SENDS

        def make():
            return pltpu.make_async_remote_copy(
                src_ref=src,
                dst_ref=dst,
                send_sem=self.send_sems.at[index],
                recv_sem=self.recv_sems.at[slot],
                device_id=device,
                device_id_type=ROUTE,
            )

        @pl.when(jnp.logical_not(is_self))
        def away():
            make().start()

        @pl.when(is_self)
        def keep():
            pltpu.make_async_copy(src, dst, self.recv_sems.at[slot]).start()

        self.open.append((group, is_self, make))

    def settle(self, group=None, everything=False):
        rest = []
        for entry in self.open:
            name, is_self, make = entry
            if not everything and name != group:
                rest.append(entry)
            elif is_self is None:
                make().wait_send()
            else:
                pl.when(jnp.logical_not(is_self))(lambda make=make: make().wait_send())
        self.open = rest

    def arrive(self, dst, slot):
        pltpu.make_async_remote_copy(
            src_ref=dst,
            dst_ref=dst,
            send_sem=self.send_sems.at[0],
            recv_sem=self.recv_sems.at[slot],
            device_id=self.here,
            device_id_type=ROUTE,
        ).wait_recv()


def row_stats(values):
    mean = jnp.mean(values, axis=-1, keepdims=True)
    centered = values - mean
    inverse = lax.rsqrt(jnp.mean(centered * centered, axis=-1, keepdims=True) + epsilon)
    return centered * inverse, inverse


def norm_pullback(grad, scaled, inverse, gain):
    wide = grad * gain
    first = jnp.mean(wide, axis=-1, keepdims=True)
    second = jnp.mean(wide * scaled, axis=-1, keepdims=True)
    return (wide - first - scaled * second) * inverse


def column_sum(values):
    return jnp.sum(values, axis=0, keepdims=True)


SCRATCH = dict(
    xr=((8, 2, 64, 1024), bf16),
    n1=((8, 128, 1024), bf16),
    aux=((64, 128), jnp.int32),
    bias=((16, 4, 1024), f32),
    sv=((4, 2, 2, 2, 8, 128), f32),
    vec=((8, 1024), f32),
    b1=((1, 2048), f32),
    wqs=((4, 32, 768), bf16),
    wq=((4, 2, 2, 2, 32, 768), bf16),
    wo=((4, 2, 2, 2, 32, 1024), bf16),
    w1s=((32, 2048), bf16),
    w1=((4, 2, 2, 2, 32, 2048), bf16),
    w2=((4, 2, 2, 128, 1024), bf16),
    qkv=((1024, 768), bf16),
    lse=((1024, 128), f32),
    at=((8, 128, 256), bf16),
    att=((2, 4, 128, 256), bf16),
    mid=((256, 1024), f32),
    nt2=((2, 256, 1024), bf16),
    dyx=((2, 256, 1024), bf16),
    act=((512, 2048), bf16),
    gp=((512, 2048), bf16),
    dw2=((4, 2, 2, 128, 1024), bf16),
    xs=((256, 1024), f32),
    xg=((256, 1024), f32),
    own=((256, 1024), f32),
    gb=((256, 1024), bf16),
    gm=((256, 1024), f32),
    da=((2, 4, 128, 256), bf16),
    do=((8, 128, 256), bf16),
    dk=((1024, 128), f32),
    dv=((1024, 128), f32),
    rgs=((8, 64, 1024), bf16),
    rgx=((4, 64, 1024), bf16),
    gnr=((2, 2, 64, 1024), bf16),
    r1y=((4, 2, 2, 32, 2048), bf16),
    r1x=((4, 2, 32, 2048), bf16),
    r1z=((4, 2, 32, 2048), bf16),
    f1=((2, 32, 2048), f32),
    r1f=((32, 2048), f32),
    r2y=((4, 2, 128, 1024), bf16),
    r2x=((4, 128, 1024), bf16),
    r2z=((4, 128, 1024), bf16),
    ros=((4, 2, 2, 32, 1024), bf16),
    roy=((4, 2, 32, 1024), bf16),
    rox=((4, 32, 1024), bf16),
    roz=((4, 32, 1024), bf16),
    rqy=((4, 2, 2, 32, 768), bf16),
    rqz=((4, 2, 2, 32, 768), bf16),
    fq=((2, 2, 32, 768), f32),
    rqf=((4, 32, 768), f32),
    sg=((8, 8, 128), f32),
    rsg=((8, 8, 128), f32),
    sgt=((2, 8, 128), f32),
    rsy=((2, 8, 128), f32),
)
SENDS, RECVS = 256, 256
VMEM_BYTES = 64 * 2**20


def layer_kernel(
    x_in, dy_in, aux_in, wq_in, wo_in, w1_in, w2_in, sv_in,
    out_ref, gx_ref, dwq_ref, dwo_ref, dw1_ref, dw2_ref, sg_ref,
    *rest,
):
    names = list(SCRATCH)
    R = types.SimpleNamespace(**dict(zip(names, rest[: len(names)])))
    send_sems, recv_sems, ready_sem = rest[len(names):]
    s, d = lax.axis_index("seq"), lax.axis_index("doc")
    z, x, y, c = s // NX, s % NX, d // NC, d % NC
    hd = 2 * x + c
    flip = 1 - c

    def at(zz, xx, yy, cc):
        return (zz * NX + xx, yy * NC + cc)

    here = (s, d)
    sib, xn, yn = at(z, x, y, flip), at(z, 1 - x, y, c), at(z, x, 1 - y, c)
    net = Net(send_sems, recv_sems, here)
    turn = [(z + k) % NZ for k in range(NZ)]

    barrier = pltpu.get_barrier_semaphore()

    def greet(step, _):
        other = (s * NC + c + step) % 16
        pl.semaphore_signal(
            barrier, inc=1, device_id=(other // NC, y * NC + other % NC), device_id_type=ROUTE
        )
        return 0

    lax.fori_loop(1, 16, greet, 0)
    pl.semaphore_signal(barrier, inc=1, device_id=yn, device_id_type=ROUTE)
    pl.semaphore_wait(barrier, 16)

    half = pl.ds(pl.multiple_of(c * 512, 512), 512)
    other_half = pl.ds(pl.multiple_of(flip * 512, 512), 512)
    xz = net.slots(4)
    for b in range(2):
        for ch in range(2):
            zt = 2 * c + b
            net.send_or_keep(
                x_in.at[b, :, :, ch * 512:(ch + 1) * 512],
                R.xr.at[s, :, :, ch * 512:(ch + 1) * 512],
                at(zt, x, y, ch),
                xz + z,
                jnp.logical_and(zt == z, c == ch),
            )

    sv_s = net.slots(1)
    R.sv[z, x, y, c] = sv_in[...]
    net.send(R.sv.at[z, x, y, c], R.sv.at[z, x, y, c], sib, sv_s)

    for h in range(4):
        for t in range(3):
            R.wqs[h, :, t * 256:(t + 1) * 256] = wq_in[
                :, t * 1024 + h * 256:t * 1024 + (h + 1) * 256
            ]
    R.wq[z, x, y, c] = R.wqs[hd]
    wqa = net.slots(4)
    for xx, cc, dev in ((x, flip, sib), (1 - x, c, xn), (1 - x, flip, at(z, 1 - x, y, flip))):
        net.send(R.wqs.at[2 * xx + cc], R.wq.at[z, x, y, c], dev, wqa + hd)

    aux_s = net.slots(1)
    has_table = c == z // 2

    @pl.when(has_table)
    def table():
        R.aux[...] = aux_in[z % 2, hd]

    def table_copy():
        return pltpu.make_async_remote_copy(
            src_ref=aux_in.at[z % 2, 2 * x + flip],
            dst_ref=R.aux,
            send_sem=send_sems.at[SENDS - 1],
            recv_sem=recv_sems.at[aux_s],
            device_id=sib,
            device_id_type=ROUTE,
        )

    @pl.when(has_table)
    def table_away():
        table_copy().start()

    w1_sib = net.slots(1)

    def parity(ref_value, which):
        return jnp.concatenate(
            [ref_value[:, (2 * k + which) * 128:(2 * k + which + 1) * 128] for k in range(16)],
            axis=1,
        )

    w1_all = w1_in[...]
    even, odd = parity(w1_all, 0), parity(w1_all, 1)
    R.w1[z, x, y, c] = jnp.where(c == 0, even, odd)
    R.w1s[...] = jnp.where(c == 0, odd, even)
    net.send(R.w1s, R.w1.at[z, x, y, c], sib, w1_sib)
    R.wo[z, x, y, c] = wo_in[...]
    R.w2[z, x, y] = w2_in[...]
    dy_s = net.slots(1)
    R.dyx[c] = dy_in[...].reshape(256, 1024)
    net.send(R.dyx.at[c], R.dyx.at[c], sib, dy_s)

    for xx, cc, dev in ((x, flip, sib), (1 - x, c, xn), (1 - x, flip, at(z, 1 - x, y, flip))):
        net.arrive(R.wq.at[z, xx, y, cc], wqa + 2 * xx + cc)
    wqz = net.slots(4)
    for zt in turn[1:]:
        net.send(R.wq.at[z, :, y], R.wq.at[z, :, y], at(zt, x, y, c), wqz + z, "w")
    wqy = net.slots(4)
    net.send(R.wq.at[z, :, y], R.wq.at[z, :, y], yn, wqy + z, "w")

    net.arrive(R.sv.at[z, x, y, flip], sv_s)
    sv_z, sv_x, sv_y = net.slots(4), net.slots(1), net.slots(1)
    for zt in turn[1:]:
        net.send(R.sv.at[z, x, y], R.sv.at[z, x, y], at(zt, x, y, c), sv_z + z)

    xx_r, xs_r = net.slots(4), net.slots(8)
    for zt in turn:
        net.arrive(R.xr.at[zt * 2 + x, :, :, half], xz + zt)
        part = R.xr.at[zt * 2 + x, :, :, half]
        net.send(part, part, xn, xx_r + zt, "xr")
        net.send(part, part, sib, xs_r + zt * 2 + x, "xr")
    for zt in turn[1:]:
        net.arrive(R.sv.at[zt, x, y], sv_z + zt)
    net.send(R.sv.at[:, x, y], R.sv.at[:, x, y], xn, sv_x)
    for zt in turn[1:]:
        part = R.wq.at[zt, :, y]
        net.arrive(part, wqz + zt)
        net.send(part, part, yn, wqy + zt, "w")

    def gather_start(ref, piece, group):
        base_z, base_a, base_b = net.slots(4), net.slots(4), net.slots(8)
        own = piece(z, x, y)
        for zt in turn[1:]:
            net.send(own, own, at(zt, x, y, c), base_z + z, group)
        return base_z, base_a, base_b

    def piece_of(ref):
        return lambda zz, xx, yy: ref.at[zz, xx, yy]

    wo_piece = lambda zz, xx, yy: R.wo.at[zz, xx, yy, c]
    w1_piece, w2_piece = piece_of(R.w1), piece_of(R.w2)
    net.arrive(R.w1.at[z, x, y, flip], w1_sib)
    wo_sl = gather_start(R.wo, wo_piece, "w")
    w1_sl = gather_start(R.w1, w1_piece, "w")
    w2_sl = gather_start(R.w2, w2_piece, "w")

    def spread(piece, slots, group, x_first):
        base_z, base_a, base_b = slots
        first, second = (xn, yn) if x_first else (yn, xn)

        def from_first(zz):
            return piece(zz, 1 - x, y) if x_first else piece(zz, x, 1 - y)

        def step_column(k):
            zt = turn[k]
            part = piece(zt, x, y)
            if k:
                net.arrive(part, base_z + zt)
            net.send(part, part, first, base_a + zt, group)
            net.send(part, part, second, base_b + 2 * zt, group)

        def step_first(k):
            zt = turn[k]
            part = from_first(zt)
            net.arrive(part, base_a + zt)
            net.send(part, part, second, base_b + 2 * zt + 1, group)

        def step_last():
            for zt in turn:
                if x_first:
                    net.arrive(piece(zt, x, 1 - y), base_b + 2 * zt)
                    net.arrive(piece(zt, 1 - x, 1 - y), base_b + 2 * zt + 1)
                else:
                    net.arrive(piece(zt, 1 - x, y), base_b + 2 * zt)
                    net.arrive(piece(zt, 1 - x, 1 - y), base_b + 2 * zt + 1)

        steps = [lambda k=k: step_column(k) for k in range(4)] + [lambda k=k: step_first(k) for k in range(4)]
        return steps, step_last

    wo_steps, wo_last = spread(wo_piece, wo_sl, "w", True)
    w1_steps, w1_last = spread(w1_piece, w1_sl, "w", True)
    w2_steps, w2_last = spread(w2_piece, w2_sl, "w", False)

    net.arrive(R.sv.at[:, 1 - x, y], sv_x)
    net.send(R.sv.at[:, :, y], R.sv.at[:, :, y], yn, sv_y)
    for zt in turn:
        part = R.xr.at[zt * 2 + (1 - x), :, :, half]
        net.arrive(part, xx_r + zt)
        net.send(part, part, sib, xs_r + zt * 2 + 1 - x, "xr")

    @pl.when(has_table)
    def table_sent():
        table_copy().wait_send()

    @pl.when(jnp.logical_not(has_table))
    def table_here():
        net.arrive(R.aux, aux_s)

    for g in range(16):
        tiles = R.aux[g * 4:(g + 1) * 4, :]
        place = lax.broadcasted_iota(jnp.int32, (4, 1024), 1)
        block = place >> 6
        row = lax.broadcasted_iota(jnp.int32, (4, 1024), 0) + (g % 4) * 4
        extent = tiles[:, 3:4]
        last = (extent - 1) >> 6
        seen = jnp.abs(row - block) <= 1
        for k in range(3):
            seen = seen | (block == tiles[:, k:k + 1])
        seen = seen | (block == 0) | (block == last) | (row == 0) | (row == last)
        seen = seen & (place < extent)
        R.bias[g] = jnp.where(seen, 0.0, negative).astype(f32)

    net.arrive(R.sv.at[:, :, 1 - y], sv_y)
    lane = lax.broadcasted_iota(jnp.int32, (1, 128), 1) >> 5
    for r in range(8):
        for k in range(5):
            total = jnp.zeros((1, 128), f32)
            for q in range(4):
                line = R.sv[r // 2, r % 2, q // 2, q % 2, k // 4:k // 4 + 1, :]
                shift = (32 * (q - k % 4)) % 128
                if shift:
                    line = pltpu.roll(line, shift, 1)
                total = jnp.where(lane == q, line, total)
            R.vec[k:k + 1, r * 128:(r + 1) * 128] = total
    for p in range(16):
        R.b1[:, p * 128:(p + 1) * 128] = R.sv[p // 4, p // 2 % 2, p % 2, c, 2:3, :]

    for k in range(8):
        net.arrive(R.xr.at[k, :, :, other_half], xs_r + k)
    for zt in turn:
        part = R.wq.at[zt, :, 1 - y]
        net.arrive(part, wqy + zt)

    def project(step, _):
        for k in range(2):
            scaled, _inverse = row_stats(R.xr[2 * step + k].reshape(128, 1024).astype(f32))
            R.n1[2 * step + k] = (scaled * R.vec[0:1, :] + R.vec[1:2, :]).astype(bf16)
        rows = R.n1[pl.ds(2 * step, 2)].reshape(256, 1024)
        made = nn(rows, R.wq[...].reshape(1024, 768)).astype(bf16)
        where = pl.ds(pl.multiple_of(step * 256, 256), 256)
        R.qkv[where, :] = jnp.concatenate([made[:, :256] * jnp.asarray(0.125, bf16), made[:, 256:]], axis=1)
        return 0

    lax.fori_loop(0, 4, project, 0)

    low_lane = lax.broadcasted_iota(jnp.int32, (1, 128), 1) < 64

    def only(values, e):
        return jnp.where(low_lane if e == 0 else jnp.logical_not(low_lane), values, jnp.zeros_like(values))

    def attend(pair):
        cols = slice(pair * 128, pair * 128 + 128)
        kcols = slice(256 + pair * 128, 256 + pair * 128 + 128)
        vcols = slice(512 + pair * 128, 512 + pair * 128 + 128)

        def tile(t, _):
            where = pl.ds(pl.multiple_of(t * 256, 256), 256)
            q = R.qkv[where, cols]
            mixed = None
            for e in range(2):
                h = pair * 2 + e
                scores = nt(only(q, e), R.qkv[:, kcols])
                scores = (scores.reshape(4, 64, 1024) + R.bias[h * 4 + t][:, None, :]).reshape(256, 1024)
                top = jnp.max(scores, axis=-1, keepdims=True)
                grown = jnp.exp(scores - top)
                total = jnp.sum(grown, axis=-1, keepdims=True)
                low = (grown * (1.0 / total)).astype(bf16)
                R.lse[where, h:h + 1] = top + jnp.log(total)
                got = nn(low, R.qkv[:, vcols])
                mixed = got if e == 0 else jnp.where(low_lane, mixed, got)
            R.at[pl.ds(2 * t, 2), :, cols] = mixed.astype(bf16).reshape(2, 128, 128)
            return 0

        lax.fori_loop(0, 4, tile, 0)

    for k in range(4):
        wo_steps[k]()
    for k in range(4):
        w1_steps[k]()
    attend(0)
    for k in range(4):
        wo_steps[4 + k]()
    for k in range(4):
        w1_steps[4 + k]()
    for k in range(4):
        w2_steps[k]()
    attend(1)

    at_r = net.slots(8)
    back_c = z // 2
    for k in range(4):
        for xx in (x, 1 - x):
            zt = turn[k]
            net.send_or_keep(
                R.at.at[zt * 2 + xx],
                R.att.at[z % 2, hd],
                at(zt, xx, y, back_c),
                at_r + (z % 2) * 4 + hd,
                jnp.logical_and(jnp.logical_and(zt == z, xx == x), c == back_c),
            )
    for k in range(4):
        w2_steps[4 + k]()
    wo_last()
    wo_s = net.slots(1)
    net.send(R.wo.at[:, :, :, c], R.wo.at[:, :, :, c], sib, wo_s, "w")
    net.arrive(R.wo.at[:, :, :, flip], wo_s)
    for b in range(2):
        for h in range(4):
            net.arrive(R.att.at[b, h], at_r + b * 4 + h)

    for n in range(4):
        cols = slice(n * 256, n * 256 + 256)
        made = x_in[:, :, :, cols].reshape(256, 256).astype(f32)
        for h in range(4):
            made = made + nn(
                R.att[:, h].reshape(256, 256),
                R.wo[h, :, :, :, :, cols].reshape(256, 256),
            )
        R.mid[:, cols] = made
    for k in range(2):
        where = slice(k * 128, k * 128 + 128)
        scaled, _inverse = row_stats(R.mid[where, :])
        R.nt2[c, where, :] = (scaled * R.vec[2:3, :] + R.vec[3:4, :]).astype(bf16)
    nt_s = net.slots(1)
    net.send(R.nt2.at[c], R.nt2.at[c], sib, nt_s)
    net.arrive(R.dyx.at[flip], dy_s)

    w1_last()
    net.arrive(R.nt2.at[flip], nt_s)

    def widen(j, _):
        where = pl.ds(pl.multiple_of(j * 256, 256), 256)
        for k in range(2):
            rows = slice(k * 256, k * 256 + 256)
            pre = nn(R.nt2[k], R.w1[:, :, :, :, :, where].reshape(1024, 256))
            pre = pre + R.b1[:, where]
            share = 0.5 * (1.0 + lax.erf(pre * (2.0 ** -0.5)))
            R.act[rows, where] = (pre * share).astype(bf16)
            slope = share + pre * (jnp.exp(-0.5 * pre * pre) * (1.0 / (2.0 * jnp.pi) ** 0.5))
            R.gp[rows, where] = slope.astype(bf16)
        return 0

    lax.fori_loop(0, 8, widen, 0)

    def outer_two(j, _):
        where = pl.ds(pl.multiple_of(j * 256, 256), 256)
        made = tn(R.act[:, where], R.dyx[...].reshape(512, 1024))
        p = 2 * j
        R.dw2[p // 4, p // 2 % 2, 0] = made[:128].astype(bf16)
        R.dw2[p // 4, p // 2 % 2, 1] = made[128:].astype(bf16)
        return 0

    lax.fori_loop(0, 8, outer_two, 0)

    def scatter_steps(piece, ra, rb, rz, slots, x_first):
        base_a, base_b, base_z = slots
        first, second = (xn, yn) if x_first else (yn, xn)

        def spot(zz, near, far):
            xx, yy = (near, far) if x_first else (far, near)
            return piece(zz, jnp.where(xx, x, 1 - x), jnp.where(yy, y, 1 - y))

        def begin():
            for far in (0, 1):
                for k in (1, 2, 3, 0):
                    zt = turn[k]
                    net.send(spot(zt, 0, far), ra.at[zt, far], first, base_a + 2 * zt + far)

        def middle(k):
            zt = turn[k]
            net.arrive(ra.at[zt, 0], base_a + 2 * zt)
            here_ = spot(zt, 1, 0)
            here_[...] = (here_[...].astype(f32) + ra[zt, 0].astype(f32)).astype(bf16)
            net.send(here_, rb.at[zt], second, base_b + zt)

        def late(k):
            zt = turn[k]
            net.arrive(ra.at[zt, 1], base_a + 2 * zt + 1)
            net.arrive(rb.at[zt], base_b + zt)
            here_ = spot(zt, 1, 1)
            here_[...] = (
                here_[...].astype(f32) + ra[zt, 1].astype(f32) + rb[zt].astype(f32)
            ).astype(bf16)
            if k:
                net.send(here_, rz.at[z], at(zt, x, y, c), base_z + z)

        def final():
            total = spot(z, 1, 1)[...].astype(f32)
            for zt in turn[1:]:
                net.arrive(rz.at[zt], base_z + zt)
                total = total + rz[zt].astype(f32)
            return total

        return begin, middle, late, final

    def scatter_slots():
        return net.slots(8), net.slots(4), net.slots(4)

    two_begin, two_middle, two_late, two_final = scatter_steps(
        lambda zz, xx, yy: R.dw2.at[zz, xx, yy], R.r2y, R.r2x, R.r2z, scatter_slots(), True
    )
    two_begin()

    w2_last()

    def narrow_back(j, _):
        where = pl.ds(pl.multiple_of(j * 256, 256), 256)
        p = 2 * j
        rows2 = R.w2[p // 4, p // 2 % 2].reshape(256, 1024)
        made = nt(R.dyx[...].reshape(512, 1024), rows2) * R.gp[:, where].astype(f32)
        R.gp[:, where] = made.astype(bf16)
        return 0

    lax.fori_loop(0, 8, narrow_back, 0)

    gn_s = net.slots(1)

    def partial_norm(n, which):
        rows = pl.ds(pl.multiple_of(which * 256, 256), 256)
        return nt(R.gp[rows, :], R.w1[n].reshape(256, 2048))

    for n in range(4):
        R.xs[:, n * 256:(n + 1) * 256] = partial_norm(n, flip)
    net.send(R.xs, R.xg, sib, gn_s, "xs")
    for n in range(4):
        R.own[:, n * 256:(n + 1) * 256] = partial_norm(n, c)
    net.arrive(R.xg, gn_s)
    sums = [jnp.zeros((1, 1024), f32) for _ in range(3)]
    for k in range(4):
        where = slice(k * 64, k * 64 + 64)
        grad = R.own[where, :] + R.xg[where, :]
        scaled, inverse = row_stats(R.mid[where, :])
        flow = dy_in[k // 2, (k % 2) * 64:(k % 2) * 64 + 64, :].astype(f32)
        sums[0] = sums[0] + column_sum(grad * scaled)
        sums[1] = sums[1] + column_sum(grad)
        sums[2] = sums[2] + column_sum(flow)
        total = flow + norm_pullback(grad, scaled, inverse, R.vec[2:3, :])
        R.gm[where, :] = total
        R.gb[where, :] = total.astype(bf16)

    def note(row, line):
        for r in range(8):
            R.sg[r, row:row + 1, :] = line[:, r * 128:(r + 1) * 128]

    R.sg[...] = jnp.zeros((8, 8, 128), f32)
    for k in range(3):
        note(2 + k, sums[k])

    do_r = net.slots(8)
    for h in range(4):
        made = nt(R.gb[...], R.wo[h].reshape(256, 1024)).astype(bf16)
        R.da[:, h] = made.reshape(2, 128, 256)
    for b in range(2):
        for xx in (x, 1 - x):
            for cc in (c, flip):
                zt = 2 * c + b
                net.send_or_keep(
                    R.da.at[b, 2 * xx + cc],
                    R.do.at[s],
                    at(zt, xx, y, cc),
                    do_r + s,
                    jnp.logical_and(zt == z, jnp.logical_and(xx == x, cc == c)),
                )

    net.settle("w")

    def outer_one(n, _):
        for m in range(2):
            cols = slice(m * 1024, m * 1024 + 1024)
            left = R.nt2[:, :, pl.ds(pl.multiple_of(n * 256, 256), 256)].reshape(512, 256)
            made = tn(left, R.gp[:, cols]).astype(bf16)
            R.w1[n, :, :, :, :, cols] = made.reshape(2, 2, 2, 32, 1024)
        return 0

    lax.fori_loop(0, 4, outer_one, 0)
    one_begin, one_middle, one_late, one_final = scatter_steps(
        w1_piece, R.r1y, R.r1x, R.r1z, scatter_slots(), False
    )
    one_begin()
    for h in range(4):
        made = tn(R.att[:, h].reshape(256, 256), R.gb[...]).astype(bf16)
        R.wo[h] = made.reshape(2, 2, 2, 32, 1024)
    ros_s = net.slots(1)
    net.send(R.wo.at[:, :, :, flip], R.ros, sib, ros_s)
    for k in range(4):
        two_middle(k)

    out_s = net.slots(1)
    net.settle("xs")

    def contracted(n, which):
        cols = slice(n * 256, n * 256 + 256)
        rows = pl.ds(pl.multiple_of(which * 256, 256), 256)
        return nn(R.act[rows, :], R.w2[:, :, :, :, cols].reshape(2048, 256))

    for n in range(4):
        R.xs[:, n * 256:(n + 1) * 256] = contracted(n, flip)
    pl.semaphore_signal(ready_sem, inc=1, device_id=sib, device_id_type=ROUTE)
    pl.semaphore_wait(ready_sem, 1)
    net.send(R.xs, R.xg, sib, out_s)
    for n in range(4):
        cols = slice(n * 256, n * 256 + 256)
        R.own[:, cols] = R.mid[:, cols] + contracted(n, c) + R.vec[4:5, cols]
    up = [jnp.zeros((1, 2048), f32)]
    for k in range(8):
        up[0] = up[0] + column_sum(R.gp[k * 64:(k + 1) * 64, :].astype(f32))
    for p in range(16):
        R.sg[p // 2, 5 + p % 2:6 + p % 2, :] = up[0][:, p * 128:(p + 1) * 128]
    net.arrive(R.xg, out_s)
    for k in range(2):
        where = slice(k * 128, k * 128 + 128)
        out_ref[k] = (R.own[where, :] + R.xg[where, :]).astype(bf16)
    net.arrive(R.ros, ros_s)
    for k in range(4):
        R.wo[k, :, :, c] = (R.wo[k, :, :, c].astype(f32) + R.ros[k].astype(f32)).astype(bf16)
    o_begin, o_middle, o_late, o_final = scatter_steps(
        wo_piece, R.roy, R.rox, R.roz, scatter_slots(), False
    )
    o_begin()

    for k in range(8):
        net.arrive(R.do.at[k], do_r + k)
    for k in range(4):
        one_middle(k)

    def attend_back(pair):
        cols = slice(pair * 128, pair * 128 + 128)
        kcols = slice(256 + pair * 128, 256 + pair * 128 + 128)
        vcols = slice(512 + pair * 128, 512 + pair * 128 + 128)
        R.dk[...] = jnp.zeros((1024, 128), f32)
        R.dv[...] = jnp.zeros((1024, 128), f32)

        def tile(t, _):
            where = pl.ds(pl.multiple_of(t * 256, 256), 256)
            two = pl.ds(2 * t, 2)
            q = R.qkv[where, cols]
            grad = R.do[two, :, cols].reshape(256, 128)
            prod = grad.astype(f32) * R.at[two, :, cols].reshape(256, 128).astype(f32)
            query = None
            for e in range(2):
                h = pair * 2 + e
                qe, ge = only(q, e), only(grad, e)
                scores = nt(qe, R.qkv[:, kcols])
                scores = (scores.reshape(4, 64, 1024) + R.bias[h * 4 + t][:, None, :]).reshape(256, 1024)
                chances = jnp.exp(scores - R.lse[where, h:h + 1])
                central = jnp.sum(only(prod, e), axis=-1, keepdims=True)
                moved = nt(ge, R.qkv[:, vcols])
                back = (chances * (moved - central)).astype(bf16)
                R.dv[...] += tn(chances.astype(bf16), ge)
                R.dk[...] += tn(back, qe)
                got = nn(back, R.qkv[:, kcols])
                query = got if e == 0 else jnp.where(low_lane, query, got)
            R.qkv[where, cols] = (query * 0.125).astype(bf16)
            return 0

        lax.fori_loop(0, 4, tile, 0)
        R.qkv[:, kcols] = R.dk[...].astype(bf16)
        R.qkv[:, vcols] = R.dv[...].astype(bf16)

    attend_back(0)
    for k in range(4):
        two_late(k)
    for k in range(4):
        o_middle(k)
    attend_back(1)
    for k in range(4):
        one_late(k)
    for k in range(4):
        o_late(k)

    net.settle("xr")

    def unproject(step, _):
        where = pl.ds(pl.multiple_of(step * 256, 256), 256)
        made = nt(R.qkv[where, :], R.wq[...].reshape(1024, 768)).astype(bf16)
        R.xr[pl.ds(2 * step, 2)] = made.reshape(2, 2, 64, 1024)
        return 0

    lax.fori_loop(0, 4, unproject, 0)
    rgs_s, rgx_s, gnr_s = net.slots(1), net.slots(4), net.slots(4)
    net.send(R.xr.at[:, flip], R.rgs, sib, rgs_s)

    def outer_in(n, _):
        cols = pl.ds(pl.multiple_of(n * 256, 256), 256)
        made = tn(R.n1[:, :, cols].reshape(1024, 256), R.qkv[...]).astype(bf16)
        R.wq[n] = made.reshape(2, 2, 2, 32, 768)
        return 0

    lax.fori_loop(0, 4, outer_in, 0)
    rqy_s, rqz_s, rqf_s = net.slots(4), net.slots(4), net.slots(4)
    for k in (1, 2, 3, 0):
        zt = turn[k]
        net.send(R.wq.at[zt, :, 1 - y], R.rqy.at[zt], yn, rqy_s + zt)
    net.arrive(R.rgs, rgs_s)
    for k in range(4):
        zt = turn[k]
        i = zt * 2 + 1 - x
        R.xr[i, c] = (R.xr[i, c].astype(f32) + R.rgs[i].astype(f32)).astype(bf16)
        net.send(R.xr.at[i, c], R.rgx.at[zt], xn, rgx_s + zt)
    for k in (1, 2, 3, 0):
        zt = turn[k]
        i = zt * 2 + x
        net.arrive(R.rgx.at[zt], rgx_s + zt)
        R.xr[i, c] = (
            R.xr[i, c].astype(f32) + R.rgs[i].astype(f32) + R.rgx[zt].astype(f32)
        ).astype(bf16)
        net.send_or_keep(
            R.xr.at[i, c],
            R.gnr.at[z % 2, c],
            at(zt, x, y, back_c),
            gnr_s + 2 * (z % 2) + c,
            jnp.logical_and(zt == z, c == back_c),
        )
    for k in (1, 2, 3, 0):
        zt = turn[k]
        net.arrive(R.rqy.at[zt], rqy_s + zt)
        R.wq[zt, :, y] = (R.wq[zt, :, y].astype(f32) + R.rqy[zt].astype(f32)).astype(bf16)
        if k:
            net.send(R.wq.at[zt, :, y], R.rqz.at[z], at(zt, x, y, c), rqz_s + z)

    dw2_ref[...] = two_final()
    dwo_ref[...] = o_final()

    for b in range(2):
        for cc in range(2):
            net.arrive(R.gnr.at[b, cc], gnr_s + 2 * b + cc)
    sums = [jnp.zeros((1, 1024), f32) for _ in range(2)]
    for k in range(4):
        rows = slice((k % 2) * 64, (k % 2) * 64 + 64)
        grad = R.gnr[k // 2, k % 2].astype(f32)
        scaled, inverse = row_stats(x_in[k // 2, k % 2].astype(f32))
        sums[0] = sums[0] + column_sum(grad * scaled)
        sums[1] = sums[1] + column_sum(grad)
        gx_ref[k // 2, rows, :] = R.gm[k * 64:(k + 1) * 64, :] + norm_pullback(
            grad, scaled, inverse, R.vec[0:1, :]
        )
    for k in range(2):
        note(k, sums[k])
    sg_r = net.slots(8)
    for k in range(4):
        for xx in (x, 1 - x):
            if k == 0 and xx is x:
                continue
            zt = turn[k]
            net.send(R.sg.at[zt * 2 + xx], R.rsg.at[s], at(zt, xx, y, c), sg_r + s)

    made = one_final()
    R.f1[...] = made
    r1f_s = net.slots(1)
    net.send(R.f1.at[flip], R.r1f, sib, r1f_s)

    total = R.wq[z, :, y].astype(f32)
    for zt in turn[1:]:
        net.arrive(R.rqz.at[zt], rqz_s + zt)
        total = total + R.rqz[zt].astype(f32)
    R.fq[...] = total
    R.rqf[hd] = R.fq[x, c]
    for xx, cc, dev in ((x, flip, sib), (1 - x, c, xn), (1 - x, flip, at(z, 1 - x, y, flip))):
        net.send(R.fq.at[xx, cc], R.rqf.at[hd], dev, rqf_s + hd)

    total = R.sg[s]
    for k in range(4):
        for xx in (x, 1 - x):
            if k == 0 and xx is x:
                continue
            i = turn[k] * 2 + xx
            net.arrive(R.rsg.at[i], sg_r + i)
            total = total + R.rsg[i]
    R.sgt[0] = total
    sy, ss = net.slots(1), net.slots(1)
    net.send(R.sgt.at[0], R.rsy.at[0], yn, sy)
    net.arrive(R.rsy.at[0], sy)
    total = total + R.rsy[0]
    R.sgt[1] = total
    net.send(R.sgt.at[1], R.rsy.at[1], sib, ss)

    net.arrive(R.r1f, r1f_s)
    mine, theirs = R.f1[c], R.r1f[...]
    first = jnp.where(c == 0, mine, theirs)
    second = jnp.where(c == 0, theirs, mine)
    for k in range(16):
        dw1_ref[:, 2 * k * 128:(2 * k + 1) * 128] = first[:, k * 128:(k + 1) * 128]
        dw1_ref[:, (2 * k + 1) * 128:(2 * k + 2) * 128] = second[:, k * 128:(k + 1) * 128]
    for xx, cc in ((x, flip), (1 - x, c), (1 - x, flip)):
        net.arrive(R.rqf.at[2 * xx + cc], rqf_s + 2 * xx + cc)
    for h in range(4):
        for t in range(3):
            dwq_ref[:, t * 1024 + h * 256:t * 1024 + (h + 1) * 256] = R.rqf[
                h, :, t * 256:(t + 1) * 256
            ]
    net.arrive(R.rsy.at[1], ss)
    row = lax.broadcasted_iota(jnp.int32, (8, 128), 0)
    sg_ref[...] = total + jnp.where(row < 5, R.rsy[1], 0.0)
    net.settle(everything=True)


def local_fused(
    arriving_features,
    valid_extents,
    sampled_target_tiles,
    query_context_mapping,
    attention_outflow_weights,
    expansion_weights,
    contraction_weights,
    opening_scale_vector,
    opening_shift_vector,
    closing_scale_vector,
    closing_shift_vector,
    expansion_shift,
    contraction_shift,
    output_sensitivity,
):
    docs, heads, blocks, count = sampled_target_tiles.shape
    tiles = sampled_target_tiles.reshape(docs, heads * blocks, count)
    extents = jnp.broadcast_to(valid_extents[:, None, None], (docs, heads * blocks, 1))
    aux = jnp.concatenate([tiles, extents], axis=2)
    aux = jnp.pad(aux, ((0, 0), (0, 0), (0, 124))).reshape(docs, 4, 64, 128)
    line_one = jnp.concatenate(
        [opening_scale_vector, opening_shift_vector, closing_scale_vector, closing_shift_vector]
    )
    line_two = jnp.pad(contraction_shift, (0, 96))
    small = jnp.pad(jnp.stack([line_one, line_two, expansion_shift]), ((0, 5), (0, 0))).astype(f32)
    shapes = (
        (arriving_features.shape, bf16),
        (arriving_features.shape, f32),
        (query_context_mapping.shape, f32),
        (attention_outflow_weights.shape, f32),
        (expansion_weights.shape, f32),
        (contraction_weights.shape, f32),
        ((8, 128), f32),
    )
    whole = pl.BlockSpec(memory_space=pltpu.VMEM)
    made = pl.pallas_call(
        layer_kernel,
        name="layer",
        out_shape=[jax.ShapeDtypeStruct(a, b) for a, b in shapes],
        in_specs=[whole] * 8,
        out_specs=[whole] * 7,
        scratch_shapes=[pltpu.VMEM(a, b) for a, b in SCRATCH.values()]
        + [
            pltpu.SemaphoreType.DMA((SENDS,)),
            pltpu.SemaphoreType.DMA((RECVS,)),
            pltpu.SemaphoreType.REGULAR,
        ],
        compiler_params=pltpu.CompilerParams(
            collective_id=0, has_side_effects=True, vmem_limit_bytes=VMEM_BYTES
        ),
    )(
        arriving_features.reshape(2, 2, 64, 1024),
        output_sensitivity,
        aux,
        query_context_mapping,
        attention_outflow_weights,
        expansion_weights,
        contraction_weights,
        small,
    )
    sums = made[6]
    doc = lax.axis_index("doc")
    narrow = lax.dynamic_slice(sums, (0, doc * 32), (5, 32))
    up = lax.dynamic_slice(sums, (5 + doc // 2, 0), (1, 128))
    return tuple(made[:6]) + (narrow[0], narrow[1], narrow[2], narrow[3], up[0], narrow[4])


def fits_fused(mesh, arguments):
    features, tiles, expand = arguments[0], arguments[2], arguments[5]
    return (
        dict(mesh.shape) == {"seq": 8, "doc": 4}
        and features.shape == (8, 1024, 1024)
        and tiles.shape == (8, 16, 16, 3)
        and expand.shape == (1024, 4096)
    )


def solution(mesh):
    in_specs = (
        P("doc", "seq", None),
        P("doc"),
        P("doc", None, None, None),
        P(("seq", "doc"), None),
        P(("seq", "doc"), None),
        P(("seq", "doc"), None),
        P(("seq", "doc"), None),
        P(("seq", "doc")),
        P(("seq", "doc")),
        P(("seq", "doc")),
        P(("seq", "doc")),
        P(("seq", "doc")),
        P(("seq", "doc")),
        P("doc", "seq", None),
    )
    out_specs = (
        P("doc", "seq", None),
        P("doc", "seq", None),
        P(("seq", "doc"), None),
        P(("seq", "doc"), None),
        P(("seq", "doc"), None),
        P(("seq", "doc"), None),
        P(("seq", "doc")),
        P(("seq", "doc")),
        P(("seq", "doc")),
        P(("seq", "doc")),
        P(("seq", "doc")),
        P(("seq", "doc")),
    )

    def run(*arguments):
        body = local_fused if fits_fused(mesh, arguments) else local
        mapped = jax.shard_map(
            body, mesh=mesh, in_specs=in_specs, out_specs=out_specs, check_vma=False
        )
        return mapped(*arguments)

    return run
```

```python
import types

import jax
import jax.numpy as jnp
from jax import lax
from jax.experimental import pallas as pl
from jax.experimental.pallas import tpu as pltpu
from jax.sharding import PartitionSpec as P

group_heads = 4
epsilon = 1e-05
negative = -1e30


def normalise_each_line(values, scaling, shifting):
    centered = values - jnp.mean(values, axis=-1, keepdims=True)
    inverse = lax.rsqrt(jnp.mean(centered * centered, axis=-1, keepdims=True) + epsilon)
    scaled = centered * inverse
    return (scaled * scaling + shifting, scaled, inverse)


def standardize_rows_pullback(grad_norm, scaled, inverse, scaling):
    grad_scaled = grad_norm * scaling
    centred_grad = grad_scaled - jnp.mean(grad_scaled, axis=-1, keepdims=True)
    centred_grad = centred_grad - scaled * jnp.mean(grad_scaled * scaled, axis=-1, keepdims=True)
    return (centred_grad * inverse, jnp.sum(grad_norm * scaled, axis=0), jnp.sum(grad_norm, axis=0))


def exact_gelu(values):
    return jax.nn.gelu(values, approximate=False)


def dense_width():
    return 8


def split_heads(array):
    return array.reshape((array.shape[0] // group_heads, group_heads) + array.shape[1:])


def join_heads(array):
    return array.reshape((array.shape[0] * array.shape[1],) + array.shape[2:])


def candidate_table(span_number, drawn_ordering, first_block, local_blocks, block_size):
    head_count, slot_blocks, random_count = drawn_ordering.shape
    query_blocks = first_block + jnp.arange(local_blocks, dtype=jnp.int32)
    last_block = (span_number - 1) // block_size
    picked = lax.dynamic_slice_in_dim(drawn_ordering, first_block, local_blocks, 1)
    window = jnp.stack([query_blocks - 1, query_blocks, query_blocks + 1], axis=1)
    edges = jnp.stack(
        [jnp.zeros_like(query_blocks), jnp.zeros_like(query_blocks) + last_block], axis=1
    )
    window = jnp.broadcast_to(window[None], (head_count, local_blocks, 3))
    edges = jnp.broadcast_to(edges[None], (head_count, local_blocks, 2))
    candidates = jnp.concatenate([window, picked, edges], axis=2)
    candidate_count = candidates.shape[2]
    inside = (candidates >= 0) & (candidates < slot_blocks)
    earlier = jnp.arange(candidate_count)[:, None] > jnp.arange(candidate_count)[None, :]
    repeated = jnp.any((candidates[:, :, :, None] == candidates[:, :, None, :]) & earlier, axis=3)
    usable = inside & jnp.logical_not(repeated)
    clipped = jnp.clip(candidates, 0, slot_blocks - 1)
    places = clipped[:, :, :, None] * block_size + jnp.arange(block_size, dtype=jnp.int32)
    keep = usable[:, :, :, None] & (places < span_number)
    flags = (query_blocks == 0) | (query_blocks == last_block)
    return (clipped, keep, flags)


def select_blocks(rows, clipped, block_size):
    slot_size, head_count, head_dim = rows.shape
    shaped = rows.reshape(slot_size // block_size, block_size, head_count, head_dim)
    head_index = jnp.arange(head_count, dtype=jnp.int32)[:, None, None]
    return shaped[clipped, :, head_index, :]


def sparse_forward(parts):
    query_group, key_group, value_group, keep_group = parts
    scale = query_group.shape[-1] ** (-0.5)
    scores = (
        jnp.einsum("hitd,hickd->hitck", query_group, key_group, preferred_element_type=jnp.float32)
        * scale
    )
    scores = jnp.where(keep_group[:, :, None], scores, negative)
    shape = scores.shape
    flat = scores.reshape(shape[0], shape[1], shape[2], shape[3] * shape[4])
    highest = jnp.max(flat, axis=-1, keepdims=True)
    weights_exp = jnp.exp(flat - highest)
    totals = jnp.sum(weights_exp, axis=-1, keepdims=True)
    chances_low = (weights_exp / totals).astype(jnp.bfloat16).reshape(shape)
    mixed = jnp.einsum(
        "hitck,hickd->hitd", chances_low, value_group, preferred_element_type=jnp.float32
    )
    return (mixed, (highest + jnp.log(totals))[..., 0])


def sparse_backward(parts):
    query_group, key_group, value_group, keep_group, log_group, grad_group = parts
    scale = query_group.shape[-1] ** (-0.5)
    scores = (
        jnp.einsum("hitd,hickd->hitck", query_group, key_group, preferred_element_type=jnp.float32)
        * scale
    )
    scores = jnp.where(keep_group[:, :, None], scores, negative)
    chances = jnp.exp(scores - log_group[..., None, None])
    grad_chances = jnp.einsum(
        "hitd,hickd->hitck", grad_group, value_group, preferred_element_type=jnp.float32
    )
    central = jnp.sum(chances * grad_chances, axis=(3, 4), keepdims=True)
    grad_scores = (chances * (grad_chances - central)).astype(jnp.bfloat16)
    query_term = (
        jnp.einsum("hitck,hickd->hitd", grad_scores, key_group, preferred_element_type=jnp.float32)
        * scale
    )
    key_term = (
        jnp.einsum(
            "hitck,hitd->hickd", grad_scores, query_group, preferred_element_type=jnp.float32
        )
        * scale
    )
    value_term = jnp.einsum(
        "hitck,hitd->hickd",
        chances.astype(jnp.bfloat16),
        grad_group,
        preferred_element_type=jnp.float32,
    )
    return (query_term, key_term, value_term)


def dense_forward(query_block, key_rows, value_rows, span_number):
    block_size, head_count, head_dim = query_block.shape
    width_group = dense_width()
    scale = head_dim ** (-0.5)
    valid = jnp.arange(key_rows.shape[0], dtype=jnp.int32) < span_number

    def one_group(number):
        offset = number * width_group
        query_part = lax.dynamic_slice_in_dim(query_block, offset, width_group, 1)
        key_part = lax.dynamic_slice_in_dim(key_rows, offset, width_group, 1)
        value_part = lax.dynamic_slice_in_dim(value_rows, offset, width_group, 1)
        scores = (
            jnp.einsum("tgd,kgd->gtk", query_part, key_part, preferred_element_type=jnp.float32)
            * scale
        )
        scores = jnp.where(valid[None, None, :], scores, negative)
        highest = jnp.max(scores, axis=-1, keepdims=True)
        weights_exp = jnp.exp(scores - highest)
        totals = jnp.sum(weights_exp, axis=-1, keepdims=True)
        chances_low = (weights_exp / totals).astype(jnp.bfloat16)
        mixed = jnp.einsum(
            "gtk,kgd->gtd", chances_low, value_part, preferred_element_type=jnp.float32
        )
        return (mixed, (highest + jnp.log(totals))[:, :, 0])

    mixed_all, logs_all = lax.map(one_group, jnp.arange(head_count // width_group, dtype=jnp.int32))
    mixed_all = mixed_all.reshape(head_count, block_size, head_dim).transpose(1, 0, 2)
    return (mixed_all, logs_all.reshape(head_count, block_size))


def dense_skip(query_block, key_rows, value_rows, span_number):
    block_size, head_count, head_dim = query_block.shape
    return (
        jnp.zeros((block_size, head_count, head_dim), jnp.float32),
        jnp.zeros((head_count, block_size), jnp.float32),
    )


def dense_back(query_block, grad_block, key_rows, value_rows, log_block, span_number):
    block_size, head_count, head_dim = query_block.shape
    slot_size = key_rows.shape[0]
    width_group = dense_width()
    scale = head_dim ** (-0.5)
    valid = jnp.arange(slot_size, dtype=jnp.int32) < span_number

    def one_group(number):
        offset = number * width_group
        query_part = lax.dynamic_slice_in_dim(query_block, offset, width_group, 1)
        grad_part = lax.dynamic_slice_in_dim(grad_block, offset, width_group, 1)
        key_part = lax.dynamic_slice_in_dim(key_rows, offset, width_group, 1)
        value_part = lax.dynamic_slice_in_dim(value_rows, offset, width_group, 1)
        scores = (
            jnp.einsum("tgd,kgd->gtk", query_part, key_part, preferred_element_type=jnp.float32)
            * scale
        )
        scores = jnp.where(valid[None, None, :], scores, negative)
        chances = jnp.exp(
            scores - lax.dynamic_slice_in_dim(log_block, offset, width_group, 0)[:, :, None]
        )
        grad_chances = jnp.einsum(
            "tgd,kgd->gtk", grad_part, value_part, preferred_element_type=jnp.float32
        )
        central = jnp.sum(chances * grad_chances, axis=-1, keepdims=True)
        grad_scores = (chances * (grad_chances - central)).astype(jnp.bfloat16)
        query_new = (
            jnp.einsum("gtk,kgd->gtd", grad_scores, key_part, preferred_element_type=jnp.float32)
            * scale
        )
        key_new = (
            jnp.einsum("gtk,tgd->gkd", grad_scores, query_part, preferred_element_type=jnp.float32)
            * scale
        )
        value_new = jnp.einsum(
            "gtk,tgd->gkd",
            chances.astype(jnp.bfloat16),
            grad_part,
            preferred_element_type=jnp.float32,
        )
        return (key_new, value_new, query_new)

    key_all, value_all, query_all = lax.map(
        one_group, jnp.arange(head_count // width_group, dtype=jnp.int32)
    )
    slot_terms = jnp.stack(
        [
            key_all.reshape(head_count, slot_size, head_dim),
            value_all.reshape(head_count, slot_size, head_dim),
        ]
    )
    return (slot_terms, query_all.reshape(head_count, block_size, head_dim).transpose(1, 0, 2))


def dense_pass(query_block, grad_block, key_rows, value_rows, log_block, span_number):
    block_size, head_count, head_dim = query_block.shape
    return (
        jnp.zeros((2, head_count, key_rows.shape[0], head_dim), jnp.float32),
        jnp.zeros(query_block.shape, jnp.float32),
    )


def return_grads(slot_grads):
    owned = lax.psum_scatter(
        slot_grads.astype(jnp.bfloat16), "seq", scatter_dimension=2, tiled=True
    ).astype(jnp.float32)
    pair_count, head_count, tok_count, head_dim = owned.shape
    return owned.transpose(2, 0, 1, 3).reshape(tok_count, pair_count * head_count * head_dim)


def flagged_place(flags):
    return jnp.sum(jnp.where(flags, jnp.arange(flags.shape[0], dtype=jnp.int32), 0))


def local(
    arriving_features,
    valid_extents,
    sampled_target_tiles,
    query_context_mapping,
    attention_outflow_weights,
    expansion_weights,
    contraction_weights,
    opening_scale_vector,
    opening_shift_vector,
    closing_scale_vector,
    closing_shift_vector,
    expansion_shift,
    contraction_shift,
    output_sensitivity,
):
    doc_count, tok_count, feature_breadth = arriving_features.shape
    head_count = sampled_target_tiles.shape[1]
    slot_blocks = sampled_target_tiles.shape[2]
    head_dim = feature_breadth // head_count
    slot_size = tok_count * lax.axis_size("seq")
    block_size = slot_size // slot_blocks
    local_blocks = tok_count // block_size
    first_block = lax.axis_index("seq") * local_blocks
    per_line_summation = doc_count * tok_count
    (
        full_inward,
        entire_outflow,
        full_expand,
        full_contract,
        overall_premultiplier,
        overall_shift_term,
        full_midscale,
        full_midshift,
        full_upshift,
        full_downshift,
    ) = (
        lax.all_gather(query_context_mapping, ("seq", "doc"), axis=0, tiled=True),
        lax.all_gather(attention_outflow_weights, ("seq", "doc"), axis=0, tiled=True),
        lax.all_gather(expansion_weights, ("seq", "doc"), axis=0, tiled=True),
        lax.all_gather(contraction_weights, ("seq", "doc"), axis=0, tiled=True),
        lax.all_gather(opening_scale_vector, ("seq", "doc"), axis=0, tiled=True),
        lax.all_gather(opening_shift_vector, ("seq", "doc"), axis=0, tiled=True),
        lax.all_gather(closing_scale_vector, ("seq", "doc"), axis=0, tiled=True),
        lax.all_gather(closing_shift_vector, ("seq", "doc"), axis=0, tiled=True),
        lax.all_gather(expansion_shift, ("seq", "doc"), axis=0, tiled=True),
        lax.all_gather(contraction_shift, ("seq", "doc"), axis=0, tiled=True),
    )
    shortcut_holder = arriving_features.reshape(per_line_summation, feature_breadth).astype(
        jnp.float32
    )
    opening_normalised, scaled_one, inverse_one = normalise_each_line(
        shortcut_holder,
        overall_premultiplier.astype(jnp.float32),
        overall_shift_term.astype(jnp.float32),
    )
    opening_normalised = opening_normalised.astype(jnp.bfloat16)
    projected = jnp.dot(opening_normalised, full_inward, preferred_element_type=jnp.float32).astype(
        jnp.bfloat16
    )
    query_local = projected[:, :feature_breadth].reshape(doc_count, tok_count, head_count, head_dim)
    pair_local = projected[:, feature_breadth:].reshape(doc_count, tok_count, 2 * feature_breadth)
    pair_full = lax.all_gather(pair_local, "seq", axis=1, tiled=True)

    def table_one(span_number, drawn_ordering):
        return candidate_table(span_number, drawn_ordering, first_block, local_blocks, block_size)

    clipped_all, keep_all, flags_all = jax.vmap(table_one)(valid_extents, sampled_target_tiles)
    query_heads = query_local.reshape(
        doc_count, local_blocks, block_size, head_count, head_dim
    ).transpose(0, 3, 1, 2, 4)
    block_flags = flags_all[:, :, None, None, None]

    def doc_forward(items):
        queries, pair_rows, clipped, keep = items
        key_sel = select_blocks(
            pair_rows[:, :feature_breadth].reshape(slot_size, head_count, head_dim),
            clipped,
            block_size,
        )
        value_sel = select_blocks(
            pair_rows[:, feature_breadth:].reshape(slot_size, head_count, head_dim),
            clipped,
            block_size,
        )
        mixed, log_sums = lax.map(
            sparse_forward,
            (split_heads(queries), split_heads(key_sel), split_heads(value_sel), split_heads(keep)),
        )
        return (join_heads(mixed), join_heads(log_sums))

    sparse_mixed, sparse_logs = lax.map(
        doc_forward, (query_heads, pair_full, clipped_all, keep_all)
    )
    mixed_rows = sparse_mixed.transpose(0, 2, 3, 1, 4)

    def doc_dense(items):
        queries, pair_rows, span_number, flags = items
        key_rows = pair_rows[:, :feature_breadth].reshape(slot_size, head_count, head_dim)
        value_rows = pair_rows[:, feature_breadth:].reshape(slot_size, head_count, head_dim)
        query_block = lax.dynamic_slice_in_dim(
            queries, flagged_place(flags) * block_size, block_size, 0
        )
        return lax.cond(
            jnp.any(flags),
            dense_forward,
            dense_skip,
            query_block,
            key_rows,
            value_rows,
            span_number,
        )

    dense_mixed, dense_logs = lax.map(doc_dense, (query_local, pair_full, valid_extents, flags_all))
    mixed_rows = jnp.where(block_flags, dense_mixed[:, None], mixed_rows)
    context_mixture = mixed_rows.reshape(per_line_summation, feature_breadth).astype(jnp.bfloat16)
    intermediate_state = shortcut_holder + jnp.dot(
        context_mixture, entire_outflow, preferred_element_type=jnp.float32
    )
    normed_two, scaled_two, inverse_two = normalise_each_line(
        intermediate_state, full_midscale.astype(jnp.float32), full_midshift.astype(jnp.float32)
    )
    normed_two = normed_two.astype(jnp.bfloat16)
    pre_act = jnp.dot(
        normed_two, full_expand, preferred_element_type=jnp.float32
    ) + full_upshift.astype(jnp.float32)
    activated = exact_gelu(pre_act).astype(jnp.bfloat16)
    final_rows = (
        intermediate_state
        + jnp.dot(activated, full_contract, preferred_element_type=jnp.float32)
        + full_downshift.astype(jnp.float32)
    )
    output = final_rows.astype(jnp.bfloat16).reshape(doc_count, tok_count, feature_breadth)
    back_inward, back_outward, back_expand, back_contract, back_prescale, back_midscale = (
        full_inward,
        entire_outflow,
        full_expand,
        full_contract,
        overall_premultiplier,
        full_midscale,
    )
    grad_out_rows = output_sensitivity.reshape(per_line_summation, feature_breadth)
    grad_out_wide = grad_out_rows.astype(jnp.float32)
    contract_grad = jnp.einsum(
        "rf,rd->fd", activated, grad_out_rows, preferred_element_type=jnp.float32
    )
    downshift_grad = jnp.sum(grad_out_wide, axis=0)
    grad_act = jnp.einsum(
        "rd,fd->rf", grad_out_rows, back_contract, preferred_element_type=jnp.float32
    )
    unused_value, gelu_back = jax.vjp(exact_gelu, pre_act)
    grad_pre = gelu_back(grad_act)[0].astype(jnp.bfloat16)
    expand_grad = jnp.einsum("rd,rf->df", normed_two, grad_pre, preferred_element_type=jnp.float32)
    upshift_grad = jnp.sum(grad_pre.astype(jnp.float32), axis=0)
    grad_norm_two = jnp.einsum(
        "rf,df->rd", grad_pre, back_expand, preferred_element_type=jnp.float32
    )
    middle_part, midscale_grad, midshift_grad = standardize_rows_pullback(
        grad_norm_two, scaled_two, inverse_two, back_midscale.astype(jnp.float32)
    )
    grad_middle = grad_out_wide + middle_part
    grad_branch = grad_middle.astype(jnp.bfloat16)
    outward_grad = jnp.einsum(
        "rd,re->de", context_mixture, grad_branch, preferred_element_type=jnp.float32
    )
    grad_attended = jnp.einsum(
        "re,de->rd", grad_branch, back_outward, preferred_element_type=jnp.float32
    ).astype(jnp.bfloat16)
    grad_attended = grad_attended.reshape(doc_count, tok_count, head_count, head_dim)
    grad_blocks = grad_attended.reshape(doc_count, local_blocks, block_size, head_count, head_dim)
    sparse_grads = jnp.where(block_flags, jnp.zeros_like(grad_blocks), grad_blocks).transpose(
        0, 3, 1, 2, 4
    )
    block_ids = jnp.arange(slot_blocks, dtype=jnp.int32)

    def sparse_back(queries, pair_rows, clipped, keep, log_sums, grad_part):
        key_rows = pair_rows[:, :feature_breadth].reshape(slot_size, head_count, head_dim)
        value_rows = pair_rows[:, feature_breadth:].reshape(slot_size, head_count, head_dim)
        key_sel = select_blocks(key_rows, clipped, block_size)
        value_sel = select_blocks(value_rows, clipped, block_size)
        grouped = (
            split_heads(queries),
            split_heads(key_sel),
            split_heads(value_sel),
            split_heads(keep),
            split_heads(log_sums),
            split_heads(grad_part),
        )
        query_term, key_term, value_term = lax.map(sparse_backward, grouped)
        query_term = join_heads(query_term)
        key_term = join_heads(key_term)
        value_term = join_heads(value_term)
        placing = (clipped[..., None] == block_ids).astype(jnp.float32)
        key_slot = jnp.einsum(
            "hlcn,hlcbd->hnbd",
            placing,
            key_term,
            precision=lax.Precision.HIGHEST,
            preferred_element_type=jnp.float32,
        )
        value_slot = jnp.einsum(
            "hlcn,hlcbd->hnbd",
            placing,
            value_term,
            precision=lax.Precision.HIGHEST,
            preferred_element_type=jnp.float32,
        )
        slot_grads = jnp.stack(
            [
                key_slot.reshape(head_count, slot_size, head_dim),
                value_slot.reshape(head_count, slot_size, head_dim),
            ]
        )
        return (query_term, slot_grads, key_rows, value_rows)

    def doc_backward(carry, items):
        (
            queries,
            pair_rows,
            clipped,
            keep,
            log_sums,
            grad_part,
            grad_rows,
            query_rows,
            dense_log,
            span_number,
            flags,
        ) = items
        query_term, slot_grads, key_rows, value_rows = sparse_back(
            queries, pair_rows, clipped, keep, log_sums, grad_part
        )
        start = flagged_place(flags) * block_size
        query_block = lax.dynamic_slice_in_dim(query_rows, start, block_size, 0)
        grad_block = lax.dynamic_slice_in_dim(grad_rows, start, block_size, 0)
        dense_slot, dense_term = lax.cond(
            jnp.any(flags),
            dense_back,
            dense_pass,
            query_block,
            grad_block,
            key_rows,
            value_rows,
            dense_log,
            span_number,
        )
        owned = return_grads(slot_grads + dense_slot)
        return (carry, (query_term, dense_term, owned))

    unused_carry, (sparse_query, dense_query, pair_grads) = lax.scan(
        doc_backward,
        jnp.zeros((), jnp.int32),
        (
            query_heads,
            pair_full,
            clipped_all,
            keep_all,
            sparse_logs,
            sparse_grads,
            grad_attended,
            query_local,
            dense_logs,
            valid_extents,
            flags_all,
        ),
    )
    query_grad = sparse_query.transpose(0, 2, 3, 1, 4) + jnp.where(
        block_flags, dense_query[:, None], 0.0
    )
    grad_projected = jnp.concatenate(
        [
            query_grad.reshape(per_line_summation, feature_breadth),
            pair_grads.reshape(per_line_summation, 2 * feature_breadth),
        ],
        axis=1,
    ).astype(jnp.bfloat16)
    inward_grad = jnp.einsum(
        "rd,re->de", opening_normalised, grad_projected, preferred_element_type=jnp.float32
    )
    grad_norm_one = jnp.einsum(
        "re,de->rd", grad_projected, back_inward, preferred_element_type=jnp.float32
    )
    incoming_slice, leading_gain_sensitivity, leading_offset_sensitivity = (
        standardize_rows_pullback(
            grad_norm_one, scaled_one, inverse_one, back_prescale.astype(jnp.float32)
        )
    )
    grad_inputs = (grad_middle + incoming_slice).reshape(doc_count, tok_count, feature_breadth)
    summed = (
        lax.psum_scatter(inward_grad, ("seq", "doc"), scatter_dimension=0, tiled=True),
        lax.psum_scatter(outward_grad, ("seq", "doc"), scatter_dimension=0, tiled=True),
        lax.psum_scatter(expand_grad, ("seq", "doc"), scatter_dimension=0, tiled=True),
        lax.psum_scatter(contract_grad, ("seq", "doc"), scatter_dimension=0, tiled=True),
        lax.psum_scatter(leading_gain_sensitivity, ("seq", "doc"), scatter_dimension=0, tiled=True),
        lax.psum_scatter(
            leading_offset_sensitivity, ("seq", "doc"), scatter_dimension=0, tiled=True
        ),
        lax.psum_scatter(midscale_grad, ("seq", "doc"), scatter_dimension=0, tiled=True),
        lax.psum_scatter(midshift_grad, ("seq", "doc"), scatter_dimension=0, tiled=True),
        lax.psum_scatter(upshift_grad, ("seq", "doc"), scatter_dimension=0, tiled=True),
        lax.psum_scatter(downshift_grad, ("seq", "doc"), scatter_dimension=0, tiled=True),
    )
    return (output, grad_inputs) + tuple(summed)


ROUTE = pl.DeviceIdType.MESH
NZ, NX, NY, NC = 4, 2, 2, 2
bf16, f32 = jnp.bfloat16, jnp.float32


def nn(left, right):
    return lax.dot_general(left, right, (((1,), (0,)), ((), ())), preferred_element_type=f32)


def nt(left, right):
    return lax.dot_general(left, right, (((1,), (1,)), ((), ())), preferred_element_type=f32)


def tn(left, right):
    return lax.dot_general(left, right, (((0,), (0,)), ((), ())), preferred_element_type=f32)


def loop(count, body):
    lax.fori_loop(0, count, body, 0)


class Net:
    def __init__(self, send_sems, recv_sems, here):
        self.send_sems, self.recv_sems, self.here = send_sems, recv_sems, here
        self.sent, self.taken = 0, 0
        self.open = []

    def slots(self, count):
        first = self.taken
        self.taken += count
        assert self.taken <= RECVS
        return first

    def copy(self, src, dst, device, slot, index):
        return pltpu.make_async_remote_copy(
            src_ref=src,
            dst_ref=dst,
            send_sem=self.send_sems.at[index],
            recv_sem=self.recv_sems.at[slot],
            device_id=device,
            device_id_type=ROUTE,
        )

    def series(self, count, describe, group=None):
        base = self.sent
        self.sent += count
        assert self.sent <= SENDS

        def start(i):
            src, dst, device, slot, is_self, made = describe(i)
            copy = self.copy(src, dst, device, slot, base + i)
            if is_self is None:
                if made is None:
                    copy.start()
                else:
                    pl.when(made)(copy.start)
            else:
                pl.when(jnp.logical_not(is_self))(copy.start)
                pl.when(is_self)(pltpu.make_async_copy(src, dst, self.recv_sems.at[slot]).start)

        def finish():
            for i in range(count):
                src, dst, device, slot, is_self, made = describe(i)
                copy = self.copy(src, dst, device, slot, base + i)
                if is_self is not None:
                    made = jnp.logical_not(is_self)
                if made is None:
                    copy.wait_send()
                else:
                    pl.when(made)(copy.wait_send)

        self.open.append((group, finish))
        return start

    def send(self, src, dst, device, slot, group=None, is_self=None, made=None):
        self.series(1, lambda i: (src, dst, device, slot, is_self, made), group)(0)

    def settle(self, group=None, everything=False):
        rest = []
        for name, finish in self.open:
            if everything or name == group:
                finish()
            else:
                rest.append((name, finish))
        self.open = rest

    def arrive(self, dst, slot):
        self.copy(dst, dst, self.here, slot, 0).wait_recv()


def row_stats(values):
    mean = jnp.mean(values, axis=-1, keepdims=True)
    centered = values - mean
    inverse = lax.rsqrt(jnp.mean(centered * centered, axis=-1, keepdims=True) + epsilon)
    return centered * inverse, inverse


def norm_pullback(grad, scaled, inverse, gain):
    wide = grad * gain
    first = jnp.mean(wide, axis=-1, keepdims=True)
    second = jnp.mean(wide * scaled, axis=-1, keepdims=True)
    return (wide - first - scaled * second) * inverse


def column_sum(values):
    return jnp.sum(values, axis=0, keepdims=True)


SCRATCH = dict(
    xr=((8, 2, 64, 1024), bf16),
    n1=((8, 128, 1024), bf16),
    aux=((64, 128), jnp.int32),
    bias=((16, 4, 1024), f32),
    sv=((4, 2, 2, 2, 8, 128), f32),
    vec=((8, 1024), f32),
    b1=((1, 1024), f32),
    wqs=((4, 32, 768), bf16),
    wq=((4, 2, 2, 2, 32, 768), bf16),
    wo=((4, 2, 2, 2, 32, 1024), bf16),
    w1s=((4, 32, 1024), bf16),
    w1=((4, 2, 2, 2, 32, 1024), bf16),
    w2=((4, 2, 128, 1024), bf16),
    qkv=((1024, 768), bf16),
    lse=((1024, 128), f32),
    at=((8, 128, 256), bf16),
    att=((2, 4, 128, 256), bf16),
    mid=((256, 1024), f32),
    nt2=((4, 256, 1024), bf16),
    dyx=((4, 256, 1024), bf16),
    act=((4, 256, 1024), bf16),
    gp=((4, 256, 1024), bf16),
    dw2=((4, 2, 128, 1024), bf16),
    own=((256, 1024), f32),
    gps=((4, 256, 1024), bf16),
    gpr=((2, 256, 1024), bf16),
    gpx=((256, 1024), bf16),
    ops=((4, 256, 1024), bf16),
    opr=((2, 256, 1024), bf16),
    opx=((256, 1024), bf16),
    gb=((256, 1024), bf16),
    gm=((256, 1024), f32),
    da=((2, 4, 128, 256), bf16),
    do=((8, 128, 256), bf16),
    dk=((1024, 256), f32),
    dv=((1024, 256), f32),
    rgs=((8, 64, 1024), bf16),
    rgx=((4, 64, 1024), bf16),
    gnr=((2, 2, 64, 1024), bf16),
    r1y=((4, 2, 2, 32, 1024), bf16),
    r1z=((4, 2, 2, 32, 1024), bf16),
    r1v=((2, 2, 32, 1024), bf16),
    f1=((2, 2, 32, 1024), f32),
    r1f=((4, 32, 1024), f32),
    r2y=((4, 128, 1024), bf16),
    r2z=((4, 128, 1024), bf16),
    r2v=((128, 1024), bf16),
    ros=((4, 2, 2, 32, 1024), bf16),
    roa=((4, 32, 1024), bf16),
    rob=((4, 32, 1024), bf16),
    rof=((4, 32, 1024), bf16),
    roz=((4, 32, 1024), bf16),
    rov=((32, 1024), bf16),
    rqy=((4, 2, 2, 32, 768), bf16),
    rqz=((4, 2, 2, 32, 768), bf16),
    rqv=((2, 2, 32, 768), bf16),
    fq=((2, 2, 32, 768), f32),
    rqf=((4, 32, 768), f32),
    sg=((2, 8, 8, 128), f32),
    rsg=((2, 8, 8, 128), f32),
    sgt=((2, 8, 128), f32),
    rst=((2, 4, 8, 128), f32),
)
SENDS, RECVS = 256, 256
VMEM_BYTES = 63 * 2**20


def layer_kernel(
    x_in, dy_in, aux_in, wq_in, wo_in, w1_in, w2_in, sv_in,
    out_ref, gx_ref, dwq_ref, dwo_ref, dw1_ref, dw2_ref, sg_ref,
    *rest,
):
    names = list(SCRATCH)
    R = types.SimpleNamespace(**dict(zip(names, rest[: len(names)])))
    send_sems, recv_sems = rest[len(names):]
    s, d = lax.axis_index("seq"), lax.axis_index("doc")
    z, x, y, c = s // NX, s % NX, d // NC, d % NC
    g = 2 * x + c
    flip, xo, yo = 1 - c, 1 - x, 1 - y

    def at(zz, xx, yy, cc):
        return (zz * NX + xx, yy * NC + cc)

    here = (s, d)
    sib, xn, yn, cross = at(z, x, y, flip), at(z, xo, y, c), at(z, x, yo, c), at(z, xo, y, flip)
    group = ((x, flip, sib), (xo, c, xn), (xo, flip, cross))
    net = Net(send_sems, recv_sems, here)
    order = [z, z + 1 - 2 * (z // 2), (2 + 3 * z) % 5, 3 * (1 - z // 2)]
    middle = jnp.logical_or(z == 1, z == 2)

    barrier = pltpu.get_barrier_semaphore()

    def greet(step, _):
        other = (s * NC + c + step) % 16
        pl.semaphore_signal(
            barrier, inc=1, device_id=(other // NC, y * NC + other % NC), device_id_type=ROUTE
        )
        return 0

    lax.fori_loop(1, 16, greet, 0)
    for cc in (c, flip):
        pl.semaphore_signal(barrier, inc=1, device_id=at(z, x, yo, cc), device_id_type=ROUTE)
    pl.semaphore_wait(barrier, 17)

    def z_start(piece, base, name):
        for k in (1, 2, 3):
            net.send(
                piece(z), piece(z), at(order[k], x, y, c), base + z, name, made=middle if k == 3 else None
            )

    def z_take(piece, base, name, k):
        part = piece(order[k])
        net.arrive(part, base + order[k])
        if k == 3:
            net.send(part, part, at(order[2], x, y, c), base + order[3], name, made=middle)
        return part

    half = pl.ds(pl.multiple_of(c * 512, 512), 512)
    other_half = pl.ds(pl.multiple_of(flip * 512, 512), 512)
    xz = net.slots(4)
    for b in range(2):
        for ch in range(2):
            zt = 2 * c + b
            net.send(
                x_in.at[b, :, :, ch * 512:(ch + 1) * 512],
                R.xr.at[s, :, :, ch * 512:(ch + 1) * 512],
                at(zt, x, y, ch),
                xz + z,
                is_self=jnp.logical_and(zt == z, c == ch),
            )

    for h in range(4):
        for t in range(3):
            R.wqs[h, :, t * 256:(t + 1) * 256] = wq_in[:, t * 1024 + h * 256:t * 1024 + (h + 1) * 256]
    R.wq[z, x, y, c] = R.wqs[g]
    wqa = net.slots(4)
    for xx, cc, dev in group:
        net.send(R.wqs.at[2 * xx + cc], R.wq.at[z, x, y, c], dev, wqa + g)

    sv_s, sv_z, sv_x, sv_y = net.slots(1), net.slots(4), net.slots(1), net.slots(1)
    R.sv[z, x, y, c] = sv_in[...]
    net.send(R.sv.at[z, x, y, c], R.sv.at[z, x, y, c], sib, sv_s)

    aux_s = net.slots(1)
    has_table = c == z // 2

    @pl.when(has_table)
    def table():
        R.aux[...] = aux_in[z % 2, g]

    net.send(aux_in.at[z % 2, 2 * x + flip], R.aux, sib, aux_s, made=has_table)

    for h in range(4):
        for q in range(8):
            block = 8 * (q // 2) + 4 * (h // 2) + 2 * (q % 2) + h % 2
            R.w1s[h, :, q * 128:(q + 1) * 128] = w1_in[:, block * 128:(block + 1) * 128]
    R.w1[z, x, y, c] = R.w1s[g]
    w1a = net.slots(4)
    for xx, cc, dev in group:
        net.send(R.w1s.at[2 * xx + cc], R.w1.at[z, x, y, c], dev, w1a + g)
    R.wo[z, x, y, c] = wo_in[...]
    R.w2[z, y] = w2_in[...]
    R.dyx[g] = dy_in[...].reshape(256, 1024)

    def wq_piece(zz):
        return R.wq.at[zz, :, y]

    def w1_piece(zz):
        return R.w1.at[zz, :, y]

    def w2_piece(zz):
        return R.w2.at[zz, y]

    def wo_piece(zz):
        return R.wo.at[zz, x, y, c]

    wqz, wqy, w1z, w1y = net.slots(4), net.slots(4), net.slots(4), net.slots(4)
    w2z, w2y, woz = net.slots(4), net.slots(4), net.slots(4)
    for xx, cc, dev in group:
        net.arrive(R.wq.at[z, xx, y, cc], wqa + 2 * xx + cc)
    z_start(wq_piece, wqz, "w")
    net.send(wq_piece(z), wq_piece(z), yn, wqy + z, "w")
    net.arrive(R.sv.at[z, x, y, flip], sv_s)
    z_start(lambda zz: R.sv.at[zz, x, y], sv_z, None)
    for xx, cc, dev in group:
        net.arrive(R.w1.at[z, xx, y, cc], w1a + 2 * xx + cc)
    net.send(w1_piece(z), w1_piece(z), yn, w1y + z, "w")
    net.send(w2_piece(z), w2_piece(z), yn, w2y + z, "w")

    xx_r, xs_r = net.slots(4), net.slots(8)
    for k in range(4):
        zt = order[k]
        part = R.xr.at[zt * 2 + x, :, :, half]
        net.arrive(part, xz + zt)
        net.send(part, part, xn, xx_r + zt, "xr")
        net.send(part, part, sib, xs_r + zt * 2 + x, "xr")
        if k:
            part = z_take(wq_piece, wqz, "w", k)
            net.send(part, part, yn, wqy + zt, "w")
    z_start(w1_piece, w1z, "w")
    z_start(wo_piece, woz, "w")
    for k in (1, 2, 3):
        z_take(lambda zz: R.sv.at[zz, x, y], sv_z, None, k)
    net.send(R.sv.at[:, x, y], R.sv.at[:, x, y], xn, sv_x)
    for k in range(4):
        zt = order[k]
        part = R.xr.at[zt * 2 + xo, :, :, half]
        net.arrive(part, xx_r + zt)
        net.send(part, part, sib, xs_r + zt * 2 + xo, "xr")
        if k == 0:
            net.arrive(R.sv.at[:, xo, y], sv_x)
            net.send(R.sv.at[:, :, y], R.sv.at[:, :, y], yn, sv_y)

    def group_gather(buf):
        own_s, far_x, far_s = net.slots(1), net.slots(1), net.slots(1)

        def begin():
            net.send(buf.at[g], buf.at[g], sib, own_s)
            net.send(buf.at[g], buf.at[g], xn, far_x)

        def step():
            net.arrive(buf.at[2 * xo + c], far_x)
            net.send(buf.at[2 * xo + c], buf.at[2 * xo + c], sib, far_s)

        def take(which):
            if which == 1:
                net.arrive(buf.at[2 * x + flip], own_s)
            if which == 3:
                net.arrive(buf.at[2 * xo + flip], far_s)

        return begin, step, take

    members = (g, 2 * x + flip, 2 * xo + c, 2 * xo + flip)
    dy_begin, dy_step, dy_take = group_gather(R.dyx)
    nt_begin, nt_step, nt_take = group_gather(R.nt2)

    @pl.when(jnp.logical_not(has_table))
    def table_here():
        net.arrive(R.aux, aux_s)

    for i in range(16):
        tiles = R.aux[i * 4:(i + 1) * 4, :]
        place = lax.broadcasted_iota(jnp.int32, (4, 1024), 1)
        block = place >> 6
        row = lax.broadcasted_iota(jnp.int32, (4, 1024), 0) + (i % 4) * 4
        extent = tiles[:, 3:4]
        last = (extent - 1) >> 6
        seen = jnp.abs(row - block) <= 1
        for k in range(3):
            seen = seen | (block == tiles[:, k:k + 1])
        seen = seen | (block == 0) | (block == last) | (row == 0) | (row == last)
        seen = seen & (place < extent)
        R.bias[i] = jnp.where(seen, 0.0, negative).astype(f32)

    net.arrive(R.sv.at[:, :, yo], sv_y)
    lane = lax.broadcasted_iota(jnp.int32, (1, 128), 1) >> 5
    for r in range(8):
        for k in range(5):
            total = jnp.zeros((1, 128), f32)
            for q in range(4):
                line = R.sv[r // 2, r % 2, q // 2, q % 2, k // 4:k // 4 + 1, :]
                shift = (32 * (q - k % 4)) % 128
                if shift:
                    line = pltpu.roll(line, shift, 1)
                total = jnp.where(lane == q, line, total)
            R.vec[k:k + 1, r * 128:(r + 1) * 128] = total
    for q in range(8):
        R.b1[:, q * 128:(q + 1) * 128] = R.sv[q // 2, x, q % 2, c, 2:3, :]

    def first_norm(step, _):
        zt = (z + step) % NZ
        for k in range(2):
            i = 2 * zt + k
            net.arrive(R.xr.at[i, :, :, other_half], xs_r + i)
            scaled, _inverse = row_stats(R.xr[i].reshape(128, 1024).astype(f32))
            R.n1[i] = (scaled * R.vec[0:1, :] + R.vec[1:2, :]).astype(bf16)
        return 0

    loop(4, first_norm)
    for k in range(4):
        net.arrive(R.wq.at[order[k], :, yo], wqy + order[k])

    def project(step, _):
        rows = R.n1[pl.ds(2 * step, 2)].reshape(256, 1024)
        made = nn(rows, R.wq[...].reshape(1024, 768)).astype(bf16)
        where = pl.ds(pl.multiple_of(step * 256, 256), 256)
        R.qkv[where, :] = jnp.concatenate([made[:, :256] * jnp.asarray(0.125, bf16), made[:, 256:]], axis=1)
        return 0

    loop(4, project)
    dy_begin()
    z_start(w2_piece, w2z, "w")

    low_lane = lax.broadcasted_iota(jnp.int32, (1, 128), 1) < 64

    def only(values, e):
        return jnp.where(low_lane if e == 0 else jnp.logical_not(low_lane), values, jnp.zeros_like(values))

    at_r = net.slots(8)
    back_c = z // 2

    def at_copy(i):
        zt, xx = i // 2, i % 2
        mine = jnp.logical_and(jnp.logical_and(zt == z, xx == x), c == back_c)
        return R.at.at[i], R.att.at[z % 2, g], at(zt, xx, y, back_c), at_r + (z % 2) * 4 + g, mine, None

    at_start = net.series(8, at_copy)

    def attend_tile(step, _):
        t = (z + step) % NZ
        where = pl.ds(pl.multiple_of(t * 256, 256), 256)
        for pair in range(2):
            cols = slice(pair * 128, pair * 128 + 128)
            kcols = slice(256 + pair * 128, 256 + pair * 128 + 128)
            vcols = slice(512 + pair * 128, 512 + pair * 128 + 128)
            q = R.qkv[where, cols]
            mixed = None
            for e in range(2):
                h = pair * 2 + e
                scores = nt(only(q, e), R.qkv[:, kcols])
                scores = (scores.reshape(4, 64, 1024) + R.bias[h * 4 + t][:, None, :]).reshape(256, 1024)
                top = jnp.max(scores, axis=-1, keepdims=True)
                grown = jnp.exp(scores - top)
                total = jnp.sum(grown, axis=-1, keepdims=True)
                low = (grown * (1.0 / total)).astype(bf16)
                R.lse[where, h:h + 1] = top + jnp.log(total)
                got = nn(low, R.qkv[:, vcols])
                mixed = got if e == 0 else jnp.where(low_lane, mixed, got)
            R.at[pl.ds(2 * t, 2), :, cols] = mixed.astype(bf16).reshape(2, 128, 128)
        at_start(2 * t)
        at_start(2 * t + 1)
        return 0

    def attend(low, high):
        lax.fori_loop(low, high, attend_tile, 0)

    attend(1, 3)
    for k in (1, 2):
        part = z_take(w1_piece, w1z, "w", k)
        net.send(part, part, yn, w1y + order[k], "w")
    attend(3, 5)
    part = z_take(w1_piece, w1z, "w", 3)
    net.send(part, part, yn, w1y + order[3], "w")

    ax, ay = (x + flip) % 2, (y + c) % 2
    bx, by = (x + c) % 2, (y + flip) % 2
    near, far = at(z, ax, ay, c), at(z, bx, by, c)
    wo_a, wo_b, wo_d, wo_s = net.slots(1), net.slots(1), net.slots(1), net.slots(1)
    for k in (1, 2, 3):
        z_take(wo_piece, woz, "w", k)

    def wo_column(xx, yy):
        return R.wo.at[:, xx, yy, c]

    net.send(wo_column(x, y), wo_column(x, y), near, wo_a, "w")
    net.send(wo_column(x, y), wo_column(x, y), far, wo_b, "w")
    dy_step()
    part = z_take(w2_piece, w2z, "w", 1)
    net.send(part, part, yn, w2y + order[1], "w")
    net.arrive(wo_column(ax, ay), wo_a)
    net.send(wo_column(ax, ay), wo_column(ax, ay), far, wo_d, "w")
    for k in (2, 3):
        part = z_take(w2_piece, w2z, "w", k)
        net.send(part, part, yn, w2y + order[k], "w")
    net.arrive(wo_column(bx, by), wo_b)
    net.arrive(wo_column(xo, yo), wo_d)
    net.send(R.wo.at[:, :, :, c], R.wo.at[:, :, :, c], sib, wo_s, "w")
    net.arrive(R.wo.at[:, :, :, flip], wo_s)
    for b in range(2):
        for h in range(4):
            net.arrive(R.att.at[b, h], at_r + b * 4 + h)

    def outflow():
        for n in range(4):
            cols = slice(n * 256, n * 256 + 256)
            made = x_in[:, :, :, cols].reshape(256, 256).astype(f32)
            for h in range(4):
                made = made + nn(
                    R.att[:, h].reshape(256, 256),
                    R.wo[h, :, :, :, :, cols].reshape(256, 256),
                )
            R.mid[:, cols] = made
        for k in range(2):
            where = slice(k * 128, k * 128 + 128)
            scaled, _inverse = row_stats(R.mid[where, :])
            R.nt2[g, where, :] = (scaled * R.vec[2:3, :] + R.vec[3:4, :]).astype(bf16)

    outflow()
    nt_begin()

    for k in range(4):
        net.arrive(R.w1.at[order[k], :, yo], w1y + order[k])

    def widen_rows(which):
        def widen(j, _):
            where = pl.ds(pl.multiple_of(j * 256, 256), 256)
            pre = nn(R.nt2[which], R.w1[:, :, :, :, :, where].reshape(1024, 256))
            pre = pre + R.b1[:, where]
            share = 0.5 * (1.0 + lax.erf(pre * (2.0 ** -0.5)))
            R.act[which, :, where] = (pre * share).astype(bf16)
            slope = share + pre * (jnp.exp(-0.5 * pre * pre) * (1.0 / (2.0 * jnp.pi) ** 0.5))
            R.gp[which, :, where] = slope.astype(bf16)
            return 0

        loop(4, widen)

    widen_rows(members[0])
    nt_take(1)
    widen_rows(members[1])
    nt_step()
    widen_rows(members[2])
    nt_take(3)
    widen_rows(members[3])
    dy_take(1)
    dy_take(3)

    def outer_two(j, _):
        where = pl.ds(pl.multiple_of(j * 256, 256), 256)
        made = tn(R.act[:, :, where].reshape(1024, 256), R.dyx[...].reshape(1024, 1024))
        R.dw2[j] = made.astype(bf16).reshape(2, 128, 1024)
        return 0

    loop(4, outer_two)

    def scatter(piece, away, landing_y, landing_z, landing_v, name):
        base_y, base_z, base_v = net.slots(4), net.slots(4), net.slots(1)

        def begin(ks=(3, 2, 1, 0)):
            for k in ks:
                net.send(away(order[k]), landing_y.at[order[k]], yn, base_y + order[k], name)

        def add(ref, other):
            ref[...] = (ref[...].astype(f32) + other[...].astype(f32)).astype(bf16)

        def take(k):
            net.arrive(landing_y.at[order[k]], base_y + order[k])
            add(piece(order[k]), landing_y.at[order[k]])

        def along(k):
            part = piece(order[k])
            if k == 3:
                net.send(part, landing_v, at(order[1], x, y, c), base_v, name, made=jnp.logical_not(middle))

                @pl.when(middle)
                def pass_on():
                    net.arrive(landing_v, base_v)
                    add(part, landing_v)

                net.send(part, landing_z.at[z], at(order[3], x, y, c), base_z + z, name, made=middle)
            else:
                net.send(part, landing_z.at[z], at(order[k], x, y, c), base_z + z, name)

        def final(out):
            out[...] = piece(z)[...].astype(f32)
            for k in (1, 2):
                net.arrive(landing_z.at[order[k]], base_z + order[k])
                out[...] += landing_z[order[k]].astype(f32)

            @pl.when(middle)
            def from_end():
                net.arrive(landing_z.at[order[3]], base_z + order[3])
                out[...] += landing_z[order[3]].astype(f32)

        return begin, take, along, final

    two_begin, two_take, two_along, two_final = scatter(
        lambda zz: R.dw2.at[zz, y], lambda zz: R.dw2.at[zz, yo], R.r2y, R.r2z, R.r2v, "s2"
    )
    two_begin()

    for k in range(4):
        net.arrive(R.w2.at[order[k], yo], w2y + order[k])

    def narrow_back_rows(which):
        def narrow_back(j, _):
            where = pl.ds(pl.multiple_of(j * 256, 256), 256)
            made = nt(R.dyx[which], R.w2[j].reshape(256, 1024)) * R.gp[which, :, where].astype(f32)
            R.gp[which, :, where] = made.astype(bf16)
            return 0

        loop(4, narrow_back)

    def group_reduce(product, sent, landing, landing_x):
        slot_s, slot_x = net.slots(2), net.slots(1)
        for which, where in ((members[3], xo), (members[2], None), (members[1], x), (members[0], None)):
            if which is members[0]:
                product(which, R.own)
            else:
                product(which, sent.at[which])
            if where is not None:
                net.send(sent.at[which], landing.at[where], sib, slot_s + where)
            elif which is members[2]:
                net.arrive(landing.at[xo], slot_s + xo)
                sent[which] = (sent[which].astype(f32) + landing[xo].astype(f32)).astype(bf16)
                net.send(sent.at[which], landing_x, xn, slot_x)
        net.arrive(landing.at[x], slot_s + x)
        net.arrive(landing_x, slot_x)

    def grad_norm_part(which, out):
        narrow_back_rows(which)

        def back(n, _):
            made = nt(R.gp[which], R.w1[n].reshape(256, 1024))
            out[:, pl.ds(pl.multiple_of(n * 256, 256), 256)] = made.astype(out.dtype)
            return 0

        loop(4, back)

    group_reduce(grad_norm_part, R.gps, R.gpr, R.gpx)
    sums = [jnp.zeros((1, 1024), f32) for _ in range(3)]

    def norm_two_back():
        for k in range(4):
            where = slice(k * 64, k * 64 + 64)
            grad = R.own[where, :] + R.gpr[x, where, :].astype(f32) + R.gpx[where, :].astype(f32)
            scaled, inverse = row_stats(R.mid[where, :])
            flow = dy_in[k // 2, (k % 2) * 64:(k % 2) * 64 + 64, :].astype(f32)
            sums[0] = sums[0] + column_sum(grad * scaled)
            sums[1] = sums[1] + column_sum(grad)
            sums[2] = sums[2] + column_sum(flow)
            total = flow + norm_pullback(grad, scaled, inverse, R.vec[2:3, :])
            R.gm[where, :] = total
            R.gb[where, :] = total.astype(bf16)

    norm_two_back()

    do_r = net.slots(8)

    def outflow_back(h, _):
        made = nt(R.gb[...], R.wo[h].reshape(256, 1024)).astype(bf16)
        R.da[:, h] = made.reshape(2, 128, 256)
        return 0

    loop(4, outflow_back)
    for b in range(2):
        for xx in (x, xo):
            for cc in (c, flip):
                zt = 2 * c + b
                net.send(
                    R.da.at[b, 2 * xx + cc],
                    R.do.at[s],
                    at(zt, xx, y, cc),
                    do_r + s,
                    is_self=jnp.logical_and(zt == z, jnp.logical_and(xx == x, cc == c)),
                )

    net.settle("w")

    def outer_one(n, _):
        left = R.nt2[:, :, pl.ds(pl.multiple_of(n * 256, 256), 256)].reshape(1024, 256)
        made = tn(left, R.gp[...].reshape(1024, 1024)).astype(bf16)
        R.w1[n] = made.reshape(2, 2, 2, 32, 1024)
        return 0

    loop(4, outer_one)
    one_begin, one_take, one_along, one_final = scatter(
        w1_piece, lambda zz: R.w1.at[zz, :, yo], R.r1y, R.r1z, R.r1v, "s1"
    )
    one_begin()

    def outer_flow():
        for h in range(4):
            made = tn(R.att[:, h].reshape(256, 256), R.gb[...]).astype(bf16)
            R.wo[h] = made.reshape(2, 2, 2, 32, 1024)

    outer_flow()
    ros_s = net.slots(1)
    net.send(R.wo.at[:, :, :, flip], R.ros, sib, ros_s)
    for k in (3, 2, 1, 0):
        two_take(k)
        if k:
            two_along(k)

    R.dk[...] = jnp.zeros((1024, 256), f32)
    R.dv[...] = jnp.zeros((1024, 256), f32)

    def attend_back_tile(step, _):
        t = (z + step) % NZ
        where = pl.ds(pl.multiple_of(t * 256, 256), 256)
        two = pl.ds(2 * t, 2)
        for k in range(2):
            net.arrive(R.do.at[2 * t + k], do_r + 2 * t + k)
        for pair in range(2):
            cols = slice(pair * 128, pair * 128 + 128)
            kcols = slice(256 + pair * 128, 256 + pair * 128 + 128)
            vcols = slice(512 + pair * 128, 512 + pair * 128 + 128)
            q = R.qkv[where, cols]
            grad = R.do[two, :, cols].reshape(256, 128)
            prod = grad.astype(f32) * R.at[two, :, cols].reshape(256, 128).astype(f32)
            query = None
            for e in range(2):
                h = pair * 2 + e
                qe, ge = only(q, e), only(grad, e)
                scores = nt(qe, R.qkv[:, kcols])
                scores = (scores.reshape(4, 64, 1024) + R.bias[h * 4 + t][:, None, :]).reshape(256, 1024)
                chances = jnp.exp(scores - R.lse[where, h:h + 1])
                central = jnp.sum(only(prod, e), axis=-1, keepdims=True)
                moved = nt(ge, R.qkv[:, vcols])
                back = (chances * (moved - central)).astype(bf16)
                R.dv[:, cols] += tn(chances.astype(bf16), ge)
                R.dk[:, cols] += tn(back, qe)
                got = nn(back, R.qkv[:, kcols])
                query = got if e == 0 else jnp.where(low_lane, query, got)
            R.qkv[where, cols] = (query * 0.125).astype(bf16)
        return 0

    def attend_back(low, high):
        lax.fori_loop(low, high, attend_back_tile, 0)

    attend_back(0, 2)
    for k in (3, 2, 1, 0):
        one_take(k)
        if k:
            one_along(k)
    net.arrive(R.ros, ros_s)
    for k in range(4):
        R.wo[k, :, :, c] = (R.wo[k, :, :, c].astype(f32) + R.ros[k].astype(f32)).astype(bf16)
    roa_s, rob_s, rof_s, roz_s, rov_s = net.slots(1), net.slots(1), net.slots(1), net.slots(4), net.slots(1)
    net.send(wo_column(xo, yo), R.roa, far, roa_s)
    net.send(wo_column(bx, by), R.rob, far, rob_s)
    attend_back(2, 4)
    R.qkv[:, 256:512] = R.dk[...].astype(bf16)
    R.qkv[:, 512:768] = R.dv[...].astype(bf16)

    net.settle("xr")

    def unproject(step, _):
        t = (z + 1 + step) % NZ
        where = pl.ds(pl.multiple_of(t * 256, 256), 256)
        made = nt(R.qkv[where, :], R.wq[...].reshape(1024, 768)).astype(bf16)
        R.xr[pl.ds(2 * t, 2)] = made.reshape(2, 2, 64, 1024)
        gs_start(t)
        return 0

    rgs_s, rgx_s, gnr_s = net.slots(4), net.slots(4), net.slots(4)
    gs_start = net.series(
        4,
        lambda t: (
            R.xr.at[pl.ds(2 * t, 2), flip], R.rgs.at[pl.ds(2 * t, 2)], sib, rgs_s + t, None, None
        ),
    )
    loop(4, unproject)

    def outer_in(n, _):
        cols = pl.ds(pl.multiple_of(n * 256, 256), 256)
        made = tn(R.n1[:, :, cols].reshape(1024, 256), R.qkv[...]).astype(bf16)
        R.wq[n] = made.reshape(2, 2, 2, 32, 768)
        return 0

    loop(4, outer_in)
    q_begin, q_take, q_along, q_final = scatter(
        wq_piece, lambda zz: R.wq.at[zz, :, yo], R.rqy, R.rqz, R.rqv, "sq"
    )
    q_begin()
    for k in (3, 2, 1, 0):
        zt = order[k]
        i = zt * 2 + xo
        net.arrive(R.rgs.at[pl.ds(2 * zt, 2)], rgs_s + zt)
        R.xr[i, c] = (R.xr[i, c].astype(f32) + R.rgs[i].astype(f32)).astype(bf16)
        net.send(R.xr.at[i, c], R.rgx.at[zt], xn, rgx_s + zt)
    net.arrive(R.roa, roa_s)
    part = wo_column(ax, ay)
    part[...] = (part[...].astype(f32) + R.roa[...].astype(f32)).astype(bf16)
    net.send(part, R.rof, near, rof_s)
    for k in (3, 2, 1, 0):
        zt = order[k]
        i = zt * 2 + x
        net.arrive(R.rgx.at[zt], rgx_s + zt)
        R.xr[i, c] = (
            R.xr[i, c].astype(f32) + R.rgs[i].astype(f32) + R.rgx[zt].astype(f32)
        ).astype(bf16)
        net.send(
            R.xr.at[i, c],
            R.gnr.at[z % 2, c],
            at(zt, x, y, back_c),
            gnr_s + 2 * (z % 2) + c,
            is_self=jnp.logical_and(zt == z, c == back_c),
        )
    for k in (3, 2, 1, 0):
        q_take(k)
        if k:
            q_along(k)

    net.arrive(R.rob, rob_s)
    net.arrive(R.rof, rof_s)
    part = wo_column(x, y)
    part[...] = (part[...].astype(f32) + R.rob[...].astype(f32) + R.rof[...].astype(f32)).astype(bf16)
    for k in (1, 2, 3):
        net.send(wo_piece(order[k]), R.roz.at[z], at(order[k], x, y, c), roz_s + z)

    def contract_part(which, out):
        def forth(n, _):
            cols = pl.ds(pl.multiple_of(n * 256, 256), 256)
            made = nn(R.act[which], R.w2[:, :, :, cols].reshape(1024, 256))
            out[:, cols] = made.astype(out.dtype)
            return 0

        loop(4, forth)

    group_reduce(contract_part, R.ops, R.opr, R.opx)
    for k in range(2):
        where = slice(k * 128, k * 128 + 128)
        total = R.mid[where, :] + R.own[where, :] + R.opr[x, where, :].astype(f32)
        out_ref[k] = (total + R.opx[where, :].astype(f32) + R.vec[4:5, :]).astype(bf16)

    def note(which, row, line):
        for r in range(8):
            R.sg[which, r, row:row + 1, :] = line[:, r * 128:(r + 1) * 128]

    def small_begin(which):
        base = net.slots(8)
        for k in (3, 2, 1, 0):
            for xx in (xo, x):
                if k == 0 and xx is x:
                    continue
                zt = order[k]
                net.send(R.sg.at[which, zt * 2 + xx], R.rsg.at[which, s], at(zt, xx, y, c), base + s)
        return base

    def small_middle(which, base):
        total = R.sg[which, s]
        for k in (1, 2, 3, 0):
            for xx in (x, xo):
                if k == 0 and xx is x:
                    continue
                i = order[k] * 2 + xx
                net.arrive(R.rsg.at[which, i], base + i)
                total = total + R.rsg[which, i]
        R.sgt[which] = total
        slot = net.slots(4)
        for yy, cc in ((y, flip), (yo, c), (yo, flip)):
            net.send(R.sgt.at[which], R.rst.at[which, 2 * y + c], at(z, x, yy, cc), slot + 2 * y + c)
        return slot

    def small_end(which, slot):
        row = lax.broadcasted_iota(jnp.int32, (8, 128), 0)
        total = R.sgt[which]
        for yy, cc in ((y, flip), (yo, c), (yo, flip)):
            i = 2 * yy + cc
            net.arrive(R.rst.at[which, i], slot + i)
            got = R.rst[which, i]
            total = total + (got if cc is c else jnp.where(row < 5, got, 0.0))
        return total

    R.sg[...] = jnp.zeros((2, 8, 8, 128), f32)
    for k in range(3):
        note(0, 2 + k, sums[k])
    up = [jnp.zeros((1, 1024), f32)]

    def up_sum():
        for k in range(16):
            rows = slice((k % 4) * 64, (k % 4) * 64 + 64)
            up[0] = up[0] + column_sum(R.gp[k // 4, rows, :].astype(f32))

    up_sum()
    for q in range(8):
        R.sg[0, 2 * (q // 2) + x, 5 + q % 2:6 + q % 2, :] = up[0][:, q * 128:(q + 1) * 128]
    early = small_begin(0)
    two_final(dw2_ref)
    early = small_middle(0, early)

    for b in range(2):
        for cc in range(2):
            net.arrive(R.gnr.at[b, cc], gnr_s + 2 * b + cc)
    sums = [jnp.zeros((1, 1024), f32) for _ in range(2)]
    for k in range(4):
        rows = slice((k % 2) * 64, (k % 2) * 64 + 64)
        grad = R.gnr[k // 2, k % 2].astype(f32)
        scaled, inverse = row_stats(x_in[k // 2, k % 2].astype(f32))
        sums[0] = sums[0] + column_sum(grad * scaled)
        sums[1] = sums[1] + column_sum(grad)
        gx_ref[k // 2, rows, :] = R.gm[k * 64:(k + 1) * 64, :] + norm_pullback(
            grad, scaled, inverse, R.vec[0:1, :]
        )
    for k in range(2):
        note(1, k, sums[k])
    late = small_begin(1)

    r1f_s, rqf_s = net.slots(4), net.slots(4)
    one_final(R.f1)
    for xx, cc, dev in group:
        net.send(R.f1.at[xx, cc], R.r1f.at[g], dev, r1f_s + g)
    R.r1f[g] = R.f1[x, c]
    q_final(R.fq)
    for xx, cc, dev in group:
        net.send(R.fq.at[xx, cc], R.rqf.at[g], dev, rqf_s + g)
    R.rqf[g] = R.fq[x, c]
    late = small_middle(1, late)

    dwo_ref[...] = wo_piece(z)[...].astype(f32)
    for k in (1, 2, 3):
        net.arrive(R.roz.at[order[k]], roz_s + order[k])
        dwo_ref[...] += R.roz[order[k]].astype(f32)
    for xx, cc, dev in group:
        net.arrive(R.r1f.at[2 * xx + cc], r1f_s + 2 * xx + cc)
    for h in range(4):
        for q in range(8):
            block = 8 * (q // 2) + 4 * (h // 2) + 2 * (q % 2) + h % 2
            dw1_ref[:, block * 128:(block + 1) * 128] = R.r1f[h, :, q * 128:(q + 1) * 128]
    for xx, cc, dev in group:
        net.arrive(R.rqf.at[2 * xx + cc], rqf_s + 2 * xx + cc)
    for h in range(4):
        for t in range(3):
            dwq_ref[:, t * 1024 + h * 256:t * 1024 + (h + 1) * 256] = R.rqf[h, :, t * 256:(t + 1) * 256]
    sg_ref[...] = small_end(0, early) + small_end(1, late)
    net.settle(everything=True)


def local_fused(
    arriving_features,
    valid_extents,
    sampled_target_tiles,
    query_context_mapping,
    attention_outflow_weights,
    expansion_weights,
    contraction_weights,
    opening_scale_vector,
    opening_shift_vector,
    closing_scale_vector,
    closing_shift_vector,
    expansion_shift,
    contraction_shift,
    output_sensitivity,
):
    docs, heads, blocks, count = sampled_target_tiles.shape
    tiles = sampled_target_tiles.reshape(docs, heads * blocks, count)
    extents = jnp.broadcast_to(valid_extents[:, None, None], (docs, heads * blocks, 1))
    aux = jnp.concatenate([tiles, extents], axis=2)
    aux = jnp.pad(aux, ((0, 0), (0, 0), (0, 124))).reshape(docs, 4, 64, 128)
    line_one = jnp.concatenate(
        [opening_scale_vector, opening_shift_vector, closing_scale_vector, closing_shift_vector]
    )
    line_two = jnp.pad(contraction_shift, (0, 96))
    small = jnp.pad(jnp.stack([line_one, line_two, expansion_shift]), ((0, 5), (0, 0))).astype(f32)
    shapes = (
        (arriving_features.shape, bf16),
        (arriving_features.shape, f32),
        (query_context_mapping.shape, f32),
        (attention_outflow_weights.shape, f32),
        (expansion_weights.shape, f32),
        (contraction_weights.shape, f32),
        ((8, 128), f32),
    )
    whole = pl.BlockSpec(memory_space=pltpu.VMEM)
    made = pl.pallas_call(
        layer_kernel,
        name="layer",
        out_shape=[jax.ShapeDtypeStruct(a, b) for a, b in shapes],
        in_specs=[whole] * 8,
        out_specs=[whole] * 7,
        scratch_shapes=[pltpu.VMEM(a, b) for a, b in SCRATCH.values()]
        + [
            pltpu.SemaphoreType.DMA((SENDS,)),
            pltpu.SemaphoreType.DMA((RECVS,)),
        ],
        compiler_params=pltpu.CompilerParams(
            collective_id=0, has_side_effects=True, vmem_limit_bytes=VMEM_BYTES
        ),
    )(
        arriving_features.reshape(2, 2, 64, 1024),
        output_sensitivity,
        aux,
        query_context_mapping,
        attention_outflow_weights,
        expansion_weights,
        contraction_weights,
        small,
    )
    sums = made[6]
    doc = lax.axis_index("doc")
    narrow = lax.dynamic_slice(sums, (0, doc * 32), (5, 32))
    up = lax.dynamic_slice(sums, (5 + doc // 2, 0), (1, 128))
    return tuple(made[:6]) + (narrow[0], narrow[1], narrow[2], narrow[3], up[0], narrow[4])


def fits_fused(mesh, arguments):
    features, tiles, expand = arguments[0], arguments[2], arguments[5]
    return (
        dict(mesh.shape) == {"seq": 8, "doc": 4}
        and features.shape == (8, 1024, 1024)
        and tiles.shape == (8, 16, 16, 3)
        and expand.shape == (1024, 4096)
    )


def solution(mesh):
    in_specs = (
        P("doc", "seq", None),
        P("doc"),
        P("doc", None, None, None),
        P(("seq", "doc"), None),
        P(("seq", "doc"), None),
        P(("seq", "doc"), None),
        P(("seq", "doc"), None),
        P(("seq", "doc")),
        P(("seq", "doc")),
        P(("seq", "doc")),
        P(("seq", "doc")),
        P(("seq", "doc")),
        P(("seq", "doc")),
        P("doc", "seq", None),
    )
    out_specs = (
        P("doc", "seq", None),
        P("doc", "seq", None),
        P(("seq", "doc"), None),
        P(("seq", "doc"), None),
        P(("seq", "doc"), None),
        P(("seq", "doc"), None),
        P(("seq", "doc")),
        P(("seq", "doc")),
        P(("seq", "doc")),
        P(("seq", "doc")),
        P(("seq", "doc")),
        P(("seq", "doc")),
    )

    def run(*arguments):
        body = local_fused if fits_fused(mesh, arguments) else local
        mapped = jax.shard_map(
            body, mesh=mesh, in_specs=in_specs, out_specs=out_specs, check_vma=False
        )
        return mapped(*arguments)

    return run
```

```python
import types

import jax
import jax.numpy as jnp
from jax import lax
from jax.experimental import pallas as pl
from jax.experimental.pallas import tpu as pltpu
from jax.sharding import PartitionSpec as P

group_heads = 4
epsilon = 1e-05
negative = -1e30


def normalise_each_line(values, scaling, shifting):
    centered = values - jnp.mean(values, axis=-1, keepdims=True)
    inverse = lax.rsqrt(jnp.mean(centered * centered, axis=-1, keepdims=True) + epsilon)
    scaled = centered * inverse
    return (scaled * scaling + shifting, scaled, inverse)


def standardize_rows_pullback(grad_norm, scaled, inverse, scaling):
    grad_scaled = grad_norm * scaling
    centred_grad = grad_scaled - jnp.mean(grad_scaled, axis=-1, keepdims=True)
    centred_grad = centred_grad - scaled * jnp.mean(grad_scaled * scaled, axis=-1, keepdims=True)
    return (centred_grad * inverse, jnp.sum(grad_norm * scaled, axis=0), jnp.sum(grad_norm, axis=0))


def exact_gelu(values):
    return jax.nn.gelu(values, approximate=False)


def dense_width():
    return 8


def split_heads(array):
    return array.reshape((array.shape[0] // group_heads, group_heads) + array.shape[1:])


def join_heads(array):
    return array.reshape((array.shape[0] * array.shape[1],) + array.shape[2:])


def candidate_table(span_number, drawn_ordering, first_block, local_blocks, block_size):
    head_count, slot_blocks, random_count = drawn_ordering.shape
    query_blocks = first_block + jnp.arange(local_blocks, dtype=jnp.int32)
    last_block = (span_number - 1) // block_size
    picked = lax.dynamic_slice_in_dim(drawn_ordering, first_block, local_blocks, 1)
    window = jnp.stack([query_blocks - 1, query_blocks, query_blocks + 1], axis=1)
    edges = jnp.stack(
        [jnp.zeros_like(query_blocks), jnp.zeros_like(query_blocks) + last_block], axis=1
    )
    window = jnp.broadcast_to(window[None], (head_count, local_blocks, 3))
    edges = jnp.broadcast_to(edges[None], (head_count, local_blocks, 2))
    candidates = jnp.concatenate([window, picked, edges], axis=2)
    candidate_count = candidates.shape[2]
    inside = (candidates >= 0) & (candidates < slot_blocks)
    earlier = jnp.arange(candidate_count)[:, None] > jnp.arange(candidate_count)[None, :]
    repeated = jnp.any((candidates[:, :, :, None] == candidates[:, :, None, :]) & earlier, axis=3)
    usable = inside & jnp.logical_not(repeated)
    clipped = jnp.clip(candidates, 0, slot_blocks - 1)
    places = clipped[:, :, :, None] * block_size + jnp.arange(block_size, dtype=jnp.int32)
    keep = usable[:, :, :, None] & (places < span_number)
    flags = (query_blocks == 0) | (query_blocks == last_block)
    return (clipped, keep, flags)


def select_blocks(rows, clipped, block_size):
    slot_size, head_count, head_dim = rows.shape
    shaped = rows.reshape(slot_size // block_size, block_size, head_count, head_dim)
    head_index = jnp.arange(head_count, dtype=jnp.int32)[:, None, None]
    return shaped[clipped, :, head_index, :]


def sparse_forward(parts):
    query_group, key_group, value_group, keep_group = parts
    scale = query_group.shape[-1] ** (-0.5)
    scores = (
        jnp.einsum("hitd,hickd->hitck", query_group, key_group, preferred_element_type=jnp.float32)
        * scale
    )
    scores = jnp.where(keep_group[:, :, None], scores, negative)
    shape = scores.shape
    flat = scores.reshape(shape[0], shape[1], shape[2], shape[3] * shape[4])
    highest = jnp.max(flat, axis=-1, keepdims=True)
    weights_exp = jnp.exp(flat - highest)
    totals = jnp.sum(weights_exp, axis=-1, keepdims=True)
    chances_low = (weights_exp / totals).astype(jnp.bfloat16).reshape(shape)
    mixed = jnp.einsum(
        "hitck,hickd->hitd", chances_low, value_group, preferred_element_type=jnp.float32
    )
    return (mixed, (highest + jnp.log(totals))[..., 0])


def sparse_backward(parts):
    query_group, key_group, value_group, keep_group, log_group, grad_group = parts
    scale = query_group.shape[-1] ** (-0.5)
    scores = (
        jnp.einsum("hitd,hickd->hitck", query_group, key_group, preferred_element_type=jnp.float32)
        * scale
    )
    scores = jnp.where(keep_group[:, :, None], scores, negative)
    chances = jnp.exp(scores - log_group[..., None, None])
    grad_chances = jnp.einsum(
        "hitd,hickd->hitck", grad_group, value_group, preferred_element_type=jnp.float32
    )
    central = jnp.sum(chances * grad_chances, axis=(3, 4), keepdims=True)
    grad_scores = (chances * (grad_chances - central)).astype(jnp.bfloat16)
    query_term = (
        jnp.einsum("hitck,hickd->hitd", grad_scores, key_group, preferred_element_type=jnp.float32)
        * scale
    )
    key_term = (
        jnp.einsum(
            "hitck,hitd->hickd", grad_scores, query_group, preferred_element_type=jnp.float32
        )
        * scale
    )
    value_term = jnp.einsum(
        "hitck,hitd->hickd",
        chances.astype(jnp.bfloat16),
        grad_group,
        preferred_element_type=jnp.float32,
    )
    return (query_term, key_term, value_term)


def dense_forward(query_block, key_rows, value_rows, span_number):
    block_size, head_count, head_dim = query_block.shape
    width_group = dense_width()
    scale = head_dim ** (-0.5)
    valid = jnp.arange(key_rows.shape[0], dtype=jnp.int32) < span_number

    def one_group(number):
        offset = number * width_group
        query_part = lax.dynamic_slice_in_dim(query_block, offset, width_group, 1)
        key_part = lax.dynamic_slice_in_dim(key_rows, offset, width_group, 1)
        value_part = lax.dynamic_slice_in_dim(value_rows, offset, width_group, 1)
        scores = (
            jnp.einsum("tgd,kgd->gtk", query_part, key_part, preferred_element_type=jnp.float32)
            * scale
        )
        scores = jnp.where(valid[None, None, :], scores, negative)
        highest = jnp.max(scores, axis=-1, keepdims=True)
        weights_exp = jnp.exp(scores - highest)
        totals = jnp.sum(weights_exp, axis=-1, keepdims=True)
        chances_low = (weights_exp / totals).astype(jnp.bfloat16)
        mixed = jnp.einsum(
            "gtk,kgd->gtd", chances_low, value_part, preferred_element_type=jnp.float32
        )
        return (mixed, (highest + jnp.log(totals))[:, :, 0])

    mixed_all, logs_all = lax.map(one_group, jnp.arange(head_count // width_group, dtype=jnp.int32))
    mixed_all = mixed_all.reshape(head_count, block_size, head_dim).transpose(1, 0, 2)
    return (mixed_all, logs_all.reshape(head_count, block_size))


def dense_skip(query_block, key_rows, value_rows, span_number):
    block_size, head_count, head_dim = query_block.shape
    return (
        jnp.zeros((block_size, head_count, head_dim), jnp.float32),
        jnp.zeros((head_count, block_size), jnp.float32),
    )


def dense_back(query_block, grad_block, key_rows, value_rows, log_block, span_number):
    block_size, head_count, head_dim = query_block.shape
    slot_size = key_rows.shape[0]
    width_group = dense_width()
    scale = head_dim ** (-0.5)
    valid = jnp.arange(slot_size, dtype=jnp.int32) < span_number

    def one_group(number):
        offset = number * width_group
        query_part = lax.dynamic_slice_in_dim(query_block, offset, width_group, 1)
        grad_part = lax.dynamic_slice_in_dim(grad_block, offset, width_group, 1)
        key_part = lax.dynamic_slice_in_dim(key_rows, offset, width_group, 1)
        value_part = lax.dynamic_slice_in_dim(value_rows, offset, width_group, 1)
        scores = (
            jnp.einsum("tgd,kgd->gtk", query_part, key_part, preferred_element_type=jnp.float32)
            * scale
        )
        scores = jnp.where(valid[None, None, :], scores, negative)
        chances = jnp.exp(
            scores - lax.dynamic_slice_in_dim(log_block, offset, width_group, 0)[:, :, None]
        )
        grad_chances = jnp.einsum(
            "tgd,kgd->gtk", grad_part, value_part, preferred_element_type=jnp.float32
        )
        central = jnp.sum(chances * grad_chances, axis=-1, keepdims=True)
        grad_scores = (chances * (grad_chances - central)).astype(jnp.bfloat16)
        query_new = (
            jnp.einsum("gtk,kgd->gtd", grad_scores, key_part, preferred_element_type=jnp.float32)
            * scale
        )
        key_new = (
            jnp.einsum("gtk,tgd->gkd", grad_scores, query_part, preferred_element_type=jnp.float32)
            * scale
        )
        value_new = jnp.einsum(
            "gtk,tgd->gkd",
            chances.astype(jnp.bfloat16),
            grad_part,
            preferred_element_type=jnp.float32,
        )
        return (key_new, value_new, query_new)

    key_all, value_all, query_all = lax.map(
        one_group, jnp.arange(head_count // width_group, dtype=jnp.int32)
    )
    slot_terms = jnp.stack(
        [
            key_all.reshape(head_count, slot_size, head_dim),
            value_all.reshape(head_count, slot_size, head_dim),
        ]
    )
    return (slot_terms, query_all.reshape(head_count, block_size, head_dim).transpose(1, 0, 2))


def dense_pass(query_block, grad_block, key_rows, value_rows, log_block, span_number):
    block_size, head_count, head_dim = query_block.shape
    return (
        jnp.zeros((2, head_count, key_rows.shape[0], head_dim), jnp.float32),
        jnp.zeros(query_block.shape, jnp.float32),
    )


def return_grads(slot_grads):
    owned = lax.psum_scatter(
        slot_grads.astype(jnp.bfloat16), "seq", scatter_dimension=2, tiled=True
    ).astype(jnp.float32)
    pair_count, head_count, tok_count, head_dim = owned.shape
    return owned.transpose(2, 0, 1, 3).reshape(tok_count, pair_count * head_count * head_dim)


def flagged_place(flags):
    return jnp.sum(jnp.where(flags, jnp.arange(flags.shape[0], dtype=jnp.int32), 0))


def local(
    arriving_features,
    valid_extents,
    sampled_target_tiles,
    query_context_mapping,
    attention_outflow_weights,
    expansion_weights,
    contraction_weights,
    opening_scale_vector,
    opening_shift_vector,
    closing_scale_vector,
    closing_shift_vector,
    expansion_shift,
    contraction_shift,
    output_sensitivity,
):
    doc_count, tok_count, feature_breadth = arriving_features.shape
    head_count = sampled_target_tiles.shape[1]
    slot_blocks = sampled_target_tiles.shape[2]
    head_dim = feature_breadth // head_count
    slot_size = tok_count * lax.axis_size("seq")
    block_size = slot_size // slot_blocks
    local_blocks = tok_count // block_size
    first_block = lax.axis_index("seq") * local_blocks
    per_line_summation = doc_count * tok_count
    (
        full_inward,
        entire_outflow,
        full_expand,
        full_contract,
        overall_premultiplier,
        overall_shift_term,
        full_midscale,
        full_midshift,
        full_upshift,
        full_downshift,
    ) = (
        lax.all_gather(query_context_mapping, ("seq", "doc"), axis=0, tiled=True),
        lax.all_gather(attention_outflow_weights, ("seq", "doc"), axis=0, tiled=True),
        lax.all_gather(expansion_weights, ("seq", "doc"), axis=0, tiled=True),
        lax.all_gather(contraction_weights, ("seq", "doc"), axis=0, tiled=True),
        lax.all_gather(opening_scale_vector, ("seq", "doc"), axis=0, tiled=True),
        lax.all_gather(opening_shift_vector, ("seq", "doc"), axis=0, tiled=True),
        lax.all_gather(closing_scale_vector, ("seq", "doc"), axis=0, tiled=True),
        lax.all_gather(closing_shift_vector, ("seq", "doc"), axis=0, tiled=True),
        lax.all_gather(expansion_shift, ("seq", "doc"), axis=0, tiled=True),
        lax.all_gather(contraction_shift, ("seq", "doc"), axis=0, tiled=True),
    )
    shortcut_holder = arriving_features.reshape(per_line_summation, feature_breadth).astype(
        jnp.float32
    )
    opening_normalised, scaled_one, inverse_one = normalise_each_line(
        shortcut_holder,
        overall_premultiplier.astype(jnp.float32),
        overall_shift_term.astype(jnp.float32),
    )
    opening_normalised = opening_normalised.astype(jnp.bfloat16)
    projected = jnp.dot(opening_normalised, full_inward, preferred_element_type=jnp.float32).astype(
        jnp.bfloat16
    )
    query_local = projected[:, :feature_breadth].reshape(doc_count, tok_count, head_count, head_dim)
    pair_local = projected[:, feature_breadth:].reshape(doc_count, tok_count, 2 * feature_breadth)
    pair_full = lax.all_gather(pair_local, "seq", axis=1, tiled=True)

    def table_one(span_number, drawn_ordering):
        return candidate_table(span_number, drawn_ordering, first_block, local_blocks, block_size)

    clipped_all, keep_all, flags_all = jax.vmap(table_one)(valid_extents, sampled_target_tiles)
    query_heads = query_local.reshape(
        doc_count, local_blocks, block_size, head_count, head_dim
    ).transpose(0, 3, 1, 2, 4)
    block_flags = flags_all[:, :, None, None, None]

    def doc_forward(items):
        queries, pair_rows, clipped, keep = items
        key_sel = select_blocks(
            pair_rows[:, :feature_breadth].reshape(slot_size, head_count, head_dim),
            clipped,
            block_size,
        )
        value_sel = select_blocks(
            pair_rows[:, feature_breadth:].reshape(slot_size, head_count, head_dim),
            clipped,
            block_size,
        )
        mixed, log_sums = lax.map(
            sparse_forward,
            (split_heads(queries), split_heads(key_sel), split_heads(value_sel), split_heads(keep)),
        )
        return (join_heads(mixed), join_heads(log_sums))

    sparse_mixed, sparse_logs = lax.map(
        doc_forward, (query_heads, pair_full, clipped_all, keep_all)
    )
    mixed_rows = sparse_mixed.transpose(0, 2, 3, 1, 4)

    def doc_dense(items):
        queries, pair_rows, span_number, flags = items
        key_rows = pair_rows[:, :feature_breadth].reshape(slot_size, head_count, head_dim)
        value_rows = pair_rows[:, feature_breadth:].reshape(slot_size, head_count, head_dim)
        query_block = lax.dynamic_slice_in_dim(
            queries, flagged_place(flags) * block_size, block_size, 0
        )
        return lax.cond(
            jnp.any(flags),
            dense_forward,
            dense_skip,
            query_block,
            key_rows,
            value_rows,
            span_number,
        )

    dense_mixed, dense_logs = lax.map(doc_dense, (query_local, pair_full, valid_extents, flags_all))
    mixed_rows = jnp.where(block_flags, dense_mixed[:, None], mixed_rows)
    context_mixture = mixed_rows.reshape(per_line_summation, feature_breadth).astype(jnp.bfloat16)
    intermediate_state = shortcut_holder + jnp.dot(
        context_mixture, entire_outflow, preferred_element_type=jnp.float32
    )
    normed_two, scaled_two, inverse_two = normalise_each_line(
        intermediate_state, full_midscale.astype(jnp.float32), full_midshift.astype(jnp.float32)
    )
    normed_two = normed_two.astype(jnp.bfloat16)
    pre_act = jnp.dot(
        normed_two, full_expand, preferred_element_type=jnp.float32
    ) + full_upshift.astype(jnp.float32)
    activated = exact_gelu(pre_act).astype(jnp.bfloat16)
    final_rows = (
        intermediate_state
        + jnp.dot(activated, full_contract, preferred_element_type=jnp.float32)
        + full_downshift.astype(jnp.float32)
    )
    output = final_rows.astype(jnp.bfloat16).reshape(doc_count, tok_count, feature_breadth)
    back_inward, back_outward, back_expand, back_contract, back_prescale, back_midscale = (
        full_inward,
        entire_outflow,
        full_expand,
        full_contract,
        overall_premultiplier,
        full_midscale,
    )
    grad_out_rows = output_sensitivity.reshape(per_line_summation, feature_breadth)
    grad_out_wide = grad_out_rows.astype(jnp.float32)
    contract_grad = jnp.einsum(
        "rf,rd->fd", activated, grad_out_rows, preferred_element_type=jnp.float32
    )
    downshift_grad = jnp.sum(grad_out_wide, axis=0)
    grad_act = jnp.einsum(
        "rd,fd->rf", grad_out_rows, back_contract, preferred_element_type=jnp.float32
    )
    unused_value, gelu_back = jax.vjp(exact_gelu, pre_act)
    grad_pre = gelu_back(grad_act)[0].astype(jnp.bfloat16)
    expand_grad = jnp.einsum("rd,rf->df", normed_two, grad_pre, preferred_element_type=jnp.float32)
    upshift_grad = jnp.sum(grad_pre.astype(jnp.float32), axis=0)
    grad_norm_two = jnp.einsum(
        "rf,df->rd", grad_pre, back_expand, preferred_element_type=jnp.float32
    )
    middle_part, midscale_grad, midshift_grad = standardize_rows_pullback(
        grad_norm_two, scaled_two, inverse_two, back_midscale.astype(jnp.float32)
    )
    grad_middle = grad_out_wide + middle_part
    grad_branch = grad_middle.astype(jnp.bfloat16)
    outward_grad = jnp.einsum(
        "rd,re->de", context_mixture, grad_branch, preferred_element_type=jnp.float32
    )
    grad_attended = jnp.einsum(
        "re,de->rd", grad_branch, back_outward, preferred_element_type=jnp.float32
    ).astype(jnp.bfloat16)
    grad_attended = grad_attended.reshape(doc_count, tok_count, head_count, head_dim)
    grad_blocks = grad_attended.reshape(doc_count, local_blocks, block_size, head_count, head_dim)
    sparse_grads = jnp.where(block_flags, jnp.zeros_like(grad_blocks), grad_blocks).transpose(
        0, 3, 1, 2, 4
    )
    block_ids = jnp.arange(slot_blocks, dtype=jnp.int32)

    def sparse_back(queries, pair_rows, clipped, keep, log_sums, grad_part):
        key_rows = pair_rows[:, :feature_breadth].reshape(slot_size, head_count, head_dim)
        value_rows = pair_rows[:, feature_breadth:].reshape(slot_size, head_count, head_dim)
        key_sel = select_blocks(key_rows, clipped, block_size)
        value_sel = select_blocks(value_rows, clipped, block_size)
        grouped = (
            split_heads(queries),
            split_heads(key_sel),
            split_heads(value_sel),
            split_heads(keep),
            split_heads(log_sums),
            split_heads(grad_part),
        )
        query_term, key_term, value_term = lax.map(sparse_backward, grouped)
        query_term = join_heads(query_term)
        key_term = join_heads(key_term)
        value_term = join_heads(value_term)
        placing = (clipped[..., None] == block_ids).astype(jnp.float32)
        key_slot = jnp.einsum(
            "hlcn,hlcbd->hnbd",
            placing,
            key_term,
            precision=lax.Precision.HIGHEST,
            preferred_element_type=jnp.float32,
        )
        value_slot = jnp.einsum(
            "hlcn,hlcbd->hnbd",
            placing,
            value_term,
            precision=lax.Precision.HIGHEST,
            preferred_element_type=jnp.float32,
        )
        slot_grads = jnp.stack(
            [
                key_slot.reshape(head_count, slot_size, head_dim),
                value_slot.reshape(head_count, slot_size, head_dim),
            ]
        )
        return (query_term, slot_grads, key_rows, value_rows)

    def doc_backward(carry, items):
        (
            queries,
            pair_rows,
            clipped,
            keep,
            log_sums,
            grad_part,
            grad_rows,
            query_rows,
            dense_log,
            span_number,
            flags,
        ) = items
        query_term, slot_grads, key_rows, value_rows = sparse_back(
            queries, pair_rows, clipped, keep, log_sums, grad_part
        )
        start = flagged_place(flags) * block_size
        query_block = lax.dynamic_slice_in_dim(query_rows, start, block_size, 0)
        grad_block = lax.dynamic_slice_in_dim(grad_rows, start, block_size, 0)
        dense_slot, dense_term = lax.cond(
            jnp.any(flags),
            dense_back,
            dense_pass,
            query_block,
            grad_block,
            key_rows,
            value_rows,
            dense_log,
            span_number,
        )
        owned = return_grads(slot_grads + dense_slot)
        return (carry, (query_term, dense_term, owned))

    unused_carry, (sparse_query, dense_query, pair_grads) = lax.scan(
        doc_backward,
        jnp.zeros((), jnp.int32),
        (
            query_heads,
            pair_full,
            clipped_all,
            keep_all,
            sparse_logs,
            sparse_grads,
            grad_attended,
            query_local,
            dense_logs,
            valid_extents,
            flags_all,
        ),
    )
    query_grad = sparse_query.transpose(0, 2, 3, 1, 4) + jnp.where(
        block_flags, dense_query[:, None], 0.0
    )
    grad_projected = jnp.concatenate(
        [
            query_grad.reshape(per_line_summation, feature_breadth),
            pair_grads.reshape(per_line_summation, 2 * feature_breadth),
        ],
        axis=1,
    ).astype(jnp.bfloat16)
    inward_grad = jnp.einsum(
        "rd,re->de", opening_normalised, grad_projected, preferred_element_type=jnp.float32
    )
    grad_norm_one = jnp.einsum(
        "re,de->rd", grad_projected, back_inward, preferred_element_type=jnp.float32
    )
    incoming_slice, leading_gain_sensitivity, leading_offset_sensitivity = (
        standardize_rows_pullback(
            grad_norm_one, scaled_one, inverse_one, back_prescale.astype(jnp.float32)
        )
    )
    grad_inputs = (grad_middle + incoming_slice).reshape(doc_count, tok_count, feature_breadth)
    summed = (
        lax.psum_scatter(inward_grad, ("seq", "doc"), scatter_dimension=0, tiled=True),
        lax.psum_scatter(outward_grad, ("seq", "doc"), scatter_dimension=0, tiled=True),
        lax.psum_scatter(expand_grad, ("seq", "doc"), scatter_dimension=0, tiled=True),
        lax.psum_scatter(contract_grad, ("seq", "doc"), scatter_dimension=0, tiled=True),
        lax.psum_scatter(leading_gain_sensitivity, ("seq", "doc"), scatter_dimension=0, tiled=True),
        lax.psum_scatter(
            leading_offset_sensitivity, ("seq", "doc"), scatter_dimension=0, tiled=True
        ),
        lax.psum_scatter(midscale_grad, ("seq", "doc"), scatter_dimension=0, tiled=True),
        lax.psum_scatter(midshift_grad, ("seq", "doc"), scatter_dimension=0, tiled=True),
        lax.psum_scatter(upshift_grad, ("seq", "doc"), scatter_dimension=0, tiled=True),
        lax.psum_scatter(downshift_grad, ("seq", "doc"), scatter_dimension=0, tiled=True),
    )
    return (output, grad_inputs) + tuple(summed)


ROUTE = pl.DeviceIdType.MESH
NZ, NX, NY, NC = 4, 2, 2, 2
bf16, f32 = jnp.bfloat16, jnp.float32


def nn(left, right):
    return lax.dot_general(left, right, (((1,), (0,)), ((), ())), preferred_element_type=f32)


def nt(left, right):
    return lax.dot_general(left, right, (((1,), (1,)), ((), ())), preferred_element_type=f32)


def tn(left, right):
    return lax.dot_general(left, right, (((0,), (0,)), ((), ())), preferred_element_type=f32)


def loop(count, body):
    lax.fori_loop(0, count, body, 0)


class Net:
    def __init__(self, send_sems, recv_sems, here):
        self.send_sems, self.recv_sems, self.here = send_sems, recv_sems, here
        self.sent, self.taken = 0, 0
        self.open = []

    def slots(self, count):
        first = self.taken
        self.taken += count
        assert self.taken <= RECVS
        return first

    def copy(self, src, dst, device, slot, index):
        return pltpu.make_async_remote_copy(
            src_ref=src,
            dst_ref=dst,
            send_sem=self.send_sems.at[index],
            recv_sem=self.recv_sems.at[slot],
            device_id=device,
            device_id_type=ROUTE,
        )

    def series(self, count, describe, group=None):
        base = self.sent
        self.sent += count
        assert self.sent <= SENDS

        def start(i):
            src, dst, device, slot, is_self, made = describe(i)
            copy = self.copy(src, dst, device, slot, base + i)
            if is_self is None:
                if made is None:
                    copy.start()
                else:
                    pl.when(made)(copy.start)
            else:
                pl.when(jnp.logical_not(is_self))(copy.start)
                pl.when(is_self)(pltpu.make_async_copy(src, dst, self.recv_sems.at[slot]).start)

        def finish():
            for i in range(count):
                src, dst, device, slot, is_self, made = describe(i)
                copy = self.copy(src, dst, device, slot, base + i)
                if is_self is not None:
                    made = jnp.logical_not(is_self)
                if made is None:
                    copy.wait_send()
                else:
                    pl.when(made)(copy.wait_send)

        self.open.append((group, finish))
        return start

    def send(self, src, dst, device, slot, group=None, is_self=None, made=None):
        self.series(1, lambda i: (src, dst, device, slot, is_self, made), group)(0)

    def settle(self, group=None, everything=False):
        rest = []
        for name, finish in self.open:
            if everything or name == group:
                finish()
            else:
                rest.append((name, finish))
        self.open = rest

    def arrive(self, dst, slot):
        self.copy(dst, dst, self.here, slot, 0).wait_recv()


def row_stats(values):
    mean = jnp.mean(values, axis=-1, keepdims=True)
    centered = values - mean
    inverse = lax.rsqrt(jnp.mean(centered * centered, axis=-1, keepdims=True) + epsilon)
    return centered * inverse, inverse


def norm_pullback(grad, scaled, inverse, gain):
    wide = grad * gain
    first = jnp.mean(wide, axis=-1, keepdims=True)
    second = jnp.mean(wide * scaled, axis=-1, keepdims=True)
    return (wide - first - scaled * second) * inverse


def column_sum(values):
    return jnp.sum(values, axis=0, keepdims=True)


SCRATCH = dict(
    xr=((8, 2, 64, 1024), bf16),
    n1=((8, 128, 1024), bf16),
    aux=((64, 128), jnp.int32),
    aux2=((4, 16, 128), jnp.int32),
    table=((16, 16, 128), jnp.int32),
    bias=((16, 4, 1024), f32),
    sv=((4, 2, 2, 2, 8, 128), f32),
    vec=((8, 1024), f32),
    b1=((1, 1024), f32),
    wqs=((4, 32, 768), bf16),
    wq=((4, 2, 2, 2, 32, 768), bf16),
    wo=((4, 2, 2, 2, 32, 1024), bf16),
    w1s=((4, 32, 1024), bf16),
    w1=((4, 2, 2, 2, 32, 1024), bf16),
    w2=((4, 2, 128, 1024), bf16),
    qkv=((1024, 768), bf16),
    lse=((1024, 128), f32),
    at=((8, 128, 256), bf16),
    att=((2, 4, 128, 256), bf16),
    mid=((256, 1024), f32),
    nt2=((4, 256, 1024), bf16),
    dyx=((4, 256, 1024), bf16),
    act=((4, 256, 1024), bf16),
    gp=((4, 256, 1024), bf16),
    dw2=((4, 2, 128, 1024), bf16),
    own=((256, 1024), f32),
    gps=((4, 256, 1024), bf16),
    gpr=((2, 256, 1024), bf16),
    gpx=((256, 1024), bf16),
    ops=((4, 256, 1024), bf16),
    opr=((2, 256, 1024), bf16),
    opx=((256, 1024), bf16),
    gb=((256, 1024), bf16),
    gm=((256, 1024), f32),
    da=((2, 4, 128, 256), bf16),
    do=((8, 128, 256), bf16),
    dk=((1024, 128), f32),
    dv=((1024, 128), f32),
    dwq=((2, 4, 2, 2, 2, 32, 384), bf16),
    rgs=((8, 64, 1024), bf16),
    rgx=((4, 64, 1024), bf16),
    gnr=((2, 2, 64, 1024), bf16),
    r1y=((4, 2, 2, 32, 1024), bf16),
    r1z=((4, 2, 2, 32, 1024), bf16),
    r1v=((2, 2, 32, 1024), bf16),
    f1=((2, 2, 32, 1024), f32),
    r1f=((4, 32, 1024), f32),
    r2y=((4, 128, 1024), bf16),
    r2z=((4, 128, 1024), bf16),
    r2v=((128, 1024), bf16),
    ros=((4, 2, 2, 32, 1024), bf16),
    roa=((4, 32, 1024), bf16),
    rob=((4, 32, 1024), bf16),
    rof=((4, 32, 1024), bf16),
    roz=((4, 32, 1024), bf16),
    rov=((32, 1024), bf16),
    rqy=((2, 4, 2, 2, 32, 384), bf16),
    rqz=((2, 4, 2, 2, 32, 384), bf16),
    rqv=((2, 2, 2, 32, 384), bf16),
    fq=((2, 2, 32, 768), f32),
    rqf=((4, 32, 768), f32),
    sg=((2, 8, 8, 128), f32),
    rsg=((2, 8, 8, 128), f32),
    sgt=((2, 8, 128), f32),
    rst=((2, 4, 8, 128), f32),
)
SENDS, RECVS = 256, 256
VMEM_BYTES = 63 * 2**20


def layer_kernel(
    x_in, dy_in, extent_in, tiles_in, wq_in, wo_in, w1_in, w2_in,
    gain_one, shift_one, gain_two, shift_two, shift_up, shift_down,
    out_ref, gx_ref, dwq_ref, dwo_ref, dw1_ref, dw2_ref, sg_ref,
    *rest,
):
    names = list(SCRATCH)
    R = types.SimpleNamespace(**dict(zip(names, rest[: len(names)])))
    send_sems, recv_sems = rest[len(names):]
    s, d = lax.axis_index("seq"), lax.axis_index("doc")
    z, x, y, c = s // NX, s % NX, d // NC, d % NC
    g = 2 * x + c
    flip, xo, yo = 1 - c, 1 - x, 1 - y

    def at(zz, xx, yy, cc):
        return (zz * NX + xx, yy * NC + cc)

    here = (s, d)
    sib, xn, yn, cross = at(z, x, y, flip), at(z, xo, y, c), at(z, x, yo, c), at(z, xo, y, flip)
    group = ((x, flip, sib), (xo, c, xn), (xo, flip, cross))
    net = Net(send_sems, recv_sems, here)
    order = [z, z + 1 - 2 * (z // 2), (2 + 3 * z) % 5, 3 * (1 - z // 2)]
    middle = jnp.logical_or(z == 1, z == 2)

    barrier = pltpu.get_barrier_semaphore()

    def greet(step, _):
        other = (s * NC + c + step) % 16
        pl.semaphore_signal(
            barrier, inc=1, device_id=(other // NC, y * NC + other % NC), device_id_type=ROUTE
        )
        return 0

    lax.fori_loop(1, 16, greet, 0)
    for cc in (c, flip):
        pl.semaphore_signal(barrier, inc=1, device_id=at(z, x, yo, cc), device_id_type=ROUTE)
    for h in range(4):
        for t in range(3):
            for pair in range(2):
                src = t * 1024 + h * 256 + pair * 128
                dst = pair * 384 + t * 128
                R.wqs[h, :, dst:dst + 128] = wq_in[:, src:src + 128]
    R.wq[z, x, y, c] = R.wqs[g]
    small = R.sv.at[z, x, y, c]
    small[...] = jnp.zeros((8, 128), f32)
    for k, vector in enumerate((gain_one, shift_one, gain_two, shift_two)):
        small[0:1, k * 32:(k + 1) * 32] = vector[...].astype(f32)
    small[1:2, 0:32] = shift_down[...].astype(f32)
    small[2:3, :] = shift_up[...].astype(f32)
    for h in range(4):
        for q in range(8):
            block = 8 * (q // 2) + 4 * (h // 2) + 2 * (q % 2) + h % 2
            R.w1s[h, :, q * 128:(q + 1) * 128] = w1_in[:, block * 128:(block + 1) * 128]
    R.w1[z, x, y, c] = R.w1s[g]
    R.wo[z, x, y, c] = wo_in[...]
    R.w2[z, y] = w2_in[...]
    R.dyx[g] = dy_in[...].reshape(256, 1024)
    R.sg[...] = jnp.zeros((2, 8, 8, 128), f32)
    has_table = c == z // 2

    for h in range(16):
        R.table[h, :, 0:3] = tiles_in[z % 2, h]
    R.table[:, :, 3:4] = jnp.full((16, 16, 1), extent_in[z % 2], jnp.int32)

    @pl.when(has_table)
    def table():
        R.aux[...] = R.table[pl.ds(4 * g, 4)].reshape(64, 128)

    pl.semaphore_wait(barrier, 17)

    def z_start(piece, base, name):
        for k in (1, 2, 3):
            net.send(
                piece(z), piece(z), at(order[k], x, y, c), base + z, name, made=middle if k == 3 else None
            )

    def z_take(piece, base, name, k):
        part = piece(order[k])
        net.arrive(part, base + order[k])
        if k == 3:
            net.send(part, part, at(order[2], x, y, c), base + order[3], name, made=middle)
        return part

    half = pl.ds(pl.multiple_of(c * 512, 512), 512)
    other_half = pl.ds(pl.multiple_of(flip * 512, 512), 512)
    xz = net.slots(4)
    for b in range(2):
        for ch in range(2):
            zt = 2 * c + b
            net.send(
                x_in.at[b, :, :, ch * 512:(ch + 1) * 512],
                R.xr.at[s, :, :, ch * 512:(ch + 1) * 512],
                at(zt, x, y, ch),
                xz + z,
                is_self=jnp.logical_and(zt == z, c == ch),
            )

    wqa = net.slots(4)
    for xx, cc, dev in group:
        net.send(R.wqs.at[2 * xx + cc], R.wq.at[z, x, y, c], dev, wqa + g)

    sv_s, sv_z, sv_x, sv_y = net.slots(1), net.slots(4), net.slots(1), net.slots(1)
    net.send(R.sv.at[z, x, y, c], R.sv.at[z, x, y, c], sib, sv_s)

    aux_s = net.slots(1)
    net.send(R.table.at[pl.ds(4 * (2 * x + flip), 4)], R.aux2, sib, aux_s, made=has_table)

    w1a = net.slots(4)
    for xx, cc, dev in group:
        net.send(R.w1s.at[2 * xx + cc], R.w1.at[z, x, y, c], dev, w1a + g)

    def wq_piece(zz):
        return R.wq.at[zz, :, y]

    def w1_piece(zz):
        return R.w1.at[zz, :, y]

    def w2_piece(zz):
        return R.w2.at[zz, y]

    def wo_piece(zz):
        return R.wo.at[zz, x, y, c]

    wqz, wqy, w1z, w1y = net.slots(4), net.slots(4), net.slots(4), net.slots(4)
    w2z, w2y, woz = net.slots(4), net.slots(4), net.slots(4)
    for xx, cc, dev in group:
        net.arrive(R.wq.at[z, xx, y, cc], wqa + 2 * xx + cc)
    z_start(wq_piece, wqz, "w")
    net.send(wq_piece(z), wq_piece(z), yn, wqy + 0, "w")
    net.arrive(R.sv.at[z, x, y, flip], sv_s)
    z_start(lambda zz: R.sv.at[zz, x, y], sv_z, None)
    for xx, cc, dev in group:
        net.arrive(R.w1.at[z, xx, y, cc], w1a + 2 * xx + cc)
    net.send(w1_piece(z), w1_piece(z), yn, w1y + 0, "w")

    xx_r, xs_a, xs_b = net.slots(4), net.slots(4), net.slots(4)
    for k in range(4):
        zt = order[k]
        part = R.xr.at[zt * 2 + x, :, :, half]
        net.arrive(part, xz + zt)
        net.send(part, part, xn, xx_r + k, "xr")
        net.send(part, part, sib, xs_a + k, "xr")
        if k:
            part = z_take(wq_piece, wqz, "w", k)
            net.send(part, part, yn, wqy + k, "w")
    z_start(wo_piece, woz, "w")
    z_start(w1_piece, w1z, "w")
    for k in (1, 2, 3):
        z_take(lambda zz: R.sv.at[zz, x, y], sv_z, None, k)
    net.send(R.sv.at[:, x, y], R.sv.at[:, x, y], xn, sv_x)
    for k in range(4):
        zt = order[k]
        part = R.xr.at[zt * 2 + xo, :, :, half]
        net.arrive(part, xx_r + k)
        net.send(part, part, sib, xs_b + k, "xr")
        if k == 0:
            net.arrive(R.sv.at[:, xo, y], sv_x)
            net.send(R.sv.at[:, :, y], R.sv.at[:, :, y], yn, sv_y)

    def group_gather(buf):
        own_s, far_x, far_s = net.slots(1), net.slots(1), net.slots(1)

        def begin():
            net.send(buf.at[g], buf.at[g], sib, own_s)
            net.send(buf.at[g], buf.at[g], xn, far_x)

        def step():
            net.arrive(buf.at[2 * xo + c], far_x)
            net.send(buf.at[2 * xo + c], buf.at[2 * xo + c], sib, far_s)

        def take(which):
            if which == 1:
                net.arrive(buf.at[2 * x + flip], own_s)
            if which == 3:
                net.arrive(buf.at[2 * xo + flip], far_s)

        return begin, step, take

    members = (g, 2 * x + flip, 2 * xo + c, 2 * xo + flip)
    dy_begin, dy_step, dy_take = group_gather(R.dyx)
    nt_begin, nt_step, nt_take = group_gather(R.nt2)

    @pl.when(jnp.logical_not(has_table))
    def table_here():
        net.arrive(R.aux2, aux_s)
        R.aux[...] = R.aux2[...].reshape(64, 128)

    for i in range(16):
        tiles = R.aux[i * 4:(i + 1) * 4, :]
        place = lax.broadcasted_iota(jnp.int32, (4, 1024), 1)
        block = place >> 6
        row = lax.broadcasted_iota(jnp.int32, (4, 1024), 0) + (i % 4) * 4
        extent = tiles[:, 3:4]
        last = (extent - 1) >> 6
        seen = jnp.abs(row - block) <= 1
        for k in range(3):
            seen = seen | (block == tiles[:, k:k + 1])
        seen = seen | (block == 0) | (block == last) | (row == 0) | (row == last)
        seen = seen & (place < extent)
        R.bias[i] = jnp.where(seen, 0.0, negative).astype(f32)

    net.arrive(R.sv.at[:, :, yo], sv_y)
    lane = lax.broadcasted_iota(jnp.int32, (1, 128), 1) >> 5
    for r in range(8):
        for k in range(5):
            total = jnp.zeros((1, 128), f32)
            for q in range(4):
                line = R.sv[r // 2, r % 2, q // 2, q % 2, k // 4:k // 4 + 1, :]
                shift = (32 * (q - k % 4)) % 128
                if shift:
                    line = pltpu.roll(line, shift, 1)
                total = jnp.where(lane == q, line, total)
            R.vec[k:k + 1, r * 128:(r + 1) * 128] = total
    for q in range(8):
        R.b1[:, q * 128:(q + 1) * 128] = R.sv[q // 2, x, q % 2, c, 2:3, :]

    def first_norm(zt):
        def rows(k, _):
            i = 2 * zt + k
            scaled, _inverse = row_stats(R.xr[i].reshape(128, 1024).astype(f32))
            R.n1[i] = (scaled * R.vec[0:1, :] + R.vec[1:2, :]).astype(bf16)
            return 0

        loop(2, rows)

    for k in range(4):
        zt = order[k]
        net.arrive(R.xr.at[zt * 2 + x, :, :, other_half], xs_a + k)
        net.arrive(R.xr.at[zt * 2 + xo, :, :, other_half], xs_b + k)
        first_norm(zt)
    for k in range(4):
        net.arrive(R.wq.at[order[k], :, yo], wqy + k)

    def project(step, _):
        rows = R.n1[pl.ds(2 * step, 2)].reshape(256, 1024)
        made = nn(rows, R.wq[...].reshape(1024, 768)).astype(bf16)
        where = pl.ds(pl.multiple_of(step * 256, 256), 256)
        eighth = jnp.asarray(0.125, bf16)
        R.qkv[where, :] = jnp.concatenate(
            [made[:, :128] * eighth, made[:, 128:384], made[:, 384:512] * eighth, made[:, 512:]], axis=1
        )
        return 0

    loop(4, project)

    low_lane = lax.broadcasted_iota(jnp.int32, (1, 128), 1) < 64

    def only(values, e):
        return jnp.where(low_lane if e == 0 else jnp.logical_not(low_lane), values, jnp.zeros_like(values))

    def pair_columns(pair):
        first = pair * 384
        return (
            slice(pair * 128, pair * 128 + 128),
            slice(first, first + 128),
            slice(first + 128, first + 256),
            slice(first + 256, first + 384),
        )

    at_r = net.slots(8)
    back_c = z // 2

    def at_copy(i):
        zt, xx = i // 2, i % 2
        mine = jnp.logical_and(jnp.logical_and(zt == z, xx == x), c == back_c)
        return R.at.at[i], R.att.at[z % 2, g], at(zt, xx, y, back_c), at_r + (z % 2) * 4 + g, mine, None

    at_start = net.series(8, at_copy)

    def attend_tile(step, _):
        t = (z + step) % NZ
        where = pl.ds(pl.multiple_of(t * 256, 256), 256)
        for pair in range(2):
            cols, qcols, kcols, vcols = pair_columns(pair)
            q = R.qkv[where, qcols]
            mixed = None
            for e in range(2):
                h = pair * 2 + e
                scores = nt(only(q, e), R.qkv[:, kcols])
                scores = (scores.reshape(4, 64, 1024) + R.bias[h * 4 + t][:, None, :]).reshape(256, 1024)
                top = jnp.max(scores, axis=-1, keepdims=True)
                grown = jnp.exp(scores - top)
                total = jnp.sum(grown, axis=-1, keepdims=True)
                low = (grown * (1.0 / total)).astype(bf16)
                R.lse[where, h:h + 1] = top + jnp.log(total)
                got = nn(low, R.qkv[:, vcols])
                mixed = got if e == 0 else jnp.where(low_lane, mixed, got)
            R.at[pl.ds(2 * t, 2), :, cols] = mixed.astype(bf16).reshape(2, 128, 128)
        at_start(2 * t)
        at_start(2 * t + 1)
        return 0

    def attend(low, high):
        lax.fori_loop(low, high, attend_tile, 0)

    ax, ay = (x + flip) % 2, (y + c) % 2
    bx, by = (x + c) % 2, (y + flip) % 2
    near, far = at(z, ax, ay, c), at(z, bx, by, c)
    wo_a, wo_b, wo_d, wo_s = net.slots(1), net.slots(1), net.slots(1), net.slots(1)

    def wo_column(xx, yy):
        return R.wo.at[:, xx, yy, c]

    def w1_step(k):
        part = z_take(w1_piece, w1z, "w", k)
        net.send(part, part, yn, w1y + k, "w")

    def w2_step(k):
        part = z_take(w2_piece, w2z, "w", k)
        net.send(part, part, yn, w2y + k, "w")

    for k in (1, 2, 3):
        z_take(wo_piece, woz, "w", k)
    net.send(wo_column(x, y), wo_column(x, y), near, wo_a, "w")
    net.send(wo_column(x, y), wo_column(x, y), far, wo_b, "w")
    attend(1, 2)
    net.arrive(wo_column(ax, ay), wo_a)
    net.send(wo_column(ax, ay), wo_column(ax, ay), far, wo_d, "w")
    w1_step(1)
    attend(2, 3)
    dy_begin()
    w1_step(2)
    attend(3, 4)
    w1_step(3)
    attend(4, 5)
    dy_step()
    net.arrive(wo_column(bx, by), wo_b)
    net.arrive(wo_column(xo, yo), wo_d)
    net.send(R.wo.at[:, :, :, c], R.wo.at[:, :, :, c], sib, wo_s, "w")
    net.arrive(R.wo.at[:, :, :, flip], wo_s)
    for b in range(2):
        for h in range(4):
            net.arrive(R.att.at[b, h], at_r + b * 4 + h)
    z_start(w2_piece, w2z, "w")
    net.send(w2_piece(z), w2_piece(z), yn, w2y + 0, "w")

    def outflow():
        for n in range(4):
            cols = slice(n * 256, n * 256 + 256)
            made = x_in[:, :, :, cols].reshape(256, 256).astype(f32)
            for h in range(4):
                made = made + nn(
                    R.att[:, h].reshape(256, 256),
                    R.wo[h, :, :, :, :, cols].reshape(256, 256),
                )
            R.mid[:, cols] = made
        for k in range(2):
            where = slice(k * 128, k * 128 + 128)
            scaled, _inverse = row_stats(R.mid[where, :])
            R.nt2[g, where, :] = (scaled * R.vec[2:3, :] + R.vec[3:4, :]).astype(bf16)

    outflow()
    nt_begin()

    for k in range(4):
        net.arrive(R.w1.at[order[k], :, yo], w1y + k)

    def widen_rows(which):
        def widen(j, _):
            where = pl.ds(pl.multiple_of(j * 256, 256), 256)
            pre = nn(R.nt2[which], R.w1[:, :, :, :, :, where].reshape(1024, 256))
            pre = pre + R.b1[:, where]
            share = 0.5 * (1.0 + lax.erf(pre * (2.0 ** -0.5)))
            R.act[which, :, where] = (pre * share).astype(bf16)
            slope = share + pre * (jnp.exp(-0.5 * pre * pre) * (1.0 / (2.0 * jnp.pi) ** 0.5))
            R.gp[which, :, where] = slope.astype(bf16)
            return 0

        loop(4, widen)

    widen_rows(members[0])
    w2_step(1)
    nt_take(1)
    widen_rows(members[1])
    nt_step()
    w2_step(2)
    widen_rows(members[2])
    nt_take(3)
    w2_step(3)
    widen_rows(members[3])
    dy_take(1)
    dy_take(3)

    def outer_two(j, _):
        where = pl.ds(pl.multiple_of(j * 256, 256), 256)
        made = tn(R.act[:, :, where].reshape(1024, 256), R.dyx[...].reshape(1024, 1024))
        R.dw2[j] = made.astype(bf16).reshape(2, 128, 1024)
        return 0

    loop(4, outer_two)

    def scatter(piece, away, landing_y, landing_z, landing_v, name):
        base_y, base_z, base_v = net.slots(4), net.slots(4), net.slots(1)

        def begin(ks=(3, 2, 1, 0)):
            for k in ks:
                net.send(away(order[k]), landing_y.at[order[k]], yn, base_y + k, name)

        def add(ref, other):
            ref[...] = (ref[...].astype(f32) + other[...].astype(f32)).astype(bf16)

        def take(k):
            net.arrive(landing_y.at[order[k]], base_y + k)
            add(piece(order[k]), landing_y.at[order[k]])

        def along(k):
            part = piece(order[k])
            if k == 3:
                net.send(part, landing_v, at(order[1], x, y, c), base_v, name, made=jnp.logical_not(middle))

                @pl.when(middle)
                def pass_on():
                    net.arrive(landing_v, base_v)
                    add(part, landing_v)

                net.send(part, landing_z.at[z], at(order[3], x, y, c), base_z + z, name, made=middle)
            else:
                net.send(part, landing_z.at[z], at(order[k], x, y, c), base_z + z, name)

        def final(out):
            out[...] = piece(z)[...].astype(f32)
            for k in (1, 2):
                net.arrive(landing_z.at[order[k]], base_z + order[k])
                out[...] += landing_z[order[k]].astype(f32)

            @pl.when(middle)
            def from_end():
                net.arrive(landing_z.at[order[3]], base_z + order[3])
                out[...] += landing_z[order[3]].astype(f32)

        return begin, take, along, final

    two_begin, two_take, two_along, two_final = scatter(
        lambda zz: R.dw2.at[zz, y], lambda zz: R.dw2.at[zz, yo], R.r2y, R.r2z, R.r2v, "s2"
    )
    two_begin()

    for k in range(4):
        net.arrive(R.w2.at[order[k], yo], w2y + k)

    def narrow_back_rows(which):
        def narrow_back(j, _):
            where = pl.ds(pl.multiple_of(j * 256, 256), 256)
            made = nt(R.dyx[which], R.w2[j].reshape(256, 1024)) * R.gp[which, :, where].astype(f32)
            R.gp[which, :, where] = made.astype(bf16)
            return 0

        loop(4, narrow_back)

    def group_reduce(product, sent, landing, landing_x, kept):
        slot_s, slot_x = net.slots(2), net.slots(1)
        for which, where in ((members[3], xo), (members[2], None), (members[1], x), (members[0], None)):
            if which is members[0]:
                product(which, kept)
            else:
                product(which, sent.at[which])
            if where is not None:
                net.send(sent.at[which], landing.at[where], sib, slot_s + where)
            elif which is members[2]:
                net.arrive(landing.at[xo], slot_s + xo)
                sent[which] = (sent[which].astype(f32) + landing[xo].astype(f32)).astype(bf16)
                net.send(sent.at[which], landing_x, xn, slot_x)

        def finish():
            net.arrive(landing.at[x], slot_s + x)
            net.arrive(landing_x, slot_x)

        return finish

    def grad_norm_part(which, out):
        narrow_back_rows(which)

        def back(n, _):
            made = nt(R.gp[which], R.w1[n].reshape(256, 1024))
            out[:, pl.ds(pl.multiple_of(n * 256, 256), 256)] = made.astype(out.dtype)
            return 0

        loop(4, back)

    gn_finish = group_reduce(grad_norm_part, R.gps, R.gpr, R.gpx, R.own)
    net.settle("w")

    def outer_one(n, _):
        left = R.nt2[:, :, pl.ds(pl.multiple_of(n * 256, 256), 256)].reshape(1024, 256)
        made = tn(left, R.gp[...].reshape(1024, 1024)).astype(bf16)
        R.w1[n] = made.reshape(2, 2, 2, 32, 1024)
        return 0

    loop(4, outer_one)
    one_begin, one_take, one_along, one_final = scatter(
        w1_piece, lambda zz: R.w1.at[zz, :, yo], R.r1y, R.r1z, R.r1v, "s1"
    )
    one_begin()

    gn_finish()
    sums = [jnp.zeros((1, 1024), f32) for _ in range(3)]

    def norm_two_back():
        for k in range(4):
            where = slice(k * 64, k * 64 + 64)
            grad = R.own[where, :] + R.gpr[x, where, :].astype(f32) + R.gpx[where, :].astype(f32)
            scaled, inverse = row_stats(R.mid[where, :])
            flow = dy_in[k // 2, (k % 2) * 64:(k % 2) * 64 + 64, :].astype(f32)
            sums[0] = sums[0] + column_sum(grad * scaled)
            sums[1] = sums[1] + column_sum(grad)
            sums[2] = sums[2] + column_sum(flow)
            total = flow + norm_pullback(grad, scaled, inverse, R.vec[2:3, :])
            R.gm[where, :] = total
            R.gb[where, :] = total.astype(bf16)

    norm_two_back()

    do_r = net.slots(8)

    def outflow_back(h, _):
        made = nt(R.gb[...], R.wo[h].reshape(256, 1024)).astype(bf16)
        R.da[:, h] = made.reshape(2, 128, 256)
        return 0

    loop(4, outflow_back)
    for b in range(2):
        for xx in (x, xo):
            for cc in (c, flip):
                zt = 2 * c + b
                net.send(
                    R.da.at[b, 2 * xx + cc],
                    R.do.at[s],
                    at(zt, xx, y, cc),
                    do_r + s,
                    is_self=jnp.logical_and(zt == z, jnp.logical_and(xx == x, cc == c)),
                )


    def outer_flow():
        for h in range(4):
            made = tn(R.att[:, h].reshape(256, 256), R.gb[...]).astype(bf16)
            R.wo[h] = made.reshape(2, 2, 2, 32, 1024)

    outer_flow()
    ros_s = net.slots(1)
    net.send(R.wo.at[:, :, :, flip], R.ros, sib, ros_s)

    def contract_part(which, out):
        def forth(n, _):
            cols = pl.ds(pl.multiple_of(n * 256, 256), 256)
            made = nn(R.act[which], R.w2[:, :, :, cols].reshape(1024, 256))
            out[:, cols] = made.astype(out.dtype)
            return 0

        loop(4, forth)

    out_finish = group_reduce(contract_part, R.ops, R.opr, R.opx, R.own)
    for k in (3, 2, 1, 0):
        two_take(k)
        if k:
            two_along(k)

    def note(which, row, line):
        for r in range(8):
            R.sg[which, r, row:row + 1, :] = line[:, r * 128:(r + 1) * 128]

    def small_begin(which):
        base = net.slots(8)
        for k in (3, 2, 1, 0):
            for xx in (xo, x):
                if k == 0 and xx is x:
                    continue
                zt = order[k]
                net.send(R.sg.at[which, zt * 2 + xx], R.rsg.at[which, s], at(zt, xx, y, c), base + s)
        return base

    def small_middle(which, base):
        total = R.sg[which, s]
        for k in (1, 2, 3, 0):
            for xx in (x, xo):
                if k == 0 and xx is x:
                    continue
                i = order[k] * 2 + xx
                net.arrive(R.rsg.at[which, i], base + i)
                total = total + R.rsg[which, i]
        R.sgt[which] = total
        slot = net.slots(4)
        for yy, cc in ((y, flip), (yo, c), (yo, flip)):
            net.send(R.sgt.at[which], R.rst.at[which, 2 * y + c], at(z, x, yy, cc), slot + 2 * y + c)
        return slot

    def small_end(which, slot):
        row = lax.broadcasted_iota(jnp.int32, (8, 128), 0)
        total = R.sgt[which]
        for yy, cc in ((y, flip), (yo, c), (yo, flip)):
            i = 2 * yy + cc
            net.arrive(R.rst.at[which, i], slot + i)
            got = R.rst[which, i]
            total = total + (got if cc is c else jnp.where(row < 5, got, 0.0))
        return total

    for k in range(3):
        note(0, 2 + k, sums[k])
    up = [jnp.zeros((1, 1024), f32)]

    def up_sum():
        for k in range(16):
            rows = slice((k % 4) * 64, (k % 4) * 64 + 64)
            up[0] = up[0] + column_sum(R.gp[k // 4, rows, :].astype(f32))

    up_sum()
    for q in range(8):
        R.sg[0, 2 * (q // 2) + x, 5 + q % 2:6 + q % 2, :] = up[0][:, q * 128:(q + 1) * 128]
    early = small_begin(0)

    def attend_back(pair):
        cols, qcols, kcols, vcols = pair_columns(pair)
        R.dk[...] = jnp.zeros((1024, 128), f32)
        R.dv[...] = jnp.zeros((1024, 128), f32)

        def tile(step, _):
            t = (z + step) % NZ
            where = pl.ds(pl.multiple_of(t * 256, 256), 256)
            two = pl.ds(2 * t, 2)
            if pair == 0:
                for k in range(2):
                    net.arrive(R.do.at[2 * t + k], do_r + 2 * t + k)
            q = R.qkv[where, qcols]
            grad = R.do[two, :, cols].reshape(256, 128)
            prod = grad.astype(f32) * R.at[two, :, cols].reshape(256, 128).astype(f32)
            query = None
            for e in range(2):
                h = pair * 2 + e
                qe, ge = only(q, e), only(grad, e)
                scores = nt(qe, R.qkv[:, kcols])
                scores = (scores.reshape(4, 64, 1024) + R.bias[h * 4 + t][:, None, :]).reshape(256, 1024)
                chances = jnp.exp(scores - R.lse[where, h:h + 1])
                central = jnp.sum(only(prod, e), axis=-1, keepdims=True)
                moved = nt(ge, R.qkv[:, vcols])
                back = (chances * (moved - central)).astype(bf16)
                R.dv[...] += tn(chances.astype(bf16), ge)
                R.dk[...] += tn(back, qe)
                got = nn(back, R.qkv[:, kcols])
                query = got if e == 0 else jnp.where(low_lane, query, got)
            R.qkv[where, qcols] = (query * 0.125).astype(bf16)
            return 0

        lax.fori_loop(0, 4, tile, 0)
        R.qkv[:, kcols] = R.dk[...].astype(bf16)
        R.qkv[:, vcols] = R.dv[...].astype(bf16)

    def outer_in_pair(pair):
        def outer_in(n, _):
            rows = pl.ds(pl.multiple_of(n * 256, 256), 256)
            made = tn(R.n1[:, :, rows].reshape(1024, 256), R.qkv[:, pair * 384:pair * 384 + 384])
            R.dwq[pair, n] = made.astype(bf16).reshape(2, 2, 2, 32, 384)
            return 0

        loop(4, outer_in)
        steps = scatter(
            lambda zz: R.dwq.at[pair, zz, :, y],
            lambda zz: R.dwq.at[pair, zz, :, yo],
            R.rqy.at[pair],
            R.rqz.at[pair],
            R.rqv.at[pair],
            None,
        )
        steps[0]()
        return steps

    attend_back(0)
    for k in (3, 2, 1, 0):
        one_take(k)
        if k:
            one_along(k)
    net.arrive(R.ros, ros_s)
    for k in range(4):
        R.wo[k, :, :, c] = (R.wo[k, :, :, c].astype(f32) + R.ros[k].astype(f32)).astype(bf16)
    roa_s, rob_s, rof_s, roz_s = net.slots(1), net.slots(1), net.slots(1), net.slots(4)
    net.send(wo_column(xo, yo), R.roa, far, roa_s)
    net.send(wo_column(bx, by), R.rob, far, rob_s)
    q0_begin, q0_take, q0_along, q0_final = outer_in_pair(0)
    early = small_middle(0, early)
    out_finish()
    for k in range(2):
        where = slice(k * 128, k * 128 + 128)
        total = R.mid[where, :] + R.own[where, :] + R.opr[x, where, :].astype(f32)
        out_ref[k] = (total + R.opx[where, :].astype(f32) + R.vec[4:5, :]).astype(bf16)
    attend_back(1)

    net.settle("xr")

    def unproject(step, _):
        t = (z + 1 + step) % NZ
        where = pl.ds(pl.multiple_of(t * 256, 256), 256)
        made = nt(R.qkv[where, :], R.wq[...].reshape(1024, 768)).astype(bf16)
        R.xr[pl.ds(2 * t, 2)] = made.reshape(2, 2, 64, 1024)
        gs_start(t)
        return 0

    rgs_s, rgx_s, gnr_s = net.slots(4), net.slots(4), net.slots(4)
    gs_start = net.series(
        4,
        lambda t: (
            R.xr.at[pl.ds(2 * t, 2), flip], R.rgs.at[pl.ds(2 * t, 2)], sib, rgs_s + t, None, None
        ),
    )
    loop(4, unproject)

    for k in (3, 2, 1, 0):
        q0_take(k)
        if k:
            q0_along(k)
    q1_begin, q1_take, q1_along, q1_final = outer_in_pair(1)
    for k in (3, 2, 1, 0):
        zt = order[k]
        i = zt * 2 + xo
        net.arrive(R.rgs.at[pl.ds(2 * zt, 2)], rgs_s + zt)
        R.xr[i, c] = (R.xr[i, c].astype(f32) + R.rgs[i].astype(f32)).astype(bf16)
        net.send(R.xr.at[i, c], R.rgx.at[zt], xn, rgx_s + k)
    net.arrive(R.roa, roa_s)
    part = wo_column(ax, ay)
    part[...] = (part[...].astype(f32) + R.roa[...].astype(f32)).astype(bf16)
    net.send(part, R.rof, near, rof_s)
    for k in (3, 2, 1, 0):
        zt = order[k]
        i = zt * 2 + x
        net.arrive(R.rgx.at[zt], rgx_s + k)
        R.xr[i, c] = (
            R.xr[i, c].astype(f32) + R.rgs[i].astype(f32) + R.rgx[zt].astype(f32)
        ).astype(bf16)
        net.send(
            R.xr.at[i, c],
            R.gnr.at[z % 2, c],
            at(zt, x, y, back_c),
            gnr_s + 2 * (z % 2) + c,
            is_self=jnp.logical_and(zt == z, c == back_c),
        )
    for k in (3, 2, 1, 0):
        q1_take(k)
        if k:
            q1_along(k)

    net.arrive(R.rob, rob_s)
    net.arrive(R.rof, rof_s)
    part = wo_column(x, y)
    part[...] = (part[...].astype(f32) + R.rob[...].astype(f32) + R.rof[...].astype(f32)).astype(bf16)
    for k in (1, 2, 3):
        net.send(wo_piece(order[k]), R.roz.at[z], at(order[k], x, y, c), roz_s + z)


    two_final(dw2_ref)
    sums = [jnp.zeros((1, 1024), f32) for _ in range(2)]
    for k in range(4):
        net.arrive(R.gnr.at[k // 2, k % 2], gnr_s + k)
        rows = slice((k % 2) * 64, (k % 2) * 64 + 64)
        grad = R.gnr[k // 2, k % 2].astype(f32)
        scaled, inverse = row_stats(x_in[k // 2, k % 2].astype(f32))
        sums[0] = sums[0] + column_sum(grad * scaled)
        sums[1] = sums[1] + column_sum(grad)
        gx_ref[k // 2, rows, :] = R.gm[k * 64:(k + 1) * 64, :] + norm_pullback(
            grad, scaled, inverse, R.vec[0:1, :]
        )
    for k in range(2):
        note(1, k, sums[k])
    late = small_begin(1)

    r1f_s, rqf_s = net.slots(4), net.slots(4)
    one_final(R.f1)
    for xx, cc, dev in group:
        net.send(R.f1.at[xx, cc], R.r1f.at[g], dev, r1f_s + g)
    R.r1f[g] = R.f1[x, c]
    q0_final(R.fq.at[:, :, :, 0:384])
    q1_final(R.fq.at[:, :, :, 384:768])
    for xx, cc, dev in group:
        net.send(R.fq.at[xx, cc], R.rqf.at[g], dev, rqf_s + g)
    R.rqf[g] = R.fq[x, c]
    late = small_middle(1, late)

    dwo_ref[...] = wo_piece(z)[...].astype(f32)
    for k in (1, 2, 3):
        net.arrive(R.roz.at[order[k]], roz_s + order[k])
        dwo_ref[...] += R.roz[order[k]].astype(f32)
    for xx, cc, dev in group:
        net.arrive(R.r1f.at[2 * xx + cc], r1f_s + 2 * xx + cc)
    for h in range(4):
        for q in range(8):
            block = 8 * (q // 2) + 4 * (h // 2) + 2 * (q % 2) + h % 2
            dw1_ref[:, block * 128:(block + 1) * 128] = R.r1f[h, :, q * 128:(q + 1) * 128]
    for xx, cc, dev in group:
        net.arrive(R.rqf.at[2 * xx + cc], rqf_s + 2 * xx + cc)
    for h in range(4):
        for t in range(3):
            for pair in range(2):
                src = pair * 384 + t * 128
                dst = t * 1024 + h * 256 + pair * 128
                dwq_ref[:, dst:dst + 128] = R.rqf[h, :, src:src + 128]
    total = small_end(0, early) + small_end(1, late)
    sg_ref[...] = pltpu.roll(total, (128 - 32 * d) % 128, 1)
    sg_ref[5:6, :] = jnp.where(y == 0, total[5:6, :], total[6:7, :])
    net.settle(everything=True)


def local_fused(
    arriving_features,
    valid_extents,
    sampled_target_tiles,
    query_context_mapping,
    attention_outflow_weights,
    expansion_weights,
    contraction_weights,
    opening_scale_vector,
    opening_shift_vector,
    closing_scale_vector,
    closing_shift_vector,
    expansion_shift,
    contraction_shift,
    output_sensitivity,
):
    shapes = (
        (arriving_features.shape, bf16),
        (arriving_features.shape, f32),
        (query_context_mapping.shape, f32),
        (attention_outflow_weights.shape, f32),
        (expansion_weights.shape, f32),
        (contraction_weights.shape, f32),
        ((8, 128), f32),
    )
    whole = pl.BlockSpec(memory_space=pltpu.VMEM)
    scalars = pl.BlockSpec(memory_space=pltpu.SMEM)
    made = pl.pallas_call(
        layer_kernel,
        name="layer",
        out_shape=[jax.ShapeDtypeStruct(a, b) for a, b in shapes],
        in_specs=[whole] * 2 + [scalars] + [whole] * 11,
        out_specs=[whole] * 7,
        scratch_shapes=[pltpu.VMEM(a, b) for a, b in SCRATCH.values()]
        + [
            pltpu.SemaphoreType.DMA((SENDS,)),
            pltpu.SemaphoreType.DMA((RECVS,)),
        ],
        compiler_params=pltpu.CompilerParams(
            collective_id=0, has_side_effects=True, vmem_limit_bytes=VMEM_BYTES
        ),
    )(
        arriving_features.reshape(2, 2, 64, 1024),
        output_sensitivity,
        valid_extents,
        sampled_target_tiles,
        query_context_mapping,
        attention_outflow_weights,
        expansion_weights,
        contraction_weights,
        opening_scale_vector.reshape(1, 32),
        opening_shift_vector.reshape(1, 32),
        closing_scale_vector.reshape(1, 32),
        closing_shift_vector.reshape(1, 32),
        expansion_shift.reshape(1, 128),
        contraction_shift.reshape(1, 32),
    )
    place = pl.BlockSpec(memory_space=pl.ANY)
    rows = ((1, 32), (1, 32), (1, 32), (1, 32), (1, 128), (1, 32))
    done = pl.pallas_call(
        leave_kernel,
        name="leave",
        out_shape=[jax.ShapeDtypeStruct(a, b) for a, b in shapes[:6]]
        + [jax.ShapeDtypeStruct(a, f32) for a in rows],
        in_specs=[place] * 6 + [whole],
        out_specs=[place] * 6 + [whole] * 6,
        scratch_shapes=[pltpu.SemaphoreType.DMA((6,))],
    )(*made)
    return tuple(done[:6]) + tuple(line.reshape(-1) for line in done[6:])


def leave_kernel(*refs):
    large, small, out, rows, sems = refs[:6], refs[6], refs[7:13], refs[13:19], refs[19]
    copies = [pltpu.make_async_copy(large[k], out[k], sems.at[k]) for k in range(6)]
    for copy in copies:
        copy.start()
    for k, row in enumerate((0, 1, 2, 3, 5, 4)):
        rows[k][...] = small[row:row + 1, :rows[k].shape[1]]
    for copy in copies:
        copy.wait()


def fits_fused(mesh, arguments):
    features, tiles, expand = arguments[0], arguments[2], arguments[5]
    return (
        dict(mesh.shape) == {"seq": 8, "doc": 4}
        and features.shape == (8, 1024, 1024)
        and tiles.shape == (8, 16, 16, 3)
        and expand.shape == (1024, 4096)
    )


def solution(mesh):
    in_specs = (
        P("doc", "seq", None),
        P("doc"),
        P("doc", None, None, None),
        P(("seq", "doc"), None),
        P(("seq", "doc"), None),
        P(("seq", "doc"), None),
        P(("seq", "doc"), None),
        P(("seq", "doc")),
        P(("seq", "doc")),
        P(("seq", "doc")),
        P(("seq", "doc")),
        P(("seq", "doc")),
        P(("seq", "doc")),
        P("doc", "seq", None),
    )
    out_specs = (
        P("doc", "seq", None),
        P("doc", "seq", None),
        P(("seq", "doc"), None),
        P(("seq", "doc"), None),
        P(("seq", "doc"), None),
        P(("seq", "doc"), None),
        P(("seq", "doc")),
        P(("seq", "doc")),
        P(("seq", "doc")),
        P(("seq", "doc")),
        P(("seq", "doc")),
        P(("seq", "doc")),
    )

    def run(*arguments):
        body = local_fused if fits_fused(mesh, arguments) else local
        mapped = jax.shard_map(
            body, mesh=mesh, in_specs=in_specs, out_specs=out_specs, check_vma=False
        )
        return mapped(*arguments)

    return run
```

```python
import types

import jax
import jax.numpy as jnp
from jax import lax
from jax.experimental import pallas as pl
from jax.experimental.pallas import tpu as pltpu
from jax.sharding import PartitionSpec as P

group_heads = 4
epsilon = 1e-05
negative = -1e30


def normalise_each_line(values, scaling, shifting):
    centered = values - jnp.mean(values, axis=-1, keepdims=True)
    inverse = lax.rsqrt(jnp.mean(centered * centered, axis=-1, keepdims=True) + epsilon)
    scaled = centered * inverse
    return (scaled * scaling + shifting, scaled, inverse)


def standardize_rows_pullback(grad_norm, scaled, inverse, scaling):
    grad_scaled = grad_norm * scaling
    centred_grad = grad_scaled - jnp.mean(grad_scaled, axis=-1, keepdims=True)
    centred_grad = centred_grad - scaled * jnp.mean(grad_scaled * scaled, axis=-1, keepdims=True)
    return (centred_grad * inverse, jnp.sum(grad_norm * scaled, axis=0), jnp.sum(grad_norm, axis=0))


def exact_gelu(values):
    return jax.nn.gelu(values, approximate=False)


def dense_width():
    return 8


def split_heads(array):
    return array.reshape((array.shape[0] // group_heads, group_heads) + array.shape[1:])


def join_heads(array):
    return array.reshape((array.shape[0] * array.shape[1],) + array.shape[2:])


def candidate_table(span_number, drawn_ordering, first_block, local_blocks, block_size):
    head_count, slot_blocks, random_count = drawn_ordering.shape
    query_blocks = first_block + jnp.arange(local_blocks, dtype=jnp.int32)
    last_block = (span_number - 1) // block_size
    picked = lax.dynamic_slice_in_dim(drawn_ordering, first_block, local_blocks, 1)
    window = jnp.stack([query_blocks - 1, query_blocks, query_blocks + 1], axis=1)
    edges = jnp.stack(
        [jnp.zeros_like(query_blocks), jnp.zeros_like(query_blocks) + last_block], axis=1
    )
    window = jnp.broadcast_to(window[None], (head_count, local_blocks, 3))
    edges = jnp.broadcast_to(edges[None], (head_count, local_blocks, 2))
    candidates = jnp.concatenate([window, picked, edges], axis=2)
    candidate_count = candidates.shape[2]
    inside = (candidates >= 0) & (candidates < slot_blocks)
    earlier = jnp.arange(candidate_count)[:, None] > jnp.arange(candidate_count)[None, :]
    repeated = jnp.any((candidates[:, :, :, None] == candidates[:, :, None, :]) & earlier, axis=3)
    usable = inside & jnp.logical_not(repeated)
    clipped = jnp.clip(candidates, 0, slot_blocks - 1)
    places = clipped[:, :, :, None] * block_size + jnp.arange(block_size, dtype=jnp.int32)
    keep = usable[:, :, :, None] & (places < span_number)
    flags = (query_blocks == 0) | (query_blocks == last_block)
    return (clipped, keep, flags)


def select_blocks(rows, clipped, block_size):
    slot_size, head_count, head_dim = rows.shape
    shaped = rows.reshape(slot_size // block_size, block_size, head_count, head_dim)
    head_index = jnp.arange(head_count, dtype=jnp.int32)[:, None, None]
    return shaped[clipped, :, head_index, :]


def sparse_forward(parts):
    query_group, key_group, value_group, keep_group = parts
    scale = query_group.shape[-1] ** (-0.5)
    scores = (
        jnp.einsum("hitd,hickd->hitck", query_group, key_group, preferred_element_type=jnp.float32)
        * scale
    )
    scores = jnp.where(keep_group[:, :, None], scores, negative)
    shape = scores.shape
    flat = scores.reshape(shape[0], shape[1], shape[2], shape[3] * shape[4])
    highest = jnp.max(flat, axis=-1, keepdims=True)
    weights_exp = jnp.exp(flat - highest)
    totals = jnp.sum(weights_exp, axis=-1, keepdims=True)
    chances_low = (weights_exp / totals).astype(jnp.bfloat16).reshape(shape)
    mixed = jnp.einsum(
        "hitck,hickd->hitd", chances_low, value_group, preferred_element_type=jnp.float32
    )
    return (mixed, (highest + jnp.log(totals))[..., 0])


def sparse_backward(parts):
    query_group, key_group, value_group, keep_group, log_group, grad_group = parts
    scale = query_group.shape[-1] ** (-0.5)
    scores = (
        jnp.einsum("hitd,hickd->hitck", query_group, key_group, preferred_element_type=jnp.float32)
        * scale
    )
    scores = jnp.where(keep_group[:, :, None], scores, negative)
    chances = jnp.exp(scores - log_group[..., None, None])
    grad_chances = jnp.einsum(
        "hitd,hickd->hitck", grad_group, value_group, preferred_element_type=jnp.float32
    )
    central = jnp.sum(chances * grad_chances, axis=(3, 4), keepdims=True)
    grad_scores = (chances * (grad_chances - central)).astype(jnp.bfloat16)
    query_term = (
        jnp.einsum("hitck,hickd->hitd", grad_scores, key_group, preferred_element_type=jnp.float32)
        * scale
    )
    key_term = (
        jnp.einsum(
            "hitck,hitd->hickd", grad_scores, query_group, preferred_element_type=jnp.float32
        )
        * scale
    )
    value_term = jnp.einsum(
        "hitck,hitd->hickd",
        chances.astype(jnp.bfloat16),
        grad_group,
        preferred_element_type=jnp.float32,
    )
    return (query_term, key_term, value_term)


def dense_forward(query_block, key_rows, value_rows, span_number):
    block_size, head_count, head_dim = query_block.shape
    width_group = dense_width()
    scale = head_dim ** (-0.5)
    valid = jnp.arange(key_rows.shape[0], dtype=jnp.int32) < span_number

    def one_group(number):
        offset = number * width_group
        query_part = lax.dynamic_slice_in_dim(query_block, offset, width_group, 1)
        key_part = lax.dynamic_slice_in_dim(key_rows, offset, width_group, 1)
        value_part = lax.dynamic_slice_in_dim(value_rows, offset, width_group, 1)
        scores = (
            jnp.einsum("tgd,kgd->gtk", query_part, key_part, preferred_element_type=jnp.float32)
            * scale
        )
        scores = jnp.where(valid[None, None, :], scores, negative)
        highest = jnp.max(scores, axis=-1, keepdims=True)
        weights_exp = jnp.exp(scores - highest)
        totals = jnp.sum(weights_exp, axis=-1, keepdims=True)
        chances_low = (weights_exp / totals).astype(jnp.bfloat16)
        mixed = jnp.einsum(
            "gtk,kgd->gtd", chances_low, value_part, preferred_element_type=jnp.float32
        )
        return (mixed, (highest + jnp.log(totals))[:, :, 0])

    mixed_all, logs_all = lax.map(one_group, jnp.arange(head_count // width_group, dtype=jnp.int32))
    mixed_all = mixed_all.reshape(head_count, block_size, head_dim).transpose(1, 0, 2)
    return (mixed_all, logs_all.reshape(head_count, block_size))


def dense_skip(query_block, key_rows, value_rows, span_number):
    block_size, head_count, head_dim = query_block.shape
    return (
        jnp.zeros((block_size, head_count, head_dim), jnp.float32),
        jnp.zeros((head_count, block_size), jnp.float32),
    )


def dense_back(query_block, grad_block, key_rows, value_rows, log_block, span_number):
    block_size, head_count, head_dim = query_block.shape
    slot_size = key_rows.shape[0]
    width_group = dense_width()
    scale = head_dim ** (-0.5)
    valid = jnp.arange(slot_size, dtype=jnp.int32) < span_number

    def one_group(number):
        offset = number * width_group
        query_part = lax.dynamic_slice_in_dim(query_block, offset, width_group, 1)
        grad_part = lax.dynamic_slice_in_dim(grad_block, offset, width_group, 1)
        key_part = lax.dynamic_slice_in_dim(key_rows, offset, width_group, 1)
        value_part = lax.dynamic_slice_in_dim(value_rows, offset, width_group, 1)
        scores = (
            jnp.einsum("tgd,kgd->gtk", query_part, key_part, preferred_element_type=jnp.float32)
            * scale
        )
        scores = jnp.where(valid[None, None, :], scores, negative)
        chances = jnp.exp(
            scores - lax.dynamic_slice_in_dim(log_block, offset, width_group, 0)[:, :, None]
        )
        grad_chances = jnp.einsum(
            "tgd,kgd->gtk", grad_part, value_part, preferred_element_type=jnp.float32
        )
        central = jnp.sum(chances * grad_chances, axis=-1, keepdims=True)
        grad_scores = (chances * (grad_chances - central)).astype(jnp.bfloat16)
        query_new = (
            jnp.einsum("gtk,kgd->gtd", grad_scores, key_part, preferred_element_type=jnp.float32)
            * scale
        )
        key_new = (
            jnp.einsum("gtk,tgd->gkd", grad_scores, query_part, preferred_element_type=jnp.float32)
            * scale
        )
        value_new = jnp.einsum(
            "gtk,tgd->gkd",
            chances.astype(jnp.bfloat16),
            grad_part,
            preferred_element_type=jnp.float32,
        )
        return (key_new, value_new, query_new)

    key_all, value_all, query_all = lax.map(
        one_group, jnp.arange(head_count // width_group, dtype=jnp.int32)
    )
    slot_terms = jnp.stack(
        [
            key_all.reshape(head_count, slot_size, head_dim),
            value_all.reshape(head_count, slot_size, head_dim),
        ]
    )
    return (slot_terms, query_all.reshape(head_count, block_size, head_dim).transpose(1, 0, 2))


def dense_pass(query_block, grad_block, key_rows, value_rows, log_block, span_number):
    block_size, head_count, head_dim = query_block.shape
    return (
        jnp.zeros((2, head_count, key_rows.shape[0], head_dim), jnp.float32),
        jnp.zeros(query_block.shape, jnp.float32),
    )


def return_grads(slot_grads):
    owned = lax.psum_scatter(
        slot_grads.astype(jnp.bfloat16), "seq", scatter_dimension=2, tiled=True
    ).astype(jnp.float32)
    pair_count, head_count, tok_count, head_dim = owned.shape
    return owned.transpose(2, 0, 1, 3).reshape(tok_count, pair_count * head_count * head_dim)


def flagged_place(flags):
    return jnp.sum(jnp.where(flags, jnp.arange(flags.shape[0], dtype=jnp.int32), 0))


def local(
    arriving_features,
    valid_extents,
    sampled_target_tiles,
    query_context_mapping,
    attention_outflow_weights,
    expansion_weights,
    contraction_weights,
    opening_scale_vector,
    opening_shift_vector,
    closing_scale_vector,
    closing_shift_vector,
    expansion_shift,
    contraction_shift,
    output_sensitivity,
):
    doc_count, tok_count, feature_breadth = arriving_features.shape
    head_count = sampled_target_tiles.shape[1]
    slot_blocks = sampled_target_tiles.shape[2]
    head_dim = feature_breadth // head_count
    slot_size = tok_count * lax.axis_size("seq")
    block_size = slot_size // slot_blocks
    local_blocks = tok_count // block_size
    first_block = lax.axis_index("seq") * local_blocks
    per_line_summation = doc_count * tok_count
    (
        full_inward,
        entire_outflow,
        full_expand,
        full_contract,
        overall_premultiplier,
        overall_shift_term,
        full_midscale,
        full_midshift,
        full_upshift,
        full_downshift,
    ) = (
        lax.all_gather(query_context_mapping, ("seq", "doc"), axis=0, tiled=True),
        lax.all_gather(attention_outflow_weights, ("seq", "doc"), axis=0, tiled=True),
        lax.all_gather(expansion_weights, ("seq", "doc"), axis=0, tiled=True),
        lax.all_gather(contraction_weights, ("seq", "doc"), axis=0, tiled=True),
        lax.all_gather(opening_scale_vector, ("seq", "doc"), axis=0, tiled=True),
        lax.all_gather(opening_shift_vector, ("seq", "doc"), axis=0, tiled=True),
        lax.all_gather(closing_scale_vector, ("seq", "doc"), axis=0, tiled=True),
        lax.all_gather(closing_shift_vector, ("seq", "doc"), axis=0, tiled=True),
        lax.all_gather(expansion_shift, ("seq", "doc"), axis=0, tiled=True),
        lax.all_gather(contraction_shift, ("seq", "doc"), axis=0, tiled=True),
    )
    shortcut_holder = arriving_features.reshape(per_line_summation, feature_breadth).astype(
        jnp.float32
    )
    opening_normalised, scaled_one, inverse_one = normalise_each_line(
        shortcut_holder,
        overall_premultiplier.astype(jnp.float32),
        overall_shift_term.astype(jnp.float32),
    )
    opening_normalised = opening_normalised.astype(jnp.bfloat16)
    projected = jnp.dot(opening_normalised, full_inward, preferred_element_type=jnp.float32).astype(
        jnp.bfloat16
    )
    query_local = projected[:, :feature_breadth].reshape(doc_count, tok_count, head_count, head_dim)
    pair_local = projected[:, feature_breadth:].reshape(doc_count, tok_count, 2 * feature_breadth)
    pair_full = lax.all_gather(pair_local, "seq", axis=1, tiled=True)

    def table_one(span_number, drawn_ordering):
        return candidate_table(span_number, drawn_ordering, first_block, local_blocks, block_size)

    clipped_all, keep_all, flags_all = jax.vmap(table_one)(valid_extents, sampled_target_tiles)
    query_heads = query_local.reshape(
        doc_count, local_blocks, block_size, head_count, head_dim
    ).transpose(0, 3, 1, 2, 4)
    block_flags = flags_all[:, :, None, None, None]

    def doc_forward(items):
        queries, pair_rows, clipped, keep = items
        key_sel = select_blocks(
            pair_rows[:, :feature_breadth].reshape(slot_size, head_count, head_dim),
            clipped,
            block_size,
        )
        value_sel = select_blocks(
            pair_rows[:, feature_breadth:].reshape(slot_size, head_count, head_dim),
            clipped,
            block_size,
        )
        mixed, log_sums = lax.map(
            sparse_forward,
            (split_heads(queries), split_heads(key_sel), split_heads(value_sel), split_heads(keep)),
        )
        return (join_heads(mixed), join_heads(log_sums))

    sparse_mixed, sparse_logs = lax.map(
        doc_forward, (query_heads, pair_full, clipped_all, keep_all)
    )
    mixed_rows = sparse_mixed.transpose(0, 2, 3, 1, 4)

    def doc_dense(items):
        queries, pair_rows, span_number, flags = items
        key_rows = pair_rows[:, :feature_breadth].reshape(slot_size, head_count, head_dim)
        value_rows = pair_rows[:, feature_breadth:].reshape(slot_size, head_count, head_dim)
        query_block = lax.dynamic_slice_in_dim(
            queries, flagged_place(flags) * block_size, block_size, 0
        )
        return lax.cond(
            jnp.any(flags),
            dense_forward,
            dense_skip,
            query_block,
            key_rows,
            value_rows,
            span_number,
        )

    dense_mixed, dense_logs = lax.map(doc_dense, (query_local, pair_full, valid_extents, flags_all))
    mixed_rows = jnp.where(block_flags, dense_mixed[:, None], mixed_rows)
    context_mixture = mixed_rows.reshape(per_line_summation, feature_breadth).astype(jnp.bfloat16)
    intermediate_state = shortcut_holder + jnp.dot(
        context_mixture, entire_outflow, preferred_element_type=jnp.float32
    )
    normed_two, scaled_two, inverse_two = normalise_each_line(
        intermediate_state, full_midscale.astype(jnp.float32), full_midshift.astype(jnp.float32)
    )
    normed_two = normed_two.astype(jnp.bfloat16)
    pre_act = jnp.dot(
        normed_two, full_expand, preferred_element_type=jnp.float32
    ) + full_upshift.astype(jnp.float32)
    activated = exact_gelu(pre_act).astype(jnp.bfloat16)
    final_rows = (
        intermediate_state
        + jnp.dot(activated, full_contract, preferred_element_type=jnp.float32)
        + full_downshift.astype(jnp.float32)
    )
    output = final_rows.astype(jnp.bfloat16).reshape(doc_count, tok_count, feature_breadth)
    back_inward, back_outward, back_expand, back_contract, back_prescale, back_midscale = (
        full_inward,
        entire_outflow,
        full_expand,
        full_contract,
        overall_premultiplier,
        full_midscale,
    )
    grad_out_rows = output_sensitivity.reshape(per_line_summation, feature_breadth)
    grad_out_wide = grad_out_rows.astype(jnp.float32)
    contract_grad = jnp.einsum(
        "rf,rd->fd", activated, grad_out_rows, preferred_element_type=jnp.float32
    )
    downshift_grad = jnp.sum(grad_out_wide, axis=0)
    grad_act = jnp.einsum(
        "rd,fd->rf", grad_out_rows, back_contract, preferred_element_type=jnp.float32
    )
    unused_value, gelu_back = jax.vjp(exact_gelu, pre_act)
    grad_pre = gelu_back(grad_act)[0].astype(jnp.bfloat16)
    expand_grad = jnp.einsum("rd,rf->df", normed_two, grad_pre, preferred_element_type=jnp.float32)
    upshift_grad = jnp.sum(grad_pre.astype(jnp.float32), axis=0)
    grad_norm_two = jnp.einsum(
        "rf,df->rd", grad_pre, back_expand, preferred_element_type=jnp.float32
    )
    middle_part, midscale_grad, midshift_grad = standardize_rows_pullback(
        grad_norm_two, scaled_two, inverse_two, back_midscale.astype(jnp.float32)
    )
    grad_middle = grad_out_wide + middle_part
    grad_branch = grad_middle.astype(jnp.bfloat16)
    outward_grad = jnp.einsum(
        "rd,re->de", context_mixture, grad_branch, preferred_element_type=jnp.float32
    )
    grad_attended = jnp.einsum(
        "re,de->rd", grad_branch, back_outward, preferred_element_type=jnp.float32
    ).astype(jnp.bfloat16)
    grad_attended = grad_attended.reshape(doc_count, tok_count, head_count, head_dim)
    grad_blocks = grad_attended.reshape(doc_count, local_blocks, block_size, head_count, head_dim)
    sparse_grads = jnp.where(block_flags, jnp.zeros_like(grad_blocks), grad_blocks).transpose(
        0, 3, 1, 2, 4
    )
    block_ids = jnp.arange(slot_blocks, dtype=jnp.int32)

    def sparse_back(queries, pair_rows, clipped, keep, log_sums, grad_part):
        key_rows = pair_rows[:, :feature_breadth].reshape(slot_size, head_count, head_dim)
        value_rows = pair_rows[:, feature_breadth:].reshape(slot_size, head_count, head_dim)
        key_sel = select_blocks(key_rows, clipped, block_size)
        value_sel = select_blocks(value_rows, clipped, block_size)
        grouped = (
            split_heads(queries),
            split_heads(key_sel),
            split_heads(value_sel),
            split_heads(keep),
            split_heads(log_sums),
            split_heads(grad_part),
        )
        query_term, key_term, value_term = lax.map(sparse_backward, grouped)
        query_term = join_heads(query_term)
        key_term = join_heads(key_term)
        value_term = join_heads(value_term)
        placing = (clipped[..., None] == block_ids).astype(jnp.float32)
        key_slot = jnp.einsum(
            "hlcn,hlcbd->hnbd",
            placing,
            key_term,
            precision=lax.Precision.HIGHEST,
            preferred_element_type=jnp.float32,
        )
        value_slot = jnp.einsum(
            "hlcn,hlcbd->hnbd",
            placing,
            value_term,
            precision=lax.Precision.HIGHEST,
            preferred_element_type=jnp.float32,
        )
        slot_grads = jnp.stack(
            [
                key_slot.reshape(head_count, slot_size, head_dim),
                value_slot.reshape(head_count, slot_size, head_dim),
            ]
        )
        return (query_term, slot_grads, key_rows, value_rows)

    def doc_backward(carry, items):
        (
            queries,
            pair_rows,
            clipped,
            keep,
            log_sums,
            grad_part,
            grad_rows,
            query_rows,
            dense_log,
            span_number,
            flags,
        ) = items
        query_term, slot_grads, key_rows, value_rows = sparse_back(
            queries, pair_rows, clipped, keep, log_sums, grad_part
        )
        start = flagged_place(flags) * block_size
        query_block = lax.dynamic_slice_in_dim(query_rows, start, block_size, 0)
        grad_block = lax.dynamic_slice_in_dim(grad_rows, start, block_size, 0)
        dense_slot, dense_term = lax.cond(
            jnp.any(flags),
            dense_back,
            dense_pass,
            query_block,
            grad_block,
            key_rows,
            value_rows,
            dense_log,
            span_number,
        )
        owned = return_grads(slot_grads + dense_slot)
        return (carry, (query_term, dense_term, owned))

    unused_carry, (sparse_query, dense_query, pair_grads) = lax.scan(
        doc_backward,
        jnp.zeros((), jnp.int32),
        (
            query_heads,
            pair_full,
            clipped_all,
            keep_all,
            sparse_logs,
            sparse_grads,
            grad_attended,
            query_local,
            dense_logs,
            valid_extents,
            flags_all,
        ),
    )
    query_grad = sparse_query.transpose(0, 2, 3, 1, 4) + jnp.where(
        block_flags, dense_query[:, None], 0.0
    )
    grad_projected = jnp.concatenate(
        [
            query_grad.reshape(per_line_summation, feature_breadth),
            pair_grads.reshape(per_line_summation, 2 * feature_breadth),
        ],
        axis=1,
    ).astype(jnp.bfloat16)
    inward_grad = jnp.einsum(
        "rd,re->de", opening_normalised, grad_projected, preferred_element_type=jnp.float32
    )
    grad_norm_one = jnp.einsum(
        "re,de->rd", grad_projected, back_inward, preferred_element_type=jnp.float32
    )
    incoming_slice, leading_gain_sensitivity, leading_offset_sensitivity = (
        standardize_rows_pullback(
            grad_norm_one, scaled_one, inverse_one, back_prescale.astype(jnp.float32)
        )
    )
    grad_inputs = (grad_middle + incoming_slice).reshape(doc_count, tok_count, feature_breadth)
    summed = (
        lax.psum_scatter(inward_grad, ("seq", "doc"), scatter_dimension=0, tiled=True),
        lax.psum_scatter(outward_grad, ("seq", "doc"), scatter_dimension=0, tiled=True),
        lax.psum_scatter(expand_grad, ("seq", "doc"), scatter_dimension=0, tiled=True),
        lax.psum_scatter(contract_grad, ("seq", "doc"), scatter_dimension=0, tiled=True),
        lax.psum_scatter(leading_gain_sensitivity, ("seq", "doc"), scatter_dimension=0, tiled=True),
        lax.psum_scatter(
            leading_offset_sensitivity, ("seq", "doc"), scatter_dimension=0, tiled=True
        ),
        lax.psum_scatter(midscale_grad, ("seq", "doc"), scatter_dimension=0, tiled=True),
        lax.psum_scatter(midshift_grad, ("seq", "doc"), scatter_dimension=0, tiled=True),
        lax.psum_scatter(upshift_grad, ("seq", "doc"), scatter_dimension=0, tiled=True),
        lax.psum_scatter(downshift_grad, ("seq", "doc"), scatter_dimension=0, tiled=True),
    )
    return (output, grad_inputs) + tuple(summed)


ROUTE = pl.DeviceIdType.MESH
NZ, NX, NY, NC = 4, 2, 2, 2
bf16, f32 = jnp.bfloat16, jnp.float32


def nn(left, right):
    return lax.dot_general(left, right, (((1,), (0,)), ((), ())), preferred_element_type=f32)


def nt(left, right):
    return lax.dot_general(left, right, (((1,), (1,)), ((), ())), preferred_element_type=f32)


def tn(left, right):
    return lax.dot_general(left, right, (((0,), (0,)), ((), ())), preferred_element_type=f32)


def loop(count, body):
    lax.fori_loop(0, count, body, 0)


class Net:
    def __init__(self, send_sems, recv_sems, here):
        self.send_sems, self.recv_sems, self.here = send_sems, recv_sems, here
        self.sent, self.taken = 0, 0
        self.open = []

    def slots(self, count):
        first = self.taken
        self.taken += count
        assert self.taken <= RECVS
        return first

    def copy(self, src, dst, device, slot, index):
        return pltpu.make_async_remote_copy(
            src_ref=src,
            dst_ref=dst,
            send_sem=self.send_sems.at[index],
            recv_sem=self.recv_sems.at[slot],
            device_id=device,
            device_id_type=ROUTE,
        )

    def series(self, count, describe, group=None):
        base = self.sent
        self.sent += count
        assert self.sent <= SENDS

        def start(i):
            src, dst, device, slot, is_self, made = describe(i)
            copy = self.copy(src, dst, device, slot, base + i)
            if is_self is None:
                if made is None:
                    copy.start()
                else:
                    pl.when(made)(copy.start)
            else:
                pl.when(jnp.logical_not(is_self))(copy.start)
                pl.when(is_self)(pltpu.make_async_copy(src, dst, self.recv_sems.at[slot]).start)

        def finish():
            for i in range(count):
                src, dst, device, slot, is_self, made = describe(i)
                copy = self.copy(src, dst, device, slot, base + i)
                if is_self is not None:
                    made = jnp.logical_not(is_self)
                if made is None:
                    copy.wait_send()
                else:
                    pl.when(made)(copy.wait_send)

        self.open.append((group, finish))
        return start

    def send(self, src, dst, device, slot, group=None, is_self=None, made=None):
        self.series(1, lambda i: (src, dst, device, slot, is_self, made), group)(0)

    def settle(self, group=None, everything=False):
        rest = []
        for name, finish in self.open:
            if everything or name == group:
                finish()
            else:
                rest.append((name, finish))
        self.open = rest

    def arrive(self, dst, slot):
        self.copy(dst, dst, self.here, slot, 0).wait_recv()


def row_stats(values):
    mean = jnp.mean(values, axis=-1, keepdims=True)
    centered = values - mean
    inverse = lax.rsqrt(jnp.mean(centered * centered, axis=-1, keepdims=True) + epsilon)
    return centered * inverse, inverse


def norm_pullback(grad, scaled, inverse, gain):
    wide = grad * gain
    first = jnp.mean(wide, axis=-1, keepdims=True)
    second = jnp.mean(wide * scaled, axis=-1, keepdims=True)
    return (wide - first - scaled * second) * inverse


def column_sum(values):
    return jnp.sum(values, axis=0, keepdims=True)


SCRATCH = dict(
    xr=((8, 2, 64, 1024), bf16),
    n1=((8, 128, 1024), bf16),
    aux=((64, 128), jnp.int32),
    aux2=((4, 16, 128), jnp.int32),
    table=((16, 16, 128), jnp.int32),
    bias=((16, 4, 1024), f32),
    sv=((4, 2, 2, 2, 8, 128), f32),
    vec=((8, 1024), f32),
    b1=((1, 1024), f32),
    wqs=((4, 32, 768), bf16),
    wq=((4, 2, 2, 2, 32, 768), bf16),
    wo=((4, 2, 2, 2, 32, 1024), bf16),
    w1s=((4, 32, 1024), bf16),
    w1=((4, 2, 2, 2, 32, 1024), bf16),
    w2=((4, 2, 128, 1024), bf16),
    qkv=((1024, 768), bf16),
    lse=((1024, 128), f32),
    at=((8, 128, 256), bf16),
    att=((2, 4, 128, 256), bf16),
    mid=((256, 1024), f32),
    nt2=((4, 256, 1024), bf16),
    dyx=((4, 256, 1024), bf16),
    act=((4, 256, 1024), bf16),
    gp=((4, 256, 1024), bf16),
    dw2=((4, 2, 128, 1024), bf16),
    own=((256, 1024), f32),
    gps=((4, 256, 1024), bf16),
    gpr=((2, 256, 1024), bf16),
    gpx=((256, 1024), bf16),
    ops=((4, 256, 1024), bf16),
    opr=((2, 256, 1024), bf16),
    opx=((256, 1024), bf16),
    gb=((256, 1024), bf16),
    gm=((256, 1024), f32),
    da=((2, 4, 128, 256), bf16),
    do=((8, 128, 256), bf16),
    dk=((1024, 128), f32),
    dv=((1024, 128), f32),
    dwq=((2, 4, 2, 2, 2, 32, 384), bf16),
    rgs=((8, 64, 1024), bf16),
    rgx=((4, 64, 1024), bf16),
    gnr=((2, 2, 64, 1024), bf16),
    r1y=((4, 2, 2, 32, 1024), bf16),
    r1z=((4, 2, 2, 32, 1024), bf16),
    r1v=((2, 2, 32, 1024), bf16),
    f1=((2, 2, 32, 1024), f32),
    r1f=((4, 32, 1024), f32),
    r2y=((4, 128, 1024), bf16),
    r2z=((4, 128, 1024), bf16),
    r2v=((128, 1024), bf16),
    ros=((4, 2, 2, 32, 1024), bf16),
    roa=((4, 32, 1024), bf16),
    rob=((4, 32, 1024), bf16),
    rof=((4, 32, 1024), bf16),
    roz=((4, 32, 1024), bf16),
    rov=((32, 1024), bf16),
    rqy=((2, 4, 2, 2, 32, 384), bf16),
    rqz=((2, 4, 2, 2, 32, 384), bf16),
    rqv=((2, 2, 2, 32, 384), bf16),
    fq=((2, 2, 32, 768), f32),
    rqf=((4, 32, 768), f32),
    sg=((2, 8, 8, 128), f32),
    rsg=((2, 8, 8, 128), f32),
    sgt=((2, 8, 128), f32),
    rst=((2, 4, 8, 128), f32),
)
SENDS, RECVS = 256, 256
VMEM_BYTES = 63 * 2**20


def layer_kernel(
    x_in, dy_in, extent_in, tiles_in, wq_in, wo_in, w1_in, w2_in,
    gain_one, shift_one, gain_two, shift_two, shift_up, shift_down,
    out_ref, gx_ref, dwq_ref, dwo_ref, dw1_ref, dw2_ref, sg_ref,
    *rest,
):
    names = list(SCRATCH)
    R = types.SimpleNamespace(**dict(zip(names, rest[: len(names)])))
    send_sems, recv_sems = rest[len(names):]
    s, d = lax.axis_index("seq"), lax.axis_index("doc")
    z, x, y, c = s // NX, s % NX, d // NC, d % NC
    g = 2 * x + c
    flip, xo, yo = 1 - c, 1 - x, 1 - y

    def at(zz, xx, yy, cc):
        return (zz * NX + xx, yy * NC + cc)

    here = (s, d)
    sib, xn, yn, cross = at(z, x, y, flip), at(z, xo, y, c), at(z, x, yo, c), at(z, xo, y, flip)
    group = ((x, flip, sib), (xo, c, xn), (xo, flip, cross))
    net = Net(send_sems, recv_sems, here)
    order = [z, z + 1 - 2 * (z // 2), (2 + 3 * z) % 5, 3 * (1 - z // 2)]
    middle = jnp.logical_or(z == 1, z == 2)

    barrier = pltpu.get_barrier_semaphore()

    def greet(step, _):
        other = (s * NC + c + step) % 16
        pl.semaphore_signal(
            barrier, inc=1, device_id=(other // NC, y * NC + other % NC), device_id_type=ROUTE
        )
        return 0

    lax.fori_loop(1, 16, greet, 0)
    for cc in (c, flip):
        pl.semaphore_signal(barrier, inc=1, device_id=at(z, x, yo, cc), device_id_type=ROUTE)
    for h in range(4):
        for t in range(3):
            for pair in range(2):
                src = t * 1024 + h * 256 + pair * 128
                dst = pair * 384 + t * 128
                R.wqs[h, :, dst:dst + 128] = wq_in[:, src:src + 128]
    R.wq[z, x, y, c] = R.wqs[g]
    small = R.sv.at[z, x, y, c]
    small[...] = jnp.zeros((8, 128), f32)
    for k, vector in enumerate((gain_one, shift_one, gain_two, shift_two)):
        small[0:1, k * 32:(k + 1) * 32] = vector[...].astype(f32)
    small[1:2, 0:32] = shift_down[...].astype(f32)
    small[2:3, :] = shift_up[...].astype(f32)
    for h in range(4):
        for q in range(8):
            block = 8 * (q // 2) + 4 * (h // 2) + 2 * (q % 2) + h % 2
            R.w1s[h, :, q * 128:(q + 1) * 128] = w1_in[:, block * 128:(block + 1) * 128]
    R.w1[z, x, y, c] = R.w1s[g]
    R.wo[z, x, y, c] = wo_in[...]
    R.w2[z, y] = w2_in[...]
    R.dyx[g] = dy_in[...].reshape(256, 1024)
    R.sg[...] = jnp.zeros((2, 8, 8, 128), f32)
    has_table = c == z // 2

    for h in range(16):
        R.table[h, :, 0:3] = tiles_in[z % 2, h]
    R.table[:, :, 3:4] = jnp.full((16, 16, 1), extent_in[z % 2], jnp.int32)

    @pl.when(has_table)
    def table():
        R.aux[...] = R.table[pl.ds(4 * g, 4)].reshape(64, 128)

    pl.semaphore_wait(barrier, 17)

    def z_start(piece, base, name):
        for k in (1, 2, 3):
            net.send(
                piece(z), piece(z), at(order[k], x, y, c), base + z, name, made=middle if k == 3 else None
            )

    def z_take(piece, base, name, k):
        part = piece(order[k])
        net.arrive(part, base + order[k])
        if k == 3:
            net.send(part, part, at(order[2], x, y, c), base + order[3], name, made=middle)
        return part

    half = pl.ds(pl.multiple_of(c * 512, 512), 512)
    other_half = pl.ds(pl.multiple_of(flip * 512, 512), 512)
    xz = net.slots(4)
    for b in range(2):
        for ch in range(2):
            zt = 2 * c + b
            net.send(
                x_in.at[b, :, :, ch * 512:(ch + 1) * 512],
                R.xr.at[s, :, :, ch * 512:(ch + 1) * 512],
                at(zt, x, y, ch),
                xz + z,
                is_self=jnp.logical_and(zt == z, c == ch),
            )

    wqa = net.slots(4)
    for xx, cc, dev in group:
        net.send(R.wqs.at[2 * xx + cc], R.wq.at[z, x, y, c], dev, wqa + g)

    sv_s, sv_z, sv_x, sv_y = net.slots(1), net.slots(4), net.slots(1), net.slots(1)
    net.send(R.sv.at[z, x, y, c], R.sv.at[z, x, y, c], sib, sv_s)

    aux_s = net.slots(1)
    net.send(R.table.at[pl.ds(4 * (2 * x + flip), 4)], R.aux2, sib, aux_s, made=has_table)

    w1a = net.slots(4)
    for xx, cc, dev in group:
        net.send(R.w1s.at[2 * xx + cc], R.w1.at[z, x, y, c], dev, w1a + g)

    def wq_piece(zz):
        return R.wq.at[zz, :, y]

    def w1_piece(zz):
        return R.w1.at[zz, :, y]

    def w2_piece(zz):
        return R.w2.at[zz, y]

    def wo_piece(zz):
        return R.wo.at[zz, x, y, c]

    wqz, wqy, w1z, w1y = net.slots(4), net.slots(4), net.slots(4), net.slots(4)
    w2z, w2y, woz = net.slots(4), net.slots(4), net.slots(4)
    for xx, cc, dev in group:
        net.arrive(R.wq.at[z, xx, y, cc], wqa + 2 * xx + cc)
    z_start(wq_piece, wqz, "w")
    net.send(wq_piece(z), wq_piece(z), yn, wqy + 0, "w")
    net.arrive(R.sv.at[z, x, y, flip], sv_s)
    z_start(lambda zz: R.sv.at[zz, x, y], sv_z, None)
    for xx, cc, dev in group:
        net.arrive(R.w1.at[z, xx, y, cc], w1a + 2 * xx + cc)
    net.send(w1_piece(z), w1_piece(z), yn, w1y + 0, "w")

    xx_r, xs_a, xs_b = net.slots(4), net.slots(4), net.slots(4)
    for k in range(4):
        zt = order[k]
        part = R.xr.at[zt * 2 + x, :, :, half]
        net.arrive(part, xz + zt)
        net.send(part, part, xn, xx_r + k, "xr")
        net.send(part, part, sib, xs_a + k, "xr")
        if k:
            part = z_take(wq_piece, wqz, "w", k)
            net.send(part, part, yn, wqy + k, "w")
    z_start(wo_piece, woz, "w")
    z_start(w1_piece, w1z, "w")
    for k in (1, 2, 3):
        z_take(lambda zz: R.sv.at[zz, x, y], sv_z, None, k)
    net.send(R.sv.at[:, x, y], R.sv.at[:, x, y], xn, sv_x)
    for k in range(4):
        zt = order[k]
        part = R.xr.at[zt * 2 + xo, :, :, half]
        net.arrive(part, xx_r + k)
        net.send(part, part, sib, xs_b + k, "xr")
        if k == 0:
            net.arrive(R.sv.at[:, xo, y], sv_x)
            net.send(R.sv.at[:, :, y], R.sv.at[:, :, y], yn, sv_y)

    def group_gather(buf):
        own_s, far_x, far_s = net.slots(1), net.slots(1), net.slots(1)

        def begin():
            net.send(buf.at[g], buf.at[g], sib, own_s)
            net.send(buf.at[g], buf.at[g], xn, far_x)

        def step():
            net.arrive(buf.at[2 * xo + c], far_x)
            net.send(buf.at[2 * xo + c], buf.at[2 * xo + c], sib, far_s)

        def take(which):
            if which == 1:
                net.arrive(buf.at[2 * x + flip], own_s)
            if which == 3:
                net.arrive(buf.at[2 * xo + flip], far_s)

        return begin, step, take

    members = (g, 2 * x + flip, 2 * xo + c, 2 * xo + flip)
    dy_begin, dy_step, dy_take = group_gather(R.dyx)
    nt_begin, nt_step, nt_take = group_gather(R.nt2)

    @pl.when(jnp.logical_not(has_table))
    def table_here():
        net.arrive(R.aux2, aux_s)
        R.aux[...] = R.aux2[...].reshape(64, 128)

    for i in range(16):
        tiles = R.aux[i * 4:(i + 1) * 4, :]
        place = lax.broadcasted_iota(jnp.int32, (4, 1024), 1)
        block = place >> 6
        row = lax.broadcasted_iota(jnp.int32, (4, 1024), 0) + (i % 4) * 4
        extent = tiles[:, 3:4]
        last = (extent - 1) >> 6
        seen = jnp.abs(row - block) <= 1
        for k in range(3):
            seen = seen | (block == tiles[:, k:k + 1])
        seen = seen | (block == 0) | (block == last) | (row == 0) | (row == last)
        seen = seen & (place < extent)
        R.bias[i] = jnp.where(seen, 0.0, negative).astype(f32)

    net.arrive(R.sv.at[:, :, yo], sv_y)
    lane = lax.broadcasted_iota(jnp.int32, (1, 128), 1) >> 5
    for r in range(8):
        for k in range(5):
            total = jnp.zeros((1, 128), f32)
            for q in range(4):
                line = R.sv[r // 2, r % 2, q // 2, q % 2, k // 4:k // 4 + 1, :]
                shift = (32 * (q - k % 4)) % 128
                if shift:
                    line = pltpu.roll(line, shift, 1)
                total = jnp.where(lane == q, line, total)
            R.vec[k:k + 1, r * 128:(r + 1) * 128] = total
    for q in range(8):
        R.b1[:, q * 128:(q + 1) * 128] = R.sv[q // 2, x, q % 2, c, 2:3, :]

    def first_norm(zt):
        def rows(k, _):
            i = 2 * zt + k
            scaled, _inverse = row_stats(R.xr[i].reshape(128, 1024).astype(f32))
            R.n1[i] = (scaled * R.vec[0:1, :] + R.vec[1:2, :]).astype(bf16)
            return 0

        loop(2, rows)

    for k in range(4):
        zt = order[k]
        net.arrive(R.xr.at[zt * 2 + x, :, :, other_half], xs_a + k)
        net.arrive(R.xr.at[zt * 2 + xo, :, :, other_half], xs_b + k)
        first_norm(zt)
    for k in range(4):
        net.arrive(R.wq.at[order[k], :, yo], wqy + k)

    def project(step, _):
        rows = R.n1[pl.ds(2 * step, 2)].reshape(256, 1024)
        made = nn(rows, R.wq[...].reshape(1024, 768)).astype(bf16)
        where = pl.ds(pl.multiple_of(step * 256, 256), 256)
        eighth = jnp.asarray(0.125, bf16)
        R.qkv[where, :] = jnp.concatenate(
            [made[:, :128] * eighth, made[:, 128:384], made[:, 384:512] * eighth, made[:, 512:]], axis=1
        )
        return 0

    loop(4, project)

    low_lane = lax.broadcasted_iota(jnp.int32, (1, 128), 1) < 64

    def only(values, e):
        return jnp.where(low_lane if e == 0 else jnp.logical_not(low_lane), values, jnp.zeros_like(values))

    def pair_columns(pair):
        first = pair * 384
        return (
            slice(pair * 128, pair * 128 + 128),
            slice(first, first + 128),
            slice(first + 128, first + 256),
            slice(first + 256, first + 384),
        )

    at_r = net.slots(8)
    back_c = z // 2

    def at_copy(i):
        zt, xx = i // 2, i % 2
        mine = jnp.logical_and(jnp.logical_and(zt == z, xx == x), c == back_c)
        return R.at.at[i], R.att.at[z % 2, g], at(zt, xx, y, back_c), at_r + (z % 2) * 4 + g, mine, None

    at_start = net.series(8, at_copy)

    def attend_tile(step, _):
        t = (z + step) % NZ
        where = pl.ds(pl.multiple_of(t * 256, 256), 256)
        for pair in range(2):
            cols, qcols, kcols, vcols = pair_columns(pair)
            q = R.qkv[where, qcols]
            mixed = None
            for e in range(2):
                h = pair * 2 + e
                scores = nt(only(q, e), R.qkv[:, kcols])
                scores = (scores.reshape(4, 64, 1024) + R.bias[h * 4 + t][:, None, :]).reshape(256, 1024)
                top = jnp.max(scores, axis=-1, keepdims=True)
                grown = jnp.exp(scores - top)
                total = jnp.sum(grown, axis=-1, keepdims=True)
                low = (grown * (1.0 / total)).astype(bf16)
                R.lse[where, h:h + 1] = top + jnp.log(total)
                got = nn(low, R.qkv[:, vcols])
                mixed = got if e == 0 else jnp.where(low_lane, mixed, got)
            R.at[pl.ds(2 * t, 2), :, cols] = mixed.astype(bf16).reshape(2, 128, 128)
        at_start(2 * t)
        at_start(2 * t + 1)
        return 0

    def attend(low, high):
        lax.fori_loop(low, high, attend_tile, 0)

    ax, ay = (x + flip) % 2, (y + c) % 2
    bx, by = (x + c) % 2, (y + flip) % 2
    near, far = at(z, ax, ay, c), at(z, bx, by, c)
    wo_a, wo_b, wo_d, wo_s = net.slots(1), net.slots(1), net.slots(1), net.slots(1)

    def wo_column(xx, yy):
        return R.wo.at[:, xx, yy, c]

    def w1_step(k):
        part = z_take(w1_piece, w1z, "w", k)
        net.send(part, part, yn, w1y + k, "w")

    def w2_step(k):
        part = z_take(w2_piece, w2z, "w", k)
        net.send(part, part, yn, w2y + k, "w")

    for k in (1, 2, 3):
        z_take(wo_piece, woz, "w", k)
    net.send(wo_column(x, y), wo_column(x, y), near, wo_a, "w")
    net.send(wo_column(x, y), wo_column(x, y), far, wo_b, "w")
    attend(1, 2)
    net.arrive(wo_column(ax, ay), wo_a)
    net.send(wo_column(ax, ay), wo_column(ax, ay), far, wo_d, "w")
    w1_step(1)
    attend(2, 3)
    dy_begin()
    w1_step(2)
    attend(3, 4)
    w1_step(3)
    attend(4, 5)
    dy_step()
    net.arrive(wo_column(bx, by), wo_b)
    net.arrive(wo_column(xo, yo), wo_d)
    net.send(R.wo.at[:, :, :, c], R.wo.at[:, :, :, c], sib, wo_s, "w")
    net.arrive(R.wo.at[:, :, :, flip], wo_s)
    for b in range(2):
        for h in range(4):
            net.arrive(R.att.at[b, h], at_r + b * 4 + h)
    z_start(w2_piece, w2z, "w")
    net.send(w2_piece(z), w2_piece(z), yn, w2y + 0, "w")

    def outflow():
        for n in range(4):
            cols = slice(n * 256, n * 256 + 256)
            made = x_in[:, :, :, cols].reshape(256, 256).astype(f32)
            for h in range(4):
                made = made + nn(
                    R.att[:, h].reshape(256, 256),
                    R.wo[h, :, :, :, :, cols].reshape(256, 256),
                )
            R.mid[:, cols] = made
        for k in range(2):
            where = slice(k * 128, k * 128 + 128)
            scaled, _inverse = row_stats(R.mid[where, :])
            R.nt2[g, where, :] = (scaled * R.vec[2:3, :] + R.vec[3:4, :]).astype(bf16)

    outflow()
    nt_begin()

    for k in range(4):
        net.arrive(R.w1.at[order[k], :, yo], w1y + k)

    def widen_rows(which):
        def widen(j, _):
            where = pl.ds(pl.multiple_of(j * 256, 256), 256)
            pre = nn(R.nt2[which], R.w1[:, :, :, :, :, where].reshape(1024, 256))
            pre = pre + R.b1[:, where]
            share = 0.5 * (1.0 + lax.erf(pre * (2.0 ** -0.5)))
            R.act[which, :, where] = (pre * share).astype(bf16)
            slope = share + pre * (jnp.exp(-0.5 * pre * pre) * (1.0 / (2.0 * jnp.pi) ** 0.5))
            R.gp[which, :, where] = slope.astype(bf16)
            return 0

        loop(4, widen)

    widen_rows(members[0])
    w2_step(1)
    nt_take(1)
    widen_rows(members[1])
    nt_step()
    w2_step(2)
    widen_rows(members[2])
    nt_take(3)
    w2_step(3)
    widen_rows(members[3])
    dy_take(1)
    dy_take(3)

    def outer_two(j, _):
        where = pl.ds(pl.multiple_of(j * 256, 256), 256)
        made = tn(R.act[:, :, where].reshape(1024, 256), R.dyx[...].reshape(1024, 1024))
        R.dw2[j] = made.astype(bf16).reshape(2, 128, 1024)
        return 0

    loop(4, outer_two)

    def scatter(piece, away, landing_y, landing_z, landing_v, name):
        base_y, base_z, base_v = net.slots(4), net.slots(4), net.slots(1)

        def begin(ks=(3, 2, 1, 0)):
            for k in ks:
                net.send(away(order[k]), landing_y.at[order[k]], yn, base_y + k, name)

        def add(ref, other):
            ref[...] = (ref[...].astype(f32) + other[...].astype(f32)).astype(bf16)

        def take(k):
            net.arrive(landing_y.at[order[k]], base_y + k)
            add(piece(order[k]), landing_y.at[order[k]])

        def along(k):
            part = piece(order[k])
            if k == 3:
                net.send(part, landing_v, at(order[1], x, y, c), base_v, name, made=jnp.logical_not(middle))

                @pl.when(middle)
                def pass_on():
                    net.arrive(landing_v, base_v)
                    add(part, landing_v)

                net.send(part, landing_z.at[z], at(order[3], x, y, c), base_z + z, name, made=middle)
            else:
                net.send(part, landing_z.at[z], at(order[k], x, y, c), base_z + z, name)

        def final(out):
            out[...] = piece(z)[...].astype(f32)
            for k in (1, 2):
                net.arrive(landing_z.at[order[k]], base_z + order[k])
                out[...] += landing_z[order[k]].astype(f32)

            @pl.when(middle)
            def from_end():
                net.arrive(landing_z.at[order[3]], base_z + order[3])
                out[...] += landing_z[order[3]].astype(f32)

        return begin, take, along, final

    two_begin, two_take, two_along, two_final = scatter(
        lambda zz: R.dw2.at[zz, y], lambda zz: R.dw2.at[zz, yo], R.r2y, R.r2z, R.r2v, "s2"
    )
    two_begin()

    for k in range(4):
        net.arrive(R.w2.at[order[k], yo], w2y + k)

    def narrow_back_rows(which):
        def narrow_back(j, _):
            where = pl.ds(pl.multiple_of(j * 256, 256), 256)
            made = nt(R.dyx[which], R.w2[j].reshape(256, 1024)) * R.gp[which, :, where].astype(f32)
            R.gp[which, :, where] = made.astype(bf16)
            return 0

        loop(4, narrow_back)

    def group_reduce(product, sent, landing, landing_x, kept):
        slot_s, slot_x = net.slots(2), net.slots(1)
        for which, where in ((members[3], xo), (members[2], None), (members[1], x), (members[0], None)):
            if which is members[0]:
                product(which, kept)
            else:
                product(which, sent.at[which])
            if where is not None:
                net.send(sent.at[which], landing.at[where], sib, slot_s + where)
            elif which is members[2]:
                net.arrive(landing.at[xo], slot_s + xo)
                sent[which] = (sent[which].astype(f32) + landing[xo].astype(f32)).astype(bf16)
                net.send(sent.at[which], landing_x, xn, slot_x)

        def finish():
            net.arrive(landing.at[x], slot_s + x)
            net.arrive(landing_x, slot_x)

        return finish

    def grad_norm_part(which, out):
        narrow_back_rows(which)

        def back(n, _):
            made = nt(R.gp[which], R.w1[n].reshape(256, 1024))
            out[:, pl.ds(pl.multiple_of(n * 256, 256), 256)] = made.astype(out.dtype)
            return 0

        loop(4, back)

    gn_finish = group_reduce(grad_norm_part, R.gps, R.gpr, R.gpx, R.own)
    net.settle("w")

    def outer_one(n, _):
        left = R.nt2[:, :, pl.ds(pl.multiple_of(n * 256, 256), 256)].reshape(1024, 256)
        made = tn(left, R.gp[...].reshape(1024, 1024)).astype(bf16)
        R.w1[n] = made.reshape(2, 2, 2, 32, 1024)
        return 0

    loop(4, outer_one)
    one_begin, one_take, one_along, one_final = scatter(
        w1_piece, lambda zz: R.w1.at[zz, :, yo], R.r1y, R.r1z, R.r1v, "s1"
    )
    one_begin()

    gn_finish()
    sums = [jnp.zeros((1, 1024), f32) for _ in range(3)]

    def norm_two_back():
        for k in range(4):
            where = slice(k * 64, k * 64 + 64)
            grad = R.own[where, :] + R.gpr[x, where, :].astype(f32) + R.gpx[where, :].astype(f32)
            scaled, inverse = row_stats(R.mid[where, :])
            flow = dy_in[k // 2, (k % 2) * 64:(k % 2) * 64 + 64, :].astype(f32)
            sums[0] = sums[0] + column_sum(grad * scaled)
            sums[1] = sums[1] + column_sum(grad)
            sums[2] = sums[2] + column_sum(flow)
            total = flow + norm_pullback(grad, scaled, inverse, R.vec[2:3, :])
            R.gm[where, :] = total
            R.gb[where, :] = total.astype(bf16)

    norm_two_back()

    do_r = net.slots(8)

    def outflow_back(h, _):
        made = nt(R.gb[...], R.wo[h].reshape(256, 1024)).astype(bf16)
        R.da[:, h] = made.reshape(2, 128, 256)
        return 0

    loop(4, outflow_back)
    for b in range(2):
        for xx in (x, xo):
            for cc in (c, flip):
                zt = 2 * c + b
                net.send(
                    R.da.at[b, 2 * xx + cc],
                    R.do.at[s],
                    at(zt, xx, y, cc),
                    do_r + s,
                    is_self=jnp.logical_and(zt == z, jnp.logical_and(xx == x, cc == c)),
                )


    def outer_flow():
        for h in range(4):
            made = tn(R.att[:, h].reshape(256, 256), R.gb[...]).astype(bf16)
            R.wo[h] = made.reshape(2, 2, 2, 32, 1024)

    outer_flow()
    ros_s = net.slots(1)
    net.send(R.wo.at[:, :, :, flip], R.ros, sib, ros_s)

    def contract_part(which, out):
        def forth(n, _):
            cols = pl.ds(pl.multiple_of(n * 256, 256), 256)
            made = nn(R.act[which], R.w2[:, :, :, cols].reshape(1024, 256))
            out[:, cols] = made.astype(out.dtype)
            return 0

        loop(4, forth)

    out_finish = group_reduce(contract_part, R.ops, R.opr, R.opx, R.own)
    for k in (3, 2, 1, 0):
        two_take(k)
        if k:
            two_along(k)

    def note(which, row, line):
        for r in range(8):
            R.sg[which, r, row:row + 1, :] = line[:, r * 128:(r + 1) * 128]

    def small_begin(which):
        base = net.slots(8)
        for k in (3, 2, 1, 0):
            for xx in (xo, x):
                if k == 0 and xx is x:
                    continue
                zt = order[k]
                net.send(R.sg.at[which, zt * 2 + xx], R.rsg.at[which, s], at(zt, xx, y, c), base + s)
        return base

    def small_middle(which, base):
        total = R.sg[which, s]
        for k in (1, 2, 3, 0):
            for xx in (x, xo):
                if k == 0 and xx is x:
                    continue
                i = order[k] * 2 + xx
                net.arrive(R.rsg.at[which, i], base + i)
                total = total + R.rsg[which, i]
        R.sgt[which] = total
        slot = net.slots(4)
        for yy, cc in ((y, flip), (yo, c), (yo, flip)):
            net.send(R.sgt.at[which], R.rst.at[which, 2 * y + c], at(z, x, yy, cc), slot + 2 * y + c)
        return slot

    def small_end(which, slot):
        row = lax.broadcasted_iota(jnp.int32, (8, 128), 0)
        total = R.sgt[which]
        for yy, cc in ((y, flip), (yo, c), (yo, flip)):
            i = 2 * yy + cc
            net.arrive(R.rst.at[which, i], slot + i)
            got = R.rst[which, i]
            total = total + (got if cc is c else jnp.where(row < 5, got, 0.0))
        return total

    for k in range(3):
        note(0, 2 + k, sums[k])
    up = [jnp.zeros((1, 1024), f32)]

    def up_sum():
        for k in range(16):
            rows = slice((k % 4) * 64, (k % 4) * 64 + 64)
            up[0] = up[0] + column_sum(R.gp[k // 4, rows, :].astype(f32))

    up_sum()
    for q in range(8):
        R.sg[0, 2 * (q // 2) + x, 5 + q % 2:6 + q % 2, :] = up[0][:, q * 128:(q + 1) * 128]
    early = small_begin(0)

    def attend_back(pair):
        cols, qcols, kcols, vcols = pair_columns(pair)
        R.dk[...] = jnp.zeros((1024, 128), f32)
        R.dv[...] = jnp.zeros((1024, 128), f32)

        def tile(step, _):
            t = (z + step) % NZ
            where = pl.ds(pl.multiple_of(t * 256, 256), 256)
            two = pl.ds(2 * t, 2)
            if pair == 0:
                for k in range(2):
                    net.arrive(R.do.at[2 * t + k], do_r + 2 * t + k)
            q = R.qkv[where, qcols]
            grad = R.do[two, :, cols].reshape(256, 128)
            prod = grad.astype(f32) * R.at[two, :, cols].reshape(256, 128).astype(f32)
            query = None
            for e in range(2):
                h = pair * 2 + e
                qe, ge = only(q, e), only(grad, e)
                scores = nt(qe, R.qkv[:, kcols])
                scores = (scores.reshape(4, 64, 1024) + R.bias[h * 4 + t][:, None, :]).reshape(256, 1024)
                chances = jnp.exp(scores - R.lse[where, h:h + 1])
                central = jnp.sum(only(prod, e), axis=-1, keepdims=True)
                moved = nt(ge, R.qkv[:, vcols])
                back = (chances * (moved - central)).astype(bf16)
                R.dv[...] += tn(chances.astype(bf16), ge)
                R.dk[...] += tn(back, qe)
                got = nn(back, R.qkv[:, kcols])
                query = got if e == 0 else jnp.where(low_lane, query, got)
            R.qkv[where, qcols] = (query * 0.125).astype(bf16)
            return 0

        lax.fori_loop(0, 4, tile, 0)
        R.qkv[:, kcols] = R.dk[...].astype(bf16)
        R.qkv[:, vcols] = R.dv[...].astype(bf16)

    def outer_in_pair(pair):
        def outer_in(n, _):
            rows = pl.ds(pl.multiple_of(n * 256, 256), 256)
            made = tn(R.n1[:, :, rows].reshape(1024, 256), R.qkv[:, pair * 384:pair * 384 + 384])
            R.dwq[pair, n] = made.astype(bf16).reshape(2, 2, 2, 32, 384)
            return 0

        loop(4, outer_in)
        steps = scatter(
            lambda zz: R.dwq.at[pair, zz, :, y],
            lambda zz: R.dwq.at[pair, zz, :, yo],
            R.rqy.at[pair],
            R.rqz.at[pair],
            R.rqv.at[pair],
            None,
        )
        steps[0]()
        return steps

    attend_back(0)
    for k in (3, 2, 1, 0):
        one_take(k)
        if k:
            one_along(k)
    net.arrive(R.ros, ros_s)
    for k in range(4):
        R.wo[k, :, :, c] = (R.wo[k, :, :, c].astype(f32) + R.ros[k].astype(f32)).astype(bf16)
    roa_s, rob_s, rof_s, roz_s = net.slots(1), net.slots(1), net.slots(1), net.slots(4)
    net.send(wo_column(xo, yo), R.roa, far, roa_s)
    net.send(wo_column(bx, by), R.rob, far, rob_s)
    q0_begin, q0_take, q0_along, q0_final = outer_in_pair(0)
    early = small_middle(0, early)
    out_finish()
    for k in range(2):
        where = slice(k * 128, k * 128 + 128)
        total = R.mid[where, :] + R.own[where, :] + R.opr[x, where, :].astype(f32)
        out_ref[k] = (total + R.opx[where, :].astype(f32) + R.vec[4:5, :]).astype(bf16)
    attend_back(1)

    net.settle("xr")

    def unproject(step, _):
        t = (z + 1 + step) % NZ
        where = pl.ds(pl.multiple_of(t * 256, 256), 256)
        made = nt(R.qkv[where, :], R.wq[...].reshape(1024, 768)).astype(bf16)
        R.xr[pl.ds(2 * t, 2)] = made.reshape(2, 2, 64, 1024)
        gs_start(t)
        return 0

    rgs_s, rgx_s, gnr_s = net.slots(4), net.slots(4), net.slots(4)
    gs_start = net.series(
        4,
        lambda t: (
            R.xr.at[pl.ds(2 * t, 2), flip], R.rgs.at[pl.ds(2 * t, 2)], sib, rgs_s + t, None, None
        ),
    )
    loop(4, unproject)

    for k in (3, 2, 1, 0):
        q0_take(k)
        if k:
            q0_along(k)
    q1_begin, q1_take, q1_along, q1_final = outer_in_pair(1)
    for k in (3, 2, 1, 0):
        zt = order[k]
        i = zt * 2 + xo
        net.arrive(R.rgs.at[pl.ds(2 * zt, 2)], rgs_s + zt)
        R.xr[i, c] = (R.xr[i, c].astype(f32) + R.rgs[i].astype(f32)).astype(bf16)
        net.send(R.xr.at[i, c], R.rgx.at[zt], xn, rgx_s + k)
    net.arrive(R.roa, roa_s)
    part = wo_column(ax, ay)
    part[...] = (part[...].astype(f32) + R.roa[...].astype(f32)).astype(bf16)
    net.send(part, R.rof, near, rof_s)
    for k in (3, 2, 1, 0):
        zt = order[k]
        i = zt * 2 + x
        net.arrive(R.rgx.at[zt], rgx_s + k)
        R.xr[i, c] = (
            R.xr[i, c].astype(f32) + R.rgs[i].astype(f32) + R.rgx[zt].astype(f32)
        ).astype(bf16)
        net.send(
            R.xr.at[i, c],
            R.gnr.at[z % 2, c],
            at(zt, x, y, back_c),
            gnr_s + 2 * (z % 2) + c,
            is_self=jnp.logical_and(zt == z, c == back_c),
        )
    for k in (3, 2, 1, 0):
        q1_take(k)
        if k:
            q1_along(k)

    net.arrive(R.rob, rob_s)
    net.arrive(R.rof, rof_s)
    part = wo_column(x, y)
    part[...] = (part[...].astype(f32) + R.rob[...].astype(f32) + R.rof[...].astype(f32)).astype(bf16)
    for k in (1, 2, 3):
        net.send(wo_piece(order[k]), R.roz.at[z], at(order[k], x, y, c), roz_s + z)


    two_final(dw2_ref)
    sums = [jnp.zeros((1, 1024), f32) for _ in range(2)]
    for k in range(4):
        net.arrive(R.gnr.at[k // 2, k % 2], gnr_s + k)
        rows = slice((k % 2) * 64, (k % 2) * 64 + 64)
        grad = R.gnr[k // 2, k % 2].astype(f32)
        scaled, inverse = row_stats(x_in[k // 2, k % 2].astype(f32))
        sums[0] = sums[0] + column_sum(grad * scaled)
        sums[1] = sums[1] + column_sum(grad)
        gx_ref[k // 2, rows, :] = R.gm[k * 64:(k + 1) * 64, :] + norm_pullback(
            grad, scaled, inverse, R.vec[0:1, :]
        )
    for k in range(2):
        note(1, k, sums[k])
    late = small_begin(1)

    r1f_s, rqf_s = net.slots(4), net.slots(4)
    one_final(R.f1)
    for xx, cc, dev in group:
        net.send(R.f1.at[xx, cc], R.r1f.at[g], dev, r1f_s + g)
    R.r1f[g] = R.f1[x, c]
    q0_final(R.fq.at[:, :, :, 0:384])
    q1_final(R.fq.at[:, :, :, 384:768])
    for xx, cc, dev in group:
        net.send(R.fq.at[xx, cc], R.rqf.at[g], dev, rqf_s + g)
    R.rqf[g] = R.fq[x, c]
    late = small_middle(1, late)

    dwo_ref[...] = wo_piece(z)[...].astype(f32)
    for k in (1, 2, 3):
        net.arrive(R.roz.at[order[k]], roz_s + order[k])
        dwo_ref[...] += R.roz[order[k]].astype(f32)
    for xx, cc, dev in group:
        net.arrive(R.r1f.at[2 * xx + cc], r1f_s + 2 * xx + cc)
    for h in range(4):
        for q in range(8):
            block = 8 * (q // 2) + 4 * (h // 2) + 2 * (q % 2) + h % 2
            dw1_ref[:, block * 128:(block + 1) * 128] = R.r1f[h, :, q * 128:(q + 1) * 128]
    for xx, cc, dev in group:
        net.arrive(R.rqf.at[2 * xx + cc], rqf_s + 2 * xx + cc)
    for h in range(4):
        for t in range(3):
            for pair in range(2):
                src = pair * 384 + t * 128
                dst = t * 1024 + h * 256 + pair * 128
                dwq_ref[:, dst:dst + 128] = R.rqf[h, :, src:src + 128]
    total = small_end(0, early) + small_end(1, late)
    sg_ref[...] = pltpu.roll(total, (128 - 32 * d) % 128, 1)
    sg_ref[5:6, :] = jnp.where(y == 0, total[5:6, :], total[6:7, :])
    net.settle(everything=True)


def local_fused(
    arriving_features,
    valid_extents,
    sampled_target_tiles,
    query_context_mapping,
    attention_outflow_weights,
    expansion_weights,
    contraction_weights,
    opening_scale_vector,
    opening_shift_vector,
    closing_scale_vector,
    closing_shift_vector,
    expansion_shift,
    contraction_shift,
    output_sensitivity,
):
    shapes = (
        (arriving_features.shape, bf16),
        (arriving_features.shape, f32),
        (query_context_mapping.shape, f32),
        (attention_outflow_weights.shape, f32),
        (expansion_weights.shape, f32),
        (contraction_weights.shape, f32),
        ((8, 128), f32),
    )
    whole = pl.BlockSpec(memory_space=pltpu.VMEM)
    scalars = pl.BlockSpec(memory_space=pltpu.SMEM)
    made = pl.pallas_call(
        layer_kernel,
        name="layer",
        out_shape=[jax.ShapeDtypeStruct(a, b) for a, b in shapes],
        in_specs=[whole] * 2 + [scalars] + [whole] * 11,
        out_specs=[whole] * 7,
        scratch_shapes=[pltpu.VMEM(a, b) for a, b in SCRATCH.values()]
        + [
            pltpu.SemaphoreType.DMA((SENDS,)),
            pltpu.SemaphoreType.DMA((RECVS,)),
        ],
        compiler_params=pltpu.CompilerParams(
            collective_id=0, has_side_effects=True, vmem_limit_bytes=VMEM_BYTES
        ),
    )(
        arriving_features.reshape(2, 2, 64, 1024),
        output_sensitivity,
        valid_extents,
        sampled_target_tiles,
        query_context_mapping,
        attention_outflow_weights,
        expansion_weights,
        contraction_weights,
        opening_scale_vector.reshape(1, 32),
        opening_shift_vector.reshape(1, 32),
        closing_scale_vector.reshape(1, 32),
        closing_shift_vector.reshape(1, 32),
        expansion_shift.reshape(1, 128),
        contraction_shift.reshape(1, 32),
    )
    place = pl.BlockSpec(memory_space=pl.ANY)
    rows = ((1, 32), (1, 32), (1, 32), (1, 32), (1, 128), (1, 32))
    done = pl.pallas_call(
        leave_kernel,
        name="leave",
        out_shape=[jax.ShapeDtypeStruct(a, b) for a, b in shapes[:6]]
        + [jax.ShapeDtypeStruct(a, f32) for a in rows],
        in_specs=[place] * 6 + [whole],
        out_specs=[place] * 6 + [whole] * 6,
        scratch_shapes=[pltpu.VMEM(a, b) for a, b in shapes[:6]]
        + [pltpu.SemaphoreType.DMA((6,)), pltpu.SemaphoreType.DMA((6,))],
    )(*made)
    return tuple(done[:6]) + tuple(line.reshape(-1) for line in done[6:])


def leave_kernel(*refs):
    large, small, out, rows, held = refs[:6], refs[6], refs[7:13], refs[13:19], refs[19:25]
    come, go = refs[25:]
    for k in range(6):
        pltpu.make_async_copy(large[k], held[k], come.at[k]).start()
    for k, row in enumerate((0, 1, 2, 3, 5, 4)):
        rows[k][...] = small[row:row + 1, :rows[k].shape[1]]
    for k in range(6):
        pltpu.make_async_copy(large[k], held[k], come.at[k]).wait()
        pltpu.make_async_copy(held[k], out[k], go.at[k]).start()
    for k in range(6):
        pltpu.make_async_copy(held[k], out[k], go.at[k]).wait()


def fits_fused(mesh, arguments):
    features, tiles, expand = arguments[0], arguments[2], arguments[5]
    return (
        dict(mesh.shape) == {"seq": 8, "doc": 4}
        and features.shape == (8, 1024, 1024)
        and tiles.shape == (8, 16, 16, 3)
        and expand.shape == (1024, 4096)
    )


def solution(mesh):
    in_specs = (
        P("doc", "seq", None),
        P("doc"),
        P("doc", None, None, None),
        P(("seq", "doc"), None),
        P(("seq", "doc"), None),
        P(("seq", "doc"), None),
        P(("seq", "doc"), None),
        P(("seq", "doc")),
        P(("seq", "doc")),
        P(("seq", "doc")),
        P(("seq", "doc")),
        P(("seq", "doc")),
        P(("seq", "doc")),
        P("doc", "seq", None),
    )
    out_specs = (
        P("doc", "seq", None),
        P("doc", "seq", None),
        P(("seq", "doc"), None),
        P(("seq", "doc"), None),
        P(("seq", "doc"), None),
        P(("seq", "doc"), None),
        P(("seq", "doc")),
        P(("seq", "doc")),
        P(("seq", "doc")),
        P(("seq", "doc")),
        P(("seq", "doc")),
        P(("seq", "doc")),
    )

    def run(*arguments):
        body = local_fused if fits_fused(mesh, arguments) else local
        mapped = jax.shard_map(
            body, mesh=mesh, in_specs=in_specs, out_specs=out_specs, check_vma=False
        )
        return mapped(*arguments)

    return run
```

```python
import types

import jax
import jax.numpy as jnp
from jax import lax
from jax.experimental import pallas as pl
from jax.experimental.pallas import tpu as pltpu
from jax.sharding import PartitionSpec as P

group_heads = 4
epsilon = 1e-05
negative = -1e30


def normalise_each_line(values, scaling, shifting):
    centered = values - jnp.mean(values, axis=-1, keepdims=True)
    inverse = lax.rsqrt(jnp.mean(centered * centered, axis=-1, keepdims=True) + epsilon)
    scaled = centered * inverse
    return (scaled * scaling + shifting, scaled, inverse)


def standardize_rows_pullback(grad_norm, scaled, inverse, scaling):
    grad_scaled = grad_norm * scaling
    centred_grad = grad_scaled - jnp.mean(grad_scaled, axis=-1, keepdims=True)
    centred_grad = centred_grad - scaled * jnp.mean(grad_scaled * scaled, axis=-1, keepdims=True)
    return (centred_grad * inverse, jnp.sum(grad_norm * scaled, axis=0), jnp.sum(grad_norm, axis=0))


def exact_gelu(values):
    return jax.nn.gelu(values, approximate=False)


def dense_width():
    return 8


def split_heads(array):
    return array.reshape((array.shape[0] // group_heads, group_heads) + array.shape[1:])


def join_heads(array):
    return array.reshape((array.shape[0] * array.shape[1],) + array.shape[2:])


def candidate_table(span_number, drawn_ordering, first_block, local_blocks, block_size):
    head_count, slot_blocks, random_count = drawn_ordering.shape
    query_blocks = first_block + jnp.arange(local_blocks, dtype=jnp.int32)
    last_block = (span_number - 1) // block_size
    picked = lax.dynamic_slice_in_dim(drawn_ordering, first_block, local_blocks, 1)
    window = jnp.stack([query_blocks - 1, query_blocks, query_blocks + 1], axis=1)
    edges = jnp.stack(
        [jnp.zeros_like(query_blocks), jnp.zeros_like(query_blocks) + last_block], axis=1
    )
    window = jnp.broadcast_to(window[None], (head_count, local_blocks, 3))
    edges = jnp.broadcast_to(edges[None], (head_count, local_blocks, 2))
    candidates = jnp.concatenate([window, picked, edges], axis=2)
    candidate_count = candidates.shape[2]
    inside = (candidates >= 0) & (candidates < slot_blocks)
    earlier = jnp.arange(candidate_count)[:, None] > jnp.arange(candidate_count)[None, :]
    repeated = jnp.any((candidates[:, :, :, None] == candidates[:, :, None, :]) & earlier, axis=3)
    usable = inside & jnp.logical_not(repeated)
    clipped = jnp.clip(candidates, 0, slot_blocks - 1)
    places = clipped[:, :, :, None] * block_size + jnp.arange(block_size, dtype=jnp.int32)
    keep = usable[:, :, :, None] & (places < span_number)
    flags = (query_blocks == 0) | (query_blocks == last_block)
    return (clipped, keep, flags)


def select_blocks(rows, clipped, block_size):
    slot_size, head_count, head_dim = rows.shape
    shaped = rows.reshape(slot_size // block_size, block_size, head_count, head_dim)
    head_index = jnp.arange(head_count, dtype=jnp.int32)[:, None, None]
    return shaped[clipped, :, head_index, :]


def sparse_forward(parts):
    query_group, key_group, value_group, keep_group = parts
    scale = query_group.shape[-1] ** (-0.5)
    scores = (
        jnp.einsum("hitd,hickd->hitck", query_group, key_group, preferred_element_type=jnp.float32)
        * scale
    )
    scores = jnp.where(keep_group[:, :, None], scores, negative)
    shape = scores.shape
    flat = scores.reshape(shape[0], shape[1], shape[2], shape[3] * shape[4])
    highest = jnp.max(flat, axis=-1, keepdims=True)
    weights_exp = jnp.exp(flat - highest)
    totals = jnp.sum(weights_exp, axis=-1, keepdims=True)
    chances_low = (weights_exp / totals).astype(jnp.bfloat16).reshape(shape)
    mixed = jnp.einsum(
        "hitck,hickd->hitd", chances_low, value_group, preferred_element_type=jnp.float32
    )
    return (mixed, (highest + jnp.log(totals))[..., 0])


def sparse_backward(parts):
    query_group, key_group, value_group, keep_group, log_group, grad_group = parts
    scale = query_group.shape[-1] ** (-0.5)
    scores = (
        jnp.einsum("hitd,hickd->hitck", query_group, key_group, preferred_element_type=jnp.float32)
        * scale
    )
    scores = jnp.where(keep_group[:, :, None], scores, negative)
    chances = jnp.exp(scores - log_group[..., None, None])
    grad_chances = jnp.einsum(
        "hitd,hickd->hitck", grad_group, value_group, preferred_element_type=jnp.float32
    )
    central = jnp.sum(chances * grad_chances, axis=(3, 4), keepdims=True)
    grad_scores = (chances * (grad_chances - central)).astype(jnp.bfloat16)
    query_term = (
        jnp.einsum("hitck,hickd->hitd", grad_scores, key_group, preferred_element_type=jnp.float32)
        * scale
    )
    key_term = (
        jnp.einsum(
            "hitck,hitd->hickd", grad_scores, query_group, preferred_element_type=jnp.float32
        )
        * scale
    )
    value_term = jnp.einsum(
        "hitck,hitd->hickd",
        chances.astype(jnp.bfloat16),
        grad_group,
        preferred_element_type=jnp.float32,
    )
    return (query_term, key_term, value_term)


def dense_forward(query_block, key_rows, value_rows, span_number):
    block_size, head_count, head_dim = query_block.shape
    width_group = dense_width()
    scale = head_dim ** (-0.5)
    valid = jnp.arange(key_rows.shape[0], dtype=jnp.int32) < span_number

    def one_group(number):
        offset = number * width_group
        query_part = lax.dynamic_slice_in_dim(query_block, offset, width_group, 1)
        key_part = lax.dynamic_slice_in_dim(key_rows, offset, width_group, 1)
        value_part = lax.dynamic_slice_in_dim(value_rows, offset, width_group, 1)
        scores = (
            jnp.einsum("tgd,kgd->gtk", query_part, key_part, preferred_element_type=jnp.float32)
            * scale
        )
        scores = jnp.where(valid[None, None, :], scores, negative)
        highest = jnp.max(scores, axis=-1, keepdims=True)
        weights_exp = jnp.exp(scores - highest)
        totals = jnp.sum(weights_exp, axis=-1, keepdims=True)
        chances_low = (weights_exp / totals).astype(jnp.bfloat16)
        mixed = jnp.einsum(
            "gtk,kgd->gtd", chances_low, value_part, preferred_element_type=jnp.float32
        )
        return (mixed, (highest + jnp.log(totals))[:, :, 0])

    mixed_all, logs_all = lax.map(one_group, jnp.arange(head_count // width_group, dtype=jnp.int32))
    mixed_all = mixed_all.reshape(head_count, block_size, head_dim).transpose(1, 0, 2)
    return (mixed_all, logs_all.reshape(head_count, block_size))


def dense_skip(query_block, key_rows, value_rows, span_number):
    block_size, head_count, head_dim = query_block.shape
    return (
        jnp.zeros((block_size, head_count, head_dim), jnp.float32),
        jnp.zeros((head_count, block_size), jnp.float32),
    )


def dense_back(query_block, grad_block, key_rows, value_rows, log_block, span_number):
    block_size, head_count, head_dim = query_block.shape
    slot_size = key_rows.shape[0]
    width_group = dense_width()
    scale = head_dim ** (-0.5)
    valid = jnp.arange(slot_size, dtype=jnp.int32) < span_number

    def one_group(number):
        offset = number * width_group
        query_part = lax.dynamic_slice_in_dim(query_block, offset, width_group, 1)
        grad_part = lax.dynamic_slice_in_dim(grad_block, offset, width_group, 1)
        key_part = lax.dynamic_slice_in_dim(key_rows, offset, width_group, 1)
        value_part = lax.dynamic_slice_in_dim(value_rows, offset, width_group, 1)
        scores = (
            jnp.einsum("tgd,kgd->gtk", query_part, key_part, preferred_element_type=jnp.float32)
            * scale
        )
        scores = jnp.where(valid[None, None, :], scores, negative)
        chances = jnp.exp(
            scores - lax.dynamic_slice_in_dim(log_block, offset, width_group, 0)[:, :, None]
        )
        grad_chances = jnp.einsum(
            "tgd,kgd->gtk", grad_part, value_part, preferred_element_type=jnp.float32
        )
        central = jnp.sum(chances * grad_chances, axis=-1, keepdims=True)
        grad_scores = (chances * (grad_chances - central)).astype(jnp.bfloat16)
        query_new = (
            jnp.einsum("gtk,kgd->gtd", grad_scores, key_part, preferred_element_type=jnp.float32)
            * scale
        )
        key_new = (
            jnp.einsum("gtk,tgd->gkd", grad_scores, query_part, preferred_element_type=jnp.float32)
            * scale
        )
        value_new = jnp.einsum(
            "gtk,tgd->gkd",
            chances.astype(jnp.bfloat16),
            grad_part,
            preferred_element_type=jnp.float32,
        )
        return (key_new, value_new, query_new)

    key_all, value_all, query_all = lax.map(
        one_group, jnp.arange(head_count // width_group, dtype=jnp.int32)
    )
    slot_terms = jnp.stack(
        [
            key_all.reshape(head_count, slot_size, head_dim),
            value_all.reshape(head_count, slot_size, head_dim),
        ]
    )
    return (slot_terms, query_all.reshape(head_count, block_size, head_dim).transpose(1, 0, 2))


def dense_pass(query_block, grad_block, key_rows, value_rows, log_block, span_number):
    block_size, head_count, head_dim = query_block.shape
    return (
        jnp.zeros((2, head_count, key_rows.shape[0], head_dim), jnp.float32),
        jnp.zeros(query_block.shape, jnp.float32),
    )


def return_grads(slot_grads):
    owned = lax.psum_scatter(
        slot_grads.astype(jnp.bfloat16), "seq", scatter_dimension=2, tiled=True
    ).astype(jnp.float32)
    pair_count, head_count, tok_count, head_dim = owned.shape
    return owned.transpose(2, 0, 1, 3).reshape(tok_count, pair_count * head_count * head_dim)


def flagged_place(flags):
    return jnp.sum(jnp.where(flags, jnp.arange(flags.shape[0], dtype=jnp.int32), 0))


def local(
    arriving_features,
    valid_extents,
    sampled_target_tiles,
    query_context_mapping,
    attention_outflow_weights,
    expansion_weights,
    contraction_weights,
    opening_scale_vector,
    opening_shift_vector,
    closing_scale_vector,
    closing_shift_vector,
    expansion_shift,
    contraction_shift,
    output_sensitivity,
):
    doc_count, tok_count, feature_breadth = arriving_features.shape
    head_count = sampled_target_tiles.shape[1]
    slot_blocks = sampled_target_tiles.shape[2]
    head_dim = feature_breadth // head_count
    slot_size = tok_count * lax.axis_size("seq")
    block_size = slot_size // slot_blocks
    local_blocks = tok_count // block_size
    first_block = lax.axis_index("seq") * local_blocks
    per_line_summation = doc_count * tok_count
    (
        full_inward,
        entire_outflow,
        full_expand,
        full_contract,
        overall_premultiplier,
        overall_shift_term,
        full_midscale,
        full_midshift,
        full_upshift,
        full_downshift,
    ) = (
        lax.all_gather(query_context_mapping, ("seq", "doc"), axis=0, tiled=True),
        lax.all_gather(attention_outflow_weights, ("seq", "doc"), axis=0, tiled=True),
        lax.all_gather(expansion_weights, ("seq", "doc"), axis=0, tiled=True),
        lax.all_gather(contraction_weights, ("seq", "doc"), axis=0, tiled=True),
        lax.all_gather(opening_scale_vector, ("seq", "doc"), axis=0, tiled=True),
        lax.all_gather(opening_shift_vector, ("seq", "doc"), axis=0, tiled=True),
        lax.all_gather(closing_scale_vector, ("seq", "doc"), axis=0, tiled=True),
        lax.all_gather(closing_shift_vector, ("seq", "doc"), axis=0, tiled=True),
        lax.all_gather(expansion_shift, ("seq", "doc"), axis=0, tiled=True),
        lax.all_gather(contraction_shift, ("seq", "doc"), axis=0, tiled=True),
    )
    shortcut_holder = arriving_features.reshape(per_line_summation, feature_breadth).astype(
        jnp.float32
    )
    opening_normalised, scaled_one, inverse_one = normalise_each_line(
        shortcut_holder,
        overall_premultiplier.astype(jnp.float32),
        overall_shift_term.astype(jnp.float32),
    )
    opening_normalised = opening_normalised.astype(jnp.bfloat16)
    projected = jnp.dot(opening_normalised, full_inward, preferred_element_type=jnp.float32).astype(
        jnp.bfloat16
    )
    query_local = projected[:, :feature_breadth].reshape(doc_count, tok_count, head_count, head_dim)
    pair_local = projected[:, feature_breadth:].reshape(doc_count, tok_count, 2 * feature_breadth)
    pair_full = lax.all_gather(pair_local, "seq", axis=1, tiled=True)

    def table_one(span_number, drawn_ordering):
        return candidate_table(span_number, drawn_ordering, first_block, local_blocks, block_size)

    clipped_all, keep_all, flags_all = jax.vmap(table_one)(valid_extents, sampled_target_tiles)
    query_heads = query_local.reshape(
        doc_count, local_blocks, block_size, head_count, head_dim
    ).transpose(0, 3, 1, 2, 4)
    block_flags = flags_all[:, :, None, None, None]

    def doc_forward(items):
        queries, pair_rows, clipped, keep = items
        key_sel = select_blocks(
            pair_rows[:, :feature_breadth].reshape(slot_size, head_count, head_dim),
            clipped,
            block_size,
        )
        value_sel = select_blocks(
            pair_rows[:, feature_breadth:].reshape(slot_size, head_count, head_dim),
            clipped,
            block_size,
        )
        mixed, log_sums = lax.map(
            sparse_forward,
            (split_heads(queries), split_heads(key_sel), split_heads(value_sel), split_heads(keep)),
        )
        return (join_heads(mixed), join_heads(log_sums))

    sparse_mixed, sparse_logs = lax.map(
        doc_forward, (query_heads, pair_full, clipped_all, keep_all)
    )
    mixed_rows = sparse_mixed.transpose(0, 2, 3, 1, 4)

    def doc_dense(items):
        queries, pair_rows, span_number, flags = items
        key_rows = pair_rows[:, :feature_breadth].reshape(slot_size, head_count, head_dim)
        value_rows = pair_rows[:, feature_breadth:].reshape(slot_size, head_count, head_dim)
        query_block = lax.dynamic_slice_in_dim(
            queries, flagged_place(flags) * block_size, block_size, 0
        )
        return lax.cond(
            jnp.any(flags),
            dense_forward,
            dense_skip,
            query_block,
            key_rows,
            value_rows,
            span_number,
        )

    dense_mixed, dense_logs = lax.map(doc_dense, (query_local, pair_full, valid_extents, flags_all))
    mixed_rows = jnp.where(block_flags, dense_mixed[:, None], mixed_rows)
    context_mixture = mixed_rows.reshape(per_line_summation, feature_breadth).astype(jnp.bfloat16)
    intermediate_state = shortcut_holder + jnp.dot(
        context_mixture, entire_outflow, preferred_element_type=jnp.float32
    )
    normed_two, scaled_two, inverse_two = normalise_each_line(
        intermediate_state, full_midscale.astype(jnp.float32), full_midshift.astype(jnp.float32)
    )
    normed_two = normed_two.astype(jnp.bfloat16)
    pre_act = jnp.dot(
        normed_two, full_expand, preferred_element_type=jnp.float32
    ) + full_upshift.astype(jnp.float32)
    activated = exact_gelu(pre_act).astype(jnp.bfloat16)
    final_rows = (
        intermediate_state
        + jnp.dot(activated, full_contract, preferred_element_type=jnp.float32)
        + full_downshift.astype(jnp.float32)
    )
    output = final_rows.astype(jnp.bfloat16).reshape(doc_count, tok_count, feature_breadth)
    back_inward, back_outward, back_expand, back_contract, back_prescale, back_midscale = (
        full_inward,
        entire_outflow,
        full_expand,
        full_contract,
        overall_premultiplier,
        full_midscale,
    )
    grad_out_rows = output_sensitivity.reshape(per_line_summation, feature_breadth)
    grad_out_wide = grad_out_rows.astype(jnp.float32)
    contract_grad = jnp.einsum(
        "rf,rd->fd", activated, grad_out_rows, preferred_element_type=jnp.float32
    )
    downshift_grad = jnp.sum(grad_out_wide, axis=0)
    grad_act = jnp.einsum(
        "rd,fd->rf", grad_out_rows, back_contract, preferred_element_type=jnp.float32
    )
    unused_value, gelu_back = jax.vjp(exact_gelu, pre_act)
    grad_pre = gelu_back(grad_act)[0].astype(jnp.bfloat16)
    expand_grad = jnp.einsum("rd,rf->df", normed_two, grad_pre, preferred_element_type=jnp.float32)
    upshift_grad = jnp.sum(grad_pre.astype(jnp.float32), axis=0)
    grad_norm_two = jnp.einsum(
        "rf,df->rd", grad_pre, back_expand, preferred_element_type=jnp.float32
    )
    middle_part, midscale_grad, midshift_grad = standardize_rows_pullback(
        grad_norm_two, scaled_two, inverse_two, back_midscale.astype(jnp.float32)
    )
    grad_middle = grad_out_wide + middle_part
    grad_branch = grad_middle.astype(jnp.bfloat16)
    outward_grad = jnp.einsum(
        "rd,re->de", context_mixture, grad_branch, preferred_element_type=jnp.float32
    )
    grad_attended = jnp.einsum(
        "re,de->rd", grad_branch, back_outward, preferred_element_type=jnp.float32
    ).astype(jnp.bfloat16)
    grad_attended = grad_attended.reshape(doc_count, tok_count, head_count, head_dim)
    grad_blocks = grad_attended.reshape(doc_count, local_blocks, block_size, head_count, head_dim)
    sparse_grads = jnp.where(block_flags, jnp.zeros_like(grad_blocks), grad_blocks).transpose(
        0, 3, 1, 2, 4
    )
    block_ids = jnp.arange(slot_blocks, dtype=jnp.int32)

    def sparse_back(queries, pair_rows, clipped, keep, log_sums, grad_part):
        key_rows = pair_rows[:, :feature_breadth].reshape(slot_size, head_count, head_dim)
        value_rows = pair_rows[:, feature_breadth:].reshape(slot_size, head_count, head_dim)
        key_sel = select_blocks(key_rows, clipped, block_size)
        value_sel = select_blocks(value_rows, clipped, block_size)
        grouped = (
            split_heads(queries),
            split_heads(key_sel),
            split_heads(value_sel),
            split_heads(keep),
            split_heads(log_sums),
            split_heads(grad_part),
        )
        query_term, key_term, value_term = lax.map(sparse_backward, grouped)
        query_term = join_heads(query_term)
        key_term = join_heads(key_term)
        value_term = join_heads(value_term)
        placing = (clipped[..., None] == block_ids).astype(jnp.float32)
        key_slot = jnp.einsum(
            "hlcn,hlcbd->hnbd",
            placing,
            key_term,
            precision=lax.Precision.HIGHEST,
            preferred_element_type=jnp.float32,
        )
        value_slot = jnp.einsum(
            "hlcn,hlcbd->hnbd",
            placing,
            value_term,
            precision=lax.Precision.HIGHEST,
            preferred_element_type=jnp.float32,
        )
        slot_grads = jnp.stack(
            [
                key_slot.reshape(head_count, slot_size, head_dim),
                value_slot.reshape(head_count, slot_size, head_dim),
            ]
        )
        return (query_term, slot_grads, key_rows, value_rows)

    def doc_backward(carry, items):
        (
            queries,
            pair_rows,
            clipped,
            keep,
            log_sums,
            grad_part,
            grad_rows,
            query_rows,
            dense_log,
            span_number,
            flags,
        ) = items
        query_term, slot_grads, key_rows, value_rows = sparse_back(
            queries, pair_rows, clipped, keep, log_sums, grad_part
        )
        start = flagged_place(flags) * block_size
        query_block = lax.dynamic_slice_in_dim(query_rows, start, block_size, 0)
        grad_block = lax.dynamic_slice_in_dim(grad_rows, start, block_size, 0)
        dense_slot, dense_term = lax.cond(
            jnp.any(flags),
            dense_back,
            dense_pass,
            query_block,
            grad_block,
            key_rows,
            value_rows,
            dense_log,
            span_number,
        )
        owned = return_grads(slot_grads + dense_slot)
        return (carry, (query_term, dense_term, owned))

    unused_carry, (sparse_query, dense_query, pair_grads) = lax.scan(
        doc_backward,
        jnp.zeros((), jnp.int32),
        (
            query_heads,
            pair_full,
            clipped_all,
            keep_all,
            sparse_logs,
            sparse_grads,
            grad_attended,
            query_local,
            dense_logs,
            valid_extents,
            flags_all,
        ),
    )
    query_grad = sparse_query.transpose(0, 2, 3, 1, 4) + jnp.where(
        block_flags, dense_query[:, None], 0.0
    )
    grad_projected = jnp.concatenate(
        [
            query_grad.reshape(per_line_summation, feature_breadth),
            pair_grads.reshape(per_line_summation, 2 * feature_breadth),
        ],
        axis=1,
    ).astype(jnp.bfloat16)
    inward_grad = jnp.einsum(
        "rd,re->de", opening_normalised, grad_projected, preferred_element_type=jnp.float32
    )
    grad_norm_one = jnp.einsum(
        "re,de->rd", grad_projected, back_inward, preferred_element_type=jnp.float32
    )
    incoming_slice, leading_gain_sensitivity, leading_offset_sensitivity = (
        standardize_rows_pullback(
            grad_norm_one, scaled_one, inverse_one, back_prescale.astype(jnp.float32)
        )
    )
    grad_inputs = (grad_middle + incoming_slice).reshape(doc_count, tok_count, feature_breadth)
    summed = (
        lax.psum_scatter(inward_grad, ("seq", "doc"), scatter_dimension=0, tiled=True),
        lax.psum_scatter(outward_grad, ("seq", "doc"), scatter_dimension=0, tiled=True),
        lax.psum_scatter(expand_grad, ("seq", "doc"), scatter_dimension=0, tiled=True),
        lax.psum_scatter(contract_grad, ("seq", "doc"), scatter_dimension=0, tiled=True),
        lax.psum_scatter(leading_gain_sensitivity, ("seq", "doc"), scatter_dimension=0, tiled=True),
        lax.psum_scatter(
            leading_offset_sensitivity, ("seq", "doc"), scatter_dimension=0, tiled=True
        ),
        lax.psum_scatter(midscale_grad, ("seq", "doc"), scatter_dimension=0, tiled=True),
        lax.psum_scatter(midshift_grad, ("seq", "doc"), scatter_dimension=0, tiled=True),
        lax.psum_scatter(upshift_grad, ("seq", "doc"), scatter_dimension=0, tiled=True),
        lax.psum_scatter(downshift_grad, ("seq", "doc"), scatter_dimension=0, tiled=True),
    )
    return (output, grad_inputs) + tuple(summed)


ROUTE = pl.DeviceIdType.MESH
NZ, NX, NY, NC = 4, 2, 2, 2
bf16, f32 = jnp.bfloat16, jnp.float32


def nn(left, right):
    return lax.dot_general(left, right, (((1,), (0,)), ((), ())), preferred_element_type=f32)


def nt(left, right):
    return lax.dot_general(left, right, (((1,), (1,)), ((), ())), preferred_element_type=f32)


def tn(left, right):
    return lax.dot_general(left, right, (((0,), (0,)), ((), ())), preferred_element_type=f32)


def loop(count, body):
    lax.fori_loop(0, count, body, 0)


class Net:
    def __init__(self, send_sems, recv_sems, here):
        self.send_sems, self.recv_sems, self.here = send_sems, recv_sems, here
        self.sent, self.taken = 0, 0
        self.open = []

    def slots(self, count):
        first = self.taken
        self.taken += count
        assert self.taken <= RECVS
        return first

    def copy(self, src, dst, device, slot, index):
        return pltpu.make_async_remote_copy(
            src_ref=src,
            dst_ref=dst,
            send_sem=self.send_sems.at[index],
            recv_sem=self.recv_sems.at[slot],
            device_id=device,
            device_id_type=ROUTE,
        )

    def series(self, count, describe, group=None):
        base = self.sent
        self.sent += count
        assert self.sent <= SENDS

        def start(i):
            src, dst, device, slot, is_self, made = describe(i)
            copy = self.copy(src, dst, device, slot, base + i)
            if is_self is None:
                if made is None:
                    copy.start()
                else:
                    pl.when(made)(copy.start)
            else:
                pl.when(jnp.logical_not(is_self))(copy.start)
                pl.when(is_self)(pltpu.make_async_copy(src, dst, self.recv_sems.at[slot]).start)

        def finish():
            for i in range(count):
                src, dst, device, slot, is_self, made = describe(i)
                copy = self.copy(src, dst, device, slot, base + i)
                if is_self is not None:
                    made = jnp.logical_not(is_self)
                if made is None:
                    copy.wait_send()
                else:
                    pl.when(made)(copy.wait_send)

        self.open.append((group, finish))
        return start

    def send(self, src, dst, device, slot, group=None, is_self=None, made=None):
        self.series(1, lambda i: (src, dst, device, slot, is_self, made), group)(0)

    def settle(self, group=None, everything=False):
        rest = []
        for name, finish in self.open:
            if everything or name == group:
                finish()
            else:
                rest.append((name, finish))
        self.open = rest

    def arrive(self, dst, slot):
        self.copy(dst, dst, self.here, slot, 0).wait_recv()


def row_stats(values):
    mean = jnp.mean(values, axis=-1, keepdims=True)
    centered = values - mean
    inverse = lax.rsqrt(jnp.mean(centered * centered, axis=-1, keepdims=True) + epsilon)
    return centered * inverse, inverse


def norm_pullback(grad, scaled, inverse, gain):
    wide = grad * gain
    first = jnp.mean(wide, axis=-1, keepdims=True)
    second = jnp.mean(wide * scaled, axis=-1, keepdims=True)
    return (wide - first - scaled * second) * inverse


def column_sum(values):
    return jnp.sum(values, axis=0, keepdims=True)


SCRATCH = dict(
    x_in=((2, 2, 64, 1024), bf16),
    dy_in=((2, 128, 1024), bf16),
    wq_in=((32, 3072), bf16),
    wo_in=((32, 1024), bf16),
    w1_in=((32, 4096), bf16),
    w2_in=((128, 1024), bf16),
    out=((2, 128, 1024), bf16),
    gx=((2, 128, 1024), f32),
    dwq_out=((32, 3072), f32),
    dwo=((32, 1024), f32),
    dw1=((32, 4096), f32),
    dw2_out=((128, 1024), f32),
    xr=((8, 2, 64, 1024), bf16),
    n1=((8, 128, 1024), bf16),
    aux=((64, 128), jnp.int32),
    aux2=((4, 16, 128), jnp.int32),
    table=((16, 16, 128), jnp.int32),
    bias=((16, 4, 1024), f32),
    sv=((4, 2, 2, 2, 8, 128), f32),
    vec=((8, 1024), f32),
    b1=((1, 1024), f32),
    wqs=((4, 32, 768), bf16),
    wq=((4, 2, 2, 2, 32, 768), bf16),
    wo=((4, 2, 2, 2, 32, 1024), bf16),
    w1s=((4, 32, 1024), bf16),
    w1=((4, 2, 2, 2, 32, 1024), bf16),
    w2=((4, 2, 128, 1024), bf16),
    qkv=((1024, 768), bf16),
    lse=((1024, 128), f32),
    at=((8, 128, 256), bf16),
    att=((2, 4, 128, 256), bf16),
    mid=((256, 1024), f32),
    nt2=((4, 256, 1024), bf16),
    dyx=((4, 256, 1024), bf16),
    act=((4, 256, 1024), bf16),
    gp=((4, 256, 1024), bf16),
    dw2=((4, 2, 128, 1024), bf16),
    own=((256, 1024), f32),
    gps=((4, 256, 1024), bf16),
    gpr=((2, 256, 1024), bf16),
    gpx=((256, 1024), bf16),
    ops=((4, 256, 1024), bf16),
    opr=((2, 256, 1024), bf16),
    opx=((256, 1024), bf16),
    gb=((256, 1024), bf16),
    gm=((256, 1024), f32),
    da=((2, 4, 128, 256), bf16),
    do=((8, 128, 256), bf16),
    dk=((1024, 128), f32),
    dv=((1024, 128), f32),
    dwq=((2, 4, 2, 2, 2, 32, 384), bf16),
    rgs=((8, 64, 1024), bf16),
    rgx=((4, 64, 1024), bf16),
    gnr=((2, 2, 64, 1024), bf16),
    r1y=((4, 2, 2, 32, 1024), bf16),
    r1z=((4, 2, 2, 32, 1024), bf16),
    r1v=((2, 2, 32, 1024), bf16),
    f1=((2, 2, 32, 1024), f32),
    f1b=((2, 2, 32, 1024), bf16),
    r1f=((4, 32, 1024), bf16),
    r2y=((4, 128, 1024), bf16),
    r2z=((4, 128, 1024), bf16),
    r2v=((128, 1024), bf16),
    ros=((4, 2, 2, 32, 1024), bf16),
    roa=((4, 32, 1024), bf16),
    rob=((4, 32, 1024), bf16),
    rof=((4, 32, 1024), bf16),
    roz=((4, 32, 1024), bf16),
    rov=((32, 1024), bf16),
    rqy=((2, 4, 2, 2, 32, 384), bf16),
    rqz=((2, 4, 2, 2, 32, 384), bf16),
    rqv=((2, 2, 2, 32, 384), bf16),
    fq=((2, 2, 32, 768), f32),
    fqb=((2, 2, 32, 768), bf16),
    rqf=((4, 32, 768), bf16),
    sg=((2, 8, 8, 128), f32),
    rsg=((2, 8, 8, 128), f32),
    sgt=((2, 8, 128), f32),
    rst=((2, 4, 8, 128), f32),
)
SENDS, RECVS = 256, 256
VMEM_BYTES = 63 * 2**20


def layer_kernel(
    x_arg, dy_arg, extent_in, tiles_in, wq_arg, wo_arg, w1_arg, w2_arg,
    gain_one, shift_one, gain_two, shift_two, shift_up, shift_down,
    out_arg, gx_arg, dwq_arg, dwo_arg, dw1_arg, dw2_arg, sg_ref,
    *rest,
):
    names = list(SCRATCH)
    R = types.SimpleNamespace(**dict(zip(names, rest[: len(names)])))
    send_sems, recv_sems, local_sems = rest[len(names):]
    x_in, dy_in, wq_in, wo_in, w1_in, w2_in = R.x_in, R.dy_in, R.wq_in, R.wo_in, R.w1_in, R.w2_in
    out_ref, gx_ref, dwq_ref, dwo_ref, dw1_ref, dw2_ref = R.out, R.gx, R.dwq_out, R.dwo, R.dw1, R.dw2_out
    arrivals = [
        pltpu.make_async_copy(src, dst, local_sems.at[k])
        for k, (src, dst) in enumerate(
            (
                (wq_arg, wq_in), (x_arg, x_in), (w1_arg, w1_in),
                (wo_arg, wo_in), (w2_arg, w2_in), (dy_arg, dy_in),
            )
        )
    ]
    for copy in arrivals:
        copy.start()
    leaving = [
        pltpu.make_async_copy(src, dst, local_sems.at[6 + k])
        for k, (src, dst) in enumerate(
            (
                (out_ref, out_arg), (gx_ref, gx_arg), (dwq_ref, dwq_arg),
                (dwo_ref, dwo_arg), (dw1_ref, dw1_arg), (dw2_ref, dw2_arg),
            )
        )
    ]
    s, d = lax.axis_index("seq"), lax.axis_index("doc")
    z, x, y, c = s // NX, s % NX, d // NC, d % NC
    g = 2 * x + c
    flip, xo, yo = 1 - c, 1 - x, 1 - y

    def at(zz, xx, yy, cc):
        return (zz * NX + xx, yy * NC + cc)

    here = (s, d)
    sib, xn, yn, cross = at(z, x, y, flip), at(z, xo, y, c), at(z, x, yo, c), at(z, xo, y, flip)
    group = ((x, flip, sib), (xo, c, xn), (xo, flip, cross))
    net = Net(send_sems, recv_sems, here)
    order = [z, z + 1 - 2 * (z // 2), (2 + 3 * z) % 5, 3 * (1 - z // 2)]
    middle = jnp.logical_or(z == 1, z == 2)

    barrier = pltpu.get_barrier_semaphore()

    def greet(step, _):
        other = (s * NC + c + step) % 16
        pl.semaphore_signal(
            barrier, inc=1, device_id=(other // NC, y * NC + other % NC), device_id_type=ROUTE
        )
        return 0

    lax.fori_loop(1, 16, greet, 0)
    for cc in (c, flip):
        pl.semaphore_signal(barrier, inc=1, device_id=at(z, x, yo, cc), device_id_type=ROUTE)
    for copy in arrivals:
        copy.wait()
    for h in range(4):
        for t in range(3):
            for pair in range(2):
                src = t * 1024 + h * 256 + pair * 128
                dst = pair * 384 + t * 128
                R.wqs[h, :, dst:dst + 128] = wq_in[:, src:src + 128]
    R.wq[z, x, y, c] = R.wqs[g]
    small = R.sv.at[z, x, y, c]
    small[...] = jnp.zeros((8, 128), f32)
    for k, vector in enumerate((gain_one, shift_one, gain_two, shift_two)):
        small[0:1, k * 32:(k + 1) * 32] = vector[...].astype(f32)
    small[1:2, 0:32] = shift_down[...].astype(f32)
    small[2:3, :] = shift_up[...].astype(f32)
    for h in range(4):
        for q in range(8):
            block = 8 * (q // 2) + 4 * (h // 2) + 2 * (q % 2) + h % 2
            R.w1s[h, :, q * 128:(q + 1) * 128] = w1_in[:, block * 128:(block + 1) * 128]
    R.w1[z, x, y, c] = R.w1s[g]
    R.wo[z, x, y, c] = wo_in[...]
    R.w2[z, y] = w2_in[...]
    R.dyx[g] = dy_in[...].reshape(256, 1024)
    R.sg[...] = jnp.zeros((2, 8, 8, 128), f32)
    has_table = c == z // 2

    for h in range(16):
        R.table[h, :, 0:3] = tiles_in[z % 2, h]
    R.table[:, :, 3:4] = jnp.full((16, 16, 1), extent_in[z % 2], jnp.int32)

    @pl.when(has_table)
    def table():
        R.aux[...] = R.table[pl.ds(4 * g, 4)].reshape(64, 128)

    pl.semaphore_wait(barrier, 17)

    def z_start(piece, base, name):
        for k in (1, 2):
            net.send(piece(z), piece(z), at(order[k], x, y, c), base + z, name)

    def z_take(piece, base, name, k):
        part = piece(order[k])
        net.arrive(part, base + order[k])
        if k != 2:
            net.send(part, part, at(order[2], x, y, c), base + order[k], name, made=middle)
        return part

    half = pl.ds(pl.multiple_of(c * 512, 512), 512)
    other_half = pl.ds(pl.multiple_of(flip * 512, 512), 512)
    xz = net.slots(4)
    for b in range(2):
        for ch in range(2):
            zt = 2 * c + b
            net.send(
                x_in.at[b, :, :, ch * 512:(ch + 1) * 512],
                R.xr.at[s, :, :, ch * 512:(ch + 1) * 512],
                at(zt, x, y, ch),
                xz + z,
                is_self=jnp.logical_and(zt == z, c == ch),
            )

    wqa = net.slots(4)
    for xx, cc, dev in group:
        net.send(R.wqs.at[2 * xx + cc], R.wq.at[z, x, y, c], dev, wqa + g)

    sv_s, sv_z, sv_x, sv_y = net.slots(1), net.slots(4), net.slots(1), net.slots(1)
    net.send(R.sv.at[z, x, y, c], R.sv.at[z, x, y, c], sib, sv_s)

    aux_s = net.slots(1)
    net.send(R.table.at[pl.ds(4 * (2 * x + flip), 4)], R.aux2, sib, aux_s, made=has_table)

    w1a = net.slots(4)
    for xx, cc, dev in group:
        net.send(R.w1s.at[2 * xx + cc], R.w1.at[z, x, y, c], dev, w1a + g)

    def wq_piece(zz):
        return R.wq.at[zz, :, y]

    def w1_piece(zz):
        return R.w1.at[zz, :, y]

    def w2_piece(zz):
        return R.w2.at[zz, y]

    def wo_piece(zz):
        return R.wo.at[zz, x, y, c]

    wqz, wqy, w1z, w1y = net.slots(4), net.slots(4), net.slots(4), net.slots(4)
    w2z, w2y, woz = net.slots(4), net.slots(4), net.slots(4)
    for xx, cc, dev in group:
        net.arrive(R.wq.at[z, xx, y, cc], wqa + 2 * xx + cc)
    z_start(wq_piece, wqz, "w")
    net.send(wq_piece(z), wq_piece(z), yn, wqy + 0, "w")
    net.arrive(R.sv.at[z, x, y, flip], sv_s)
    z_start(lambda zz: R.sv.at[zz, x, y], sv_z, None)
    for xx, cc, dev in group:
        net.arrive(R.w1.at[z, xx, y, cc], w1a + 2 * xx + cc)
    net.send(w1_piece(z), w1_piece(z), yn, w1y + 0, "w")

    xx_r, xs_a, xs_b = net.slots(4), net.slots(4), net.slots(4)
    for k in range(4):
        zt = order[k]
        part = R.xr.at[zt * 2 + x, :, :, half]
        net.arrive(part, xz + zt)
        net.send(part, part, xn, xx_r + k, "xr")
        net.send(part, part, sib, xs_a + k, "xr")
        if k:
            part = z_take(wq_piece, wqz, "w", k)
            net.send(part, part, yn, wqy + k, "w")
    z_start(wo_piece, woz, "w")
    z_start(w1_piece, w1z, "w")
    for k in (1, 2, 3):
        z_take(lambda zz: R.sv.at[zz, x, y], sv_z, None, k)
    net.send(R.sv.at[:, x, y], R.sv.at[:, x, y], xn, sv_x)
    for k in range(4):
        zt = order[k]
        part = R.xr.at[zt * 2 + xo, :, :, half]
        net.arrive(part, xx_r + k)
        net.send(part, part, sib, xs_b + k, "xr")
        if k == 0:
            net.arrive(R.sv.at[:, xo, y], sv_x)
            net.send(R.sv.at[:, :, y], R.sv.at[:, :, y], yn, sv_y)

    def group_gather(buf):
        own_s, far_x, far_s = net.slots(1), net.slots(1), net.slots(1)

        def begin():
            net.send(buf.at[g], buf.at[g], sib, own_s)
            net.send(buf.at[g], buf.at[g], xn, far_x)

        def step():
            net.arrive(buf.at[2 * xo + c], far_x)
            net.send(buf.at[2 * xo + c], buf.at[2 * xo + c], sib, far_s)

        def take(which):
            if which == 1:
                net.arrive(buf.at[2 * x + flip], own_s)
            if which == 3:
                net.arrive(buf.at[2 * xo + flip], far_s)

        return begin, step, take

    members = (g, 2 * x + flip, 2 * xo + c, 2 * xo + flip)
    dy_begin, dy_step, dy_take = group_gather(R.dyx)
    nt_begin, nt_step, nt_take = group_gather(R.nt2)

    @pl.when(jnp.logical_not(has_table))
    def table_here():
        net.arrive(R.aux2, aux_s)
        R.aux[...] = R.aux2[...].reshape(64, 128)

    for i in range(16):
        tiles = R.aux[i * 4:(i + 1) * 4, :]
        place = lax.broadcasted_iota(jnp.int32, (4, 1024), 1)
        block = place >> 6
        row = lax.broadcasted_iota(jnp.int32, (4, 1024), 0) + (i % 4) * 4
        extent = tiles[:, 3:4]
        last = (extent - 1) >> 6
        seen = jnp.abs(row - block) <= 1
        for k in range(3):
            seen = seen | (block == tiles[:, k:k + 1])
        seen = seen | (block == 0) | (block == last) | (row == 0) | (row == last)
        seen = seen & (place < extent)
        R.bias[i] = jnp.where(seen, 0.0, negative).astype(f32)

    net.arrive(R.sv.at[:, :, yo], sv_y)
    lane = lax.broadcasted_iota(jnp.int32, (1, 128), 1) >> 5
    for r in range(8):
        for k in range(5):
            total = jnp.zeros((1, 128), f32)
            for q in range(4):
                line = R.sv[r // 2, r % 2, q // 2, q % 2, k // 4:k // 4 + 1, :]
                shift = (32 * (q - k % 4)) % 128
                if shift:
                    line = pltpu.roll(line, shift, 1)
                total = jnp.where(lane == q, line, total)
            R.vec[k:k + 1, r * 128:(r + 1) * 128] = total
    for q in range(8):
        R.b1[:, q * 128:(q + 1) * 128] = R.sv[q // 2, x, q % 2, c, 2:3, :]

    def first_norm(zt):
        def rows(k, _):
            i = 2 * zt + k
            scaled, _inverse = row_stats(R.xr[i].reshape(128, 1024).astype(f32))
            R.n1[i] = (scaled * R.vec[0:1, :] + R.vec[1:2, :]).astype(bf16)
            return 0

        loop(2, rows)

    for k in range(4):
        zt = order[k]
        net.arrive(R.xr.at[zt * 2 + x, :, :, other_half], xs_a + k)
        net.arrive(R.xr.at[zt * 2 + xo, :, :, other_half], xs_b + k)
        first_norm(zt)
    for k in range(4):
        net.arrive(R.wq.at[order[k], :, yo], wqy + k)

    def project(step, _):
        rows = R.n1[pl.ds(2 * step, 2)].reshape(256, 1024)
        made = nn(rows, R.wq[...].reshape(1024, 768)).astype(bf16)
        where = pl.ds(pl.multiple_of(step * 256, 256), 256)
        eighth = jnp.asarray(0.125, bf16)
        R.qkv[where, :] = jnp.concatenate(
            [made[:, :128] * eighth, made[:, 128:384], made[:, 384:512] * eighth, made[:, 512:]], axis=1
        )
        return 0

    loop(4, project)

    low_lane = lax.broadcasted_iota(jnp.int32, (1, 128), 1) < 64

    def only(values, e):
        return jnp.where(low_lane if e == 0 else jnp.logical_not(low_lane), values, jnp.zeros_like(values))

    def pair_columns(pair):
        first = pair * 384
        return (
            slice(pair * 128, pair * 128 + 128),
            slice(first, first + 128),
            slice(first + 128, first + 256),
            slice(first + 256, first + 384),
        )

    at_r = net.slots(8)
    back_c = z // 2

    def at_copy(i):
        zt, xx = i // 2, i % 2
        mine = jnp.logical_and(jnp.logical_and(zt == z, xx == x), c == back_c)
        return R.at.at[i], R.att.at[z % 2, g], at(zt, xx, y, back_c), at_r + (z % 2) * 4 + g, mine, None

    at_start = net.series(8, at_copy)

    def attend_tile(step, _):
        t = (z + step) % NZ
        where = pl.ds(pl.multiple_of(t * 256, 256), 256)
        for pair in range(2):
            cols, qcols, kcols, vcols = pair_columns(pair)
            q = R.qkv[where, qcols]
            mixed = None
            for e in range(2):
                h = pair * 2 + e
                scores = nt(only(q, e), R.qkv[:, kcols])
                scores = (scores.reshape(4, 64, 1024) + R.bias[h * 4 + t][:, None, :]).reshape(256, 1024)
                top = jnp.max(scores, axis=-1, keepdims=True)
                grown = jnp.exp(scores - top)
                total = jnp.sum(grown, axis=-1, keepdims=True)
                low = (grown * (1.0 / total)).astype(bf16)
                R.lse[where, h:h + 1] = top + jnp.log(total)
                got = nn(low, R.qkv[:, vcols])
                mixed = got if e == 0 else jnp.where(low_lane, mixed, got)
            R.at[pl.ds(2 * t, 2), :, cols] = mixed.astype(bf16).reshape(2, 128, 128)
        at_start(2 * t)
        at_start(2 * t + 1)
        return 0

    def attend(low, high):
        lax.fori_loop(low, high, attend_tile, 0)

    ax, ay = (x + flip) % 2, (y + c) % 2
    bx, by = (x + c) % 2, (y + flip) % 2
    near, far = at(z, ax, ay, c), at(z, bx, by, c)
    wo_a, wo_b, wo_d, wo_s = net.slots(1), net.slots(1), net.slots(1), net.slots(1)

    def wo_column(xx, yy):
        return R.wo.at[:, xx, yy, c]

    def w1_step(k):
        part = z_take(w1_piece, w1z, "w", k)
        net.send(part, part, yn, w1y + k, "w")

    def w2_step(k):
        part = z_take(w2_piece, w2z, "w", k)
        net.send(part, part, yn, w2y + k, "w")

    for k in (1, 2, 3):
        z_take(wo_piece, woz, "w", k)
    net.send(wo_column(x, y), wo_column(x, y), near, wo_a, "w")
    net.send(wo_column(x, y), wo_column(x, y), far, wo_b, "w")
    attend(1, 2)
    net.arrive(wo_column(ax, ay), wo_a)
    net.send(wo_column(ax, ay), wo_column(ax, ay), far, wo_d, "w")
    w1_step(1)
    attend(2, 3)
    dy_begin()
    w1_step(2)
    attend(3, 4)
    w1_step(3)
    attend(4, 5)
    dy_step()
    net.arrive(wo_column(bx, by), wo_b)
    net.arrive(wo_column(xo, yo), wo_d)
    net.send(R.wo.at[:, :, :, c], R.wo.at[:, :, :, c], sib, wo_s, "w")
    net.arrive(R.wo.at[:, :, :, flip], wo_s)
    for b in range(2):
        for h in range(4):
            net.arrive(R.att.at[b, h], at_r + b * 4 + h)
    z_start(w2_piece, w2z, "w")
    net.send(w2_piece(z), w2_piece(z), yn, w2y + 0, "w")

    def outflow():
        for n in range(4):
            cols = slice(n * 256, n * 256 + 256)
            made = x_in[:, :, :, cols].reshape(256, 256).astype(f32)
            for h in range(4):
                made = made + nn(
                    R.att[:, h].reshape(256, 256),
                    R.wo[h, :, :, :, :, cols].reshape(256, 256),
                )
            R.mid[:, cols] = made
        for k in range(2):
            where = slice(k * 128, k * 128 + 128)
            scaled, _inverse = row_stats(R.mid[where, :])
            R.nt2[g, where, :] = (scaled * R.vec[2:3, :] + R.vec[3:4, :]).astype(bf16)

    outflow()
    nt_begin()

    for k in range(4):
        net.arrive(R.w1.at[order[k], :, yo], w1y + k)

    def widen_rows(which):
        def widen(j, _):
            where = pl.ds(pl.multiple_of(j * 256, 256), 256)
            pre = nn(R.nt2[which], R.w1[:, :, :, :, :, where].reshape(1024, 256))
            pre = pre + R.b1[:, where]
            share = 0.5 * (1.0 + lax.erf(pre * (2.0 ** -0.5)))
            R.act[which, :, where] = (pre * share).astype(bf16)
            slope = share + pre * (jnp.exp(-0.5 * pre * pre) * (1.0 / (2.0 * jnp.pi) ** 0.5))
            R.gp[which, :, where] = slope.astype(bf16)
            return 0

        loop(4, widen)

    widen_rows(members[0])
    w2_step(1)
    nt_take(1)
    widen_rows(members[1])
    nt_step()
    w2_step(2)
    widen_rows(members[2])
    nt_take(3)
    w2_step(3)
    widen_rows(members[3])
    dy_take(1)
    dy_take(3)

    def outer_two(j, _):
        where = pl.ds(pl.multiple_of(j * 256, 256), 256)
        made = tn(R.act[:, :, where].reshape(1024, 256), R.dyx[...].reshape(1024, 1024))
        R.dw2[j] = made.astype(bf16).reshape(2, 128, 1024)
        return 0

    loop(4, outer_two)

    def scatter(piece, away, landing_y, landing_z, landing_v, name):
        base_y, base_z, base_v = net.slots(4), net.slots(4), net.slots(1)

        def begin(ks=(3, 2, 1, 0)):
            for k in ks:
                net.send(away(order[k]), landing_y.at[order[k]], yn, base_y + k, name)

        def add(ref, other):
            ref[...] = (ref[...].astype(f32) + other[...].astype(f32)).astype(bf16)

        def take(k):
            net.arrive(landing_y.at[order[k]], base_y + k)
            add(piece(order[k]), landing_y.at[order[k]])

        def along(k):
            part = piece(order[k])
            if k == 3:
                net.send(part, landing_v, at(order[1], x, y, c), base_v, name, made=jnp.logical_not(middle))

                @pl.when(middle)
                def pass_on():
                    net.arrive(landing_v, base_v)
                    add(part, landing_v)

                net.send(part, landing_z.at[z], at(order[3], x, y, c), base_z + z, name, made=middle)
            else:
                net.send(part, landing_z.at[z], at(order[k], x, y, c), base_z + z, name)

        def final(out):
            out[...] = piece(z)[...].astype(f32)
            for k in (1, 2):
                net.arrive(landing_z.at[order[k]], base_z + order[k])
                out[...] += landing_z[order[k]].astype(f32)

            @pl.when(middle)
            def from_end():
                net.arrive(landing_z.at[order[3]], base_z + order[3])
                out[...] += landing_z[order[3]].astype(f32)

        return begin, take, along, final

    two_begin, two_take, two_along, two_final = scatter(
        lambda zz: R.dw2.at[zz, y], lambda zz: R.dw2.at[zz, yo], R.r2y, R.r2z, R.r2v, "s2"
    )

    for k in range(4):
        net.arrive(R.w2.at[order[k], yo], w2y + k)
    two_begin()

    def narrow_back_rows(which):
        def narrow_back(j, _):
            where = pl.ds(pl.multiple_of(j * 256, 256), 256)
            made = nt(R.dyx[which], R.w2[j].reshape(256, 1024)) * R.gp[which, :, where].astype(f32)
            R.gp[which, :, where] = made.astype(bf16)
            return 0

        loop(4, narrow_back)

    def group_reduce(product, sent, landing, landing_x, kept):
        slot_s, slot_x = net.slots(2), net.slots(1)
        for which, where in ((members[3], xo), (members[2], None), (members[1], x), (members[0], None)):
            if which is members[0]:
                product(which, kept)
            else:
                product(which, sent.at[which])
            if where is not None:
                net.send(sent.at[which], landing.at[where], sib, slot_s + where)
            elif which is members[2]:
                net.arrive(landing.at[xo], slot_s + xo)
                sent[which] = (sent[which].astype(f32) + landing[xo].astype(f32)).astype(bf16)
                net.send(sent.at[which], landing_x, xn, slot_x)

        def finish():
            net.arrive(landing.at[x], slot_s + x)
            net.arrive(landing_x, slot_x)

        return finish

    def grad_norm_part(which, out):
        narrow_back_rows(which)

        def back(n, _):
            made = nt(R.gp[which], R.w1[n].reshape(256, 1024))
            out[:, pl.ds(pl.multiple_of(n * 256, 256), 256)] = made.astype(out.dtype)
            return 0

        loop(4, back)

    gn_finish = group_reduce(grad_norm_part, R.gps, R.gpr, R.gpx, R.own)
    net.settle("w")

    def outer_one(n, _):
        left = R.nt2[:, :, pl.ds(pl.multiple_of(n * 256, 256), 256)].reshape(1024, 256)
        made = tn(left, R.gp[...].reshape(1024, 1024)).astype(bf16)
        R.w1[n] = made.reshape(2, 2, 2, 32, 1024)
        return 0

    loop(4, outer_one)
    one_begin, one_take, one_along, one_final = scatter(
        w1_piece, lambda zz: R.w1.at[zz, :, yo], R.r1y, R.r1z, R.r1v, "s1"
    )
    one_begin()

    gn_finish()
    sums = [jnp.zeros((1, 1024), f32) for _ in range(3)]

    def norm_two_back():
        for k in range(4):
            where = slice(k * 64, k * 64 + 64)
            grad = R.own[where, :] + R.gpr[x, where, :].astype(f32) + R.gpx[where, :].astype(f32)
            scaled, inverse = row_stats(R.mid[where, :])
            flow = dy_in[k // 2, (k % 2) * 64:(k % 2) * 64 + 64, :].astype(f32)
            sums[0] = sums[0] + column_sum(grad * scaled)
            sums[1] = sums[1] + column_sum(grad)
            sums[2] = sums[2] + column_sum(flow)
            total = flow + norm_pullback(grad, scaled, inverse, R.vec[2:3, :])
            R.gm[where, :] = total
            R.gb[where, :] = total.astype(bf16)

    norm_two_back()

    do_r = net.slots(8)

    def outflow_back(h, _):
        made = nt(R.gb[...], R.wo[h].reshape(256, 1024)).astype(bf16)
        R.da[:, h] = made.reshape(2, 128, 256)
        return 0

    loop(4, outflow_back)
    for b in range(2):
        for xx in (x, xo):
            for cc in (c, flip):
                zt = 2 * c + b
                net.send(
                    R.da.at[b, 2 * xx + cc],
                    R.do.at[s],
                    at(zt, xx, y, cc),
                    do_r + s,
                    is_self=jnp.logical_and(zt == z, jnp.logical_and(xx == x, cc == c)),
                )


    def outer_flow():
        for h in range(4):
            made = tn(R.att[:, h].reshape(256, 256), R.gb[...]).astype(bf16)
            R.wo[h] = made.reshape(2, 2, 2, 32, 1024)

    outer_flow()
    ros_s = net.slots(1)
    net.send(R.wo.at[:, :, :, flip], R.ros, sib, ros_s)

    def contract_part(which, out):
        def forth(n, _):
            cols = pl.ds(pl.multiple_of(n * 256, 256), 256)
            made = nn(R.act[which], R.w2[:, :, :, cols].reshape(1024, 256))
            out[:, cols] = made.astype(out.dtype)
            return 0

        loop(4, forth)

    out_finish = group_reduce(contract_part, R.ops, R.opr, R.opx, R.own)
    for k in (3, 2, 1, 0):
        two_take(k)
        if k:
            two_along(k)

    def note(which, row, line):
        for r in range(8):
            R.sg[which, r, row:row + 1, :] = line[:, r * 128:(r + 1) * 128]

    def small_begin(which):
        base = net.slots(8)
        for k in (3, 2, 1, 0):
            for xx in (xo, x):
                if k == 0 and xx is x:
                    continue
                zt = order[k]
                net.send(R.sg.at[which, zt * 2 + xx], R.rsg.at[which, s], at(zt, xx, y, c), base + s)
        return base

    def small_middle(which, base):
        total = R.sg[which, s]
        for k in (1, 2, 3, 0):
            for xx in (x, xo):
                if k == 0 and xx is x:
                    continue
                i = order[k] * 2 + xx
                net.arrive(R.rsg.at[which, i], base + i)
                total = total + R.rsg[which, i]
        R.sgt[which] = total
        slot = net.slots(4)
        for yy, cc in ((y, flip), (yo, c), (yo, flip)):
            net.send(R.sgt.at[which], R.rst.at[which, 2 * y + c], at(z, x, yy, cc), slot + 2 * y + c)
        return slot

    def small_end(which, slot):
        row = lax.broadcasted_iota(jnp.int32, (8, 128), 0)
        total = R.sgt[which]
        for yy, cc in ((y, flip), (yo, c), (yo, flip)):
            i = 2 * yy + cc
            net.arrive(R.rst.at[which, i], slot + i)
            got = R.rst[which, i]
            total = total + (got if cc is c else jnp.where(row < 5, got, 0.0))
        return total

    for k in range(3):
        note(0, 2 + k, sums[k])
    up = [jnp.zeros((1, 1024), f32)]

    def up_sum():
        for k in range(16):
            rows = slice((k % 4) * 64, (k % 4) * 64 + 64)
            up[0] = up[0] + column_sum(R.gp[k // 4, rows, :].astype(f32))

    up_sum()
    for q in range(8):
        R.sg[0, 2 * (q // 2) + x, 5 + q % 2:6 + q % 2, :] = up[0][:, q * 128:(q + 1) * 128]
    early = small_begin(0)

    def attend_back(pair):
        cols, qcols, kcols, vcols = pair_columns(pair)
        R.dk[...] = jnp.zeros((1024, 128), f32)
        R.dv[...] = jnp.zeros((1024, 128), f32)

        def tile(step, _):
            t = (z + step) % NZ
            where = pl.ds(pl.multiple_of(t * 256, 256), 256)
            two = pl.ds(2 * t, 2)
            if pair == 0:
                for k in range(2):
                    net.arrive(R.do.at[2 * t + k], do_r + 2 * t + k)
            q = R.qkv[where, qcols]
            grad = R.do[two, :, cols].reshape(256, 128)
            prod = grad.astype(f32) * R.at[two, :, cols].reshape(256, 128).astype(f32)
            query = None
            for e in range(2):
                h = pair * 2 + e
                qe, ge = only(q, e), only(grad, e)
                scores = nt(qe, R.qkv[:, kcols])
                scores = (scores.reshape(4, 64, 1024) + R.bias[h * 4 + t][:, None, :]).reshape(256, 1024)
                chances = jnp.exp(scores - R.lse[where, h:h + 1])
                central = jnp.sum(only(prod, e), axis=-1, keepdims=True)
                moved = nt(ge, R.qkv[:, vcols])
                back = (chances * (moved - central)).astype(bf16)
                R.dv[...] += tn(chances.astype(bf16), ge)
                R.dk[...] += tn(back, qe)
                got = nn(back, R.qkv[:, kcols])
                query = got if e == 0 else jnp.where(low_lane, query, got)
            R.qkv[where, qcols] = (query * 0.125).astype(bf16)
            return 0

        lax.fori_loop(0, 4, tile, 0)
        R.qkv[:, kcols] = R.dk[...].astype(bf16)
        R.qkv[:, vcols] = R.dv[...].astype(bf16)

    def outer_in_pair(pair):
        def outer_in(n, _):
            rows = pl.ds(pl.multiple_of(n * 256, 256), 256)
            made = tn(R.n1[:, :, rows].reshape(1024, 256), R.qkv[:, pair * 384:pair * 384 + 384])
            R.dwq[pair, n] = made.astype(bf16).reshape(2, 2, 2, 32, 384)
            return 0

        loop(4, outer_in)
        steps = scatter(
            lambda zz: R.dwq.at[pair, zz, :, y],
            lambda zz: R.dwq.at[pair, zz, :, yo],
            R.rqy.at[pair],
            R.rqz.at[pair],
            R.rqv.at[pair],
            None,
        )
        steps[0]()
        return steps

    attend_back(0)
    for k in (3, 2, 1, 0):
        one_take(k)
        if k:
            one_along(k)
    net.arrive(R.ros, ros_s)
    for k in range(4):
        R.wo[k, :, :, c] = (R.wo[k, :, :, c].astype(f32) + R.ros[k].astype(f32)).astype(bf16)
    roa_s, rob_s, rof_s, roz_s = net.slots(1), net.slots(1), net.slots(1), net.slots(4)
    net.send(wo_column(xo, yo), R.roa, far, roa_s)
    net.send(wo_column(bx, by), R.rob, far, rob_s)
    q0_begin, q0_take, q0_along, q0_final = outer_in_pair(0)
    early = small_middle(0, early)
    out_finish()
    for k in range(2):
        where = slice(k * 128, k * 128 + 128)
        total = R.mid[where, :] + R.own[where, :] + R.opr[x, where, :].astype(f32)
        out_ref[k] = (total + R.opx[where, :].astype(f32) + R.vec[4:5, :]).astype(bf16)
    leaving[0].start()
    attend_back(1)

    net.settle("xr")

    def unproject(step, _):
        t = (z + 1 + step) % NZ
        where = pl.ds(pl.multiple_of(t * 256, 256), 256)
        made = nt(R.qkv[where, :], R.wq[...].reshape(1024, 768)).astype(bf16)
        R.xr[pl.ds(2 * t, 2)] = made.reshape(2, 2, 64, 1024)
        gs_start(t)
        return 0

    rgs_s, rgx_s, gnr_s = net.slots(4), net.slots(4), net.slots(4)
    gs_start = net.series(
        4,
        lambda t: (
            R.xr.at[pl.ds(2 * t, 2), flip], R.rgs.at[pl.ds(2 * t, 2)], sib, rgs_s + t, None, None
        ),
    )
    loop(4, unproject)

    for k in (3, 2, 1, 0):
        q0_take(k)
        if k:
            q0_along(k)
    q1_begin, q1_take, q1_along, q1_final = outer_in_pair(1)
    for k in (3, 2, 1, 0):
        zt = order[k]
        i = zt * 2 + xo
        net.arrive(R.rgs.at[pl.ds(2 * zt, 2)], rgs_s + zt)
        R.xr[i, c] = (R.xr[i, c].astype(f32) + R.rgs[i].astype(f32)).astype(bf16)
        net.send(R.xr.at[i, c], R.rgx.at[zt], xn, rgx_s + k)
    net.arrive(R.roa, roa_s)
    part = wo_column(ax, ay)
    part[...] = (part[...].astype(f32) + R.roa[...].astype(f32)).astype(bf16)
    net.send(part, R.rof, near, rof_s)
    for k in (3, 2, 1, 0):
        zt = order[k]
        i = zt * 2 + x
        net.arrive(R.rgx.at[zt], rgx_s + k)
        R.xr[i, c] = (
            R.xr[i, c].astype(f32) + R.rgs[i].astype(f32) + R.rgx[zt].astype(f32)
        ).astype(bf16)
        net.send(
            R.xr.at[i, c],
            R.gnr.at[z % 2, c],
            at(zt, x, y, back_c),
            gnr_s + 2 * (z % 2) + c,
            is_self=jnp.logical_and(zt == z, c == back_c),
        )
    for k in (3, 2, 1, 0):
        q1_take(k)
        if k:
            q1_along(k)

    net.arrive(R.rob, rob_s)
    net.arrive(R.rof, rof_s)
    part = wo_column(x, y)
    part[...] = (part[...].astype(f32) + R.rob[...].astype(f32) + R.rof[...].astype(f32)).astype(bf16)
    for k in (1, 2, 3):
        net.send(wo_piece(order[k]), R.roz.at[z], at(order[k], x, y, c), roz_s + z)


    r1f_s, rqf_s = net.slots(4), net.slots(4)
    one_final(R.f1)
    R.f1b[...] = R.f1[...].astype(bf16)
    for xx, cc, dev in group:
        net.send(R.f1b.at[xx, cc], R.r1f.at[g], dev, r1f_s + g)
    R.r1f[g] = R.f1b[x, c]
    two_final(dw2_ref)
    leaving[5].start()
    sums = [jnp.zeros((1, 1024), f32) for _ in range(2)]
    for k in range(4):
        net.arrive(R.gnr.at[k // 2, k % 2], gnr_s + k)
        rows = slice((k % 2) * 64, (k % 2) * 64 + 64)
        grad = R.gnr[k // 2, k % 2].astype(f32)
        scaled, inverse = row_stats(x_in[k // 2, k % 2].astype(f32))
        sums[0] = sums[0] + column_sum(grad * scaled)
        sums[1] = sums[1] + column_sum(grad)
        gx_ref[k // 2, rows, :] = R.gm[k * 64:(k + 1) * 64, :] + norm_pullback(
            grad, scaled, inverse, R.vec[0:1, :]
        )
    leaving[1].start()
    for k in range(2):
        note(1, k, sums[k])
    late = small_begin(1)

    q0_final(R.fq.at[:, :, :, 0:384])
    q1_final(R.fq.at[:, :, :, 384:768])
    R.fqb[...] = R.fq[...].astype(bf16)
    for xx, cc, dev in group:
        net.send(R.fqb.at[xx, cc], R.rqf.at[g], dev, rqf_s + g)
    R.rqf[g] = R.fqb[x, c]
    late = small_middle(1, late)

    dwo_ref[...] = wo_piece(z)[...].astype(f32)
    for k in (1, 2, 3):
        net.arrive(R.roz.at[order[k]], roz_s + order[k])
        dwo_ref[...] += R.roz[order[k]].astype(f32)
    leaving[3].start()
    for xx, cc, dev in group:
        net.arrive(R.r1f.at[2 * xx + cc], r1f_s + 2 * xx + cc)
    for h in range(4):
        for q in range(8):
            block = 8 * (q // 2) + 4 * (h // 2) + 2 * (q % 2) + h % 2
            dw1_ref[:, block * 128:(block + 1) * 128] = R.r1f[h, :, q * 128:(q + 1) * 128].astype(f32)
    leaving[4].start()
    for xx, cc, dev in group:
        net.arrive(R.rqf.at[2 * xx + cc], rqf_s + 2 * xx + cc)
    for h in range(4):
        for t in range(3):
            for pair in range(2):
                src = pair * 384 + t * 128
                dst = t * 1024 + h * 256 + pair * 128
                dwq_ref[:, dst:dst + 128] = R.rqf[h, :, src:src + 128].astype(f32)
    leaving[2].start()
    total = small_end(0, early) + small_end(1, late)
    sg_ref[...] = pltpu.roll(total, (128 - 32 * d) % 128, 1)
    sg_ref[5:6, :] = jnp.where(y == 0, total[5:6, :], total[6:7, :])
    net.settle(everything=True)
    for copy in leaving:
        copy.wait()


def local_fused(
    arriving_features,
    valid_extents,
    sampled_target_tiles,
    query_context_mapping,
    attention_outflow_weights,
    expansion_weights,
    contraction_weights,
    opening_scale_vector,
    opening_shift_vector,
    closing_scale_vector,
    closing_shift_vector,
    expansion_shift,
    contraction_shift,
    output_sensitivity,
):
    shapes = (
        (arriving_features.shape, bf16),
        (arriving_features.shape, f32),
        (query_context_mapping.shape, f32),
        (attention_outflow_weights.shape, f32),
        (expansion_weights.shape, f32),
        (contraction_weights.shape, f32),
        ((8, 128), f32),
    )
    whole = pl.BlockSpec(memory_space=pltpu.VMEM)
    scalars = pl.BlockSpec(memory_space=pltpu.SMEM)
    place = pl.BlockSpec(memory_space=pl.ANY)
    made = pl.pallas_call(
        layer_kernel,
        name="layer",
        out_shape=[jax.ShapeDtypeStruct(a, b) for a, b in shapes],
        in_specs=[place] * 2 + [scalars, whole] + [place] * 4 + [whole] * 6,
        out_specs=[place] * 6 + [whole],
        scratch_shapes=[pltpu.VMEM(a, b) for a, b in SCRATCH.values()]
        + [
            pltpu.SemaphoreType.DMA((SENDS,)),
            pltpu.SemaphoreType.DMA((RECVS,)),
            pltpu.SemaphoreType.DMA((12,)),
        ],
        compiler_params=pltpu.CompilerParams(
            collective_id=0, has_side_effects=True, vmem_limit_bytes=VMEM_BYTES
        ),
    )(
        arriving_features.reshape(2, 2, 64, 1024),
        output_sensitivity,
        valid_extents,
        sampled_target_tiles,
        query_context_mapping,
        attention_outflow_weights,
        expansion_weights,
        contraction_weights,
        opening_scale_vector.reshape(1, 32),
        opening_shift_vector.reshape(1, 32),
        closing_scale_vector.reshape(1, 32),
        closing_shift_vector.reshape(1, 32),
        expansion_shift.reshape(1, 128),
        contraction_shift.reshape(1, 32),
    )
    rows = ((1, 32), (1, 32), (1, 32), (1, 32), (1, 128), (1, 32))
    done = pl.pallas_call(
        leave_kernel,
        name="leave",
        out_shape=[jax.ShapeDtypeStruct(a, b) for a, b in shapes[:6]]
        + [jax.ShapeDtypeStruct(a, f32) for a in rows],
        in_specs=[place] * 6 + [whole],
        out_specs=[place] * 6 + [whole] * 6,
        scratch_shapes=[pltpu.VMEM(a, b) for a, b in shapes[:6]]
        + [pltpu.SemaphoreType.DMA((6,)), pltpu.SemaphoreType.DMA((6,))],
    )(*made)
    return tuple(done[:6]) + tuple(line.reshape(-1) for line in done[6:])


def leave_kernel(*refs):
    large, small, out, rows, held = refs[:6], refs[6], refs[7:13], refs[13:19], refs[19:25]
    come, go = refs[25:]
    for k in range(6):
        pltpu.make_async_copy(large[k], held[k], come.at[k]).start()
    for k, row in enumerate((0, 1, 2, 3, 5, 4)):
        rows[k][...] = small[row:row + 1, :rows[k].shape[1]]
    for k in range(6):
        pltpu.make_async_copy(large[k], held[k], come.at[k]).wait()
        pltpu.make_async_copy(held[k], out[k], go.at[k]).start()
    for k in range(6):
        pltpu.make_async_copy(held[k], out[k], go.at[k]).wait()


def fits_fused(mesh, arguments):
    features, tiles, expand = arguments[0], arguments[2], arguments[5]
    return (
        dict(mesh.shape) == {"seq": 8, "doc": 4}
        and features.shape == (8, 1024, 1024)
        and tiles.shape == (8, 16, 16, 3)
        and expand.shape == (1024, 4096)
    )


def solution(mesh):
    in_specs = (
        P("doc", "seq", None),
        P("doc"),
        P("doc", None, None, None),
        P(("seq", "doc"), None),
        P(("seq", "doc"), None),
        P(("seq", "doc"), None),
        P(("seq", "doc"), None),
        P(("seq", "doc")),
        P(("seq", "doc")),
        P(("seq", "doc")),
        P(("seq", "doc")),
        P(("seq", "doc")),
        P(("seq", "doc")),
        P("doc", "seq", None),
    )
    out_specs = (
        P("doc", "seq", None),
        P("doc", "seq", None),
        P(("seq", "doc"), None),
        P(("seq", "doc"), None),
        P(("seq", "doc"), None),
        P(("seq", "doc"), None),
        P(("seq", "doc")),
        P(("seq", "doc")),
        P(("seq", "doc")),
        P(("seq", "doc")),
        P(("seq", "doc")),
        P(("seq", "doc")),
    )

    def run(*arguments):
        body = local_fused if fits_fused(mesh, arguments) else local
        mapped = jax.shard_map(
            body, mesh=mesh, in_specs=in_specs, out_specs=out_specs, check_vma=False
        )
        return mapped(*arguments)

    return run
```

```python
import types

import jax
import jax.numpy as jnp
from jax import lax
from jax.experimental import pallas as pl
from jax.experimental.pallas import tpu as pltpu
from jax.sharding import PartitionSpec as P

group_heads = 4
epsilon = 1e-05
negative = -1e30


def normalise_each_line(values, scaling, shifting):
    centered = values - jnp.mean(values, axis=-1, keepdims=True)
    inverse = lax.rsqrt(jnp.mean(centered * centered, axis=-1, keepdims=True) + epsilon)
    scaled = centered * inverse
    return (scaled * scaling + shifting, scaled, inverse)


def standardize_rows_pullback(grad_norm, scaled, inverse, scaling):
    grad_scaled = grad_norm * scaling
    centred_grad = grad_scaled - jnp.mean(grad_scaled, axis=-1, keepdims=True)
    centred_grad = centred_grad - scaled * jnp.mean(grad_scaled * scaled, axis=-1, keepdims=True)
    return (centred_grad * inverse, jnp.sum(grad_norm * scaled, axis=0), jnp.sum(grad_norm, axis=0))


def exact_gelu(values):
    return jax.nn.gelu(values, approximate=False)


def dense_width():
    return 8


def split_heads(array):
    return array.reshape((array.shape[0] // group_heads, group_heads) + array.shape[1:])


def join_heads(array):
    return array.reshape((array.shape[0] * array.shape[1],) + array.shape[2:])


def candidate_table(span_number, drawn_ordering, first_block, local_blocks, block_size):
    head_count, slot_blocks, random_count = drawn_ordering.shape
    query_blocks = first_block + jnp.arange(local_blocks, dtype=jnp.int32)
    last_block = (span_number - 1) // block_size
    picked = lax.dynamic_slice_in_dim(drawn_ordering, first_block, local_blocks, 1)
    window = jnp.stack([query_blocks - 1, query_blocks, query_blocks + 1], axis=1)
    edges = jnp.stack(
        [jnp.zeros_like(query_blocks), jnp.zeros_like(query_blocks) + last_block], axis=1
    )
    window = jnp.broadcast_to(window[None], (head_count, local_blocks, 3))
    edges = jnp.broadcast_to(edges[None], (head_count, local_blocks, 2))
    candidates = jnp.concatenate([window, picked, edges], axis=2)
    candidate_count = candidates.shape[2]
    inside = (candidates >= 0) & (candidates < slot_blocks)
    earlier = jnp.arange(candidate_count)[:, None] > jnp.arange(candidate_count)[None, :]
    repeated = jnp.any((candidates[:, :, :, None] == candidates[:, :, None, :]) & earlier, axis=3)
    usable = inside & jnp.logical_not(repeated)
    clipped = jnp.clip(candidates, 0, slot_blocks - 1)
    places = clipped[:, :, :, None] * block_size + jnp.arange(block_size, dtype=jnp.int32)
    keep = usable[:, :, :, None] & (places < span_number)
    flags = (query_blocks == 0) | (query_blocks == last_block)
    return (clipped, keep, flags)


def select_blocks(rows, clipped, block_size):
    slot_size, head_count, head_dim = rows.shape
    shaped = rows.reshape(slot_size // block_size, block_size, head_count, head_dim)
    head_index = jnp.arange(head_count, dtype=jnp.int32)[:, None, None]
    return shaped[clipped, :, head_index, :]


def sparse_forward(parts):
    query_group, key_group, value_group, keep_group = parts
    scale = query_group.shape[-1] ** (-0.5)
    scores = (
        jnp.einsum("hitd,hickd->hitck", query_group, key_group, preferred_element_type=jnp.float32)
        * scale
    )
    scores = jnp.where(keep_group[:, :, None], scores, negative)
    shape = scores.shape
    flat = scores.reshape(shape[0], shape[1], shape[2], shape[3] * shape[4])
    highest = jnp.max(flat, axis=-1, keepdims=True)
    weights_exp = jnp.exp(flat - highest)
    totals = jnp.sum(weights_exp, axis=-1, keepdims=True)
    chances_low = (weights_exp / totals).astype(jnp.bfloat16).reshape(shape)
    mixed = jnp.einsum(
        "hitck,hickd->hitd", chances_low, value_group, preferred_element_type=jnp.float32
    )
    return (mixed, (highest + jnp.log(totals))[..., 0])


def sparse_backward(parts):
    query_group, key_group, value_group, keep_group, log_group, grad_group = parts
    scale = query_group.shape[-1] ** (-0.5)
    scores = (
        jnp.einsum("hitd,hickd->hitck", query_group, key_group, preferred_element_type=jnp.float32)
        * scale
    )
    scores = jnp.where(keep_group[:, :, None], scores, negative)
    chances = jnp.exp(scores - log_group[..., None, None])
    grad_chances = jnp.einsum(
        "hitd,hickd->hitck", grad_group, value_group, preferred_element_type=jnp.float32
    )
    central = jnp.sum(chances * grad_chances, axis=(3, 4), keepdims=True)
    grad_scores = (chances * (grad_chances - central)).astype(jnp.bfloat16)
    query_term = (
        jnp.einsum("hitck,hickd->hitd", grad_scores, key_group, preferred_element_type=jnp.float32)
        * scale
    )
    key_term = (
        jnp.einsum(
            "hitck,hitd->hickd", grad_scores, query_group, preferred_element_type=jnp.float32
        )
        * scale
    )
    value_term = jnp.einsum(
        "hitck,hitd->hickd",
        chances.astype(jnp.bfloat16),
        grad_group,
        preferred_element_type=jnp.float32,
    )
    return (query_term, key_term, value_term)


def dense_forward(query_block, key_rows, value_rows, span_number):
    block_size, head_count, head_dim = query_block.shape
    width_group = dense_width()
    scale = head_dim ** (-0.5)
    valid = jnp.arange(key_rows.shape[0], dtype=jnp.int32) < span_number

    def one_group(number):
        offset = number * width_group
        query_part = lax.dynamic_slice_in_dim(query_block, offset, width_group, 1)
        key_part = lax.dynamic_slice_in_dim(key_rows, offset, width_group, 1)
        value_part = lax.dynamic_slice_in_dim(value_rows, offset, width_group, 1)
        scores = (
            jnp.einsum("tgd,kgd->gtk", query_part, key_part, preferred_element_type=jnp.float32)
            * scale
        )
        scores = jnp.where(valid[None, None, :], scores, negative)
        highest = jnp.max(scores, axis=-1, keepdims=True)
        weights_exp = jnp.exp(scores - highest)
        totals = jnp.sum(weights_exp, axis=-1, keepdims=True)
        chances_low = (weights_exp / totals).astype(jnp.bfloat16)
        mixed = jnp.einsum(
            "gtk,kgd->gtd", chances_low, value_part, preferred_element_type=jnp.float32
        )
        return (mixed, (highest + jnp.log(totals))[:, :, 0])

    mixed_all, logs_all = lax.map(one_group, jnp.arange(head_count // width_group, dtype=jnp.int32))
    mixed_all = mixed_all.reshape(head_count, block_size, head_dim).transpose(1, 0, 2)
    return (mixed_all, logs_all.reshape(head_count, block_size))


def dense_skip(query_block, key_rows, value_rows, span_number):
    block_size, head_count, head_dim = query_block.shape
    return (
        jnp.zeros((block_size, head_count, head_dim), jnp.float32),
        jnp.zeros((head_count, block_size), jnp.float32),
    )


def dense_back(query_block, grad_block, key_rows, value_rows, log_block, span_number):
    block_size, head_count, head_dim = query_block.shape
    slot_size = key_rows.shape[0]
    width_group = dense_width()
    scale = head_dim ** (-0.5)
    valid = jnp.arange(slot_size, dtype=jnp.int32) < span_number

    def one_group(number):
        offset = number * width_group
        query_part = lax.dynamic_slice_in_dim(query_block, offset, width_group, 1)
        grad_part = lax.dynamic_slice_in_dim(grad_block, offset, width_group, 1)
        key_part = lax.dynamic_slice_in_dim(key_rows, offset, width_group, 1)
        value_part = lax.dynamic_slice_in_dim(value_rows, offset, width_group, 1)
        scores = (
            jnp.einsum("tgd,kgd->gtk", query_part, key_part, preferred_element_type=jnp.float32)
            * scale
        )
        scores = jnp.where(valid[None, None, :], scores, negative)
        chances = jnp.exp(
            scores - lax.dynamic_slice_in_dim(log_block, offset, width_group, 0)[:, :, None]
        )
        grad_chances = jnp.einsum(
            "tgd,kgd->gtk", grad_part, value_part, preferred_element_type=jnp.float32
        )
        central = jnp.sum(chances * grad_chances, axis=-1, keepdims=True)
        grad_scores = (chances * (grad_chances - central)).astype(jnp.bfloat16)
        query_new = (
            jnp.einsum("gtk,kgd->gtd", grad_scores, key_part, preferred_element_type=jnp.float32)
            * scale
        )
        key_new = (
            jnp.einsum("gtk,tgd->gkd", grad_scores, query_part, preferred_element_type=jnp.float32)
            * scale
        )
        value_new = jnp.einsum(
            "gtk,tgd->gkd",
            chances.astype(jnp.bfloat16),
            grad_part,
            preferred_element_type=jnp.float32,
        )
        return (key_new, value_new, query_new)

    key_all, value_all, query_all = lax.map(
        one_group, jnp.arange(head_count // width_group, dtype=jnp.int32)
    )
    slot_terms = jnp.stack(
        [
            key_all.reshape(head_count, slot_size, head_dim),
            value_all.reshape(head_count, slot_size, head_dim),
        ]
    )
    return (slot_terms, query_all.reshape(head_count, block_size, head_dim).transpose(1, 0, 2))


def dense_pass(query_block, grad_block, key_rows, value_rows, log_block, span_number):
    block_size, head_count, head_dim = query_block.shape
    return (
        jnp.zeros((2, head_count, key_rows.shape[0], head_dim), jnp.float32),
        jnp.zeros(query_block.shape, jnp.float32),
    )


def return_grads(slot_grads):
    owned = lax.psum_scatter(
        slot_grads.astype(jnp.bfloat16), "seq", scatter_dimension=2, tiled=True
    ).astype(jnp.float32)
    pair_count, head_count, tok_count, head_dim = owned.shape
    return owned.transpose(2, 0, 1, 3).reshape(tok_count, pair_count * head_count * head_dim)


def flagged_place(flags):
    return jnp.sum(jnp.where(flags, jnp.arange(flags.shape[0], dtype=jnp.int32), 0))


def local(
    arriving_features,
    valid_extents,
    sampled_target_tiles,
    query_context_mapping,
    attention_outflow_weights,
    expansion_weights,
    contraction_weights,
    opening_scale_vector,
    opening_shift_vector,
    closing_scale_vector,
    closing_shift_vector,
    expansion_shift,
    contraction_shift,
    output_sensitivity,
):
    doc_count, tok_count, feature_breadth = arriving_features.shape
    head_count = sampled_target_tiles.shape[1]
    slot_blocks = sampled_target_tiles.shape[2]
    head_dim = feature_breadth // head_count
    slot_size = tok_count * lax.axis_size("seq")
    block_size = slot_size // slot_blocks
    local_blocks = tok_count // block_size
    first_block = lax.axis_index("seq") * local_blocks
    per_line_summation = doc_count * tok_count
    (
        full_inward,
        entire_outflow,
        full_expand,
        full_contract,
        overall_premultiplier,
        overall_shift_term,
        full_midscale,
        full_midshift,
        full_upshift,
        full_downshift,
    ) = (
        lax.all_gather(query_context_mapping, ("seq", "doc"), axis=0, tiled=True),
        lax.all_gather(attention_outflow_weights, ("seq", "doc"), axis=0, tiled=True),
        lax.all_gather(expansion_weights, ("seq", "doc"), axis=0, tiled=True),
        lax.all_gather(contraction_weights, ("seq", "doc"), axis=0, tiled=True),
        lax.all_gather(opening_scale_vector, ("seq", "doc"), axis=0, tiled=True),
        lax.all_gather(opening_shift_vector, ("seq", "doc"), axis=0, tiled=True),
        lax.all_gather(closing_scale_vector, ("seq", "doc"), axis=0, tiled=True),
        lax.all_gather(closing_shift_vector, ("seq", "doc"), axis=0, tiled=True),
        lax.all_gather(expansion_shift, ("seq", "doc"), axis=0, tiled=True),
        lax.all_gather(contraction_shift, ("seq", "doc"), axis=0, tiled=True),
    )
    shortcut_holder = arriving_features.reshape(per_line_summation, feature_breadth).astype(
        jnp.float32
    )
    opening_normalised, scaled_one, inverse_one = normalise_each_line(
        shortcut_holder,
        overall_premultiplier.astype(jnp.float32),
        overall_shift_term.astype(jnp.float32),
    )
    opening_normalised = opening_normalised.astype(jnp.bfloat16)
    projected = jnp.dot(opening_normalised, full_inward, preferred_element_type=jnp.float32).astype(
        jnp.bfloat16
    )
    query_local = projected[:, :feature_breadth].reshape(doc_count, tok_count, head_count, head_dim)
    pair_local = projected[:, feature_breadth:].reshape(doc_count, tok_count, 2 * feature_breadth)
    pair_full = lax.all_gather(pair_local, "seq", axis=1, tiled=True)

    def table_one(span_number, drawn_ordering):
        return candidate_table(span_number, drawn_ordering, first_block, local_blocks, block_size)

    clipped_all, keep_all, flags_all = jax.vmap(table_one)(valid_extents, sampled_target_tiles)
    query_heads = query_local.reshape(
        doc_count, local_blocks, block_size, head_count, head_dim
    ).transpose(0, 3, 1, 2, 4)
    block_flags = flags_all[:, :, None, None, None]

    def doc_forward(items):
        queries, pair_rows, clipped, keep = items
        key_sel = select_blocks(
            pair_rows[:, :feature_breadth].reshape(slot_size, head_count, head_dim),
            clipped,
            block_size,
        )
        value_sel = select_blocks(
            pair_rows[:, feature_breadth:].reshape(slot_size, head_count, head_dim),
            clipped,
            block_size,
        )
        mixed, log_sums = lax.map(
            sparse_forward,
            (split_heads(queries), split_heads(key_sel), split_heads(value_sel), split_heads(keep)),
        )
        return (join_heads(mixed), join_heads(log_sums))

    sparse_mixed, sparse_logs = lax.map(
        doc_forward, (query_heads, pair_full, clipped_all, keep_all)
    )
    mixed_rows = sparse_mixed.transpose(0, 2, 3, 1, 4)

    def doc_dense(items):
        queries, pair_rows, span_number, flags = items
        key_rows = pair_rows[:, :feature_breadth].reshape(slot_size, head_count, head_dim)
        value_rows = pair_rows[:, feature_breadth:].reshape(slot_size, head_count, head_dim)
        query_block = lax.dynamic_slice_in_dim(
            queries, flagged_place(flags) * block_size, block_size, 0
        )
        return lax.cond(
            jnp.any(flags),
            dense_forward,
            dense_skip,
            query_block,
            key_rows,
            value_rows,
            span_number,
        )

    dense_mixed, dense_logs = lax.map(doc_dense, (query_local, pair_full, valid_extents, flags_all))
    mixed_rows = jnp.where(block_flags, dense_mixed[:, None], mixed_rows)
    context_mixture = mixed_rows.reshape(per_line_summation, feature_breadth).astype(jnp.bfloat16)
    intermediate_state = shortcut_holder + jnp.dot(
        context_mixture, entire_outflow, preferred_element_type=jnp.float32
    )
    normed_two, scaled_two, inverse_two = normalise_each_line(
        intermediate_state, full_midscale.astype(jnp.float32), full_midshift.astype(jnp.float32)
    )
    normed_two = normed_two.astype(jnp.bfloat16)
    pre_act = jnp.dot(
        normed_two, full_expand, preferred_element_type=jnp.float32
    ) + full_upshift.astype(jnp.float32)
    activated = exact_gelu(pre_act).astype(jnp.bfloat16)
    final_rows = (
        intermediate_state
        + jnp.dot(activated, full_contract, preferred_element_type=jnp.float32)
        + full_downshift.astype(jnp.float32)
    )
    output = final_rows.astype(jnp.bfloat16).reshape(doc_count, tok_count, feature_breadth)
    back_inward, back_outward, back_expand, back_contract, back_prescale, back_midscale = (
        full_inward,
        entire_outflow,
        full_expand,
        full_contract,
        overall_premultiplier,
        full_midscale,
    )
    grad_out_rows = output_sensitivity.reshape(per_line_summation, feature_breadth)
    grad_out_wide = grad_out_rows.astype(jnp.float32)
    contract_grad = jnp.einsum(
        "rf,rd->fd", activated, grad_out_rows, preferred_element_type=jnp.float32
    )
    downshift_grad = jnp.sum(grad_out_wide, axis=0)
    grad_act = jnp.einsum(
        "rd,fd->rf", grad_out_rows, back_contract, preferred_element_type=jnp.float32
    )
    unused_value, gelu_back = jax.vjp(exact_gelu, pre_act)
    grad_pre = gelu_back(grad_act)[0].astype(jnp.bfloat16)
    expand_grad = jnp.einsum("rd,rf->df", normed_two, grad_pre, preferred_element_type=jnp.float32)
    upshift_grad = jnp.sum(grad_pre.astype(jnp.float32), axis=0)
    grad_norm_two = jnp.einsum(
        "rf,df->rd", grad_pre, back_expand, preferred_element_type=jnp.float32
    )
    middle_part, midscale_grad, midshift_grad = standardize_rows_pullback(
        grad_norm_two, scaled_two, inverse_two, back_midscale.astype(jnp.float32)
    )
    grad_middle = grad_out_wide + middle_part
    grad_branch = grad_middle.astype(jnp.bfloat16)
    outward_grad = jnp.einsum(
        "rd,re->de", context_mixture, grad_branch, preferred_element_type=jnp.float32
    )
    grad_attended = jnp.einsum(
        "re,de->rd", grad_branch, back_outward, preferred_element_type=jnp.float32
    ).astype(jnp.bfloat16)
    grad_attended = grad_attended.reshape(doc_count, tok_count, head_count, head_dim)
    grad_blocks = grad_attended.reshape(doc_count, local_blocks, block_size, head_count, head_dim)
    sparse_grads = jnp.where(block_flags, jnp.zeros_like(grad_blocks), grad_blocks).transpose(
        0, 3, 1, 2, 4
    )
    block_ids = jnp.arange(slot_blocks, dtype=jnp.int32)

    def sparse_back(queries, pair_rows, clipped, keep, log_sums, grad_part):
        key_rows = pair_rows[:, :feature_breadth].reshape(slot_size, head_count, head_dim)
        value_rows = pair_rows[:, feature_breadth:].reshape(slot_size, head_count, head_dim)
        key_sel = select_blocks(key_rows, clipped, block_size)
        value_sel = select_blocks(value_rows, clipped, block_size)
        grouped = (
            split_heads(queries),
            split_heads(key_sel),
            split_heads(value_sel),
            split_heads(keep),
            split_heads(log_sums),
            split_heads(grad_part),
        )
        query_term, key_term, value_term = lax.map(sparse_backward, grouped)
        query_term = join_heads(query_term)
        key_term = join_heads(key_term)
        value_term = join_heads(value_term)
        placing = (clipped[..., None] == block_ids).astype(jnp.float32)
        key_slot = jnp.einsum(
            "hlcn,hlcbd->hnbd",
            placing,
            key_term,
            precision=lax.Precision.HIGHEST,
            preferred_element_type=jnp.float32,
        )
        value_slot = jnp.einsum(
            "hlcn,hlcbd->hnbd",
            placing,
            value_term,
            precision=lax.Precision.HIGHEST,
            preferred_element_type=jnp.float32,
        )
        slot_grads = jnp.stack(
            [
                key_slot.reshape(head_count, slot_size, head_dim),
                value_slot.reshape(head_count, slot_size, head_dim),
            ]
        )
        return (query_term, slot_grads, key_rows, value_rows)

    def doc_backward(carry, items):
        (
            queries,
            pair_rows,
            clipped,
            keep,
            log_sums,
            grad_part,
            grad_rows,
            query_rows,
            dense_log,
            span_number,
            flags,
        ) = items
        query_term, slot_grads, key_rows, value_rows = sparse_back(
            queries, pair_rows, clipped, keep, log_sums, grad_part
        )
        start = flagged_place(flags) * block_size
        query_block = lax.dynamic_slice_in_dim(query_rows, start, block_size, 0)
        grad_block = lax.dynamic_slice_in_dim(grad_rows, start, block_size, 0)
        dense_slot, dense_term = lax.cond(
            jnp.any(flags),
            dense_back,
            dense_pass,
            query_block,
            grad_block,
            key_rows,
            value_rows,
            dense_log,
            span_number,
        )
        owned = return_grads(slot_grads + dense_slot)
        return (carry, (query_term, dense_term, owned))

    unused_carry, (sparse_query, dense_query, pair_grads) = lax.scan(
        doc_backward,
        jnp.zeros((), jnp.int32),
        (
            query_heads,
            pair_full,
            clipped_all,
            keep_all,
            sparse_logs,
            sparse_grads,
            grad_attended,
            query_local,
            dense_logs,
            valid_extents,
            flags_all,
        ),
    )
    query_grad = sparse_query.transpose(0, 2, 3, 1, 4) + jnp.where(
        block_flags, dense_query[:, None], 0.0
    )
    grad_projected = jnp.concatenate(
        [
            query_grad.reshape(per_line_summation, feature_breadth),
            pair_grads.reshape(per_line_summation, 2 * feature_breadth),
        ],
        axis=1,
    ).astype(jnp.bfloat16)
    inward_grad = jnp.einsum(
        "rd,re->de", opening_normalised, grad_projected, preferred_element_type=jnp.float32
    )
    grad_norm_one = jnp.einsum(
        "re,de->rd", grad_projected, back_inward, preferred_element_type=jnp.float32
    )
    incoming_slice, leading_gain_sensitivity, leading_offset_sensitivity = (
        standardize_rows_pullback(
            grad_norm_one, scaled_one, inverse_one, back_prescale.astype(jnp.float32)
        )
    )
    grad_inputs = (grad_middle + incoming_slice).reshape(doc_count, tok_count, feature_breadth)
    summed = (
        lax.psum_scatter(inward_grad, ("seq", "doc"), scatter_dimension=0, tiled=True),
        lax.psum_scatter(outward_grad, ("seq", "doc"), scatter_dimension=0, tiled=True),
        lax.psum_scatter(expand_grad, ("seq", "doc"), scatter_dimension=0, tiled=True),
        lax.psum_scatter(contract_grad, ("seq", "doc"), scatter_dimension=0, tiled=True),
        lax.psum_scatter(leading_gain_sensitivity, ("seq", "doc"), scatter_dimension=0, tiled=True),
        lax.psum_scatter(
            leading_offset_sensitivity, ("seq", "doc"), scatter_dimension=0, tiled=True
        ),
        lax.psum_scatter(midscale_grad, ("seq", "doc"), scatter_dimension=0, tiled=True),
        lax.psum_scatter(midshift_grad, ("seq", "doc"), scatter_dimension=0, tiled=True),
        lax.psum_scatter(upshift_grad, ("seq", "doc"), scatter_dimension=0, tiled=True),
        lax.psum_scatter(downshift_grad, ("seq", "doc"), scatter_dimension=0, tiled=True),
    )
    return (output, grad_inputs) + tuple(summed)


ROUTE = pl.DeviceIdType.MESH
NZ, NX, NY, NC = 4, 2, 2, 2
bf16, f32 = jnp.bfloat16, jnp.float32


def nn(left, right):
    return lax.dot_general(left, right, (((1,), (0,)), ((), ())), preferred_element_type=f32)


def nt(left, right):
    return lax.dot_general(left, right, (((1,), (1,)), ((), ())), preferred_element_type=f32)


def tn(left, right):
    return lax.dot_general(left, right, (((0,), (0,)), ((), ())), preferred_element_type=f32)


def loop(count, body):
    lax.fori_loop(0, count, body, 0)


class Net:
    def __init__(self, send_sems, recv_sems, here):
        self.send_sems, self.recv_sems, self.here = send_sems, recv_sems, here
        self.sent, self.taken = 0, 0
        self.open = []

    def slots(self, count):
        first = self.taken
        self.taken += count
        assert self.taken <= RECVS
        return first

    def copy(self, src, dst, device, slot, index):
        return pltpu.make_async_remote_copy(
            src_ref=src,
            dst_ref=dst,
            send_sem=self.send_sems.at[index],
            recv_sem=self.recv_sems.at[slot],
            device_id=device,
            device_id_type=ROUTE,
        )

    def series(self, count, describe, group=None):
        base = self.sent
        self.sent += count
        assert self.sent <= SENDS

        def start(i):
            src, dst, device, slot, is_self, made = describe(i)
            copy = self.copy(src, dst, device, slot, base + i)
            if is_self is None:
                if made is None:
                    copy.start()
                else:
                    pl.when(made)(copy.start)
            else:
                pl.when(jnp.logical_not(is_self))(copy.start)
                pl.when(is_self)(pltpu.make_async_copy(src, dst, self.recv_sems.at[slot]).start)

        def finish():
            for i in range(count):
                src, dst, device, slot, is_self, made = describe(i)
                copy = self.copy(src, dst, device, slot, base + i)
                if is_self is not None:
                    made = jnp.logical_not(is_self)
                if made is None:
                    copy.wait_send()
                else:
                    pl.when(made)(copy.wait_send)

        self.open.append((group, finish))
        return start

    def send(self, src, dst, device, slot, group=None, is_self=None, made=None):
        self.series(1, lambda i: (src, dst, device, slot, is_self, made), group)(0)

    def settle(self, group=None, everything=False):
        rest = []
        for name, finish in self.open:
            if everything or name == group:
                finish()
            else:
                rest.append((name, finish))
        self.open = rest

    def arrive(self, dst, slot):
        self.copy(dst, dst, self.here, slot, 0).wait_recv()


def row_stats(values):
    mean = jnp.mean(values, axis=-1, keepdims=True)
    centered = values - mean
    inverse = lax.rsqrt(jnp.mean(centered * centered, axis=-1, keepdims=True) + epsilon)
    return centered * inverse, inverse


def norm_pullback(grad, scaled, inverse, gain):
    wide = grad * gain
    first = jnp.mean(wide, axis=-1, keepdims=True)
    second = jnp.mean(wide * scaled, axis=-1, keepdims=True)
    return (wide - first - scaled * second) * inverse


def column_sum(values):
    return jnp.sum(values, axis=0, keepdims=True)


SCRATCH = dict(
    x_in=((2, 2, 64, 1024), bf16),
    dy_in=((2, 128, 1024), bf16),
    wq_in=((32, 3072), bf16),
    wo_in=((32, 1024), bf16),
    w1_in=((32, 4096), bf16),
    w2_in=((128, 1024), bf16),
    out=((2, 128, 1024), bf16),
    gx=((2, 128, 1024), f32),
    dwq_out=((32, 3072), f32),
    dwo=((32, 1024), f32),
    dw1=((32, 4096), f32),
    dw2_out=((128, 1024), f32),
    xr=((8, 2, 64, 1024), bf16),
    n1=((8, 128, 1024), bf16),
    aux=((64, 128), jnp.int32),
    aux2=((4, 16, 128), jnp.int32),
    table=((16, 16, 128), jnp.int32),
    bias=((16, 4, 1024), f32),
    sv=((4, 2, 2, 2, 8, 128), f32),
    vec=((8, 1024), f32),
    b1=((1, 1024), f32),
    wqs=((4, 32, 768), bf16),
    wq=((4, 2, 2, 2, 32, 768), bf16),
    wo=((4, 2, 2, 2, 32, 1024), bf16),
    w1s=((4, 32, 1024), bf16),
    w1=((4, 2, 2, 2, 32, 1024), bf16),
    w2=((4, 2, 128, 1024), bf16),
    qkv=((1024, 768), bf16),
    lse=((1024, 128), f32),
    at=((8, 128, 256), bf16),
    att=((2, 4, 128, 256), bf16),
    mid=((256, 1024), f32),
    nt2=((4, 256, 1024), bf16),
    dyx=((4, 256, 1024), bf16),
    act=((4, 256, 1024), bf16),
    gp=((4, 256, 1024), bf16),
    dw2=((4, 2, 128, 1024), bf16),
    own=((256, 1024), f32),
    gps=((4, 256, 1024), bf16),
    gpr=((2, 256, 1024), bf16),
    gpx=((256, 1024), bf16),
    ops=((4, 256, 1024), bf16),
    opr=((2, 256, 1024), bf16),
    opx=((256, 1024), bf16),
    gb=((256, 1024), bf16),
    gm=((256, 1024), f32),
    da=((2, 4, 128, 256), bf16),
    do=((8, 128, 256), bf16),
    dk=((1024, 128), f32),
    dv=((1024, 128), f32),
    dwq=((2, 4, 2, 2, 2, 32, 384), bf16),
    rgs=((8, 64, 1024), bf16),
    rgx=((4, 64, 1024), bf16),
    gnr=((2, 2, 64, 1024), bf16),
    r1y=((4, 2, 2, 32, 1024), bf16),
    r1z=((4, 2, 2, 32, 1024), bf16),
    r1v=((2, 2, 32, 1024), bf16),
    f1=((2, 2, 32, 1024), f32),
    f1b=((2, 2, 32, 1024), bf16),
    r1f=((4, 32, 1024), bf16),
    r2y=((4, 128, 1024), bf16),
    r2z=((4, 128, 1024), bf16),
    r2v=((128, 1024), bf16),
    ros=((4, 2, 2, 32, 1024), bf16),
    roa=((4, 32, 1024), bf16),
    rob=((4, 32, 1024), bf16),
    rof=((4, 32, 1024), bf16),
    roz=((4, 32, 1024), bf16),
    rov=((32, 1024), bf16),
    rqy=((2, 4, 2, 2, 32, 384), bf16),
    rqz=((2, 4, 2, 2, 32, 384), bf16),
    rqv=((2, 2, 2, 32, 384), bf16),
    fq=((2, 2, 32, 768), f32),
    fqb=((2, 2, 32, 768), bf16),
    rqf=((4, 32, 768), bf16),
    sg=((2, 8, 8, 128), f32),
    rsg=((2, 8, 8, 128), f32),
    sgt=((2, 8, 128), f32),
    rst=((2, 4, 8, 128), f32),
)
SENDS, RECVS = 256, 256
VMEM_BYTES = 63 * 2**20


def layer_kernel(
    x_arg, dy_arg, extent_in, tiles_in, wq_arg, wo_arg, w1_arg, w2_arg,
    gain_one, shift_one, gain_two, shift_two, shift_up, shift_down,
    out_arg, gx_arg, dwq_arg, dwo_arg, dw1_arg, dw2_arg, sg_ref,
    *rest,
):
    names = list(SCRATCH)
    R = types.SimpleNamespace(**dict(zip(names, rest[: len(names)])))
    send_sems, recv_sems, local_sems = rest[len(names):]
    x_in, dy_in, wq_in, wo_in, w1_in, w2_in = R.x_in, R.dy_in, R.wq_in, R.wo_in, R.w1_in, R.w2_in
    out_ref, gx_ref, dwq_ref, dwo_ref, dw1_ref, dw2_ref = R.out, R.gx, R.dwq_out, R.dwo, R.dw1, R.dw2_out
    arrivals = [
        pltpu.make_async_copy(src, dst, local_sems.at[k])
        for k, (src, dst) in enumerate(
            (
                (wq_arg, wq_in), (x_arg, x_in), (w1_arg, w1_in),
                (wo_arg, wo_in), (w2_arg, w2_in), (dy_arg, dy_in),
            )
        )
    ]
    for copy in arrivals:
        copy.start()
    leaving = [
        pltpu.make_async_copy(src, dst, local_sems.at[6 + k])
        for k, (src, dst) in enumerate(
            (
                (out_ref, out_arg), (gx_ref, gx_arg), (dwq_ref, dwq_arg),
                (dwo_ref, dwo_arg), (dw1_ref, dw1_arg), (dw2_ref, dw2_arg),
            )
        )
    ]
    s, d = lax.axis_index("seq"), lax.axis_index("doc")
    z, x, y, c = s // NX, s % NX, d // NC, d % NC
    g = 2 * x + c
    flip, xo, yo = 1 - c, 1 - x, 1 - y

    def at(zz, xx, yy, cc):
        return (zz * NX + xx, yy * NC + cc)

    here = (s, d)
    sib, xn, yn, cross = at(z, x, y, flip), at(z, xo, y, c), at(z, x, yo, c), at(z, xo, y, flip)
    group = ((x, flip, sib), (xo, c, xn), (xo, flip, cross))
    net = Net(send_sems, recv_sems, here)
    order = [z, z + 1 - 2 * (z // 2), (2 + 3 * z) % 5, 3 * (1 - z // 2)]
    middle = jnp.logical_or(z == 1, z == 2)

    barrier = pltpu.get_barrier_semaphore()

    def greet(step, _):
        other = (s * NC + c + step) % 16
        pl.semaphore_signal(
            barrier, inc=1, device_id=(other // NC, y * NC + other % NC), device_id_type=ROUTE
        )
        return 0

    lax.fori_loop(1, 16, greet, 0)
    for cc in (c, flip):
        pl.semaphore_signal(barrier, inc=1, device_id=at(z, x, yo, cc), device_id_type=ROUTE)
    for copy in arrivals:
        copy.wait()
    for h in range(4):
        for t in range(3):
            for pair in range(2):
                src = t * 1024 + h * 256 + pair * 128
                dst = pair * 384 + t * 128
                R.wqs[h, :, dst:dst + 128] = wq_in[:, src:src + 128]
    R.wq[z, x, y, c] = R.wqs[g]
    small = R.sv.at[z, x, y, c]
    small[...] = jnp.zeros((8, 128), f32)
    for k, vector in enumerate((gain_one, shift_one, gain_two, shift_two)):
        small[0:1, k * 32:(k + 1) * 32] = vector[...].astype(f32)
    small[1:2, 0:32] = shift_down[...].astype(f32)
    small[2:3, :] = shift_up[...].astype(f32)
    for h in range(4):
        for q in range(8):
            block = 8 * (q // 2) + 4 * (h // 2) + 2 * (q % 2) + h % 2
            R.w1s[h, :, q * 128:(q + 1) * 128] = w1_in[:, block * 128:(block + 1) * 128]
    R.w1[z, x, y, c] = R.w1s[g]
    R.wo[z, x, y, c] = wo_in[...]
    R.w2[z, y] = w2_in[...]
    R.dyx[g] = dy_in[...].reshape(256, 1024)
    R.sg[...] = jnp.zeros((2, 8, 8, 128), f32)
    has_table = c == z // 2

    for h in range(16):
        R.table[h, :, 0:3] = tiles_in[z % 2, h]
    R.table[:, :, 3:4] = jnp.full((16, 16, 1), extent_in[z % 2], jnp.int32)

    @pl.when(has_table)
    def table():
        R.aux[...] = R.table[pl.ds(4 * g, 4)].reshape(64, 128)

    pl.semaphore_wait(barrier, 17)

    def z_start(piece, base, name):
        for k in (1, 2):
            net.send(piece(z), piece(z), at(order[k], x, y, c), base + z, name)

    def z_take(piece, base, name, k):
        part = piece(order[k])
        net.arrive(part, base + order[k])
        if k != 2:
            net.send(part, part, at(order[2], x, y, c), base + order[k], name, made=middle)
        return part

    half = pl.ds(pl.multiple_of(c * 512, 512), 512)
    other_half = pl.ds(pl.multiple_of(flip * 512, 512), 512)
    xz = net.slots(4)
    for b in range(2):
        for ch in range(2):
            zt = 2 * c + b
            net.send(
                x_in.at[b, :, :, ch * 512:(ch + 1) * 512],
                R.xr.at[s, :, :, ch * 512:(ch + 1) * 512],
                at(zt, x, y, ch),
                xz + z,
                is_self=jnp.logical_and(zt == z, c == ch),
            )

    wqa = net.slots(4)
    for xx, cc, dev in group:
        net.send(R.wqs.at[2 * xx + cc], R.wq.at[z, x, y, c], dev, wqa + g)

    sv_s, sv_z, sv_x, sv_y = net.slots(1), net.slots(4), net.slots(1), net.slots(1)
    net.send(R.sv.at[z, x, y, c], R.sv.at[z, x, y, c], sib, sv_s)

    aux_s = net.slots(1)
    net.send(R.table.at[pl.ds(4 * (2 * x + flip), 4)], R.aux2, sib, aux_s, made=has_table)

    w1a = net.slots(4)
    for xx, cc, dev in group:
        net.send(R.w1s.at[2 * xx + cc], R.w1.at[z, x, y, c], dev, w1a + g)

    def wq_piece(zz):
        return R.wq.at[zz, :, y]

    def w1_piece(zz):
        return R.w1.at[zz, :, y]

    def w2_piece(zz):
        return R.w2.at[zz, y]

    def wo_piece(zz):
        return R.wo.at[zz, x, y, c]

    wqz, wqy, w1z, w1y = net.slots(4), net.slots(4), net.slots(4), net.slots(4)
    w2z, w2y, woz = net.slots(4), net.slots(4), net.slots(4)
    for xx, cc, dev in group:
        net.arrive(R.wq.at[z, xx, y, cc], wqa + 2 * xx + cc)
    z_start(wq_piece, wqz, "w")
    net.send(wq_piece(z), wq_piece(z), yn, wqy + 0, "w")
    net.arrive(R.sv.at[z, x, y, flip], sv_s)
    z_start(lambda zz: R.sv.at[zz, x, y], sv_z, None)
    for xx, cc, dev in group:
        net.arrive(R.w1.at[z, xx, y, cc], w1a + 2 * xx + cc)
    net.send(w1_piece(z), w1_piece(z), yn, w1y + 0, "w")

    xx_r, xs_a, xs_b = net.slots(4), net.slots(4), net.slots(4)
    for k in range(4):
        zt = order[k]
        part = R.xr.at[zt * 2 + x, :, :, half]
        net.arrive(part, xz + zt)
        net.send(part, part, xn, xx_r + k, "xr")
        net.send(part, part, sib, xs_a + k, "xr")
        if k:
            part = z_take(wq_piece, wqz, "w", k)
            net.send(part, part, yn, wqy + k, "w")
    z_start(wo_piece, woz, "w")
    z_start(w1_piece, w1z, "w")
    for k in (1, 2, 3):
        z_take(lambda zz: R.sv.at[zz, x, y], sv_z, None, k)
    net.send(R.sv.at[:, x, y], R.sv.at[:, x, y], xn, sv_x)
    for k in range(4):
        zt = order[k]
        part = R.xr.at[zt * 2 + xo, :, :, half]
        net.arrive(part, xx_r + k)
        net.send(part, part, sib, xs_b + k, "xr")
        if k == 0:
            net.arrive(R.sv.at[:, xo, y], sv_x)
            net.send(R.sv.at[:, :, y], R.sv.at[:, :, y], yn, sv_y)

    def group_gather(buf):
        own_s, far_x, far_s = net.slots(1), net.slots(1), net.slots(1)

        def begin():
            net.send(buf.at[g], buf.at[g], sib, own_s)
            net.send(buf.at[g], buf.at[g], xn, far_x)

        def step():
            net.arrive(buf.at[2 * xo + c], far_x)
            net.send(buf.at[2 * xo + c], buf.at[2 * xo + c], sib, far_s)

        def take(which):
            if which == 1:
                net.arrive(buf.at[2 * x + flip], own_s)
            if which == 3:
                net.arrive(buf.at[2 * xo + flip], far_s)

        return begin, step, take

    members = (g, 2 * x + flip, 2 * xo + c, 2 * xo + flip)
    dy_begin, dy_step, dy_take = group_gather(R.dyx)
    nt_begin, nt_step, nt_take = group_gather(R.nt2)

    @pl.when(jnp.logical_not(has_table))
    def table_here():
        net.arrive(R.aux2, aux_s)
        R.aux[...] = R.aux2[...].reshape(64, 128)

    for i in range(16):
        tiles = R.aux[i * 4:(i + 1) * 4, :]
        place = lax.broadcasted_iota(jnp.int32, (4, 1024), 1)
        block = place >> 6
        row = lax.broadcasted_iota(jnp.int32, (4, 1024), 0) + (i % 4) * 4
        extent = tiles[:, 3:4]
        last = (extent - 1) >> 6
        seen = jnp.abs(row - block) <= 1
        for k in range(3):
            seen = seen | (block == tiles[:, k:k + 1])
        seen = seen | (block == 0) | (block == last) | (row == 0) | (row == last)
        seen = seen & (place < extent)
        R.bias[i] = jnp.where(seen, 0.0, negative).astype(f32)

    net.arrive(R.sv.at[:, :, yo], sv_y)
    lane = lax.broadcasted_iota(jnp.int32, (1, 128), 1) >> 5
    for r in range(8):
        for k in range(5):
            total = jnp.zeros((1, 128), f32)
            for q in range(4):
                line = R.sv[r // 2, r % 2, q // 2, q % 2, k // 4:k // 4 + 1, :]
                shift = (32 * (q - k % 4)) % 128
                if shift:
                    line = pltpu.roll(line, shift, 1)
                total = jnp.where(lane == q, line, total)
            R.vec[k:k + 1, r * 128:(r + 1) * 128] = total
    for q in range(8):
        R.b1[:, q * 128:(q + 1) * 128] = R.sv[q // 2, x, q % 2, c, 2:3, :]

    def first_norm(zt):
        def rows(k, _):
            i = 2 * zt + k
            scaled, _inverse = row_stats(R.xr[i].reshape(128, 1024).astype(f32))
            R.n1[i] = (scaled * R.vec[0:1, :] + R.vec[1:2, :]).astype(bf16)
            return 0

        loop(2, rows)

    for k in range(4):
        zt = order[k]
        net.arrive(R.xr.at[zt * 2 + x, :, :, other_half], xs_a + k)
        net.arrive(R.xr.at[zt * 2 + xo, :, :, other_half], xs_b + k)
        first_norm(zt)
    for k in range(4):
        net.arrive(R.wq.at[order[k], :, yo], wqy + k)

    def project(step, _):
        rows = R.n1[pl.ds(2 * step, 2)].reshape(256, 1024)
        made = nn(rows, R.wq[...].reshape(1024, 768)).astype(bf16)
        where = pl.ds(pl.multiple_of(step * 256, 256), 256)
        eighth = jnp.asarray(0.125, bf16)
        R.qkv[where, :] = jnp.concatenate(
            [made[:, :128] * eighth, made[:, 128:384], made[:, 384:512] * eighth, made[:, 512:]], axis=1
        )
        return 0

    loop(4, project)

    low_lane = lax.broadcasted_iota(jnp.int32, (1, 128), 1) < 64

    def only(values, e):
        return jnp.where(low_lane if e == 0 else jnp.logical_not(low_lane), values, jnp.zeros_like(values))

    def pair_columns(pair):
        first = pair * 384
        return (
            slice(pair * 128, pair * 128 + 128),
            slice(first, first + 128),
            slice(first + 128, first + 256),
            slice(first + 256, first + 384),
        )

    at_r = net.slots(8)
    back_c = z // 2

    def at_copy(i):
        zt, xx = i // 2, i % 2
        mine = jnp.logical_and(jnp.logical_and(zt == z, xx == x), c == back_c)
        return R.at.at[i], R.att.at[z % 2, g], at(zt, xx, y, back_c), at_r + (z % 2) * 4 + g, mine, None

    at_start = net.series(8, at_copy)

    def attend_tile(step, _):
        t = (z + step) % NZ
        where = pl.ds(pl.multiple_of(t * 256, 256), 256)
        for pair in range(2):
            cols, qcols, kcols, vcols = pair_columns(pair)
            q = R.qkv[where, qcols]
            mixed = None
            for e in range(2):
                h = pair * 2 + e
                scores = nt(only(q, e), R.qkv[:, kcols])
                scores = (scores.reshape(4, 64, 1024) + R.bias[h * 4 + t][:, None, :]).reshape(256, 1024)
                top = jnp.max(scores, axis=-1, keepdims=True)
                grown = jnp.exp(scores - top)
                total = jnp.sum(grown, axis=-1, keepdims=True)
                low = (grown * (1.0 / total)).astype(bf16)
                R.lse[where, h:h + 1] = top + jnp.log(total)
                got = nn(low, R.qkv[:, vcols])
                mixed = got if e == 0 else jnp.where(low_lane, mixed, got)
            R.at[pl.ds(2 * t, 2), :, cols] = mixed.astype(bf16).reshape(2, 128, 128)
        at_start(2 * t)
        at_start(2 * t + 1)
        return 0

    def attend(low, high):
        lax.fori_loop(low, high, attend_tile, 0)

    ax, ay = (x + flip) % 2, (y + c) % 2
    bx, by = (x + c) % 2, (y + flip) % 2
    near, far = at(z, ax, ay, c), at(z, bx, by, c)
    wo_a, wo_b, wo_d, wo_s = net.slots(1), net.slots(1), net.slots(1), net.slots(1)

    def wo_column(xx, yy):
        return R.wo.at[:, xx, yy, c]

    def w1_step(k):
        part = z_take(w1_piece, w1z, "w", k)
        net.send(part, part, yn, w1y + k, "w")

    def w2_step(k):
        part = z_take(w2_piece, w2z, "w", k)
        net.send(part, part, yn, w2y + k, "w")

    for k in (1, 2, 3):
        z_take(wo_piece, woz, "w", k)
    net.send(wo_column(x, y), wo_column(x, y), near, wo_a, "w")
    net.send(wo_column(x, y), wo_column(x, y), far, wo_b, "w")
    attend(1, 2)
    net.arrive(wo_column(ax, ay), wo_a)
    net.send(wo_column(ax, ay), wo_column(ax, ay), far, wo_d, "w")
    w1_step(1)
    attend(2, 3)
    dy_begin()
    w1_step(2)
    attend(3, 4)
    w1_step(3)
    attend(4, 5)
    dy_step()
    net.arrive(wo_column(bx, by), wo_b)
    net.arrive(wo_column(xo, yo), wo_d)
    net.send(R.wo.at[:, :, :, c], R.wo.at[:, :, :, c], sib, wo_s, "w")
    net.arrive(R.wo.at[:, :, :, flip], wo_s)
    for b in range(2):
        for h in range(4):
            net.arrive(R.att.at[b, h], at_r + b * 4 + h)
    z_start(w2_piece, w2z, "w")
    net.send(w2_piece(z), w2_piece(z), yn, w2y + 0, "w")

    def outflow():
        for n in range(4):
            cols = slice(n * 256, n * 256 + 256)
            made = x_in[:, :, :, cols].reshape(256, 256).astype(f32)
            for h in range(4):
                made = made + nn(
                    R.att[:, h].reshape(256, 256),
                    R.wo[h, :, :, :, :, cols].reshape(256, 256),
                )
            R.mid[:, cols] = made
        for k in range(2):
            where = slice(k * 128, k * 128 + 128)
            scaled, _inverse = row_stats(R.mid[where, :])
            R.nt2[g, where, :] = (scaled * R.vec[2:3, :] + R.vec[3:4, :]).astype(bf16)

    outflow()
    nt_begin()

    for k in range(4):
        net.arrive(R.w1.at[order[k], :, yo], w1y + k)

    def widen_rows(which):
        def widen(j, _):
            where = pl.ds(pl.multiple_of(j * 256, 256), 256)
            pre = nn(R.nt2[which], R.w1[:, :, :, :, :, where].reshape(1024, 256))
            pre = pre + R.b1[:, where]
            share = 0.5 * (1.0 + lax.erf(pre * (2.0 ** -0.5)))
            R.act[which, :, where] = (pre * share).astype(bf16)
            slope = share + pre * (jnp.exp(-0.5 * pre * pre) * (1.0 / (2.0 * jnp.pi) ** 0.5))
            R.gp[which, :, where] = slope.astype(bf16)
            return 0

        loop(4, widen)

    widen_rows(members[0])
    w2_step(1)
    nt_take(1)
    widen_rows(members[1])
    nt_step()
    w2_step(2)
    widen_rows(members[2])
    nt_take(3)
    w2_step(3)
    widen_rows(members[3])
    dy_take(1)
    dy_take(3)

    def outer_two(j, _):
        where = pl.ds(pl.multiple_of(j * 256, 256), 256)
        made = tn(R.act[:, :, where].reshape(1024, 256), R.dyx[...].reshape(1024, 1024))
        R.dw2[j] = made.astype(bf16).reshape(2, 128, 1024)
        return 0

    loop(4, outer_two)

    def scatter(piece, away, landing_y, landing_z, landing_v, name):
        base_y, base_z, base_v = net.slots(4), net.slots(4), net.slots(1)

        def begin(ks=(3, 2, 1, 0)):
            for k in ks:
                net.send(away(order[k]), landing_y.at[order[k]], yn, base_y + k, name)

        def add(ref, other):
            ref[...] = (ref[...].astype(f32) + other[...].astype(f32)).astype(bf16)

        def take(k):
            net.arrive(landing_y.at[order[k]], base_y + k)
            add(piece(order[k]), landing_y.at[order[k]])

        def along(k):
            part = piece(order[k])
            if k == 3:
                net.send(part, landing_v, at(order[1], x, y, c), base_v, name, made=jnp.logical_not(middle))

                @pl.when(middle)
                def pass_on():
                    net.arrive(landing_v, base_v)
                    add(part, landing_v)

                net.send(part, landing_z.at[z], at(order[3], x, y, c), base_z + z, name, made=middle)
            else:
                net.send(part, landing_z.at[z], at(order[k], x, y, c), base_z + z, name)

        def final(out):
            out[...] = piece(z)[...].astype(f32)
            for k in (1, 2):
                net.arrive(landing_z.at[order[k]], base_z + order[k])
                out[...] += landing_z[order[k]].astype(f32)

            @pl.when(middle)
            def from_end():
                net.arrive(landing_z.at[order[3]], base_z + order[3])
                out[...] += landing_z[order[3]].astype(f32)

        return begin, take, along, final

    two_begin, two_take, two_along, two_final = scatter(
        lambda zz: R.dw2.at[zz, y], lambda zz: R.dw2.at[zz, yo], R.r2y, R.r2z, R.r2v, "s2"
    )

    for k in range(4):
        net.arrive(R.w2.at[order[k], yo], w2y + k)
    two_begin()

    def narrow_back_rows(which):
        def narrow_back(j, _):
            where = pl.ds(pl.multiple_of(j * 256, 256), 256)
            made = nt(R.dyx[which], R.w2[j].reshape(256, 1024)) * R.gp[which, :, where].astype(f32)
            R.gp[which, :, where] = made.astype(bf16)
            return 0

        loop(4, narrow_back)

    def group_reduce(product, sent, landing, landing_x, kept):
        slot_s, slot_x = net.slots(2), net.slots(1)
        for which, where in ((members[3], xo), (members[2], None), (members[1], x), (members[0], None)):
            if which is members[0]:
                product(which, kept)
            else:
                product(which, sent.at[which])
            if where is not None:
                net.send(sent.at[which], landing.at[where], sib, slot_s + where)
            elif which is members[2]:
                net.arrive(landing.at[xo], slot_s + xo)
                sent[which] = (sent[which].astype(f32) + landing[xo].astype(f32)).astype(bf16)
                net.send(sent.at[which], landing_x, xn, slot_x)

        def finish():
            net.arrive(landing.at[x], slot_s + x)
            net.arrive(landing_x, slot_x)

        return finish

    def grad_norm_part(which, out):
        narrow_back_rows(which)

        def back(n, _):
            made = nt(R.gp[which], R.w1[n].reshape(256, 1024))
            out[:, pl.ds(pl.multiple_of(n * 256, 256), 256)] = made.astype(out.dtype)
            return 0

        loop(4, back)

    gn_finish = group_reduce(grad_norm_part, R.gps, R.gpr, R.gpx, R.own)
    net.settle("w")

    def outer_one(n, _):
        left = R.nt2[:, :, pl.ds(pl.multiple_of(n * 256, 256), 256)].reshape(1024, 256)
        made = tn(left, R.gp[...].reshape(1024, 1024)).astype(bf16)
        R.w1[n] = made.reshape(2, 2, 2, 32, 1024)
        return 0

    loop(4, outer_one)
    one_begin, one_take, one_along, one_final = scatter(
        w1_piece, lambda zz: R.w1.at[zz, :, yo], R.r1y, R.r1z, R.r1v, "s1"
    )
    one_begin()

    gn_finish()
    sums = [jnp.zeros((1, 1024), f32) for _ in range(3)]

    def norm_two_back():
        for k in range(4):
            where = slice(k * 64, k * 64 + 64)
            grad = R.own[where, :] + R.gpr[x, where, :].astype(f32) + R.gpx[where, :].astype(f32)
            scaled, inverse = row_stats(R.mid[where, :])
            flow = dy_in[k // 2, (k % 2) * 64:(k % 2) * 64 + 64, :].astype(f32)
            sums[0] = sums[0] + column_sum(grad * scaled)
            sums[1] = sums[1] + column_sum(grad)
            sums[2] = sums[2] + column_sum(flow)
            total = flow + norm_pullback(grad, scaled, inverse, R.vec[2:3, :])
            R.gm[where, :] = total
            R.gb[where, :] = total.astype(bf16)

    norm_two_back()

    do_r = net.slots(8)

    def outflow_back(h, _):
        made = nt(R.gb[...], R.wo[h].reshape(256, 1024)).astype(bf16)
        R.da[:, h] = made.reshape(2, 128, 256)
        return 0

    loop(4, outflow_back)
    for b in range(2):
        for xx in (x, xo):
            for cc in (c, flip):
                zt = 2 * c + b
                net.send(
                    R.da.at[b, 2 * xx + cc],
                    R.do.at[s],
                    at(zt, xx, y, cc),
                    do_r + s,
                    is_self=jnp.logical_and(zt == z, jnp.logical_and(xx == x, cc == c)),
                )


    def outer_flow():
        for h in range(4):
            made = tn(R.att[:, h].reshape(256, 256), R.gb[...]).astype(bf16)
            R.wo[h] = made.reshape(2, 2, 2, 32, 1024)

    outer_flow()
    ros_s = net.slots(1)
    net.send(R.wo.at[:, :, :, flip], R.ros, sib, ros_s)

    def contract_part(which, out):
        def forth(n, _):
            cols = pl.ds(pl.multiple_of(n * 256, 256), 256)
            made = nn(R.act[which], R.w2[:, :, :, cols].reshape(1024, 256))
            out[:, cols] = made.astype(out.dtype)
            return 0

        loop(4, forth)

    out_finish = group_reduce(contract_part, R.ops, R.opr, R.opx, R.own)
    for k in (3, 2, 1, 0):
        two_take(k)
        if k:
            two_along(k)

    def note(which, row, line):
        for r in range(8):
            R.sg[which, r, row:row + 1, :] = line[:, r * 128:(r + 1) * 128]

    def small_begin(which):
        base = net.slots(8)
        for k in (3, 2, 1, 0):
            for xx in (xo, x):
                if k == 0 and xx is x:
                    continue
                zt = order[k]
                net.send(R.sg.at[which, zt * 2 + xx], R.rsg.at[which, s], at(zt, xx, y, c), base + s)
        return base

    def small_middle(which, base):
        total = R.sg[which, s]
        for k in (1, 2, 3, 0):
            for xx in (x, xo):
                if k == 0 and xx is x:
                    continue
                i = order[k] * 2 + xx
                net.arrive(R.rsg.at[which, i], base + i)
                total = total + R.rsg[which, i]
        R.sgt[which] = total
        slot = net.slots(4)
        for yy, cc in ((y, flip), (yo, c), (yo, flip)):
            net.send(R.sgt.at[which], R.rst.at[which, 2 * y + c], at(z, x, yy, cc), slot + 2 * y + c)
        return slot

    def small_end(which, slot):
        row = lax.broadcasted_iota(jnp.int32, (8, 128), 0)
        total = R.sgt[which]
        for yy, cc in ((y, flip), (yo, c), (yo, flip)):
            i = 2 * yy + cc
            net.arrive(R.rst.at[which, i], slot + i)
            got = R.rst[which, i]
            total = total + (got if cc is c else jnp.where(row < 5, got, 0.0))
        return total

    for k in range(3):
        note(0, 2 + k, sums[k])
    up = [jnp.zeros((1, 1024), f32)]

    def up_sum():
        for k in range(16):
            rows = slice((k % 4) * 64, (k % 4) * 64 + 64)
            up[0] = up[0] + column_sum(R.gp[k // 4, rows, :].astype(f32))

    up_sum()
    for q in range(8):
        R.sg[0, 2 * (q // 2) + x, 5 + q % 2:6 + q % 2, :] = up[0][:, q * 128:(q + 1) * 128]
    early = small_begin(0)

    def attend_back(pair):
        cols, qcols, kcols, vcols = pair_columns(pair)
        R.dk[...] = jnp.zeros((1024, 128), f32)
        R.dv[...] = jnp.zeros((1024, 128), f32)

        def tile(step, _):
            t = (z + step) % NZ
            where = pl.ds(pl.multiple_of(t * 256, 256), 256)
            two = pl.ds(2 * t, 2)
            if pair == 0:
                for k in range(2):
                    net.arrive(R.do.at[2 * t + k], do_r + 2 * t + k)
            q = R.qkv[where, qcols]
            grad = R.do[two, :, cols].reshape(256, 128)
            prod = grad.astype(f32) * R.at[two, :, cols].reshape(256, 128).astype(f32)
            query = None
            for e in range(2):
                h = pair * 2 + e
                qe, ge = only(q, e), only(grad, e)
                scores = nt(qe, R.qkv[:, kcols])
                scores = (scores.reshape(4, 64, 1024) + R.bias[h * 4 + t][:, None, :]).reshape(256, 1024)
                chances = jnp.exp(scores - R.lse[where, h:h + 1])
                central = jnp.sum(only(prod, e), axis=-1, keepdims=True)
                moved = nt(ge, R.qkv[:, vcols])
                back = (chances * (moved - central)).astype(bf16)
                R.dv[...] += tn(chances.astype(bf16), ge)
                R.dk[...] += tn(back, qe)
                got = nn(back, R.qkv[:, kcols])
                query = got if e == 0 else jnp.where(low_lane, query, got)
            R.qkv[where, qcols] = (query * 0.125).astype(bf16)
            return 0

        lax.fori_loop(0, 4, tile, 0)
        R.qkv[:, kcols] = R.dk[...].astype(bf16)
        R.qkv[:, vcols] = R.dv[...].astype(bf16)

    def outer_in_pair(pair):
        def outer_in(n, _):
            rows = pl.ds(pl.multiple_of(n * 256, 256), 256)
            made = tn(R.n1[:, :, rows].reshape(1024, 256), R.qkv[:, pair * 384:pair * 384 + 384])
            R.dwq[pair, n] = made.astype(bf16).reshape(2, 2, 2, 32, 384)
            return 0

        loop(4, outer_in)
        steps = scatter(
            lambda zz: R.dwq.at[pair, zz, :, y],
            lambda zz: R.dwq.at[pair, zz, :, yo],
            R.rqy.at[pair],
            R.rqz.at[pair],
            R.rqv.at[pair],
            None,
        )
        steps[0]()
        return steps

    attend_back(0)
    for k in (3, 2, 1, 0):
        one_take(k)
        if k:
            one_along(k)
    net.arrive(R.ros, ros_s)
    for k in range(4):
        R.wo[k, :, :, c] = (R.wo[k, :, :, c].astype(f32) + R.ros[k].astype(f32)).astype(bf16)
    roa_s, rob_s, rof_s, roz_s = net.slots(1), net.slots(1), net.slots(1), net.slots(4)
    net.send(wo_column(xo, yo), R.roa, far, roa_s)
    net.send(wo_column(bx, by), R.rob, far, rob_s)
    q0_begin, q0_take, q0_along, q0_final = outer_in_pair(0)
    early = small_middle(0, early)
    out_finish()
    for k in range(2):
        where = slice(k * 128, k * 128 + 128)
        total = R.mid[where, :] + R.own[where, :] + R.opr[x, where, :].astype(f32)
        out_ref[k] = (total + R.opx[where, :].astype(f32) + R.vec[4:5, :]).astype(bf16)
    leaving[0].start()
    attend_back(1)

    net.settle("xr")

    def unproject(step, _):
        t = (z + 1 + step) % NZ
        where = pl.ds(pl.multiple_of(t * 256, 256), 256)
        made = nt(R.qkv[where, :], R.wq[...].reshape(1024, 768)).astype(bf16)
        R.xr[pl.ds(2 * t, 2)] = made.reshape(2, 2, 64, 1024)
        gs_start(t)
        return 0

    rgs_s, rgx_s, gnr_s = net.slots(4), net.slots(4), net.slots(4)
    gs_start = net.series(
        4,
        lambda t: (
            R.xr.at[pl.ds(2 * t, 2), flip], R.rgs.at[pl.ds(2 * t, 2)], sib, rgs_s + t, None, None
        ),
    )
    loop(4, unproject)

    for k in (3, 2, 1, 0):
        q0_take(k)
        if k:
            q0_along(k)
    q1_begin, q1_take, q1_along, q1_final = outer_in_pair(1)
    for k in (3, 2, 1, 0):
        zt = order[k]
        i = zt * 2 + xo
        net.arrive(R.rgs.at[pl.ds(2 * zt, 2)], rgs_s + zt)
        R.xr[i, c] = (R.xr[i, c].astype(f32) + R.rgs[i].astype(f32)).astype(bf16)
        net.send(R.xr.at[i, c], R.rgx.at[zt], xn, rgx_s + k)
    net.arrive(R.roa, roa_s)
    part = wo_column(ax, ay)
    part[...] = (part[...].astype(f32) + R.roa[...].astype(f32)).astype(bf16)
    net.send(part, R.rof, near, rof_s)
    for k in (3, 2, 1, 0):
        zt = order[k]
        i = zt * 2 + x
        net.arrive(R.rgx.at[zt], rgx_s + k)
        R.xr[i, c] = (
            R.xr[i, c].astype(f32) + R.rgs[i].astype(f32) + R.rgx[zt].astype(f32)
        ).astype(bf16)
        net.send(
            R.xr.at[i, c],
            R.gnr.at[z % 2, c],
            at(zt, x, y, back_c),
            gnr_s + 2 * (z % 2) + c,
            is_self=jnp.logical_and(zt == z, c == back_c),
        )
    for k in (3, 2, 1, 0):
        q1_take(k)
        if k:
            q1_along(k)

    net.arrive(R.rob, rob_s)
    net.arrive(R.rof, rof_s)
    part = wo_column(x, y)
    part[...] = (part[...].astype(f32) + R.rob[...].astype(f32) + R.rof[...].astype(f32)).astype(bf16)
    for k in (1, 2, 3):
        net.send(wo_piece(order[k]), R.roz.at[z], at(order[k], x, y, c), roz_s + z)


    r1f_s, rqf_s = net.slots(4), net.slots(4)
    one_final(R.f1)
    R.f1b[...] = R.f1[...].astype(bf16)
    for xx, cc, dev in group:
        net.send(R.f1b.at[xx, cc], R.r1f.at[g], dev, r1f_s + g)
    R.r1f[g] = R.f1b[x, c]
    two_final(dw2_ref)
    leaving[5].start()
    sums = [jnp.zeros((1, 1024), f32) for _ in range(2)]
    for k in range(4):
        net.arrive(R.gnr.at[k // 2, k % 2], gnr_s + k)
        rows = slice((k % 2) * 64, (k % 2) * 64 + 64)
        grad = R.gnr[k // 2, k % 2].astype(f32)
        scaled, inverse = row_stats(x_in[k // 2, k % 2].astype(f32))
        sums[0] = sums[0] + column_sum(grad * scaled)
        sums[1] = sums[1] + column_sum(grad)
        gx_ref[k // 2, rows, :] = R.gm[k * 64:(k + 1) * 64, :] + norm_pullback(
            grad, scaled, inverse, R.vec[0:1, :]
        )
    leaving[1].start()
    for k in range(2):
        note(1, k, sums[k])
    late = small_begin(1)

    q0_final(R.fq.at[:, :, :, 0:384])
    late = small_middle(1, late)
    q1_final(R.fq.at[:, :, :, 384:768])
    R.fqb[...] = R.fq[...].astype(bf16)
    for xx, cc, dev in group:
        net.send(R.fqb.at[xx, cc], R.rqf.at[g], dev, rqf_s + g)
    R.rqf[g] = R.fqb[x, c]

    dwo_ref[...] = wo_piece(z)[...].astype(f32)
    for k in (1, 2, 3):
        net.arrive(R.roz.at[order[k]], roz_s + order[k])
        dwo_ref[...] += R.roz[order[k]].astype(f32)
    leaving[3].start()
    for xx, cc, dev in group:
        net.arrive(R.r1f.at[2 * xx + cc], r1f_s + 2 * xx + cc)
    for h in range(4):
        for q in range(8):
            block = 8 * (q // 2) + 4 * (h // 2) + 2 * (q % 2) + h % 2
            dw1_ref[:, block * 128:(block + 1) * 128] = R.r1f[h, :, q * 128:(q + 1) * 128].astype(f32)
    leaving[4].start()
    for xx, cc, dev in group:
        net.arrive(R.rqf.at[2 * xx + cc], rqf_s + 2 * xx + cc)
    for h in range(4):
        for t in range(3):
            for pair in range(2):
                src = pair * 384 + t * 128
                dst = t * 1024 + h * 256 + pair * 128
                dwq_ref[:, dst:dst + 128] = R.rqf[h, :, src:src + 128].astype(f32)
    leaving[2].start()
    total = small_end(0, early) + small_end(1, late)
    sg_ref[...] = pltpu.roll(total, (128 - 32 * d) % 128, 1)
    sg_ref[5:6, :] = jnp.where(y == 0, total[5:6, :], total[6:7, :])
    net.settle(everything=True)
    for copy in leaving:
        copy.wait()


def local_fused(
    arriving_features,
    valid_extents,
    sampled_target_tiles,
    query_context_mapping,
    attention_outflow_weights,
    expansion_weights,
    contraction_weights,
    opening_scale_vector,
    opening_shift_vector,
    closing_scale_vector,
    closing_shift_vector,
    expansion_shift,
    contraction_shift,
    output_sensitivity,
):
    shapes = (
        (arriving_features.shape, bf16),
        (arriving_features.shape, f32),
        (query_context_mapping.shape, f32),
        (attention_outflow_weights.shape, f32),
        (expansion_weights.shape, f32),
        (contraction_weights.shape, f32),
        ((8, 128), f32),
    )
    whole = pl.BlockSpec(memory_space=pltpu.VMEM)
    scalars = pl.BlockSpec(memory_space=pltpu.SMEM)
    place = pl.BlockSpec(memory_space=pl.ANY)
    made = pl.pallas_call(
        layer_kernel,
        name="layer",
        out_shape=[jax.ShapeDtypeStruct(a, b) for a, b in shapes],
        in_specs=[place] * 2 + [scalars, whole] + [place] * 4 + [whole] * 6,
        out_specs=[place] * 6 + [whole],
        scratch_shapes=[pltpu.VMEM(a, b) for a, b in SCRATCH.values()]
        + [
            pltpu.SemaphoreType.DMA((SENDS,)),
            pltpu.SemaphoreType.DMA((RECVS,)),
            pltpu.SemaphoreType.DMA((12,)),
        ],
        compiler_params=pltpu.CompilerParams(
            collective_id=0, has_side_effects=True, vmem_limit_bytes=VMEM_BYTES
        ),
    )(
        arriving_features.reshape(2, 2, 64, 1024),
        output_sensitivity,
        valid_extents,
        sampled_target_tiles,
        query_context_mapping,
        attention_outflow_weights,
        expansion_weights,
        contraction_weights,
        opening_scale_vector.reshape(1, 32),
        opening_shift_vector.reshape(1, 32),
        closing_scale_vector.reshape(1, 32),
        closing_shift_vector.reshape(1, 32),
        expansion_shift.reshape(1, 128),
        contraction_shift.reshape(1, 32),
    )
    rows = ((1, 32), (1, 32), (1, 32), (1, 32), (1, 128), (1, 32))
    done = pl.pallas_call(
        leave_kernel,
        name="leave",
        out_shape=[jax.ShapeDtypeStruct(a, b) for a, b in shapes[:6]]
        + [jax.ShapeDtypeStruct(a, f32) for a in rows],
        in_specs=[place] * 6 + [whole],
        out_specs=[place] * 6 + [whole] * 6,
        scratch_shapes=[pltpu.VMEM(a, b) for a, b in shapes[:6]]
        + [pltpu.SemaphoreType.DMA((6,)), pltpu.SemaphoreType.DMA((6,))],
    )(*made)
    return tuple(done[:6]) + tuple(line.reshape(-1) for line in done[6:])


def leave_kernel(*refs):
    large, small, out, rows, held = refs[:6], refs[6], refs[7:13], refs[13:19], refs[19:25]
    come, go = refs[25:]
    for k in range(6):
        pltpu.make_async_copy(large[k], held[k], come.at[k]).start()
    for k, row in enumerate((0, 1, 2, 3, 5, 4)):
        rows[k][...] = small[row:row + 1, :rows[k].shape[1]]
    for k in range(6):
        pltpu.make_async_copy(large[k], held[k], come.at[k]).wait()
        pltpu.make_async_copy(held[k], out[k], go.at[k]).start()
    for k in range(6):
        pltpu.make_async_copy(held[k], out[k], go.at[k]).wait()


def fits_fused(mesh, arguments):
    features, tiles, expand = arguments[0], arguments[2], arguments[5]
    return (
        dict(mesh.shape) == {"seq": 8, "doc": 4}
        and features.shape == (8, 1024, 1024)
        and tiles.shape == (8, 16, 16, 3)
        and expand.shape == (1024, 4096)
    )


def solution(mesh):
    in_specs = (
        P("doc", "seq", None),
        P("doc"),
        P("doc", None, None, None),
        P(("seq", "doc"), None),
        P(("seq", "doc"), None),
        P(("seq", "doc"), None),
        P(("seq", "doc"), None),
        P(("seq", "doc")),
        P(("seq", "doc")),
        P(("seq", "doc")),
        P(("seq", "doc")),
        P(("seq", "doc")),
        P(("seq", "doc")),
        P("doc", "seq", None),
    )
    out_specs = (
        P("doc", "seq", None),
        P("doc", "seq", None),
        P(("seq", "doc"), None),
        P(("seq", "doc"), None),
        P(("seq", "doc"), None),
        P(("seq", "doc"), None),
        P(("seq", "doc")),
        P(("seq", "doc")),
        P(("seq", "doc")),
        P(("seq", "doc")),
        P(("seq", "doc")),
        P(("seq", "doc")),
    )

    def run(*arguments):
        body = local_fused if fits_fused(mesh, arguments) else local
        mapped = jax.shard_map(
            body, mesh=mesh, in_specs=in_specs, out_specs=out_specs, check_vma=False
        )
        return mapped(*arguments)

    return run
```
